32 devices in a mesh: expert: 8 (over y, x, core), tensor: 4 (over z).
Axes of the slice: x: 2, y: 2, z: 4, core: 2. Of those that a mesh axis runs over, the one named last changes fastest.
Arguments:
- tokens: bfloat16 [3072, 2048], P('expert'), may hold values from -6 to 6
- w_query: bfloat16 [2048, 2048], P(None, 'tensor'), may hold values from -0.125 to 0.125
- w_key: bfloat16 [2048, 2048], P(None, 'tensor'), may hold values from -0.125 to 0.125
- w_value: bfloat16 [2048, 2048], P(None, 'tensor'), may hold values from -0.125 to 0.125
- w_out: bfloat16 [2048, 2048], P('tensor'), may hold values from -0.5 to 0.5
- attn_gain: float32 [2048], replicated, may hold values from 0.5 to 1.5
- ffn_gain: float32 [2048], replicated, may hold values from 0.5 to 1.5
- qk_gain: float32 [2, 2048], P(None, 'tensor'), may hold values from 1 to 2
- router: bfloat16 [2048, 16], replicated, may hold values from -0.0625 to 0.0625
- w_gate: bfloat16 [16, 2048, 1024], P('expert', None, 'tensor'), may hold values from -0.125 to 0.125
- w_up: bfloat16 [16, 2048, 1024], P('expert', None, 'tensor'), may hold values from -0.125 to 0.125
- w_down: bfloat16 [16, 1024, 2048], P('expert', 'tensor'), may hold values from -4 to 4
- routes: int32 [3072, 8], P('expert'), may hold values from 0 to 15, all different within a row; in each aligned block of 384 rows (0 to 383, 384 to 767, ...) at most 288 rows name the same one
- cont_group: int32 [8], P('expert'), may hold values from 0 to 1, as said below
- cotangent: bfloat16 [3072, 2048], P('expert'), may hold values from -6 to 6
Outputs:
- output: bfloat16 [3072, 2048], P('expert')
- input_grad: float32 [3072, 2048], P('expert')
- w_query_grad: float32 [2048, 2048], P('expert', 'tensor')
- w_key_grad: float32 [2048, 2048], P('expert', 'tensor')
- w_value_grad: float32 [2048, 2048], P('expert', 'tensor')
- w_out_grad: float32 [2048, 2048], P('tensor', 'expert')
- attn_gain_grad: float32 [2048], P('expert')
- ffn_gain_grad: float32 [2048], P('expert')
- qk_gain_grad: float32 [2, 2048], P(None, ('tensor', 'expert'))
- router_grad: float32 [2048, 16], P('expert')
- w_gate_grad: float32 [16, 2048, 1024], P('expert', None, 'tensor')
- w_up_grad: float32 [16, 2048, 1024], P('expert', None, 'tensor')
- w_down_grad: float32 [16, 1024, 2048], P('expert', 'tensor')
The draws below stay inside these ranges and needn't reach their ends.
Inputs may be any that keep to these rules, and one draw needn't show every extreme that they name: `routes`: within the rows of one index of expert no expert is named more than 288 times, and in every draw some expert is named exactly 288 times by one index's rows. `cont_group`: every prompt is named by exactly 4 continuations.
All inputs are finite; a program needn't handle non-finite values.
Results may differ from the reference program's by a relative error of at most 0.025.
Values may be sent and summed in bfloat16 or wider, within the bound.
A program may use at most 320 MiB of HBM per device.

```python
import math
import jax
import jax.numpy as jnp
import numpy as np
from jax import lax

D = 2048
HEADS = 16
HD = 128
FF = 1024
TOPK = 8
PROMPT_DEV = 128
CLEN = 256
CONT_DEV = 1
TOK_DEV = 384
TOKENS = 3072
EXPERTS = 16
CAP = 288
PSPAN = 4
CONTS = 8
N_EXPERT = 8
N_TENSOR = 4


def draw_cont_group(key, part):
    key = jax.random.fold_in(key, 7)
    order = jax.random.permutation(key, CONTS)
    return (order // (CONT_DEV * PSPAN)).astype(jnp.int32)


def strengthened(values, key, source, target, shards_of, factor):
    def block_of(dim):
        return (jnp.arange(values.shape[dim]) // (values.shape[dim] // shards_of)).reshape((-1,) + (1,) * (values.ndim - 1 - dim))

    one_side = jax.random.permutation(key, shards_of)[block_of(target)]
    other_side = (block_of(target) + shards_of // 2) % shards_of
    return jnp.where((block_of(source) == one_side) | (block_of(source) == other_side), factor * values, values)


def block_scale(rng, shape, shards, low, largest):
    def one(dim, blocks):
        heights = jax.random.uniform(jax.random.fold_in(jax.random.fold_in(rng, 6), dim), (blocks,), jnp.float32, low / len(shards), largest / len(shards))
        return jnp.repeat(jnp.exp(heights), shape[dim] // blocks).reshape((-1,) + (1,) * (len(shape) - dim - 1))

    factor_of = one(*shards[0])
    for cut in shards[1:]:
        factor_of = factor_of * one(*cut)
    return factor_of


def routed_block(rng, own, number, rows, count, top, bound, lean):
    sequence = jax.random.permutation(rng, count)
    crowded, common = load_shares(count, rows * top, bound, lean, True), load_shares(count, rows * top, bound, lean, False)
    places = jnp.arange(count)

    def named(sizes, offset_by):
        used = int((sizes > 0).sum())
        fixed = max(1, used // 4)
        moved = fixed + (places - fixed + offset_by * (used - fixed)) % max(1, count - fixed)
        return jnp.zeros((count,), jnp.int32).at[sequence[jnp.where(places < fixed, places, moved)]].set(jnp.asarray(sizes, jnp.int32))

    sizes = jnp.where(number % 4 == 0, named(crowded, number // 4), named(common, number - number // 4 - 1))
    mixed = jax.random.permutation(jax.random.fold_in(own, 3), count)
    source_of, receiver = mixed[0:count // 2 * 2:2], mixed[1:count // 2 * 2:2]
    slack = jnp.minimum(sizes[source_of] - 1, bound - sizes[receiver]) // 2
    slack = jnp.where((source_of == sequence[0]) | (receiver == sequence[0]) | (sizes[receiver] == 0), 0, jnp.maximum(slack, 0))
    moved = jax.random.randint(jax.random.fold_in(own, 4), (count // 2,), 0, 1 << 20) % (slack + 1)
    sizes = sizes.at[source_of].add(-moved).at[receiver].add(moved)
    members = jnp.searchsorted(jnp.cumsum(sizes), jnp.arange(rows * top), side="right").astype(jnp.int32)
    grid = members.reshape(top, rows).T
    grid = grid[jax.random.permutation(jax.random.fold_in(own, 1), rows)]
    offset_by = jax.random.randint(jax.random.fold_in(own, 2), (rows, 1), 0, top)
    return jnp.take_along_axis(grid, (jnp.arange(top)[None, :] + offset_by) % top, axis=1)


def load_shares(number_of, total, most, skew, full):
    loads = [(1 << 20) // math.isqrt(rank ** skew) + 1 for rank in range(1, number_of + 1)]
    largest = most if full else min(most, max(-(-total // number_of), total * loads[0] // sum(loads)))
    least = 1 if total - largest >= number_of - 1 else 0
    given, rest = [largest] + [least] * (number_of - 1), total - largest - least * (number_of - 1)
    while rest > 0:
        movable = [i for i in range(1, number_of) if given[i] < largest] or [i for i in range(1, number_of) if given[i] < most]
        whole, budget = sum([loads[i] for i in movable]), rest
        for i in movable:
            addition = min(most - given[i], max(1, budget * loads[i] // whole), rest)
            given[i] = given[i] + addition
            rest = rest - addition
    return np.array(given)


def bell_draw(key, dims, width, bound, cuts=(), held_as=jnp.bfloat16):
    gain = block_scale(key, dims, cuts, -0.22, 0.18) if cuts else 1.0
    entries = jax.random.normal(key, dims, jnp.float32) * width * gain
    return jnp.minimum(jnp.maximum(entries, -bound), bound).astype(held_as)


def noise_with(key, dims, width, most, pieces, heavy, kind=jnp.bfloat16):
    values = width * jax.random.normal(key, dims, jnp.float32)
    if pieces:
        values = values * block_scale(key, dims, pieces, -0.22, 0.18)
    return jnp.clip(strengthened(values, jax.random.fold_in(key, 3), *heavy), -most, most).astype(kind)


def setup_inputs(seed: int = 0) -> dict:
    key_of = jax.random.split(jax.random.key(seed), 16)
    tokens = noise_with(key_of[0], (TOKENS, D), 1.0, 6.0, ((0, 8),), (0, 1, 8, 2.0))
    w_query = bell_draw(key_of[1], (D, D), D ** -0.5, 0.125, ((1, 4),))
    w_key = bell_draw(key_of[2], (D, D), D ** -0.5, 0.125, ((1, 4),))
    w_value = bell_draw(key_of[3], (D, D), D ** -0.5, 0.125, ((1, 4),))
    w_out = bell_draw(key_of[4], (D, D), (D // 16) ** -0.5, 0.5, ((0, 4),))
    attn_gain = jnp.clip(1.0 + 0.1 * jax.random.normal(key_of[5], (D,), jnp.float32), 0.5, 1.5)
    ffn_gain = jnp.clip(1.0 + 0.1 * jax.random.normal(key_of[6], (D,), jnp.float32), 0.5, 1.5)
    qk_gain = jnp.clip(1.0 + 1.0 * jax.random.uniform(key_of[7], (2, D), jnp.float32) ** block_scale(key_of[7], (2, D), ((1, 4),), -0.2, 0.2), 1.0, 2.0)
    router = bell_draw(key_of[8], (D, EXPERTS), (4 * D) ** -0.5, 0.0625)
    w_gate = bell_draw(key_of[9], (EXPERTS, D, FF), D ** -0.5, 0.125, ((0, 8), (2, 4)))
    w_up = bell_draw(key_of[10], (EXPERTS, D, FF), D ** -0.5, 0.125, ((0, 8), (2, 4)))
    w_down = bell_draw(key_of[11], (EXPERTS, FF, D), (FF // 1024 + 1) ** -0.5, 4.0, ((0, 8), (1, 4)))
    routes_keys = jax.random.split(jax.random.fold_in(key_of[12], 1), TOKENS // TOK_DEV)
    routes_turns = jax.random.permutation(jax.random.fold_in(key_of[12], 3), TOKENS // TOK_DEV)
    routes = jax.vmap(lambda own, number: routed_block(jax.random.fold_in(key_of[12], 2), own, number, TOK_DEV, EXPERTS, TOPK, CAP, 1))(routes_keys, routes_turns).reshape((TOKENS, TOPK))
    cont_group = draw_cont_group(jax.random.fold_in(key_of[15], 71), 0)
    cotangent = bell_draw(key_of[14], (TOKENS, D), 1.0, 6.0, ((0, 8),))
    return {"tokens": tokens, "w_query": w_query, "w_key": w_key, "w_value": w_value, "w_out": w_out, "attn_gain": attn_gain, "ffn_gain": ffn_gain, "qk_gain": qk_gain, "router": router, "w_gate": w_gate, "w_up": w_up, "w_down": w_down, "routes": routes, "cont_group": cont_group, "cotangent": cotangent}


@jax.custom_vjp
def low(v):
    return lax.optimization_barrier(v.astype(jnp.bfloat16)).astype(jnp.float32)

@jax.custom_vjp
def low_back(v):
    return v

def low_keep(v):
    return (low(v), None)

def low_pass(kept, grad):
    return (grad,)

def back_keep(v):
    return (v, None)

def back_low(kept, grad):
    return (low(grad),)
low.defvjp(low_keep, low_pass)
low_back.defvjp(back_keep, back_low)
epsilon = 1e-05
highest = lax.Precision.HIGHEST

def product(left, right):
    return jnp.dot(left, right, precision=highest, preferred_element_type=jnp.float32)

def rms_scale(field):
    return lax.rsqrt(lax.optimization_barrier(jnp.mean(field * field, axis=-1, keepdims=True)) + epsilon)

def rotate(field, cosine, sine):
    half = field.shape[-1] // 2
    first = field[..., :half]
    second = field[..., half:]
    return jnp.concatenate([first * cosine - second * sine, second * cosine + first * sine], axis=-1)

def layout_tables(cont_group):
    index = jnp.arange(TOKENS, dtype=jnp.int32)
    device = index // TOK_DEV
    local = index % TOK_DEV
    is_prompt = local < PROMPT_DEV
    after = jnp.maximum(local - PROMPT_DEV, 0)
    cont_index = device * CONT_DEV + after // CLEN
    group = jnp.where(is_prompt, device // PSPAN, cont_group[cont_index])
    position = jnp.where(is_prompt, device % PSPAN * PROMPT_DEV + local, PROMPT_DEV * PSPAN + after % CLEN)
    tag = jnp.where(is_prompt, -1, after // CLEN)
    return (group.astype(jnp.int32), position.astype(jnp.int32), tag.astype(jnp.int32))

def rope_tables(position):
    half = HD // 2
    frequency = 10000.0 ** (-jnp.arange(half, dtype=jnp.float32) * 2.0 / HD)
    angle = position.astype(jnp.float32)[:, None] * frequency[None, :]
    return (jnp.cos(angle)[:, None, :], jnp.sin(angle)[:, None, :])

def forward(tokens, w_query, w_key, w_value, w_out, attn_gain, ffn_gain, qk_gain, router, w_gate, w_up, w_down, routes, group, position, tag, cosine, sine):
    normed = low(tokens * rms_scale(tokens) * attn_gain)
    query_raw = low_back(product(normed, w_query))
    key_raw = low_back(product(normed, w_key))
    value_raw = low_back(product(normed, w_value))
    query = query_raw * rms_scale(query_raw) * qk_gain[0]
    key = key_raw * rms_scale(key_raw) * qk_gain[1]
    query = low(rotate(query.reshape(TOKENS, HEADS, HD), cosine, sine))
    key = low(rotate(key.reshape(TOKENS, HEADS, HD), cosine, sine))
    value = low(value_raw).reshape(TOKENS, HEADS, HD)

    def split(field):
        return field.reshape((N_EXPERT, TOK_DEV) + field.shape[1:])
    prompt_key = split(key)[:, :PROMPT_DEV].reshape(N_EXPERT * PROMPT_DEV, HEADS, HD)
    prompt_value = split(value)[:, :PROMPT_DEV].reshape(N_EXPERT * PROMPT_DEV, HEADS, HD)
    key_index = jnp.arange(N_EXPERT * PROMPT_DEV, dtype=jnp.int32)
    key_group = key_index // (PROMPT_DEV * PSPAN)
    key_position = key_index % (PROMPT_DEV * PSPAN)
    factor = HD ** (-0.5)

    def attend(block):
        block_query, block_key, block_value, block_group, block_position, block_tag = block
        prompt_mask = (block_group[:, None] == key_group[None, :]) & (key_position[None, :] <= block_position[:, None])
        own_mask = (block_tag[:, None] == block_tag[None, PROMPT_DEV:]) & (block_position[None, PROMPT_DEV:] <= block_position[:, None])
        mask = jnp.concatenate([prompt_mask, own_mask], axis=1)
        every_key = jnp.concatenate([prompt_key, block_key[PROMPT_DEV:]], axis=0)
        every_value = jnp.concatenate([prompt_value, block_value[PROMPT_DEV:]], axis=0)
        scores = jnp.einsum('qhd,khd->hqk', block_query, every_key, precision=highest) * factor
        scores = jnp.where(mask[None], low_back(scores), -1e+30)
        top = lax.optimization_barrier(jnp.max(scores, axis=-1, keepdims=True))
        weights = jnp.exp(scores - top)
        shares = low(weights / lax.optimization_barrier(jnp.sum(weights, axis=-1, keepdims=True)))
        mixed = jnp.einsum('hqk,khd->qhd', shares, every_value, precision=highest)
        return low(low_back(mixed))
    attended = lax.map(jax.checkpoint(attend), (split(query), split(key), split(value), split(group), split(position), split(tag)))
    attended = attended.reshape(TOKENS, HEADS * HD)
    attention = low_back(product(attended, w_out))
    hidden = tokens + attention
    normed_two = low(hidden * rms_scale(hidden) * ffn_gain)
    logits = low_back(product(normed_two, router))
    top = lax.optimization_barrier(jnp.max(logits, axis=-1, keepdims=True))
    weights = jnp.exp(logits - top)
    chances = weights / lax.optimization_barrier(jnp.sum(weights, axis=-1, keepdims=True))
    gates = jnp.take_along_axis(chances, routes, axis=1).reshape(-1)
    flat = routes.reshape(-1)
    quarter_width = FF // N_TENSOR
    most_rows = N_EXPERT * CAP
    slots = jnp.arange(most_rows, dtype=jnp.int32)

    def expert_step(total, expert):
        hits = flat == expert
        found = jnp.nonzero(hits, size=most_rows, fill_value=0)[0].astype(jnp.int32)
        valid = (slots < jnp.sum(hits.astype(jnp.int32))).astype(jnp.float32)
        token = found // TOPK
        rows = normed_two[token]
        gate_weight = w_gate[expert]
        up_weight = w_up[expert]
        down_weight = w_down[expert]
        summed = jnp.zeros((most_rows, D), jnp.float32)
        for quarter in range(N_TENSOR):
            start = quarter * quarter_width
            part_in = low_back(rows)
            gate_pre = low_back(product(part_in, gate_weight[:, start:start + quarter_width]))
            up_pre = low_back(product(part_in, up_weight[:, start:start + quarter_width]))
            inner = low(jax.nn.silu(gate_pre) * up_pre)
            summed = summed + low(product(inner, down_weight[start:start + quarter_width]))
        summed = low_back(summed)
        return (total.at[token].add((gates[found] * valid)[:, None] * summed), None)
    mixture, unused = lax.scan(jax.checkpoint(expert_step), jnp.zeros((TOKENS, D), jnp.float32), jnp.arange(EXPERTS, dtype=jnp.int32))
    return hidden + mixture

def reference(tokens, w_query, w_key, w_value, w_out, attn_gain, ffn_gain, qk_gain, router, w_gate, w_up, w_down, routes, cont_group, cotangent):
    group, position, tag = layout_tables(cont_group)
    cosine, sine = rope_tables(position)
    floats = [array.astype(jnp.float32) for array in (tokens, w_query, w_key, w_value, w_out, attn_gain, ffn_gain, qk_gain, router, w_gate, w_up, w_down)]

    def closed(*params):
        return forward(*params, routes, group, position, tag, cosine, sine)
    result, pullback = jax.vjp(closed, *floats)
    grads = pullback(cotangent.astype(jnp.float32))
    return (result.astype(jnp.bfloat16), grads[0], grads[1], grads[2], grads[3], grads[4], grads[5], grads[6], grads[7], grads[8], grads[9], grads[10], grads[11])
```

```python
import jax
import jax.numpy as jnp
from jax import lax
from jax.sharding import PartitionSpec as P

HD = 128
PROMPT_DEV = 128
CLEN = 256
CONT_DEV = 1


epsilon = 1e-05
masked_value = -1e30


def rotate(field, cosine, sine):
    half = field.shape[-1] // 2
    first = field[..., :half]
    second = field[..., half:]
    return jnp.concatenate(
        [first * cosine - second * sine, second * cosine + first * sine], axis=-1
    )


def unrotate(grad, cosine, sine):
    half = grad.shape[-1] // 2
    first = grad[..., :half]
    second = grad[..., half:]
    return jnp.concatenate(
        [first * cosine + second * sine, second * cosine - first * sine], axis=-1
    )


def experts(normed_two, cotangent, gates, w_gate, w_up, w_down, experts_total):
    local_experts = w_gate.shape[0]
    device = lax.axis_index("expert")
    arrived = lax.all_gather(normed_two, "expert", axis=0, tiled=True)
    arrived_grad = lax.all_gather(cotangent, "expert", axis=0, tiled=True)
    gate_pre = jnp.einsum("rd,jdf->jrf", arrived, w_gate, preferred_element_type=jnp.float32)
    up_pre = jnp.einsum("rd,jdf->jrf", arrived, w_up, preferred_element_type=jnp.float32)
    raw_grad = jnp.einsum("rd,jfd->jrf", arrived_grad, w_down, preferred_element_type=jnp.float32)
    sigma = jax.nn.sigmoid(gate_pre)
    activated = gate_pre * sigma
    inner = activated * up_pre
    gated = (gates[:, :, None] * inner).astype(jnp.bfloat16)
    mixed_part = jnp.einsum("jrf,jfd->rd", gated, w_down, preferred_element_type=jnp.float32)
    mixture = lax.psum(
        lax.psum_scatter(
            mixed_part.astype(jnp.bfloat16), "expert", scatter_dimension=0, tiled=True
        ),
        "tensor",
    ).astype(jnp.float32)
    gate_grad_part = jnp.sum(raw_grad * inner, axis=2)
    act_grad = gates[:, :, None] * raw_grad
    up_grad = (act_grad * activated).astype(jnp.bfloat16)
    gate_grad = (act_grad * up_pre * sigma * (1.0 + gate_pre * (1.0 - sigma))).astype(jnp.bfloat16)
    grad_w_down = jnp.einsum("jrf,rd->jfd", gated, arrived_grad, preferred_element_type=jnp.float32)
    grad_w_gate = jnp.einsum("rd,jrf->jdf", arrived, gate_grad, preferred_element_type=jnp.float32)
    grad_w_up = jnp.einsum("rd,jrf->jdf", arrived, up_grad, preferred_element_type=jnp.float32)
    slot_grad = jnp.einsum("jrf,jdf->rd", gate_grad, w_gate, preferred_element_type=jnp.float32)
    slot_grad = slot_grad + jnp.einsum(
        "jrf,jdf->rd", up_grad, w_up, preferred_element_type=jnp.float32
    )
    moe_input_grad = lax.psum(
        lax.psum_scatter(
            slot_grad.astype(jnp.bfloat16), "expert", scatter_dimension=0, tiled=True
        ),
        "tensor",
    ).astype(jnp.float32)
    placed = jnp.zeros((arrived.shape[0], experts_total), jnp.float32)
    placed = lax.dynamic_update_slice_in_dim(placed, gate_grad_part.T, device * local_experts, 1)
    chance_grad = lax.psum(
        lax.psum_scatter(placed, "expert", scatter_dimension=0, tiled=True), "tensor"
    )
    return mixture, moe_input_grad, chance_grad, [grad_w_gate, grad_w_up, grad_w_down]


def body(
    tokens,
    w_query,
    w_key,
    w_value,
    w_out,
    attn_gain,
    ffn_gain,
    qk_gain,
    router,
    w_gate,
    w_up,
    w_down,
    routes,
    cont_group,
    cotangent,
):
    rows, width = tokens.shape
    local_width = w_query.shape[1]
    head_count = local_width // HD
    experts_total = router.shape[1]
    local_experts = w_gate.shape[0]
    ranks = lax.axis_size("expert")
    device = lax.axis_index("expert")
    span = ranks // 2
    prompt_len = PROMPT_DEV * span
    factor = HD ** (-0.5)
    local = jnp.arange(rows, dtype=jnp.int32)
    is_prompt = local < PROMPT_DEV
    after = jnp.maximum(local - PROMPT_DEV, 0)
    slot_cont = after // CLEN
    cont_pick = jnp.sum(
        jnp.where(
            slot_cont[:, None] == jnp.arange(CONT_DEV, dtype=jnp.int32)[None, :],
            cont_group[None, :],
            0,
        ),
        axis=1,
    )
    group = jnp.where(is_prompt, device // span, cont_pick)
    position = jnp.where(is_prompt, device % span * PROMPT_DEV + local, prompt_len + after % CLEN)
    tag = jnp.where(is_prompt, -1, slot_cont)
    frequency = 10000.0 ** (-jnp.arange(HD // 2, dtype=jnp.float32) * 2.0 / HD)
    angle = position.astype(jnp.float32)[:, None] * frequency[None, :]
    cosine = jnp.cos(angle)[:, None, :]
    sine = jnp.sin(angle)[:, None, :]
    source = tokens.astype(jnp.float32)
    scale_one = lax.rsqrt(jnp.mean(source * source, axis=1, keepdims=True) + epsilon)
    normed = (source * scale_one * attn_gain).astype(jnp.bfloat16)
    query_raw = jnp.dot(normed, w_query, preferred_element_type=jnp.float32)
    key_raw = jnp.dot(normed, w_key, preferred_element_type=jnp.float32)
    value_raw = jnp.dot(normed, w_value, preferred_element_type=jnp.float32)
    squares = lax.psum(
        jnp.stack(
            [jnp.sum(query_raw * query_raw, axis=1), jnp.sum(key_raw * key_raw, axis=1)], axis=1
        ),
        "tensor",
    )
    scale_query = lax.rsqrt(squares[:, 0:1] / width + epsilon)
    scale_key = lax.rsqrt(squares[:, 1:2] / width + epsilon)
    query_rot = (
        rotate((query_raw * scale_query * qk_gain[0]).reshape(rows, head_count, HD), cosine, sine)
        .reshape(rows, local_width)
        .astype(jnp.bfloat16)
    )
    key_rot = (
        rotate((key_raw * scale_key * qk_gain[1]).reshape(rows, head_count, HD), cosine, sine)
        .reshape(rows, local_width)
        .astype(jnp.bfloat16)
    )
    value_low = value_raw.astype(jnp.bfloat16)
    prompt_keys, prompt_values = (
        lax.all_gather(key_rot[:PROMPT_DEV], "expert", axis=0, tiled=True),
        lax.all_gather(value_low[:PROMPT_DEV], "expert", axis=0, tiled=True),
    )
    prompt_count = prompt_keys.shape[0]
    all_keys = jnp.concatenate([prompt_keys, key_rot[PROMPT_DEV:]], axis=0)
    all_values = jnp.concatenate([prompt_values, value_low[PROMPT_DEV:]], axis=0)
    key_index = jnp.arange(prompt_count, dtype=jnp.int32)
    prompt_mask = (group[:, None] == (key_index // prompt_len)[None, :]) & (
        (key_index % prompt_len)[None, :] <= position[:, None]
    )
    own_mask = (tag[:, None] == tag[None, PROMPT_DEV:]) & (
        position[None, PROMPT_DEV:] <= position[:, None]
    )
    mask = jnp.concatenate([prompt_mask, own_mask], axis=1)

    def head_scores(query_head, key_head):
        scores = (
            jnp.einsum("qd,kd->qk", query_head, key_head, preferred_element_type=jnp.float32)
            * factor
        )
        return jnp.where(mask, scores, masked_value)

    outputs = []
    log_totals = []
    for head in range(head_count):
        start = head * HD
        scores = head_scores(query_rot[:, start : start + HD], all_keys[:, start : start + HD])
        top = jnp.max(scores, axis=1, keepdims=True)
        weights = jnp.exp(scores - top)
        total = jnp.sum(weights, axis=1, keepdims=True)
        shares = (weights / total).astype(jnp.bfloat16)
        outputs.append(
            jnp.dot(shares, all_values[:, start : start + HD], preferred_element_type=jnp.float32)
        )
        log_totals.append(top + jnp.log(total))
    attended = jnp.concatenate(outputs, axis=1).astype(jnp.bfloat16)
    attention = lax.psum(jnp.dot(attended, w_out, preferred_element_type=jnp.float32), "tensor")
    hidden = source + attention
    scale_two = lax.rsqrt(jnp.mean(hidden * hidden, axis=1, keepdims=True) + epsilon)
    normed_two = (hidden * scale_two * ffn_gain).astype(jnp.bfloat16)
    logits = jnp.dot(normed_two, router, preferred_element_type=jnp.float32)
    top = jnp.max(logits, axis=1, keepdims=True)
    weights = jnp.exp(logits - top)
    chances = weights / jnp.sum(weights, axis=1, keepdims=True)
    hits = (routes[:, :, None] == jnp.arange(experts_total, dtype=jnp.int32)[None, None, :]).astype(
        jnp.float32
    )
    rows_mask = jnp.sum(hits, axis=1)
    routed = lax.all_gather(
        (rows_mask * chances).astype(jnp.float32), "expert", axis=0, tiled=True
    )
    gates = lax.dynamic_slice_in_dim(routed, device * local_experts, local_experts, 1).T
    grad_out = cotangent.astype(jnp.float32)
    pieces = max(1, ranks * rows // 4096)
    piece = rows // pieces
    split_gates = gates.reshape(local_experts, ranks, rows)
    results = []
    weight_grads = None
    for number in range(pieces):
        part = slice(number * piece, (number + 1) * piece)
        sources = (normed_two[part], cotangent[part])
        if results:
            sources, results, weight_grads = lax.optimization_barrier(
                (sources, results, weight_grads)
            )
        *result, grads = experts(
            *sources,
            split_gates[:, :, part].reshape(local_experts, ranks * piece),
            w_gate,
            w_up,
            w_down,
            experts_total,
        )
        results.append(result)
        weight_grads = grads if weight_grads is None else [a + b for a, b in zip(weight_grads, grads)]
    mixture, moe_input_grad, chance_grad = (
        jnp.concatenate(list(group_of), axis=0) for group_of in zip(*results)
    )
    grad_w_gate, grad_w_up, grad_w_down = weight_grads
    chance_grad = rows_mask * chance_grad
    output = (hidden + mixture).astype(jnp.bfloat16)
    logit_grad = (
        chances * (chance_grad - jnp.sum(chances * chance_grad, axis=1, keepdims=True))
    ).astype(jnp.bfloat16)
    grad_router = jnp.einsum(
        "td,te->de", normed_two, logit_grad, preferred_element_type=jnp.float32
    )
    normed_two_grad = moe_input_grad + jnp.einsum(
        "te,de->td", logit_grad, router, preferred_element_type=jnp.float32
    )
    weighted_two = ffn_gain * normed_two_grad
    grad_ffn_gain = jnp.sum(normed_two_grad * hidden * scale_two, axis=0)
    hidden_grad = (
        grad_out
        + scale_two * weighted_two
        - hidden * (scale_two**3 / width) * jnp.sum(weighted_two * hidden, axis=1, keepdims=True)
    )
    attention_grad = hidden_grad.astype(jnp.bfloat16)
    grad_w_out = jnp.einsum(
        "td,te->de", attended, attention_grad, preferred_element_type=jnp.float32
    )
    attended_grad = jnp.einsum(
        "te,de->td", attention_grad, w_out, preferred_element_type=jnp.float32
    ).astype(jnp.bfloat16)
    query_grads = []
    key_grads = []
    value_grads = []
    for head in range(head_count):
        start = head * HD
        query_head = query_rot[:, start : start + HD]
        key_head = all_keys[:, start : start + HD]
        value_head = all_values[:, start : start + HD]
        out_grad_head = attended_grad[:, start : start + HD]
        recomputed = jnp.exp(head_scores(query_head, key_head) - log_totals[head])
        share_grad = jnp.einsum(
            "qd,kd->qk", out_grad_head, value_head, preferred_element_type=jnp.float32
        )
        delta = jnp.sum(recomputed * share_grad, axis=1, keepdims=True)
        score_grad = (recomputed * (share_grad - delta)).astype(jnp.bfloat16)
        query_grads.append(
            jnp.dot(score_grad, key_head, preferred_element_type=jnp.float32) * factor
        )
        key_grads.append(
            jnp.einsum("qk,qd->kd", score_grad, query_head, preferred_element_type=jnp.float32)
            * factor
        )
        value_grads.append(
            jnp.einsum(
                "qk,qd->kd",
                recomputed.astype(jnp.bfloat16),
                out_grad_head,
                preferred_element_type=jnp.float32,
            )
        )
    key_grad_all = jnp.concatenate(key_grads, axis=1)
    value_grad_all = jnp.concatenate(value_grads, axis=1)
    prompt_key_grad, prompt_value_grad = (
        lax.psum_scatter(
            key_grad_all[:prompt_count].astype(jnp.bfloat16),
            "expert",
            scatter_dimension=0,
            tiled=True,
        ).astype(jnp.float32),
        lax.psum_scatter(
            value_grad_all[:prompt_count].astype(jnp.bfloat16),
            "expert",
            scatter_dimension=0,
            tiled=True,
        ).astype(jnp.float32),
    )
    key_grad = jnp.concatenate([prompt_key_grad, key_grad_all[prompt_count:]], axis=0)
    value_grad = jnp.concatenate([prompt_value_grad, value_grad_all[prompt_count:]], axis=0)
    query_grad = unrotate(
        jnp.concatenate(query_grads, axis=1).reshape(rows, head_count, HD), cosine, sine
    ).reshape(rows, local_width)
    key_grad = unrotate(key_grad.reshape(rows, head_count, HD), cosine, sine).reshape(
        rows, local_width
    )
    grad_qk_gain = jnp.stack(
        [
            jnp.sum(query_grad * query_raw * scale_query, axis=0),
            jnp.sum(key_grad * key_raw * scale_key, axis=0),
        ],
        axis=0,
    )
    weighted_query = qk_gain[0] * query_grad
    weighted_key = qk_gain[1] * key_grad
    inner_sums = lax.psum(
        jnp.stack(
            [jnp.sum(weighted_query * query_raw, axis=1), jnp.sum(weighted_key * key_raw, axis=1)],
            axis=1,
        ),
        "tensor",
    )
    query_raw_grad = (
        scale_query * weighted_query - query_raw * (scale_query**3 / width) * inner_sums[:, 0:1]
    ).astype(jnp.bfloat16)
    key_raw_grad = (
        scale_key * weighted_key - key_raw * (scale_key**3 / width) * inner_sums[:, 1:2]
    ).astype(jnp.bfloat16)
    value_raw_grad = value_grad.astype(jnp.bfloat16)
    grad_w_query = jnp.einsum(
        "td,te->de", normed, query_raw_grad, preferred_element_type=jnp.float32
    )
    grad_w_key = jnp.einsum("td,te->de", normed, key_raw_grad, preferred_element_type=jnp.float32)
    grad_w_value = jnp.einsum(
        "td,te->de", normed, value_raw_grad, preferred_element_type=jnp.float32
    )
    normed_part = jnp.einsum(
        "te,de->td", query_raw_grad, w_query, preferred_element_type=jnp.float32
    )
    normed_part = normed_part + jnp.einsum(
        "te,de->td", key_raw_grad, w_key, preferred_element_type=jnp.float32
    )
    normed_part = normed_part + jnp.einsum(
        "te,de->td", value_raw_grad, w_value, preferred_element_type=jnp.float32
    )
    normed_grad = lax.psum(normed_part.astype(jnp.bfloat16), "tensor").astype(jnp.float32)
    weighted_one = attn_gain * normed_grad
    grad_attn_gain = jnp.sum(normed_grad * source * scale_one, axis=0)
    input_grad = (
        hidden_grad
        + scale_one * weighted_one
        - source * (scale_one**3 / width) * jnp.sum(weighted_one * source, axis=1, keepdims=True)
    )
    summed = (
        lax.psum_scatter(
            grad_w_query.astype(jnp.bfloat16), "expert", scatter_dimension=0, tiled=True
        ).astype(jnp.float32),
        lax.psum_scatter(
            grad_w_key.astype(jnp.bfloat16), "expert", scatter_dimension=0, tiled=True
        ).astype(jnp.float32),
        lax.psum_scatter(
            grad_w_value.astype(jnp.bfloat16), "expert", scatter_dimension=0, tiled=True
        ).astype(jnp.float32),
        lax.psum_scatter(
            grad_w_out.astype(jnp.bfloat16), "expert", scatter_dimension=1, tiled=True
        ).astype(jnp.float32),
        lax.psum_scatter(
            grad_attn_gain.astype(jnp.bfloat16), "expert", scatter_dimension=0, tiled=True
        ).astype(jnp.float32),
        lax.psum_scatter(
            grad_ffn_gain.astype(jnp.bfloat16), "expert", scatter_dimension=0, tiled=True
        ).astype(jnp.float32),
        lax.psum_scatter(
            grad_qk_gain.astype(jnp.bfloat16), "expert", scatter_dimension=1, tiled=True
        ).astype(jnp.float32),
        lax.psum_scatter(
            grad_router.astype(jnp.bfloat16), "expert", scatter_dimension=0, tiled=True
        ).astype(jnp.float32),
    )
    return (
        output,
        input_grad,
        summed[0],
        summed[1],
        summed[2],
        summed[3],
        summed[4],
        summed[5],
        summed[6],
        summed[7],
        grad_w_gate,
        grad_w_up,
        grad_w_down,
    )


def solution(mesh):
    return jax.shard_map(
        body,
        mesh=mesh,
        in_specs=(
            P("expert", None),
            P(None, "tensor"),
            P(None, "tensor"),
            P(None, "tensor"),
            P("tensor", None),
            P(),
            P(),
            P(None, "tensor"),
            P(),
            P("expert", None, "tensor"),
            P("expert", None, "tensor"),
            P("expert", "tensor", None),
            P("expert", None),
            P("expert"),
            P("expert", None),
        ),
        out_specs=(
            P("expert", None),
            P("expert", None),
            P("expert", "tensor"),
            P("expert", "tensor"),
            P("expert", "tensor"),
            P("tensor", "expert"),
            P("expert"),
            P("expert"),
            P(None, ("tensor", "expert")),
            P("expert", None),
            P("expert", None, "tensor"),
            P("expert", None, "tensor"),
            P("expert", "tensor", None),
        ),
        check_vma=False,
    )
```

```python
import jax
import jax.numpy as jnp
from jax import lax
from jax.experimental import pallas as pl
from jax.experimental.pallas import tpu as pltpu
from jax.sharding import PartitionSpec as P

HD = 128
PROMPT_DEV = 128
CLEN = 256
CONT_DEV = 1


MESH = pl.DeviceIdType.MESH
STEP = 16
LANE = 128


def remote(source, target, sent, received, **where):
    return pltpu.make_async_remote_copy(
        src_ref=source,
        dst_ref=target,
        send_sem=sent,
        recv_sem=received,
        device_id=where,
        device_id_type=MESH,
    )


def greet(places):
    barrier = pltpu.get_barrier_semaphore()
    for condition, where in places:
        def signal(where=where):
            pl.semaphore_signal(barrier, inc=1, device_id=where, device_id_type=MESH)
        if condition is None:
            signal()
        else:
            pl.when(condition)(signal)
    count = 0
    for condition, _ in places:
        count = count + (1 if condition is None else jnp.where(condition, 1, 0))
    pl.semaphore_wait(barrier, count)


class Line:
    def __init__(self, own, arrived, total, sems):
        self.own, self.arrived, self.total = own, arrived, total
        self.up_sent, self.up_got, self.down_sent, self.down_got = (sems.at[i] for i in range(4))
        self.size = lax.axis_size("tensor")
        self.here = lax.axis_index("tensor")
        self.half = own.shape[0] // 2
        self.pieces = self.half // STEP

    @staticmethod
    def semaphores(rows):
        return pltpu.SemaphoreType.DMA((4, 2, rows // 2 // STEP))

    def neighbours(self):
        here, size = self.here, self.size
        return [
            (here > 0, {"tensor": jnp.maximum(here - 1, 0)}),
            (here < size - 1, {"tensor": jnp.minimum(here + 1, size - 1)}),
        ]

    def lane(self, lane):
        here, size = self.here, self.size
        if lane == 0:
            return here, here + 1, here - 1
        return size - 1 - here, here - 1, here + 1

    def rows(self, lane, piece):
        return pl.ds(pl.multiple_of(lane * self.half + piece * STEP, STEP), STEP)

    def up_copy(self, lane, piece):
        rows = self.rows(lane, piece)
        onward = self.lane(lane)[1]
        return remote(
            self.own.at[rows], self.arrived.at[rows],
            self.up_sent.at[lane, piece], self.up_got.at[lane, piece], tensor=onward,
        )

    def down_copy(self, lane, piece):
        rows = self.rows(lane, piece)
        back = self.lane(lane)[2]
        return remote(
            self.total.at[rows], self.total.at[rows],
            self.down_sent.at[lane, piece], self.down_got.at[lane, piece], tensor=back,
        )

    def rise(self, lane, piece):
        place = self.lane(lane)[0]
        rows = self.rows(lane, piece)

        @pl.when(place > 0)
        def _():
            self.up_copy(lane, piece).wait_recv()
            summed = (
                self.own[rows].astype(jnp.float32) + self.arrived[rows].astype(jnp.float32)
            ).astype(jnp.bfloat16)

            @pl.when(place < self.size - 1)
            def _():
                self.own[rows] = summed

            @pl.when(place == self.size - 1)
            def _():
                self.total[rows] = summed
                self.down_copy(lane, piece).start()

        @pl.when(place < self.size - 1)
        def _():
            self.up_copy(lane, piece).start()

    def fall(self, lane, piece):
        place = self.lane(lane)[0]

        @pl.when(place < self.size - 1)
        def _():
            self.down_copy(lane, piece).wait_recv()

            @pl.when(place > 0)
            def _():
                self.down_copy(lane, piece).start()

    def lag(self, lane, per_hop):
        return per_hop * (self.size - 1 - self.lane(lane)[0])

    def advance(self, step, per_hop):
        @pl.when(step < self.pieces)
        def _():
            for lane in range(2):
                self.rise(lane, step)

        for lane in range(2):
            piece = step - self.lag(lane, per_hop)

            @pl.when((piece >= 0) & (piece < self.pieces))
            def _():
                self.fall(lane, piece)

    def steps(self, per_hop):
        return self.pieces + per_hop * (self.size - 1)

    def finish(self):
        def one(piece, carry):
            for lane in range(2):
                place = self.lane(lane)[0]

                @pl.when(place < self.size - 1)
                def _():
                    self.up_copy(lane, piece).wait_send()

                @pl.when(place > 0)
                def _():
                    self.down_copy(lane, piece).wait_send()
            return carry

        lax.fori_loop(0, self.pieces, one, 0)


class Plane:
    def __init__(self, own, spare, paired, from_x, from_y, pair_sems, x_sems, y_sems):
        self.own, self.spare, self.paired, self.from_x, self.from_y = own, spare, paired, from_x, from_y
        self.pair_sems, self.x_sems, self.y_sems = pair_sems, x_sems, y_sems
        here = lax.axis_index("expert")
        self.here = here
        self.core, self.x, self.y = here % 2, here // 2 % 2, here // 4
        self.sibling = here + 1 - 2 * self.core
        self.x_chip = here + 2 - 4 * self.x
        self.y_chip = here + 4 - 8 * self.y
        self.half = own.shape[1] // 2
        self.pieces = self.half // STEP

    @staticmethod
    def semaphores(rows):
        pieces = rows // 2 // STEP
        return [
            pltpu.SemaphoreType.DMA((2, 4)),
            pltpu.SemaphoreType.DMA((2, 3, pieces)),
            pltpu.SemaphoreType.DMA((2, 3, pieces)),
        ]

    def neighbours(self):
        return [(None, {"expert": i}) for i in (self.sibling, self.x_chip, self.y_chip)]

    def block(self, chip, core):
        x = self.x + (1 - chip // 2) * (1 - 2 * self.x)
        y = self.y + (1 - chip % 2) * (1 - 2 * self.y)
        return 4 * y + 2 * x + core

    def pair_copy(self, chip):
        return remote(
            self.spare.at[chip], self.paired.at[chip],
            self.pair_sems.at[0, chip], self.pair_sems.at[1, chip], expert=self.sibling,
        )

    def rows(self, side, piece):
        return pl.ds(pl.multiple_of(side * self.half + piece * STEP, STEP), STEP)

    def landing(self, piece):
        return pl.ds(pl.multiple_of(piece * STEP, STEP), STEP)

    def x_copy(self, kind, piece):
        chip, side = ((0, 0), (1, 0), (1, 1))[kind]
        return remote(
            self.own.at[chip, self.rows(side, piece)], self.from_x.at[kind, self.landing(piece)],
            self.x_sems.at[0, kind, piece], self.x_sems.at[1, kind, piece], expert=self.x_chip,
        )

    def y_copy(self, kind, piece):
        chip, side = ((0, 1), (2, 1), (2, 0))[kind]
        return remote(
            self.own.at[chip, self.rows(side, piece)], self.from_y.at[kind, self.landing(piece)],
            self.y_sems.at[0, kind, piece], self.y_sems.at[1, kind, piece], expert=self.y_chip,
        )

    def add_pair(self, chip, side, piece):
        rows = self.rows(side, piece)
        self.own[chip, rows] = (
            self.own[chip, rows].astype(jnp.float32) + self.paired[chip, rows].astype(jnp.float32)
        ).astype(jnp.bfloat16)

    def each(self, step):
        def one(piece, carry):
            step(piece)
            return carry

        lax.fori_loop(0, self.pieces, one, 0)

    def send_first(self, chip):
        def step(piece):
            if chip in (0, 1):
                self.add_pair(chip, 0, piece)
                self.x_copy(chip, piece).start()
            if chip in (0, 2):
                self.add_pair(chip, 1, piece)
                self.y_copy(chip // 2, piece).start()

        self.each(step)

    def send_second(self):
        def step(piece):
            landed = self.landing(piece)
            self.y_copy(0, piece).wait_recv()
            rows = self.rows(1, piece)
            self.own[1, rows] = (
                self.own[1, rows].astype(jnp.float32)
                + self.paired[1, rows].astype(jnp.float32)
                + self.from_y[0, landed].astype(jnp.float32)
            ).astype(jnp.bfloat16)
            self.x_copy(2, piece).start()
            self.x_copy(0, piece).wait_recv()
            rows = self.rows(0, piece)
            self.own[2, rows] = (
                self.own[2, rows].astype(jnp.float32)
                + self.paired[2, rows].astype(jnp.float32)
                + self.from_x[0, landed].astype(jnp.float32)
            ).astype(jnp.bfloat16)
            self.y_copy(2, piece).start()

        self.each(step)

    def last_sum(self, piece):
        landed = self.landing(piece)
        sums = []
        for side in range(2):
            first, second = (self.x_copy(1, piece), self.y_copy(2, piece)) if side == 0 else (self.y_copy(1, piece), self.x_copy(2, piece))
            first.wait_recv()
            second.wait_recv()
            a, b = (self.from_x[1, landed], self.from_y[2, landed]) if side == 0 else (self.from_y[1, landed], self.from_x[2, landed])
            rows = self.rows(side, piece)
            sums.append(
                self.own[3, rows].astype(jnp.float32)
                + self.paired[3, rows].astype(jnp.float32)
                + a.astype(jnp.float32)
                + b.astype(jnp.float32)
            )
        return sums

    def finish(self):
        for chip in range(4):
            self.pair_copy(chip).wait_send()

        def step(piece):
            for kind in range(3):
                self.x_copy(kind, piece).wait_send()
                self.y_copy(kind, piece).wait_send()

        self.each(step)


def wide_dot(left, right):
    return jnp.dot(left, right, preferred_element_type=jnp.float32)


def turned_dot(left, right):
    return lax.dot_general(left, right, (((1,), (1,)), ((), ())), preferred_element_type=jnp.float32)


def expert_kernel(
    x_all, g_all, mask, router, bias, w_gate, w_up, w_down,
    reduced, gated_all, gate_all, up_all, mixed_all,
    x_buf, g_buf, part, paired, from_x, from_y, line_in, small, mixed,
    in_sems, out_sems, pair_sems, x_sems, y_sems, line_sems,
):
    experts, width, hidden = w_gate.shape
    rows = x_buf.shape[1]
    tile = min(512, width)
    plane = Plane(part.at[1], part.at[0], paired, from_x, from_y, pair_sems, x_sems, y_sems)
    line = Line(part.at[1, 3], line_in, reduced, line_sems)
    first_expert = lax.axis_index("expert") * experts
    outs = (gated_all, gate_all, up_all)

    def block_of(i):
        return plane.block(i // 2, (plane.core + 1 - i % 2) % 2)

    def fetch(i):
        slot, block = i % 2, block_of(i)
        return (
            pltpu.make_async_copy(x_all.at[block], x_buf.at[slot], in_sems.at[0, slot]),
            pltpu.make_async_copy(g_all.at[block], g_buf.at[slot], in_sems.at[1, slot]),
        )

    def store(i):
        slot, block = i % 2, block_of(i)
        return [
            pltpu.make_async_copy(small.at[slot, n], outs[n].at[block], out_sems.at[n, slot])
            for n in range(3)
        ] + [pltpu.make_async_copy(mixed.at[slot], mixed_all.at[block], out_sems.at[3, slot])]

    def compute(i):
        slot = i % 2
        block = block_of(i)
        x = x_buf.at[slot]
        g = g_buf.at[slot]
        logits = wide_dot(x[...], router[...]) + bias[...]
        weights = jnp.exp(logits - jnp.max(logits, axis=1, keepdims=True))
        gates = weights / jnp.sum(weights, axis=1, keepdims=True) * mask[block]
        column = lax.broadcasted_iota(jnp.int32, (rows, LANE), 1)
        extra = jnp.zeros((rows, LANE), jnp.float32)
        for j in range(experts):
            gate_pre = wide_dot(x[...], w_gate[j])
            up_pre = wide_dot(x[...], w_up[j])
            raw = turned_dot(g[...], w_down[j])
            gate = gates[:, j : j + 1]
            sigma = jax.nn.sigmoid(gate_pre)
            activated = gate_pre * sigma
            inner = activated * up_pre
            act = gate * raw
            span = slice(j * hidden, (j + 1) * hidden)
            small[slot, 0, :, span] = (gate * inner).astype(jnp.bfloat16)
            small[slot, 1, :, span] = (
                act * up_pre * sigma * (1.0 + gate_pre * (1.0 - sigma))
            ).astype(jnp.bfloat16)
            small[slot, 2, :, span] = (act * activated).astype(jnp.bfloat16)
            gain = jnp.sum(raw * inner, axis=1, keepdims=True)
            extra = jnp.where(column == first_expert + j, gain, extra)
        for start in range(0, width, tile):
            columns = slice(start, start + tile)
            slot_grad = None
            mix = None
            for j in range(experts):
                span = slice(j * hidden, (j + 1) * hidden)
                term = turned_dot(small[slot, 1, :, span], w_gate[j, columns]) + turned_dot(
                    small[slot, 2, :, span], w_up[j, columns]
                )
                more = wide_dot(small[slot, 0, :, span], w_down[j, :, columns])
                slot_grad = term if slot_grad is None else slot_grad + term
                mix = more if mix is None else mix + more
            part[i % 2, i // 2, :, columns] = slot_grad.astype(jnp.bfloat16)
            mixed[slot, :, columns] = mix.astype(jnp.bfloat16)
        part[i % 2, i // 2, :, width:] = extra.astype(jnp.bfloat16)

    for copy in fetch(0):
        copy.start()
    greet(plane.neighbours() + line.neighbours())

    def step(i, carry):
        @pl.when(i < 7)
        def _():
            for copy in fetch(i + 1):
                copy.start()

        for copy in fetch(i):
            copy.wait()

        @pl.when(i >= 2)
        def _():
            for copy in store(i - 2):
                copy.wait()

        compute(i)
        for copy in store(i):
            copy.start()

        @pl.when(i % 2 == 0)
        def _():
            plane.pair_copy(i // 2).start()

        @pl.when(i % 2 == 1)
        def _():
            plane.pair_copy(i // 2).wait_recv()

        for chip in range(3):

            @pl.when(i == 2 * chip + 1)
            def _():
                plane.send_first(chip)
                if chip == 2:
                    plane.send_second()

        return carry

    lax.fori_loop(0, 8, step, 0)

    def last(step, carry):
        @pl.when(step < plane.pieces)
        def _():
            for side, total in enumerate(plane.last_sum(step)):
                plane.own[3, plane.rows(side, step)] = total.astype(jnp.bfloat16)

        line.advance(step, 2)
        return carry

    lax.fori_loop(0, line.steps(2), last, 0)
    for i in (6, 7):
        for copy in store(i):
            copy.wait()
    plane.finish()
    line.finish()


def experts_fused(arrived, arrived_grad, mask, router, bias, w_gate, w_up, w_down):
    ranks, rows, width = arrived.shape
    experts, _, hidden = w_gate.shape
    wide = width + LANE
    inner = experts * hidden
    half = rows // 2
    low = jnp.bfloat16
    any_space = pl.BlockSpec(memory_space=pl.ANY)
    vmem = pl.BlockSpec(memory_space=pltpu.VMEM)
    small_shape = jax.ShapeDtypeStruct((ranks, rows, inner), low)
    return pl.pallas_call(
        expert_kernel,
        out_shape=(
            jax.ShapeDtypeStruct((rows, wide), low), small_shape, small_shape, small_shape,
            jax.ShapeDtypeStruct((ranks, rows, width), low),
        ),
        in_specs=[any_space, any_space] + [vmem] * 6,
        out_specs=(vmem, any_space, any_space, any_space, any_space),
        scratch_shapes=[
            pltpu.VMEM((2, rows, width), low),
            pltpu.VMEM((2, rows, width), low),
            pltpu.VMEM((2, 4, rows, wide), low),
            pltpu.VMEM((4, rows, wide), low),
            pltpu.VMEM((3, half, wide), low),
            pltpu.VMEM((3, half, wide), low),
            pltpu.VMEM((rows, wide), low),
            pltpu.VMEM((2, 3, rows, inner), low),
            pltpu.VMEM((2, rows, width), low),
            pltpu.SemaphoreType.DMA((2, 2)),
            pltpu.SemaphoreType.DMA((4, 2)),
            *Plane.semaphores(rows),
            Line.semaphores(rows),
        ],
        compiler_params=pltpu.CompilerParams(
            collective_id=0, has_side_effects=True, vmem_limit_bytes=61 * 2**20
        ),
        cost_estimate=pl.CostEstimate(
            flops=12 * ranks * rows * width * inner, bytes_accessed=8 * ranks * rows * width, transcendentals=0
        ),
    )(arrived, arrived_grad, mask, router, bias, w_gate, w_up, w_down)


epsilon = 1e-05
masked_value = -1e30


def rotate(field, cosine, sine):
    half = field.shape[-1] // 2
    first = field[..., :half]
    second = field[..., half:]
    return jnp.concatenate(
        [first * cosine - second * sine, second * cosine + first * sine], axis=-1
    )


def unrotate(grad, cosine, sine):
    half = grad.shape[-1] // 2
    first = grad[..., :half]
    second = grad[..., half:]
    return jnp.concatenate(
        [first * cosine + second * sine, second * cosine - first * sine], axis=-1
    )


def experts(normed_two, cotangent, gates, w_gate, w_up, w_down, experts_total):
    local_experts = w_gate.shape[0]
    device = lax.axis_index("expert")
    arrived = lax.all_gather(normed_two, "expert", axis=0, tiled=True)
    arrived_grad = lax.all_gather(cotangent, "expert", axis=0, tiled=True)
    gate_pre = jnp.einsum("rd,jdf->jrf", arrived, w_gate, preferred_element_type=jnp.float32)
    up_pre = jnp.einsum("rd,jdf->jrf", arrived, w_up, preferred_element_type=jnp.float32)
    raw_grad = jnp.einsum("rd,jfd->jrf", arrived_grad, w_down, preferred_element_type=jnp.float32)
    sigma = jax.nn.sigmoid(gate_pre)
    activated = gate_pre * sigma
    inner = activated * up_pre
    gated = (gates[:, :, None] * inner).astype(jnp.bfloat16)
    mixed_part = jnp.einsum("jrf,jfd->rd", gated, w_down, preferred_element_type=jnp.float32)
    mixture = lax.psum(
        lax.psum_scatter(
            mixed_part.astype(jnp.bfloat16), "expert", scatter_dimension=0, tiled=True
        ),
        "tensor",
    ).astype(jnp.float32)
    gate_grad_part = jnp.sum(raw_grad * inner, axis=2)
    act_grad = gates[:, :, None] * raw_grad
    up_grad = (act_grad * activated).astype(jnp.bfloat16)
    gate_grad = (act_grad * up_pre * sigma * (1.0 + gate_pre * (1.0 - sigma))).astype(jnp.bfloat16)
    grad_w_down = jnp.einsum("jrf,rd->jfd", gated, arrived_grad, preferred_element_type=jnp.float32)
    grad_w_gate = jnp.einsum("rd,jrf->jdf", arrived, gate_grad, preferred_element_type=jnp.float32)
    grad_w_up = jnp.einsum("rd,jrf->jdf", arrived, up_grad, preferred_element_type=jnp.float32)
    slot_grad = jnp.einsum("jrf,jdf->rd", gate_grad, w_gate, preferred_element_type=jnp.float32)
    slot_grad = slot_grad + jnp.einsum(
        "jrf,jdf->rd", up_grad, w_up, preferred_element_type=jnp.float32
    )
    moe_input_grad = lax.psum(
        lax.psum_scatter(
            slot_grad.astype(jnp.bfloat16), "expert", scatter_dimension=0, tiled=True
        ),
        "tensor",
    ).astype(jnp.float32)
    placed = jnp.zeros((arrived.shape[0], experts_total), jnp.float32)
    placed = lax.dynamic_update_slice_in_dim(placed, gate_grad_part.T, device * local_experts, 1)
    chance_grad = lax.psum(
        lax.psum_scatter(placed, "expert", scatter_dimension=0, tiled=True), "tensor"
    )
    return mixture, moe_input_grad, chance_grad, [grad_w_gate, grad_w_up, grad_w_down]


def body(
    tokens,
    w_query,
    w_key,
    w_value,
    w_out,
    attn_gain,
    ffn_gain,
    qk_gain,
    router,
    w_gate,
    w_up,
    w_down,
    routes,
    cont_group,
    cotangent,
):
    rows, width = tokens.shape
    local_width = w_query.shape[1]
    head_count = local_width // HD
    experts_total = router.shape[1]
    local_experts = w_gate.shape[0]
    ranks = lax.axis_size("expert")
    device = lax.axis_index("expert")
    span = ranks // 2
    prompt_len = PROMPT_DEV * span
    factor = HD ** (-0.5)
    local = jnp.arange(rows, dtype=jnp.int32)
    is_prompt = local < PROMPT_DEV
    after = jnp.maximum(local - PROMPT_DEV, 0)
    slot_cont = after // CLEN
    cont_pick = jnp.sum(
        jnp.where(
            slot_cont[:, None] == jnp.arange(CONT_DEV, dtype=jnp.int32)[None, :],
            cont_group[None, :],
            0,
        ),
        axis=1,
    )
    group = jnp.where(is_prompt, device // span, cont_pick)
    position = jnp.where(is_prompt, device % span * PROMPT_DEV + local, prompt_len + after % CLEN)
    tag = jnp.where(is_prompt, -1, slot_cont)
    frequency = 10000.0 ** (-jnp.arange(HD // 2, dtype=jnp.float32) * 2.0 / HD)
    angle = position.astype(jnp.float32)[:, None] * frequency[None, :]
    cosine = jnp.cos(angle)[:, None, :]
    sine = jnp.sin(angle)[:, None, :]
    source = tokens.astype(jnp.float32)
    scale_one = lax.rsqrt(jnp.mean(source * source, axis=1, keepdims=True) + epsilon)
    normed = (source * scale_one * attn_gain).astype(jnp.bfloat16)
    query_raw = jnp.dot(normed, w_query, preferred_element_type=jnp.float32)
    key_raw = jnp.dot(normed, w_key, preferred_element_type=jnp.float32)
    value_raw = jnp.dot(normed, w_value, preferred_element_type=jnp.float32)
    squares = lax.psum(
        jnp.stack(
            [jnp.sum(query_raw * query_raw, axis=1), jnp.sum(key_raw * key_raw, axis=1)], axis=1
        ),
        "tensor",
    )
    scale_query = lax.rsqrt(squares[:, 0:1] / width + epsilon)
    scale_key = lax.rsqrt(squares[:, 1:2] / width + epsilon)
    query_rot = (
        rotate((query_raw * scale_query * qk_gain[0]).reshape(rows, head_count, HD), cosine, sine)
        .reshape(rows, local_width)
        .astype(jnp.bfloat16)
    )
    key_rot = (
        rotate((key_raw * scale_key * qk_gain[1]).reshape(rows, head_count, HD), cosine, sine)
        .reshape(rows, local_width)
        .astype(jnp.bfloat16)
    )
    value_low = value_raw.astype(jnp.bfloat16)
    prompt_keys, prompt_values = (
        lax.all_gather(key_rot[:PROMPT_DEV], "expert", axis=0, tiled=True),
        lax.all_gather(value_low[:PROMPT_DEV], "expert", axis=0, tiled=True),
    )
    prompt_count = prompt_keys.shape[0]
    all_keys = jnp.concatenate([prompt_keys, key_rot[PROMPT_DEV:]], axis=0)
    all_values = jnp.concatenate([prompt_values, value_low[PROMPT_DEV:]], axis=0)
    key_index = jnp.arange(prompt_count, dtype=jnp.int32)
    prompt_mask = (group[:, None] == (key_index // prompt_len)[None, :]) & (
        (key_index % prompt_len)[None, :] <= position[:, None]
    )
    own_mask = (tag[:, None] == tag[None, PROMPT_DEV:]) & (
        position[None, PROMPT_DEV:] <= position[:, None]
    )
    mask = jnp.concatenate([prompt_mask, own_mask], axis=1)

    def head_scores(query_head, key_head):
        scores = (
            jnp.einsum("qd,kd->qk", query_head, key_head, preferred_element_type=jnp.float32)
            * factor
        )
        return jnp.where(mask, scores, masked_value)

    outputs = []
    log_totals = []
    for head in range(head_count):
        start = head * HD
        scores = head_scores(query_rot[:, start : start + HD], all_keys[:, start : start + HD])
        top = jnp.max(scores, axis=1, keepdims=True)
        weights = jnp.exp(scores - top)
        total = jnp.sum(weights, axis=1, keepdims=True)
        shares = (weights / total).astype(jnp.bfloat16)
        outputs.append(
            jnp.dot(shares, all_values[:, start : start + HD], preferred_element_type=jnp.float32)
        )
        log_totals.append(top + jnp.log(total))
    attended = jnp.concatenate(outputs, axis=1).astype(jnp.bfloat16)
    attention = lax.psum(jnp.dot(attended, w_out, preferred_element_type=jnp.float32), "tensor")
    hidden = source + attention
    scale_two = lax.rsqrt(jnp.mean(hidden * hidden, axis=1, keepdims=True) + epsilon)
    normed_two = (hidden * scale_two * ffn_gain).astype(jnp.bfloat16)
    logits = jnp.dot(normed_two, router, preferred_element_type=jnp.float32)
    top = jnp.max(logits, axis=1, keepdims=True)
    weights = jnp.exp(logits - top)
    chances = weights / jnp.sum(weights, axis=1, keepdims=True)
    hits = (routes[:, :, None] == jnp.arange(experts_total, dtype=jnp.int32)[None, None, :]).astype(
        jnp.float32
    )
    rows_mask = jnp.sum(hits, axis=1)
    grad_out = cotangent.astype(jnp.float32)
    if ranks == 8:
        routes_all = lax.all_gather(routes, "expert", axis=0)
        own_expert = device * local_experts + jnp.arange(local_experts, dtype=jnp.int32)
        own_mask = jnp.any(routes_all[:, :, :, None] == own_expert, axis=2).astype(jnp.float32)
        own_mask = jnp.pad(own_mask, ((0, 0), (0, 0), (0, LANE - local_experts)))
        own_first = jnp.roll(router, -device * local_experts, axis=1)
        own_first = jnp.pad(own_first, ((0, 0), (0, LANE - experts_total)))
        bias = jnp.where(jnp.arange(LANE) < experts_total, 0.0, masked_value)
        bias = bias.astype(jnp.float32)[None]
        arrived = lax.all_gather(normed_two, "expert", axis=0)
        arrived_grad = lax.all_gather(cotangent, "expert", axis=0)
        reduced, gated, gate_grad, up_grad, mixed_part = experts_fused(
            arrived, arrived_grad, own_mask, own_first, bias, w_gate, w_up, w_down
        )
        moe_input_grad = reduced[:, :width].astype(jnp.float32)
        chance_grad = reduced[:, width : width + experts_total].astype(jnp.float32)
        mixture = lax.psum(
            lax.psum_scatter(
                mixed_part.reshape(ranks * rows, width), "expert", scatter_dimension=0, tiled=True
            ),
            "tensor",
        ).astype(jnp.float32)
        hidden_units = w_gate.shape[2]

        def per_expert(j):
            span = slice(j * hidden_units, (j + 1) * hidden_units)
            return (
                jnp.einsum("nrd,nrf->df", arrived, gate_grad[:, :, span], preferred_element_type=jnp.float32),
                jnp.einsum("nrd,nrf->df", arrived, up_grad[:, :, span], preferred_element_type=jnp.float32),
                jnp.einsum("nrf,nrd->fd", gated[:, :, span], arrived_grad, preferred_element_type=jnp.float32),
            )

        grad_w_gate, grad_w_up, grad_w_down = (
            jnp.stack(list(parts)) for parts in zip(*(per_expert(j) for j in range(local_experts)))
        )
    else:
        routed = lax.all_gather(
            (rows_mask * chances).astype(jnp.float32), "expert", axis=0, tiled=True
        )
        gates = lax.dynamic_slice_in_dim(routed, device * local_experts, local_experts, 1).T
        pieces = max(1, ranks * rows // 4096)
        piece = rows // pieces
        split_gates = gates.reshape(local_experts, ranks, rows)
        results = []
        weight_grads = None
        for number in range(pieces):
            part = slice(number * piece, (number + 1) * piece)
            sources = (normed_two[part], cotangent[part])
            if results:
                sources, results, weight_grads = lax.optimization_barrier(
                    (sources, results, weight_grads)
                )
            *result, grads = experts(
                *sources,
                split_gates[:, :, part].reshape(local_experts, ranks * piece),
                w_gate,
                w_up,
                w_down,
                experts_total,
            )
            results.append(result)
            weight_grads = grads if weight_grads is None else [a + b for a, b in zip(weight_grads, grads)]
        mixture, moe_input_grad, chance_grad = (
            jnp.concatenate(list(group_of), axis=0) for group_of in zip(*results)
        )
        grad_w_gate, grad_w_up, grad_w_down = weight_grads
    chance_grad = rows_mask * chance_grad
    output = (hidden + mixture).astype(jnp.bfloat16)
    logit_grad = (
        chances * (chance_grad - jnp.sum(chances * chance_grad, axis=1, keepdims=True))
    ).astype(jnp.bfloat16)
    grad_router = jnp.einsum(
        "td,te->de", normed_two, logit_grad, preferred_element_type=jnp.float32
    )
    normed_two_grad = moe_input_grad + jnp.einsum(
        "te,de->td", logit_grad, router, preferred_element_type=jnp.float32
    )
    weighted_two = ffn_gain * normed_two_grad
    grad_ffn_gain = jnp.sum(normed_two_grad * hidden * scale_two, axis=0)
    hidden_grad = (
        grad_out
        + scale_two * weighted_two
        - hidden * (scale_two**3 / width) * jnp.sum(weighted_two * hidden, axis=1, keepdims=True)
    )
    attention_grad = hidden_grad.astype(jnp.bfloat16)
    grad_w_out = jnp.einsum(
        "td,te->de", attended, attention_grad, preferred_element_type=jnp.float32
    )
    attended_grad = jnp.einsum(
        "te,de->td", attention_grad, w_out, preferred_element_type=jnp.float32
    ).astype(jnp.bfloat16)
    query_grads = []
    key_grads = []
    value_grads = []
    for head in range(head_count):
        start = head * HD
        query_head = query_rot[:, start : start + HD]
        key_head = all_keys[:, start : start + HD]
        value_head = all_values[:, start : start + HD]
        out_grad_head = attended_grad[:, start : start + HD]
        recomputed = jnp.exp(head_scores(query_head, key_head) - log_totals[head])
        share_grad = jnp.einsum(
            "qd,kd->qk", out_grad_head, value_head, preferred_element_type=jnp.float32
        )
        delta = jnp.sum(recomputed * share_grad, axis=1, keepdims=True)
        score_grad = (recomputed * (share_grad - delta)).astype(jnp.bfloat16)
        query_grads.append(
            jnp.dot(score_grad, key_head, preferred_element_type=jnp.float32) * factor
        )
        key_grads.append(
            jnp.einsum("qk,qd->kd", score_grad, query_head, preferred_element_type=jnp.float32)
            * factor
        )
        value_grads.append(
            jnp.einsum(
                "qk,qd->kd",
                recomputed.astype(jnp.bfloat16),
                out_grad_head,
                preferred_element_type=jnp.float32,
            )
        )
    key_grad_all = jnp.concatenate(key_grads, axis=1)
    value_grad_all = jnp.concatenate(value_grads, axis=1)
    prompt_key_grad, prompt_value_grad = (
        lax.psum_scatter(
            key_grad_all[:prompt_count].astype(jnp.bfloat16),
            "expert",
            scatter_dimension=0,
            tiled=True,
        ).astype(jnp.float32),
        lax.psum_scatter(
            value_grad_all[:prompt_count].astype(jnp.bfloat16),
            "expert",
            scatter_dimension=0,
            tiled=True,
        ).astype(jnp.float32),
    )
    key_grad = jnp.concatenate([prompt_key_grad, key_grad_all[prompt_count:]], axis=0)
    value_grad = jnp.concatenate([prompt_value_grad, value_grad_all[prompt_count:]], axis=0)
    query_grad = unrotate(
        jnp.concatenate(query_grads, axis=1).reshape(rows, head_count, HD), cosine, sine
    ).reshape(rows, local_width)
    key_grad = unrotate(key_grad.reshape(rows, head_count, HD), cosine, sine).reshape(
        rows, local_width
    )
    grad_qk_gain = jnp.stack(
        [
            jnp.sum(query_grad * query_raw * scale_query, axis=0),
            jnp.sum(key_grad * key_raw * scale_key, axis=0),
        ],
        axis=0,
    )
    weighted_query = qk_gain[0] * query_grad
    weighted_key = qk_gain[1] * key_grad
    inner_sums = lax.psum(
        jnp.stack(
            [jnp.sum(weighted_query * query_raw, axis=1), jnp.sum(weighted_key * key_raw, axis=1)],
            axis=1,
        ),
        "tensor",
    )
    query_raw_grad = (
        scale_query * weighted_query - query_raw * (scale_query**3 / width) * inner_sums[:, 0:1]
    ).astype(jnp.bfloat16)
    key_raw_grad = (
        scale_key * weighted_key - key_raw * (scale_key**3 / width) * inner_sums[:, 1:2]
    ).astype(jnp.bfloat16)
    value_raw_grad = value_grad.astype(jnp.bfloat16)
    grad_w_query = jnp.einsum(
        "td,te->de", normed, query_raw_grad, preferred_element_type=jnp.float32
    )
    grad_w_key = jnp.einsum("td,te->de", normed, key_raw_grad, preferred_element_type=jnp.float32)
    grad_w_value = jnp.einsum(
        "td,te->de", normed, value_raw_grad, preferred_element_type=jnp.float32
    )
    normed_part = jnp.einsum(
        "te,de->td", query_raw_grad, w_query, preferred_element_type=jnp.float32
    )
    normed_part = normed_part + jnp.einsum(
        "te,de->td", key_raw_grad, w_key, preferred_element_type=jnp.float32
    )
    normed_part = normed_part + jnp.einsum(
        "te,de->td", value_raw_grad, w_value, preferred_element_type=jnp.float32
    )
    normed_grad = lax.psum(normed_part.astype(jnp.bfloat16), "tensor").astype(jnp.float32)
    weighted_one = attn_gain * normed_grad
    grad_attn_gain = jnp.sum(normed_grad * source * scale_one, axis=0)
    input_grad = (
        hidden_grad
        + scale_one * weighted_one
        - source * (scale_one**3 / width) * jnp.sum(weighted_one * source, axis=1, keepdims=True)
    )
    summed = (
        lax.psum_scatter(
            grad_w_query.astype(jnp.bfloat16), "expert", scatter_dimension=0, tiled=True
        ).astype(jnp.float32),
        lax.psum_scatter(
            grad_w_key.astype(jnp.bfloat16), "expert", scatter_dimension=0, tiled=True
        ).astype(jnp.float32),
        lax.psum_scatter(
            grad_w_value.astype(jnp.bfloat16), "expert", scatter_dimension=0, tiled=True
        ).astype(jnp.float32),
        lax.psum_scatter(
            grad_w_out.astype(jnp.bfloat16), "expert", scatter_dimension=1, tiled=True
        ).astype(jnp.float32),
        lax.psum_scatter(
            grad_attn_gain.astype(jnp.bfloat16), "expert", scatter_dimension=0, tiled=True
        ).astype(jnp.float32),
        lax.psum_scatter(
            grad_ffn_gain.astype(jnp.bfloat16), "expert", scatter_dimension=0, tiled=True
        ).astype(jnp.float32),
        lax.psum_scatter(
            grad_qk_gain.astype(jnp.bfloat16), "expert", scatter_dimension=1, tiled=True
        ).astype(jnp.float32),
        lax.psum_scatter(
            grad_router.astype(jnp.bfloat16), "expert", scatter_dimension=0, tiled=True
        ).astype(jnp.float32),
    )
    return (
        output,
        input_grad,
        summed[0],
        summed[1],
        summed[2],
        summed[3],
        summed[4],
        summed[5],
        summed[6],
        summed[7],
        grad_w_gate,
        grad_w_up,
        grad_w_down,
    )


def solution(mesh):
    return jax.shard_map(
        body,
        mesh=mesh,
        in_specs=(
            P("expert", None),
            P(None, "tensor"),
            P(None, "tensor"),
            P(None, "tensor"),
            P("tensor", None),
            P(),
            P(),
            P(None, "tensor"),
            P(),
            P("expert", None, "tensor"),
            P("expert", None, "tensor"),
            P("expert", "tensor", None),
            P("expert", None),
            P("expert"),
            P("expert", None),
        ),
        out_specs=(
            P("expert", None),
            P("expert", None),
            P("expert", "tensor"),
            P("expert", "tensor"),
            P("expert", "tensor"),
            P("tensor", "expert"),
            P("expert"),
            P("expert"),
            P(None, ("tensor", "expert")),
            P("expert", None),
            P("expert", None, "tensor"),
            P("expert", None, "tensor"),
            P("expert", "tensor", None),
        ),
        check_vma=False,
    )
```

```python
import jax
import jax.numpy as jnp
from jax import lax
from jax.experimental import pallas as pl
from jax.experimental.pallas import tpu as pltpu
from jax.sharding import PartitionSpec as P

HD = 128
PROMPT_DEV = 128
CLEN = 256
CONT_DEV = 1


MESH = pl.DeviceIdType.MESH
STEP = 16
LANE = 128


def remote(source, target, sent, received, **where):
    return pltpu.make_async_remote_copy(
        src_ref=source,
        dst_ref=target,
        send_sem=sent,
        recv_sem=received,
        device_id=where,
        device_id_type=MESH,
    )


def greet(places):
    barrier = pltpu.get_barrier_semaphore()
    for condition, where in places:
        def signal(where=where):
            pl.semaphore_signal(barrier, inc=1, device_id=where, device_id_type=MESH)
        if condition is None:
            signal()
        else:
            pl.when(condition)(signal)
    count = 0
    for condition, _ in places:
        count = count + (1 if condition is None else jnp.where(condition, 1, 0))
    pl.semaphore_wait(barrier, count)


class Line:
    def __init__(self, own, arrived, total, sems):
        self.own, self.arrived, self.total = own, arrived, total
        self.up_sent, self.up_got, self.down_sent, self.down_got = (sems.at[i] for i in range(4))
        self.size = lax.axis_size("tensor")
        self.here = lax.axis_index("tensor")
        self.half = own.shape[0] // 2
        self.pieces = self.half // STEP

    @staticmethod
    def semaphores(rows):
        return pltpu.SemaphoreType.DMA((4, 2, rows // 2 // STEP))

    def neighbours(self):
        here, size = self.here, self.size
        return [
            (here > 0, {"tensor": jnp.maximum(here - 1, 0)}),
            (here < size - 1, {"tensor": jnp.minimum(here + 1, size - 1)}),
        ]

    def lane(self, lane):
        here, size = self.here, self.size
        if lane == 0:
            return here, here + 1, here - 1
        return size - 1 - here, here - 1, here + 1

    def rows(self, lane, piece):
        return pl.ds(pl.multiple_of(lane * self.half + piece * STEP, STEP), STEP)

    def up_copy(self, lane, piece):
        rows = self.rows(lane, piece)
        onward = self.lane(lane)[1]
        return remote(
            self.own.at[rows], self.arrived.at[rows],
            self.up_sent.at[lane, piece], self.up_got.at[lane, piece], tensor=onward,
        )

    def down_copy(self, lane, piece):
        rows = self.rows(lane, piece)
        back = self.lane(lane)[2]
        return remote(
            self.total.at[rows], self.total.at[rows],
            self.down_sent.at[lane, piece], self.down_got.at[lane, piece], tensor=back,
        )

    def rise(self, lane, piece):
        place = self.lane(lane)[0]
        rows = self.rows(lane, piece)

        @pl.when(place > 0)
        def _():
            self.up_copy(lane, piece).wait_recv()
            summed = (
                self.own[rows].astype(jnp.float32) + self.arrived[rows].astype(jnp.float32)
            ).astype(jnp.bfloat16)

            @pl.when(place < self.size - 1)
            def _():
                self.own[rows] = summed

            @pl.when(place == self.size - 1)
            def _():
                self.total[rows] = summed
                self.down_copy(lane, piece).start()

        @pl.when(place < self.size - 1)
        def _():
            self.up_copy(lane, piece).start()

    def fall(self, lane, piece):
        place = self.lane(lane)[0]

        @pl.when(place < self.size - 1)
        def _():
            self.down_copy(lane, piece).wait_recv()

            @pl.when(place > 0)
            def _():
                self.down_copy(lane, piece).start()

    def advance(self, step, skew=1):
        for act, far in ((self.rise, False), (self.fall, True)):
            for lane in range(2):
                place = self.lane(lane)[0]
                piece = step - skew * (2 * (self.size - 1) - place if far else place)

                @pl.when((piece >= 0) & (piece < self.pieces))
                def _():
                    act(lane, piece)

    def step_body(self, step, carry):
        self.advance(step)
        return carry

    def steps(self, skew=1):
        return self.pieces + skew * 2 * (self.size - 1)

    def finish(self):
        def one(piece, carry):
            for lane in range(2):
                place = self.lane(lane)[0]

                @pl.when(place < self.size - 1)
                def _():
                    self.up_copy(lane, piece).wait_send()

                @pl.when(place > 0)
                def _():
                    self.down_copy(lane, piece).wait_send()
            return carry

        lax.fori_loop(0, self.pieces, one, 0)


class Place:
    def __init__(self):
        here = lax.axis_index("expert")
        self.here = here
        self.core, self.x, self.y = here % 2, here // 2 % 2, here // 4
        self.sibling = here + 1 - 2 * self.core
        self.x_chip = here + 2 - 4 * self.x
        self.y_chip = here + 4 - 8 * self.y

    def neighbours(self):
        return [(None, {"expert": i}) for i in (self.sibling, self.x_chip, self.y_chip)]

    def block(self, chip, core):
        x = self.x + (1 - chip // 2) * (1 - 2 * self.x)
        y = self.y + (1 - chip % 2) * (1 - 2 * self.y)
        return 4 * y + 2 * x + core


class Plane(Place):
    def __init__(self, own, spare, paired, from_x, from_y, pair_sems, x_sems, y_sems):
        self.own, self.spare, self.paired, self.from_x, self.from_y = own, spare, paired, from_x, from_y
        self.pair_sems, self.x_sems, self.y_sems = pair_sems, x_sems, y_sems
        super().__init__()
        self.half = own.shape[1] // 2
        self.pieces = self.half // STEP

    @staticmethod
    def semaphores(rows):
        pieces = rows // 2 // STEP
        return [
            pltpu.SemaphoreType.DMA((2, 4)),
            pltpu.SemaphoreType.DMA((2, 3, pieces)),
            pltpu.SemaphoreType.DMA((2, 3, pieces)),
        ]

    def pair_copy(self, chip):
        return remote(
            self.spare.at[chip], self.paired.at[chip],
            self.pair_sems.at[0, chip], self.pair_sems.at[1, chip], expert=self.sibling,
        )

    def rows(self, side, piece):
        return pl.ds(pl.multiple_of(side * self.half + piece * STEP, STEP), STEP)

    def landing(self, piece):
        return pl.ds(pl.multiple_of(piece * STEP, STEP), STEP)

    def x_copy(self, kind, piece):
        chip, side = ((0, 0), (1, 0), (1, 1))[kind]
        return remote(
            self.own.at[chip, self.rows(side, piece)], self.from_x.at[kind, self.landing(piece)],
            self.x_sems.at[0, kind, piece], self.x_sems.at[1, kind, piece], expert=self.x_chip,
        )

    def y_copy(self, kind, piece):
        chip, side = ((0, 1), (2, 1), (2, 0))[kind]
        return remote(
            self.own.at[chip, self.rows(side, piece)], self.from_y.at[kind, self.landing(piece)],
            self.y_sems.at[0, kind, piece], self.y_sems.at[1, kind, piece], expert=self.y_chip,
        )

    def add_pair(self, chip, side, piece):
        rows = self.rows(side, piece)
        self.own[chip, rows] = (
            self.own[chip, rows].astype(jnp.float32) + self.paired[chip, rows].astype(jnp.float32)
        ).astype(jnp.bfloat16)

    def each(self, step):
        def one(piece, carry):
            step(piece)
            return carry

        lax.fori_loop(0, self.pieces, one, 0)

    def send_first(self, chip):
        def step(piece):
            if chip in (0, 1):
                self.add_pair(chip, 0, piece)
                self.x_copy(chip, piece).start()
            if chip in (0, 2):
                self.add_pair(chip, 1, piece)
                self.y_copy(chip // 2, piece).start()

        self.each(step)

    def second_piece(self, piece):
        landed = self.landing(piece)
        self.y_copy(0, piece).wait_recv()
        rows = self.rows(1, piece)
        self.own[1, rows] = (
            self.own[1, rows].astype(jnp.float32)
            + self.paired[1, rows].astype(jnp.float32)
            + self.from_y[0, landed].astype(jnp.float32)
        ).astype(jnp.bfloat16)
        self.x_copy(2, piece).start()
        self.x_copy(0, piece).wait_recv()
        rows = self.rows(0, piece)
        self.own[2, rows] = (
            self.own[2, rows].astype(jnp.float32)
            + self.paired[2, rows].astype(jnp.float32)
            + self.from_x[0, landed].astype(jnp.float32)
        ).astype(jnp.bfloat16)
        self.y_copy(2, piece).start()

    def send_second(self):
        self.each(self.second_piece)

    def last_sum(self, piece):
        landed = self.landing(piece)
        sums = []
        for side in range(2):
            first, second = (self.x_copy(1, piece), self.y_copy(2, piece)) if side == 0 else (self.y_copy(1, piece), self.x_copy(2, piece))
            first.wait_recv()
            second.wait_recv()
            a, b = (self.from_x[1, landed], self.from_y[2, landed]) if side == 0 else (self.from_y[1, landed], self.from_x[2, landed])
            rows = self.rows(side, piece)
            sums.append(
                self.own[3, rows].astype(jnp.float32)
                + self.paired[3, rows].astype(jnp.float32)
                + a.astype(jnp.float32)
                + b.astype(jnp.float32)
            )
        return sums

    def finish(self):
        for chip in range(4):
            self.pair_copy(chip).wait_send()

        def step(piece):
            for kind in range(3):
                self.x_copy(kind, piece).wait_send()
                self.y_copy(kind, piece).wait_send()

        self.each(step)


class Gather:
    def __init__(self, source, target, place, x_sems, y_sems, far_sems, pair_sems, own_sem, pieces):
        self.source, self.target = source, target
        self.place = place
        self.x_sems, self.y_sems, self.far_sems, self.pair_sems, self.own_sem = x_sems, y_sems, far_sems, pair_sems, own_sem
        self.pieces = pieces
        self.rows_each = source.shape[0] // pieces

    @staticmethod
    def semaphores(pieces):
        return [
            pltpu.SemaphoreType.DMA((2, pieces)),
            pltpu.SemaphoreType.DMA((2, pieces)),
            pltpu.SemaphoreType.DMA((2, pieces)),
            pltpu.SemaphoreType.DMA((2, 4, pieces)),
            pltpu.SemaphoreType.DMA,
        ]

    def rows(self, piece):
        return pl.ds(piece * self.rows_each, self.rows_each)

    def own_copy(self):
        return pltpu.make_async_copy(self.source, self.target.at[self.place.here], self.own_sem)

    def x_copy(self, piece):
        rows = self.rows(piece)
        return remote(
            self.source.at[rows], self.target.at[self.place.here, rows],
            self.x_sems.at[0, piece], self.x_sems.at[1, piece], expert=self.place.x_chip,
        )

    def y_copy(self, piece):
        rows = self.rows(piece)
        return remote(
            self.source.at[rows], self.target.at[self.place.here, rows],
            self.y_sems.at[0, piece], self.y_sems.at[1, piece], expert=self.place.y_chip,
        )

    def far_copy(self, piece):
        rows = self.rows(piece)
        came, goes = (
            (self.place.x_chip, self.place.y_chip) if piece < self.pieces // 2 else (self.place.y_chip, self.place.x_chip)
        )
        return remote(
            self.target.at[came, rows], self.target.at[came, rows],
            self.far_sems.at[0, piece], self.far_sems.at[1, piece], expert=goes,
        )

    def pair_copy(self, kind, piece):
        rows = self.rows(piece)
        block = self.place.block(kind, self.place.core)
        source = self.source.at[rows] if kind == 3 else self.target.at[block, rows]
        return remote(
            source, self.target.at[block, rows],
            self.pair_sems.at[0, kind, piece], self.pair_sems.at[1, kind, piece], expert=self.place.sibling,
        )

    def start(self):
        for piece in range(self.pieces):
            self.x_copy(piece).start()
            self.y_copy(piece).start()
            self.pair_copy(3, piece).start()
        self.own_copy().start()

    def near(self, piece):
        self.x_copy(piece).wait_recv()
        if piece < self.pieces // 2:
            self.far_copy(piece).start()
        self.pair_copy(1, piece).start()
        self.y_copy(piece).wait_recv()
        if piece >= self.pieces // 2:
            self.far_copy(piece).start()
        self.pair_copy(2, piece).start()

    def far(self, piece):
        self.far_copy(piece).wait_recv()
        self.pair_copy(0, piece).start()

    def paired(self, kind, piece):
        self.pair_copy(kind, piece).wait_recv()

    def finish_sends(self):
        self.own_copy().wait()
        for piece in range(self.pieces):
            self.x_copy(piece).wait_send()
            self.y_copy(piece).wait_send()
            self.far_copy(piece).wait_send()
            for kind in range(4):
                self.pair_copy(kind, piece).wait_send()


def wide_dot(left, right):
    return jnp.dot(left, right, preferred_element_type=jnp.float32)


def turned_dot(left, right):
    return lax.dot_general(left, right, (((1,), (1,)), ((), ())), preferred_element_type=jnp.float32)


def expert_kernel(
    x_all, g_all, mask, router, bias, w_gate, w_up, w_down,
    reduced, gated_all, gate_all, up_all, mixed_all,
    x_buf, g_buf, part, paired, from_x, from_y, line_in, small, mixed,
    in_sems, out_sems, pair_sems, x_sems, y_sems, line_sems,
):
    experts, width, hidden = w_gate.shape
    rows = x_buf.shape[1]
    tile = min(512, width)
    plane = Plane(part.at[1], part.at[0], paired, from_x, from_y, pair_sems, x_sems, y_sems)
    line = Line(part.at[1, 3], line_in, reduced, line_sems)
    first_expert = lax.axis_index("expert") * experts
    outs = (gated_all, gate_all, up_all)

    def block_of(i):
        return plane.block(i // 2, (plane.core + 1 - i % 2) % 2)

    def fetch(i):
        slot, block = i % 2, block_of(i)
        return (
            pltpu.make_async_copy(x_all.at[block], x_buf.at[slot], in_sems.at[0, slot]),
            pltpu.make_async_copy(g_all.at[block], g_buf.at[slot], in_sems.at[1, slot]),
        )

    def store(i):
        slot, block = i % 2, block_of(i)
        return [
            pltpu.make_async_copy(small.at[slot, n], outs[n].at[block], out_sems.at[n, slot])
            for n in range(3)
        ] + [pltpu.make_async_copy(mixed.at[slot], mixed_all.at[block], out_sems.at[3, slot])]

    def compute(i):
        slot = i % 2
        block = block_of(i)
        x = x_buf.at[slot]
        g = g_buf.at[slot]
        logits = wide_dot(x[...], router[...]) + bias[...]
        weights = jnp.exp(logits - jnp.max(logits, axis=1, keepdims=True))
        gates = weights / jnp.sum(weights, axis=1, keepdims=True) * mask[block]
        column = lax.broadcasted_iota(jnp.int32, (rows, LANE), 1)
        extra = jnp.zeros((rows, LANE), jnp.float32)
        for j in range(experts):
            gate_pre = wide_dot(x[...], w_gate[j])
            up_pre = wide_dot(x[...], w_up[j])
            raw = turned_dot(g[...], w_down[j])
            gate = gates[:, j : j + 1]
            sigma = jax.nn.sigmoid(gate_pre)
            activated = gate_pre * sigma
            inner = activated * up_pre
            act = gate * raw
            span = slice(j * hidden, (j + 1) * hidden)
            small[slot, 0, :, span] = (gate * inner).astype(jnp.bfloat16)
            small[slot, 1, :, span] = (
                act * up_pre * sigma * (1.0 + gate_pre * (1.0 - sigma))
            ).astype(jnp.bfloat16)
            small[slot, 2, :, span] = (act * activated).astype(jnp.bfloat16)
            gain = jnp.sum(raw * inner, axis=1, keepdims=True)
            extra = jnp.where(column == first_expert + j, gain, extra)
        for start in range(0, width, tile):
            columns = slice(start, start + tile)
            slot_grad = None
            mix = None
            for j in range(experts):
                span = slice(j * hidden, (j + 1) * hidden)
                term = turned_dot(small[slot, 1, :, span], w_gate[j, columns]) + turned_dot(
                    small[slot, 2, :, span], w_up[j, columns]
                )
                more = wide_dot(small[slot, 0, :, span], w_down[j, :, columns])
                slot_grad = term if slot_grad is None else slot_grad + term
                mix = more if mix is None else mix + more
            part[i % 2, i // 2, :, columns] = slot_grad.astype(jnp.bfloat16)
            mixed[slot, :, columns] = mix.astype(jnp.bfloat16)
        part[i % 2, i // 2, :, width:] = extra.astype(jnp.bfloat16)

    for copy in fetch(0):
        copy.start()
    greet(plane.neighbours() + line.neighbours())

    def step(i, carry):
        @pl.when(i < 7)
        def _():
            for copy in fetch(i + 1):
                copy.start()

        for copy in fetch(i):
            copy.wait()

        @pl.when(i >= 2)
        def _():
            for copy in store(i - 2):
                copy.wait()

        compute(i)
        for copy in store(i):
            copy.start()

        @pl.when(i % 2 == 0)
        def _():
            plane.pair_copy(i // 2).start()

        @pl.when(i % 2 == 1)
        def _():
            plane.pair_copy(i // 2).wait_recv()

        for chip in range(3):

            @pl.when(i == 2 * chip + 1)
            def _():
                plane.send_first(chip)
                if chip == 2:
                    plane.send_second()

        return carry

    lax.fori_loop(0, 8, step, 0)

    def last(step, carry):
        @pl.when(step < plane.pieces)
        def _():
            for side, total in enumerate(plane.last_sum(step)):
                plane.own[3, plane.rows(side, step)] = total.astype(jnp.bfloat16)

        line.advance(step)
        return carry

    lax.fori_loop(0, line.steps(), last, 0)
    for i in (6, 7):
        for copy in store(i):
            copy.wait()
    plane.finish()
    line.finish()


def experts_fused(arrived, arrived_grad, mask, router, bias, w_gate, w_up, w_down):
    ranks, rows, width = arrived.shape
    experts, _, hidden = w_gate.shape
    wide = width + LANE
    inner = experts * hidden
    half = rows // 2
    low = jnp.bfloat16
    any_space = pl.BlockSpec(memory_space=pl.ANY)
    vmem = pl.BlockSpec(memory_space=pltpu.VMEM)
    small_shape = jax.ShapeDtypeStruct((ranks, rows, inner), low)
    return pl.pallas_call(
        expert_kernel,
        out_shape=(
            jax.ShapeDtypeStruct((rows, wide), low), small_shape, small_shape, small_shape,
            jax.ShapeDtypeStruct((ranks, rows, width), low),
        ),
        in_specs=[any_space, any_space] + [vmem] * 6,
        out_specs=(vmem, any_space, any_space, any_space, any_space),
        scratch_shapes=[
            pltpu.VMEM((2, rows, width), low),
            pltpu.VMEM((2, rows, width), low),
            pltpu.VMEM((2, 4, rows, wide), low),
            pltpu.VMEM((4, rows, wide), low),
            pltpu.VMEM((3, half, wide), low),
            pltpu.VMEM((3, half, wide), low),
            pltpu.VMEM((rows, wide), low),
            pltpu.VMEM((2, 3, rows, inner), low),
            pltpu.VMEM((2, rows, width), low),
            pltpu.SemaphoreType.DMA((2, 2)),
            pltpu.SemaphoreType.DMA((4, 2)),
            *Plane.semaphores(rows),
            Line.semaphores(rows),
        ],
        compiler_params=pltpu.CompilerParams(
            collective_id=0, has_side_effects=True, vmem_limit_bytes=61 * 2**20
        ),
        cost_estimate=pl.CostEstimate(
            flops=12 * ranks * rows * width * inner, bytes_accessed=8 * ranks * rows * width, transcendentals=0
        ),
    )(arrived, arrived_grad, mask, router, bias, w_gate, w_up, w_down)


def product_kernel(left, right, spread, total, gathered, own, arrived, sems, *gather_sems):
    line = Line(own, arrived, total, sems)
    place = Place()
    gather = Gather(spread, gathered, place, *gather_sems, pieces=GATHER_PIECES)
    greet(place.neighbours() + line.neighbours())
    gather.start()
    width = right.shape[1]
    tile = min(512, width)
    for start in range(0, width, tile):
        columns = slice(start, start + tile)
        own[:, columns] = wide_dot(left[...], right[:, columns]).astype(jnp.bfloat16)
    steps = line.pieces + 2 * (line.size - 1)
    done = 0
    for piece in range(GATHER_PIECES):
        upto = steps * (piece + 1) * 2 // (3 * GATHER_PIECES)
        lax.fori_loop(done, upto, line.step_body, 0)
        done = upto
        gather.near(piece)
    lax.fori_loop(done, steps, line.step_body, 0)
    for piece in range(GATHER_PIECES):
        gather.far(piece)
    for kind in range(4):
        for piece in range(GATHER_PIECES):
            gather.paired(kind, piece)
    gather.finish_sends()
    line.finish()


GATHER_PIECES = 4


def summed_product(left, right, spread, collective_id):
    rows, width = left.shape[0], right.shape[1]
    vmem = pl.BlockSpec(memory_space=pltpu.VMEM)
    any_space = pl.BlockSpec(memory_space=pl.ANY)
    return pl.pallas_call(
        product_kernel,
        out_shape=(
            jax.ShapeDtypeStruct((rows, width), jnp.bfloat16),
            jax.ShapeDtypeStruct((lax.axis_size("expert"),) + spread.shape, spread.dtype),
        ),
        in_specs=[vmem, vmem, any_space],
        out_specs=(vmem, any_space),
        scratch_shapes=[
            pltpu.VMEM((rows, width), jnp.bfloat16),
            pltpu.VMEM((rows, width), jnp.bfloat16),
            Line.semaphores(rows),
            *Gather.semaphores(GATHER_PIECES),
        ],
        compiler_params=pltpu.CompilerParams(
            collective_id=collective_id, has_side_effects=True, vmem_limit_bytes=40 * 2**20
        ),
    )(left, right, spread)


def crossed_dot(left, right):
    return lax.dot_general(left, right, (((0,), (0,)), ((), ())), preferred_element_type=jnp.float32)


def closing_kernel(
    normed, query_grad, key_grad, value_grad, attended, attention_grad, w_query, w_key, w_value, extras,
    total, sums,
    line_own, line_in, part, paired, from_x, from_y, line_sems, pair_sems, x_sems, y_sems,
):
    rows, width = normed.shape
    heads = query_grad.shape[1]
    share = part.shape[2]
    tile = min(512, width)
    line = Line(line_own, line_in, total, line_sems)
    plane = Plane(part.at[1], part.at[0], paired, from_x, from_y, pair_sems, x_sems, y_sems)
    greet(plane.neighbours() + line.neighbours())
    for start in range(0, width, tile):
        columns = slice(start, start + tile)
        line_own[:, columns] = (
            turned_dot(query_grad[...], w_query[columns])
            + turned_dot(key_grad[...], w_key[columns])
            + turned_dot(value_grad[...], w_value[columns])
        ).astype(jnp.bfloat16)

    def pair(chip, carry):
        for sub in range(2):
            block = plane.block(chip, (plane.core + 1 - sub) % 2)
            columns = pl.ds(pl.multiple_of(block * share, share), share)
            source = normed[:, columns]
            part[sub, chip, :, 0:heads] = crossed_dot(source, query_grad[...]).astype(jnp.bfloat16)
            part[sub, chip, :, heads : 2 * heads] = crossed_dot(source, key_grad[...]).astype(jnp.bfloat16)
            part[sub, chip, :, 2 * heads : 3 * heads] = crossed_dot(source, value_grad[...]).astype(jnp.bfloat16)
            part[sub, chip, :, 3 * heads : 4 * heads] = crossed_dot(
                attention_grad[:, columns], attended[...]
            ).astype(jnp.bfloat16)
            part[sub, chip, :, 4 * heads :] = extras[block]
            if sub == 0:
                plane.pair_copy(chip).start()
        line.advance(chip)
        return carry

    lax.fori_loop(0, 4, pair, 0)
    for chip in range(4):
        plane.pair_copy(chip).wait_recv()
    for chip in range(3):
        plane.send_first(chip)
    late = plane.pieces + 2

    def step(s, carry):
        line.advance(s)

        @pl.when(s - 4 < plane.pieces)
        def _():
            plane.second_piece(s - 4)

        @pl.when((s >= 4 + late) & (s - 4 - late < plane.pieces))
        def _():
            piece = s - 4 - late
            for side, summed in enumerate(plane.last_sum(piece)):
                sums[plane.rows(side, piece)] = summed

        return carry

    lax.fori_loop(4, jnp.maximum(line.steps(), 4 + late + plane.pieces), step, 0)
    plane.finish()
    line.finish()


def closing(normed, query_grad, key_grad, value_grad, attended, attention_grad, w_query, w_key, w_value, extras):
    rows, width = normed.shape
    heads = query_grad.shape[1]
    ranks, share, more = extras.shape
    wide = 4 * heads + more
    low = jnp.bfloat16
    vmem = pl.BlockSpec(memory_space=pltpu.VMEM)
    return pl.pallas_call(
        closing_kernel,
        out_shape=(
            jax.ShapeDtypeStruct((rows, width), low),
            jax.ShapeDtypeStruct((share, wide), jnp.float32),
        ),
        in_specs=[vmem] * 10,
        out_specs=(vmem, vmem),
        scratch_shapes=[
            pltpu.VMEM((rows, width), low),
            pltpu.VMEM((rows, width), low),
            pltpu.VMEM((2, 4, share, wide), low),
            pltpu.VMEM((4, share, wide), low),
            pltpu.VMEM((3, share // 2, wide), low),
            pltpu.VMEM((3, share // 2, wide), low),
            Line.semaphores(rows),
            *Plane.semaphores(share),
        ],
        compiler_params=pltpu.CompilerParams(
            collective_id=2, has_side_effects=True, vmem_limit_bytes=58 * 2**20
        ),
    )(normed, query_grad, key_grad, value_grad, attended, attention_grad, w_query, w_key, w_value, extras)


epsilon = 1e-05
masked_value = -1e30


def rotate(field, cosine, sine):
    half = field.shape[-1] // 2
    first = field[..., :half]
    second = field[..., half:]
    return jnp.concatenate(
        [first * cosine - second * sine, second * cosine + first * sine], axis=-1
    )


def unrotate(grad, cosine, sine):
    half = grad.shape[-1] // 2
    first = grad[..., :half]
    second = grad[..., half:]
    return jnp.concatenate(
        [first * cosine + second * sine, second * cosine - first * sine], axis=-1
    )


def experts(normed_two, cotangent, gates, w_gate, w_up, w_down, experts_total):
    local_experts = w_gate.shape[0]
    device = lax.axis_index("expert")
    arrived = lax.all_gather(normed_two, "expert", axis=0, tiled=True)
    arrived_grad = lax.all_gather(cotangent, "expert", axis=0, tiled=True)
    gate_pre = jnp.einsum("rd,jdf->jrf", arrived, w_gate, preferred_element_type=jnp.float32)
    up_pre = jnp.einsum("rd,jdf->jrf", arrived, w_up, preferred_element_type=jnp.float32)
    raw_grad = jnp.einsum("rd,jfd->jrf", arrived_grad, w_down, preferred_element_type=jnp.float32)
    sigma = jax.nn.sigmoid(gate_pre)
    activated = gate_pre * sigma
    inner = activated * up_pre
    gated = (gates[:, :, None] * inner).astype(jnp.bfloat16)
    mixed_part = jnp.einsum("jrf,jfd->rd", gated, w_down, preferred_element_type=jnp.float32)
    mixture = lax.psum(
        lax.psum_scatter(
            mixed_part.astype(jnp.bfloat16), "expert", scatter_dimension=0, tiled=True
        ),
        "tensor",
    ).astype(jnp.float32)
    gate_grad_part = jnp.sum(raw_grad * inner, axis=2)
    act_grad = gates[:, :, None] * raw_grad
    up_grad = (act_grad * activated).astype(jnp.bfloat16)
    gate_grad = (act_grad * up_pre * sigma * (1.0 + gate_pre * (1.0 - sigma))).astype(jnp.bfloat16)
    grad_w_down = jnp.einsum("jrf,rd->jfd", gated, arrived_grad, preferred_element_type=jnp.float32)
    grad_w_gate = jnp.einsum("rd,jrf->jdf", arrived, gate_grad, preferred_element_type=jnp.float32)
    grad_w_up = jnp.einsum("rd,jrf->jdf", arrived, up_grad, preferred_element_type=jnp.float32)
    slot_grad = jnp.einsum("jrf,jdf->rd", gate_grad, w_gate, preferred_element_type=jnp.float32)
    slot_grad = slot_grad + jnp.einsum(
        "jrf,jdf->rd", up_grad, w_up, preferred_element_type=jnp.float32
    )
    moe_input_grad = lax.psum(
        lax.psum_scatter(
            slot_grad.astype(jnp.bfloat16), "expert", scatter_dimension=0, tiled=True
        ),
        "tensor",
    ).astype(jnp.float32)
    placed = jnp.zeros((arrived.shape[0], experts_total), jnp.float32)
    placed = lax.dynamic_update_slice_in_dim(placed, gate_grad_part.T, device * local_experts, 1)
    chance_grad = lax.psum(
        lax.psum_scatter(placed, "expert", scatter_dimension=0, tiled=True), "tensor"
    )
    return mixture, moe_input_grad, chance_grad, [grad_w_gate, grad_w_up, grad_w_down]


def body(
    tokens,
    w_query,
    w_key,
    w_value,
    w_out,
    attn_gain,
    ffn_gain,
    qk_gain,
    router,
    w_gate,
    w_up,
    w_down,
    routes,
    cont_group,
    cotangent,
):
    rows, width = tokens.shape
    local_width = w_query.shape[1]
    head_count = local_width // HD
    experts_total = router.shape[1]
    local_experts = w_gate.shape[0]
    ranks = lax.axis_size("expert")
    device = lax.axis_index("expert")
    span = ranks // 2
    compact = ranks == 8
    prompt_len = PROMPT_DEV * span
    factor = HD ** (-0.5)
    local = jnp.arange(rows, dtype=jnp.int32)
    is_prompt = local < PROMPT_DEV
    after = jnp.maximum(local - PROMPT_DEV, 0)
    slot_cont = after // CLEN
    cont_pick = jnp.sum(
        jnp.where(
            slot_cont[:, None] == jnp.arange(CONT_DEV, dtype=jnp.int32)[None, :],
            cont_group[None, :],
            0,
        ),
        axis=1,
    )
    group = jnp.where(is_prompt, device // span, cont_pick)
    position = jnp.where(is_prompt, device % span * PROMPT_DEV + local, prompt_len + after % CLEN)
    tag = jnp.where(is_prompt, -1, slot_cont)
    frequency = 10000.0 ** (-jnp.arange(HD // 2, dtype=jnp.float32) * 2.0 / HD)
    angle = position.astype(jnp.float32)[:, None] * frequency[None, :]
    cosine = jnp.cos(angle)[:, None, :]
    sine = jnp.sin(angle)[:, None, :]
    source = tokens.astype(jnp.float32)
    scale_one = lax.rsqrt(jnp.mean(source * source, axis=1, keepdims=True) + epsilon)
    normed = (source * scale_one * attn_gain).astype(jnp.bfloat16)
    query_raw = jnp.dot(normed, w_query, preferred_element_type=jnp.float32)
    key_raw = jnp.dot(normed, w_key, preferred_element_type=jnp.float32)
    value_raw = jnp.dot(normed, w_value, preferred_element_type=jnp.float32)
    squares = lax.psum(
        jnp.stack(
            [jnp.sum(query_raw * query_raw, axis=1), jnp.sum(key_raw * key_raw, axis=1)], axis=1
        ),
        "tensor",
    )
    scale_query = lax.rsqrt(squares[:, 0:1] / width + epsilon)
    scale_key = lax.rsqrt(squares[:, 1:2] / width + epsilon)
    query_rot = (
        rotate((query_raw * scale_query * qk_gain[0]).reshape(rows, head_count, HD), cosine, sine)
        .reshape(rows, local_width)
        .astype(jnp.bfloat16)
    )
    key_rot = (
        rotate((key_raw * scale_key * qk_gain[1]).reshape(rows, head_count, HD), cosine, sine)
        .reshape(rows, local_width)
        .astype(jnp.bfloat16)
    )
    value_low = value_raw.astype(jnp.bfloat16)
    prompts = lax.all_gather(
        jnp.concatenate([key_rot[:PROMPT_DEV], value_low[:PROMPT_DEV]], axis=1),
        "expert",
        axis=0,
        tiled=True,
    )
    prompt_keys, prompt_values = prompts[:, :local_width], prompts[:, local_width:]
    prompt_count = prompt_keys.shape[0]
    all_keys = jnp.concatenate([prompt_keys, key_rot[PROMPT_DEV:]], axis=0)
    all_values = jnp.concatenate([prompt_values, value_low[PROMPT_DEV:]], axis=0)
    key_index = jnp.arange(prompt_count, dtype=jnp.int32)
    prompt_mask = (group[:, None] == (key_index // prompt_len)[None, :]) & (
        (key_index % prompt_len)[None, :] <= position[:, None]
    )
    own_mask = (tag[:, None] == tag[None, PROMPT_DEV:]) & (
        position[None, PROMPT_DEV:] <= position[:, None]
    )
    mask = jnp.concatenate([prompt_mask, own_mask], axis=1)

    def head_scores(query_head, key_head):
        scores = (
            jnp.einsum("qd,kd->qk", query_head, key_head, preferred_element_type=jnp.float32)
            * factor
        )
        return jnp.where(mask, scores, masked_value)

    outputs = []
    log_totals = []
    for head in range(head_count):
        start = head * HD
        scores = head_scores(query_rot[:, start : start + HD], all_keys[:, start : start + HD])
        top = jnp.max(scores, axis=1, keepdims=True)
        weights = jnp.exp(scores - top)
        total = jnp.sum(weights, axis=1, keepdims=True)
        shares = (weights / total).astype(jnp.bfloat16)
        outputs.append(
            jnp.dot(shares, all_values[:, start : start + HD], preferred_element_type=jnp.float32)
        )
        log_totals.append(top + jnp.log(total))
    attended = jnp.concatenate(outputs, axis=1).astype(jnp.bfloat16)
    if compact:
        attention, arrived_grad = summed_product(attended, w_out, cotangent, 1)
        attention = attention.astype(jnp.float32)
    else:
        attention = lax.psum(
            jnp.dot(attended, w_out, preferred_element_type=jnp.float32), "tensor"
        )
    hidden = source + attention
    scale_two = lax.rsqrt(jnp.mean(hidden * hidden, axis=1, keepdims=True) + epsilon)
    normed_two = (hidden * scale_two * ffn_gain).astype(jnp.bfloat16)
    logits = jnp.dot(normed_two, router, preferred_element_type=jnp.float32)
    top = jnp.max(logits, axis=1, keepdims=True)
    weights = jnp.exp(logits - top)
    chances = weights / jnp.sum(weights, axis=1, keepdims=True)
    hits = (routes[:, :, None] == jnp.arange(experts_total, dtype=jnp.int32)[None, None, :]).astype(
        jnp.float32
    )
    rows_mask = jnp.sum(hits, axis=1)
    grad_out = cotangent.astype(jnp.float32)
    if compact:
        routes_all = lax.all_gather(routes, "expert", axis=0)
        own_expert = device * local_experts + jnp.arange(local_experts, dtype=jnp.int32)
        own_mask = jnp.any(routes_all[:, :, :, None] == own_expert, axis=2).astype(jnp.float32)
        own_mask = jnp.pad(own_mask, ((0, 0), (0, 0), (0, LANE - local_experts)))
        own_first = jnp.roll(router, -device * local_experts, axis=1)
        own_first = jnp.pad(own_first, ((0, 0), (0, LANE - experts_total)))
        bias = jnp.where(jnp.arange(LANE) < experts_total, 0.0, masked_value)
        bias = bias.astype(jnp.float32)[None]
        arrived = lax.all_gather(normed_two, "expert", axis=0)
        reduced, gated, gate_grad, up_grad, mixed_part = experts_fused(
            arrived, arrived_grad, own_mask, own_first, bias, w_gate, w_up, w_down
        )
        moe_input_grad = reduced[:, :width].astype(jnp.float32)
        chance_grad = reduced[:, width : width + experts_total].astype(jnp.float32)
        mixture = lax.psum(
            lax.psum_scatter(
                mixed_part.reshape(ranks * rows, width), "expert", scatter_dimension=0, tiled=True
            ),
            "tensor",
        ).astype(jnp.float32)
        hidden_units = w_gate.shape[2]

        def per_expert(j):
            span = slice(j * hidden_units, (j + 1) * hidden_units)
            return (
                jnp.einsum("nrd,nrf->df", arrived, gate_grad[:, :, span], preferred_element_type=jnp.float32),
                jnp.einsum("nrd,nrf->df", arrived, up_grad[:, :, span], preferred_element_type=jnp.float32),
                jnp.einsum("nrf,nrd->fd", gated[:, :, span], arrived_grad, preferred_element_type=jnp.float32),
            )

        grad_w_gate, grad_w_up, grad_w_down = (
            jnp.stack(list(parts)) for parts in zip(*(per_expert(j) for j in range(local_experts)))
        )
    else:
        routed = lax.all_gather(
            (rows_mask * chances).astype(jnp.float32), "expert", axis=0, tiled=True
        )
        gates = lax.dynamic_slice_in_dim(routed, device * local_experts, local_experts, 1).T
        pieces = max(1, ranks * rows // 4096)
        piece = rows // pieces
        split_gates = gates.reshape(local_experts, ranks, rows)
        results = []
        weight_grads = None
        for number in range(pieces):
            part = slice(number * piece, (number + 1) * piece)
            sources = (normed_two[part], cotangent[part])
            if results:
                sources, results, weight_grads = lax.optimization_barrier(
                    (sources, results, weight_grads)
                )
            *result, grads = experts(
                *sources,
                split_gates[:, :, part].reshape(local_experts, ranks * piece),
                w_gate,
                w_up,
                w_down,
                experts_total,
            )
            results.append(result)
            weight_grads = grads if weight_grads is None else [a + b for a, b in zip(weight_grads, grads)]
        mixture, moe_input_grad, chance_grad = (
            jnp.concatenate(list(group_of), axis=0) for group_of in zip(*results)
        )
        grad_w_gate, grad_w_up, grad_w_down = weight_grads
    chance_grad = rows_mask * chance_grad
    output = (hidden + mixture).astype(jnp.bfloat16)
    logit_grad = (
        chances * (chance_grad - jnp.sum(chances * chance_grad, axis=1, keepdims=True))
    ).astype(jnp.bfloat16)
    grad_router = jnp.einsum(
        "td,te->de", normed_two, logit_grad, preferred_element_type=jnp.float32
    )
    normed_two_grad = moe_input_grad + jnp.einsum(
        "te,de->td", logit_grad, router, preferred_element_type=jnp.float32
    )
    weighted_two = ffn_gain * normed_two_grad
    grad_ffn_gain = jnp.sum(normed_two_grad * hidden * scale_two, axis=0)
    hidden_grad = (
        grad_out
        + scale_two * weighted_two
        - hidden * (scale_two**3 / width) * jnp.sum(weighted_two * hidden, axis=1, keepdims=True)
    )
    attention_grad = hidden_grad.astype(jnp.bfloat16)
    attended_grad = jnp.einsum(
        "te,de->td", attention_grad, w_out, preferred_element_type=jnp.float32
    ).astype(jnp.bfloat16)
    query_grads = []
    key_grads = []
    value_grads = []
    for head in range(head_count):
        start = head * HD
        query_head = query_rot[:, start : start + HD]
        key_head = all_keys[:, start : start + HD]
        value_head = all_values[:, start : start + HD]
        out_grad_head = attended_grad[:, start : start + HD]
        recomputed = jnp.exp(head_scores(query_head, key_head) - log_totals[head])
        share_grad = jnp.einsum(
            "qd,kd->qk", out_grad_head, value_head, preferred_element_type=jnp.float32
        )
        delta = jnp.sum(recomputed * share_grad, axis=1, keepdims=True)
        score_grad = (recomputed * (share_grad - delta)).astype(jnp.bfloat16)
        query_grads.append(
            jnp.dot(score_grad, key_head, preferred_element_type=jnp.float32) * factor
        )
        key_grads.append(
            jnp.einsum("qk,qd->kd", score_grad, query_head, preferred_element_type=jnp.float32)
            * factor
        )
        value_grads.append(
            jnp.einsum(
                "qk,qd->kd",
                recomputed.astype(jnp.bfloat16),
                out_grad_head,
                preferred_element_type=jnp.float32,
            )
        )
    key_grad_all = jnp.concatenate(key_grads, axis=1)
    value_grad_all = jnp.concatenate(value_grads, axis=1)
    prompt_grads = lax.psum_scatter(
        jnp.concatenate(
            [key_grad_all[:prompt_count], value_grad_all[:prompt_count]], axis=1
        ).astype(jnp.bfloat16),
        "expert",
        scatter_dimension=0,
        tiled=True,
    ).astype(jnp.float32)
    prompt_key_grad, prompt_value_grad = prompt_grads[:, :local_width], prompt_grads[:, local_width:]
    key_grad = jnp.concatenate([prompt_key_grad, key_grad_all[prompt_count:]], axis=0)
    value_grad = jnp.concatenate([prompt_value_grad, value_grad_all[prompt_count:]], axis=0)
    query_grad = unrotate(
        jnp.concatenate(query_grads, axis=1).reshape(rows, head_count, HD), cosine, sine
    ).reshape(rows, local_width)
    key_grad = unrotate(key_grad.reshape(rows, head_count, HD), cosine, sine).reshape(
        rows, local_width
    )
    grad_qk_gain = jnp.stack(
        [
            jnp.sum(query_grad * query_raw * scale_query, axis=0),
            jnp.sum(key_grad * key_raw * scale_key, axis=0),
        ],
        axis=0,
    )
    weighted_query = qk_gain[0] * query_grad
    weighted_key = qk_gain[1] * key_grad
    inner_sums = lax.psum(
        jnp.stack(
            [jnp.sum(weighted_query * query_raw, axis=1), jnp.sum(weighted_key * key_raw, axis=1)],
            axis=1,
        ),
        "tensor",
    )
    query_raw_grad = (
        scale_query * weighted_query - query_raw * (scale_query**3 / width) * inner_sums[:, 0:1]
    ).astype(jnp.bfloat16)
    key_raw_grad = (
        scale_key * weighted_key - key_raw * (scale_key**3 / width) * inner_sums[:, 1:2]
    ).astype(jnp.bfloat16)
    value_raw_grad = value_grad.astype(jnp.bfloat16)
    if compact:
        small_part = local_width // ranks
        gains = jnp.pad(
            grad_qk_gain.reshape(2, ranks, small_part).transpose(1, 2, 0),
            ((0, 0), (0, width // ranks - small_part), (0, 0)),
        )
        extras = jnp.concatenate(
            [
                grad_router.reshape(ranks, width // ranks, experts_total),
                grad_ffn_gain.reshape(ranks, width // ranks, 1),
                gains,
            ],
            axis=2,
        ).astype(jnp.bfloat16)
        extras = jnp.pad(extras, ((0, 0), (0, 0), (0, LANE - experts_total - 3)))
        normed_grad, sums = closing(
            normed,
            query_raw_grad,
            key_raw_grad,
            value_raw_grad,
            attended,
            attention_grad,
            w_query,
            w_key,
            w_value,
            extras,
        )
        normed_grad = normed_grad.astype(jnp.float32)
    else:
        grad_w_out = jnp.einsum(
            "td,te->de", attended, attention_grad, preferred_element_type=jnp.float32
        )
        grad_w_query = jnp.einsum(
            "td,te->de", normed, query_raw_grad, preferred_element_type=jnp.float32
        )
        grad_w_key = jnp.einsum("td,te->de", normed, key_raw_grad, preferred_element_type=jnp.float32)
        grad_w_value = jnp.einsum(
            "td,te->de", normed, value_raw_grad, preferred_element_type=jnp.float32
        )
        normed_part = jnp.einsum(
            "te,de->td", query_raw_grad, w_query, preferred_element_type=jnp.float32
        )
        normed_part = normed_part + jnp.einsum(
            "te,de->td", key_raw_grad, w_key, preferred_element_type=jnp.float32
        )
        normed_part = normed_part + jnp.einsum(
            "te,de->td", value_raw_grad, w_value, preferred_element_type=jnp.float32
        )
        normed_grad = lax.psum(normed_part.astype(jnp.bfloat16), "tensor").astype(jnp.float32)
    weighted_one = attn_gain * normed_grad
    grad_attn_gain = jnp.sum(normed_grad * source * scale_one, axis=0)
    input_grad = (
        hidden_grad
        + scale_one * weighted_one
        - source * (scale_one**3 / width) * jnp.sum(weighted_one * source, axis=1, keepdims=True)
    )
    if compact:
        edge = 4 * local_width
        summed = (
            sums[:, :local_width],
            sums[:, local_width : 2 * local_width],
            sums[:, 2 * local_width : 3 * local_width],
            sums[:, 3 * local_width : edge].T,
            lax.psum_scatter(
                grad_attn_gain.astype(jnp.bfloat16), "expert", scatter_dimension=0, tiled=True
            ).astype(jnp.float32),
            sums[:, edge + experts_total],
            sums[:small_part, edge + experts_total + 1 : edge + experts_total + 3].T,
            sums[:, edge : edge + experts_total],
        )
    else:
        summed = (
            lax.psum_scatter(
                grad_w_query.astype(jnp.bfloat16), "expert", scatter_dimension=0, tiled=True
            ).astype(jnp.float32),
            lax.psum_scatter(
                grad_w_key.astype(jnp.bfloat16), "expert", scatter_dimension=0, tiled=True
            ).astype(jnp.float32),
            lax.psum_scatter(
                grad_w_value.astype(jnp.bfloat16), "expert", scatter_dimension=0, tiled=True
            ).astype(jnp.float32),
            lax.psum_scatter(
                grad_w_out.astype(jnp.bfloat16), "expert", scatter_dimension=1, tiled=True
            ).astype(jnp.float32),
            lax.psum_scatter(
                grad_attn_gain.astype(jnp.bfloat16), "expert", scatter_dimension=0, tiled=True
            ).astype(jnp.float32),
            lax.psum_scatter(
                grad_ffn_gain.astype(jnp.bfloat16), "expert", scatter_dimension=0, tiled=True
            ).astype(jnp.float32),
            lax.psum_scatter(
                grad_qk_gain.astype(jnp.bfloat16), "expert", scatter_dimension=1, tiled=True
            ).astype(jnp.float32),
            lax.psum_scatter(
                grad_router.astype(jnp.bfloat16), "expert", scatter_dimension=0, tiled=True
            ).astype(jnp.float32),
        )
    return (
        output,
        input_grad,
        summed[0],
        summed[1],
        summed[2],
        summed[3],
        summed[4],
        summed[5],
        summed[6],
        summed[7],
        grad_w_gate,
        grad_w_up,
        grad_w_down,
    )


def solution(mesh):
    return jax.shard_map(
        body,
        mesh=mesh,
        in_specs=(
            P("expert", None),
            P(None, "tensor"),
            P(None, "tensor"),
            P(None, "tensor"),
            P("tensor", None),
            P(),
            P(),
            P(None, "tensor"),
            P(),
            P("expert", None, "tensor"),
            P("expert", None, "tensor"),
            P("expert", "tensor", None),
            P("expert", None),
            P("expert"),
            P("expert", None),
        ),
        out_specs=(
            P("expert", None),
            P("expert", None),
            P("expert", "tensor"),
            P("expert", "tensor"),
            P("expert", "tensor"),
            P("tensor", "expert"),
            P("expert"),
            P("expert"),
            P(None, ("tensor", "expert")),
            P("expert", None),
            P("expert", None, "tensor"),
            P("expert", None, "tensor"),
            P("expert", "tensor", None),
        ),
        check_vma=False,
    )
```

```python
import jax
import jax.numpy as jnp
from jax import lax
from jax.experimental import pallas as pl
from jax.experimental.pallas import tpu as pltpu
from jax.sharding import PartitionSpec as P

HD = 128
PROMPT_DEV = 128
CLEN = 256
CONT_DEV = 1


MESH = pl.DeviceIdType.MESH
STEP = 16
LANE = 128


def remote(source, target, sent, received, **where):
    return pltpu.make_async_remote_copy(
        src_ref=source,
        dst_ref=target,
        send_sem=sent,
        recv_sem=received,
        device_id=where,
        device_id_type=MESH,
    )


def greet(places):
    barrier = pltpu.get_barrier_semaphore()
    for condition, where in places:
        def signal(where=where):
            pl.semaphore_signal(barrier, inc=1, device_id=where, device_id_type=MESH)
        if condition is None:
            signal()
        else:
            pl.when(condition)(signal)
    count = 0
    for condition, _ in places:
        count = count + (1 if condition is None else jnp.where(condition, 1, 0))
    pl.semaphore_wait(barrier, count)


class Line:
    def __init__(self, own, arrived, total, sems):
        self.own, self.arrived, self.total = own, arrived, total
        self.up_sent, self.up_got, self.down_sent, self.down_got = (sems.at[i] for i in range(4))
        self.size = lax.axis_size("tensor")
        self.here = lax.axis_index("tensor")
        self.half = own.shape[0] // 2
        self.pieces = self.half // STEP

    @staticmethod
    def semaphores(rows):
        return pltpu.SemaphoreType.DMA((4, 2, rows // 2 // STEP))

    def neighbours(self):
        here, size = self.here, self.size
        return [
            (here > 0, {"tensor": jnp.maximum(here - 1, 0)}),
            (here < size - 1, {"tensor": jnp.minimum(here + 1, size - 1)}),
        ]

    def lane(self, lane):
        here, size = self.here, self.size
        if lane == 0:
            return here, here + 1, here - 1
        return size - 1 - here, here - 1, here + 1

    def rows(self, lane, piece):
        return pl.ds(pl.multiple_of(lane * self.half + piece * STEP, STEP), STEP)

    def up_copy(self, lane, piece):
        rows = self.rows(lane, piece)
        onward = self.lane(lane)[1]
        return remote(
            self.own.at[rows], self.arrived.at[rows],
            self.up_sent.at[lane, piece], self.up_got.at[lane, piece], tensor=onward,
        )

    def down_copy(self, lane, piece):
        rows = self.rows(lane, piece)
        back = self.lane(lane)[2]
        return remote(
            self.total.at[rows], self.total.at[rows],
            self.down_sent.at[lane, piece], self.down_got.at[lane, piece], tensor=back,
        )

    def rise(self, lane, piece):
        place = self.lane(lane)[0]
        rows = self.rows(lane, piece)

        @pl.when(place > 0)
        def _():
            self.up_copy(lane, piece).wait_recv()
            summed = (
                self.own[rows].astype(jnp.float32) + self.arrived[rows].astype(jnp.float32)
            ).astype(jnp.bfloat16)

            @pl.when(place < self.size - 1)
            def _():
                self.own[rows] = summed

            @pl.when(place == self.size - 1)
            def _():
                self.total[rows] = summed
                self.down_copy(lane, piece).start()

        @pl.when(place < self.size - 1)
        def _():
            self.up_copy(lane, piece).start()

    def fall(self, lane, piece):
        place = self.lane(lane)[0]

        @pl.when(place < self.size - 1)
        def _():
            self.down_copy(lane, piece).wait_recv()

            @pl.when(place > 0)
            def _():
                self.down_copy(lane, piece).start()

    def advance(self, step, skew=1):
        for act, far in ((self.rise, False), (self.fall, True)):
            for lane in range(2):
                place = self.lane(lane)[0]
                piece = step - skew * (2 * (self.size - 1) - place if far else place)

                @pl.when((piece >= 0) & (piece < self.pieces))
                def _():
                    act(lane, piece)

    def step_body(self, step, carry):
        self.advance(step)
        return carry

    def steps(self, skew=1):
        return self.pieces + skew * 2 * (self.size - 1)

    def finish(self):
        def one(piece, carry):
            for lane in range(2):
                place = self.lane(lane)[0]

                @pl.when(place < self.size - 1)
                def _():
                    self.up_copy(lane, piece).wait_send()

                @pl.when(place > 0)
                def _():
                    self.down_copy(lane, piece).wait_send()
            return carry

        lax.fori_loop(0, self.pieces, one, 0)


class Place:
    def __init__(self):
        here = lax.axis_index("expert")
        self.here = here
        self.core, self.x, self.y = here % 2, here // 2 % 2, here // 4
        self.sibling = here + 1 - 2 * self.core
        self.x_chip = here + 2 - 4 * self.x
        self.y_chip = here + 4 - 8 * self.y

    def neighbours(self):
        return [(None, {"expert": i}) for i in (self.sibling, self.x_chip, self.y_chip)]

    def block(self, chip, core):
        x = self.x + (1 - chip // 2) * (1 - 2 * self.x)
        y = self.y + (1 - chip % 2) * (1 - 2 * self.y)
        return 4 * y + 2 * x + core


class Plane(Place):
    def __init__(self, own, spare, paired, from_x, from_y, pair_sems, x_sems, y_sems, by_device=False):
        self.by_device = by_device
        self.own, self.spare, self.paired, self.from_x, self.from_y = own, spare, paired, from_x, from_y
        self.pair_sems, self.x_sems, self.y_sems = pair_sems, x_sems, y_sems
        super().__init__()
        self.half = own.shape[1] // 2
        self.pieces = self.half // STEP

    @staticmethod
    def semaphores(rows):
        pieces = rows // 2 // STEP
        return [
            pltpu.SemaphoreType.DMA((2, 4)),
            pltpu.SemaphoreType.DMA((2, 3, pieces)),
            pltpu.SemaphoreType.DMA((2, 3, pieces)),
        ]

    def pair_copy(self, chip):
        place = self.block(chip, 1 - self.core) if self.by_device else chip
        return remote(
            self.spare.at[place], self.paired.at[chip],
            self.pair_sems.at[0, chip], self.pair_sems.at[1, chip], expert=self.sibling,
        )

    def rows(self, side, piece):
        return pl.ds(pl.multiple_of(side * self.half + piece * STEP, STEP), STEP)

    def landing(self, piece):
        return pl.ds(pl.multiple_of(piece * STEP, STEP), STEP)

    def x_copy(self, kind, piece):
        chip, side = ((0, 0), (1, 0), (1, 1))[kind]
        return remote(
            self.own.at[chip, self.rows(side, piece)], self.from_x.at[kind, self.landing(piece)],
            self.x_sems.at[0, kind, piece], self.x_sems.at[1, kind, piece], expert=self.x_chip,
        )

    def y_copy(self, kind, piece):
        chip, side = ((0, 1), (2, 1), (2, 0))[kind]
        return remote(
            self.own.at[chip, self.rows(side, piece)], self.from_y.at[kind, self.landing(piece)],
            self.y_sems.at[0, kind, piece], self.y_sems.at[1, kind, piece], expert=self.y_chip,
        )

    def add_pair(self, chip, side, piece):
        rows = self.rows(side, piece)
        self.own[chip, rows] = (
            self.own[chip, rows].astype(jnp.float32) + self.paired[chip, rows].astype(jnp.float32)
        ).astype(jnp.bfloat16)

    def each(self, step):
        def one(piece, carry):
            step(piece)
            return carry

        lax.fori_loop(0, self.pieces, one, 0)

    def send_first(self, chip):
        def step(piece):
            if chip in (0, 1):
                self.add_pair(chip, 0, piece)
                self.x_copy(chip, piece).start()
            if chip in (0, 2):
                self.add_pair(chip, 1, piece)
                self.y_copy(chip // 2, piece).start()

        self.each(step)

    def second_piece(self, piece):
        landed = self.landing(piece)
        self.y_copy(0, piece).wait_recv()
        rows = self.rows(1, piece)
        self.own[1, rows] = (
            self.own[1, rows].astype(jnp.float32)
            + self.paired[1, rows].astype(jnp.float32)
            + self.from_y[0, landed].astype(jnp.float32)
        ).astype(jnp.bfloat16)
        self.x_copy(2, piece).start()
        self.x_copy(0, piece).wait_recv()
        rows = self.rows(0, piece)
        self.own[2, rows] = (
            self.own[2, rows].astype(jnp.float32)
            + self.paired[2, rows].astype(jnp.float32)
            + self.from_x[0, landed].astype(jnp.float32)
        ).astype(jnp.bfloat16)
        self.y_copy(2, piece).start()

    def send_second(self):
        self.each(self.second_piece)

    def last_sum(self, piece):
        landed = self.landing(piece)
        sums = []
        for side in range(2):
            first, second = (self.x_copy(1, piece), self.y_copy(2, piece)) if side == 0 else (self.y_copy(1, piece), self.x_copy(2, piece))
            first.wait_recv()
            second.wait_recv()
            a, b = (self.from_x[1, landed], self.from_y[2, landed]) if side == 0 else (self.from_y[1, landed], self.from_x[2, landed])
            rows = self.rows(side, piece)
            sums.append(
                self.own[3, rows].astype(jnp.float32)
                + self.paired[3, rows].astype(jnp.float32)
                + a.astype(jnp.float32)
                + b.astype(jnp.float32)
            )
        return sums

    def finish(self):
        for chip in range(4):
            self.pair_copy(chip).wait_send()

        def step(piece):
            for kind in range(3):
                self.x_copy(kind, piece).wait_send()
                self.y_copy(kind, piece).wait_send()

        self.each(step)


class Gather:
    def __init__(self, source, target, place, x_sems, y_sems, far_sems, pair_sems, own_sem, pieces):
        self.source, self.target = source, target
        self.place = place
        self.x_sems, self.y_sems, self.far_sems, self.pair_sems, self.own_sem = x_sems, y_sems, far_sems, pair_sems, own_sem
        self.pieces = pieces
        self.rows_each = source.shape[0] // pieces

    @staticmethod
    def semaphores(pieces):
        return [
            pltpu.SemaphoreType.DMA((2, pieces)),
            pltpu.SemaphoreType.DMA((2, pieces)),
            pltpu.SemaphoreType.DMA((2, pieces)),
            pltpu.SemaphoreType.DMA((2, 4, pieces)),
            pltpu.SemaphoreType.DMA,
        ]

    def rows(self, piece):
        return pl.ds(piece * self.rows_each, self.rows_each)

    def own_copy(self):
        return pltpu.make_async_copy(self.source, self.target.at[self.place.here], self.own_sem)

    def x_copy(self, piece):
        rows = self.rows(piece)
        return remote(
            self.source.at[rows], self.target.at[self.place.here, rows],
            self.x_sems.at[0, piece], self.x_sems.at[1, piece], expert=self.place.x_chip,
        )

    def y_copy(self, piece):
        rows = self.rows(piece)
        return remote(
            self.source.at[rows], self.target.at[self.place.here, rows],
            self.y_sems.at[0, piece], self.y_sems.at[1, piece], expert=self.place.y_chip,
        )

    def far_copy(self, piece):
        rows = self.rows(piece)
        came, goes = (
            (self.place.x_chip, self.place.y_chip) if piece < self.pieces // 2 else (self.place.y_chip, self.place.x_chip)
        )
        return remote(
            self.target.at[came, rows], self.target.at[came, rows],
            self.far_sems.at[0, piece], self.far_sems.at[1, piece], expert=goes,
        )

    def pair_copy(self, kind, piece):
        rows = self.rows(piece)
        block = self.place.block(kind, self.place.core)
        source = self.source.at[rows] if kind == 3 else self.target.at[block, rows]
        return remote(
            source, self.target.at[block, rows],
            self.pair_sems.at[0, kind, piece], self.pair_sems.at[1, kind, piece], expert=self.place.sibling,
        )

    def start(self):
        for piece in range(self.pieces):
            self.x_copy(piece).start()
            self.y_copy(piece).start()
            self.pair_copy(3, piece).start()
        self.own_copy().start()

    def near(self, piece):
        self.x_copy(piece).wait_recv()
        if piece < self.pieces // 2:
            self.far_copy(piece).start()
        self.pair_copy(1, piece).start()
        self.y_copy(piece).wait_recv()
        if piece >= self.pieces // 2:
            self.far_copy(piece).start()
        self.pair_copy(2, piece).start()

    def far(self, piece):
        self.far_copy(piece).wait_recv()
        self.pair_copy(0, piece).start()

    def paired(self, kind, piece):
        self.pair_copy(kind, piece).wait_recv()

    def finish_sends(self):
        self.own_copy().wait()
        for piece in range(self.pieces):
            self.x_copy(piece).wait_send()
            self.y_copy(piece).wait_send()
            self.far_copy(piece).wait_send()
            for kind in range(4):
                self.pair_copy(kind, piece).wait_send()


def wide_dot(left, right):
    return jnp.dot(left, right, preferred_element_type=jnp.float32)


def turned_dot(left, right):
    return lax.dot_general(left, right, (((1,), (1,)), ((), ())), preferred_element_type=jnp.float32)


def expert_kernel(
    x_all, g_all, mask, router, bias, w_gate, w_up, w_down,
    reduced, gated_all, gate_all, up_all, mixed_all,
    x_buf, g_buf, part, paired, from_x, from_y, line_in, small, mixed,
    in_sems, out_sems, pair_sems, x_sems, y_sems, line_sems,
):
    experts, width, hidden = w_gate.shape
    rows = x_buf.shape[1]
    tile = min(512, width)
    plane = Plane(part.at[1], part.at[0], paired, from_x, from_y, pair_sems, x_sems, y_sems)
    line = Line(part.at[1, 3], line_in, reduced, line_sems)
    first_expert = lax.axis_index("expert") * experts
    outs = (gated_all, gate_all, up_all)

    def block_of(i):
        return plane.block(i // 2, (plane.core + 1 - i % 2) % 2)

    def fetch(i):
        slot, block = i % 2, block_of(i)
        return (
            pltpu.make_async_copy(x_all.at[block], x_buf.at[slot], in_sems.at[0, slot]),
            pltpu.make_async_copy(g_all.at[block], g_buf.at[slot], in_sems.at[1, slot]),
        )

    def store(i):
        slot, block = i % 2, block_of(i)
        return [
            pltpu.make_async_copy(small.at[slot, n], outs[n].at[block], out_sems.at[n, slot])
            for n in range(3)
        ] + [pltpu.make_async_copy(mixed.at[slot], mixed_all.at[block], out_sems.at[3, slot])]

    def compute(i):
        slot = i % 2
        block = block_of(i)
        x = x_buf.at[slot]
        g = g_buf.at[slot]
        logits = wide_dot(x[...], router[...]) + bias[...]
        weights = jnp.exp(logits - jnp.max(logits, axis=1, keepdims=True))
        gates = weights / jnp.sum(weights, axis=1, keepdims=True) * mask[block]
        column = lax.broadcasted_iota(jnp.int32, (rows, LANE), 1)
        extra = jnp.zeros((rows, LANE), jnp.float32)
        for j in range(experts):
            gate_pre = wide_dot(x[...], w_gate[j])
            up_pre = wide_dot(x[...], w_up[j])
            raw = turned_dot(g[...], w_down[j])
            gate = gates[:, j : j + 1]
            sigma = jax.nn.sigmoid(gate_pre)
            activated = gate_pre * sigma
            inner = activated * up_pre
            act = gate * raw
            span = slice(j * hidden, (j + 1) * hidden)
            small[slot, 0, :, span] = (gate * inner).astype(jnp.bfloat16)
            small[slot, 1, :, span] = (
                act * up_pre * sigma * (1.0 + gate_pre * (1.0 - sigma))
            ).astype(jnp.bfloat16)
            small[slot, 2, :, span] = (act * activated).astype(jnp.bfloat16)
            gain = jnp.sum(raw * inner, axis=1, keepdims=True)
            extra = jnp.where(column == first_expert + j, gain, extra)
        for start in range(0, width, tile):
            columns = slice(start, start + tile)
            slot_grad = None
            mix = None
            for j in range(experts):
                span = slice(j * hidden, (j + 1) * hidden)
                term = turned_dot(small[slot, 1, :, span], w_gate[j, columns]) + turned_dot(
                    small[slot, 2, :, span], w_up[j, columns]
                )
                more = wide_dot(small[slot, 0, :, span], w_down[j, :, columns])
                slot_grad = term if slot_grad is None else slot_grad + term
                mix = more if mix is None else mix + more
            part[i % 2, i // 2, :, columns] = slot_grad.astype(jnp.bfloat16)
            mixed[slot, :, columns] = mix.astype(jnp.bfloat16)
        part[i % 2, i // 2, :, width:] = extra.astype(jnp.bfloat16)

    for copy in fetch(0):
        copy.start()
    greet(plane.neighbours() + line.neighbours())

    def step(i, carry):
        @pl.when(i < 7)
        def _():
            for copy in fetch(i + 1):
                copy.start()

        for copy in fetch(i):
            copy.wait()

        @pl.when(i >= 2)
        def _():
            for copy in store(i - 2):
                copy.wait()

        compute(i)
        for copy in store(i):
            copy.start()

        @pl.when(i % 2 == 0)
        def _():
            plane.pair_copy(i // 2).start()

        @pl.when(i % 2 == 1)
        def _():
            plane.pair_copy(i // 2).wait_recv()

        for chip in range(3):

            @pl.when(i == 2 * chip + 1)
            def _():
                plane.send_first(chip)
                if chip == 2:
                    plane.send_second()

        return carry

    lax.fori_loop(0, 8, step, 0)

    def last(step, carry):
        @pl.when(step < plane.pieces)
        def _():
            for side, total in enumerate(plane.last_sum(step)):
                plane.own[3, plane.rows(side, step)] = total.astype(jnp.bfloat16)

        line.advance(step)
        return carry

    lax.fori_loop(0, line.steps(), last, 0)
    for i in (6, 7):
        for copy in store(i):
            copy.wait()
    plane.finish()
    line.finish()


def experts_fused(arrived, arrived_grad, mask, router, bias, w_gate, w_up, w_down):
    ranks, rows, width = arrived.shape
    experts, _, hidden = w_gate.shape
    wide = width + LANE
    inner = experts * hidden
    half = rows // 2
    low = jnp.bfloat16
    any_space = pl.BlockSpec(memory_space=pl.ANY)
    vmem = pl.BlockSpec(memory_space=pltpu.VMEM)
    small_shape = jax.ShapeDtypeStruct((ranks, rows, inner), low)
    return pl.pallas_call(
        expert_kernel,
        out_shape=(
            jax.ShapeDtypeStruct((rows, wide), low), small_shape, small_shape, small_shape,
            jax.ShapeDtypeStruct((ranks, rows, width), low),
        ),
        in_specs=[any_space, any_space] + [vmem] * 6,
        out_specs=(vmem, any_space, any_space, any_space, any_space),
        scratch_shapes=[
            pltpu.VMEM((2, rows, width), low),
            pltpu.VMEM((2, rows, width), low),
            pltpu.VMEM((2, 4, rows, wide), low),
            pltpu.VMEM((4, rows, wide), low),
            pltpu.VMEM((3, half, wide), low),
            pltpu.VMEM((3, half, wide), low),
            pltpu.VMEM((rows, wide), low),
            pltpu.VMEM((2, 3, rows, inner), low),
            pltpu.VMEM((2, rows, width), low),
            pltpu.SemaphoreType.DMA((2, 2)),
            pltpu.SemaphoreType.DMA((4, 2)),
            *Plane.semaphores(rows),
            Line.semaphores(rows),
        ],
        compiler_params=pltpu.CompilerParams(
            collective_id=0, has_side_effects=True, vmem_limit_bytes=61 * 2**20
        ),
        cost_estimate=pl.CostEstimate(
            flops=12 * ranks * rows * width * inner, bytes_accessed=8 * ranks * rows * width, transcendentals=0
        ),
    )(arrived, arrived_grad, mask, router, bias, w_gate, w_up, w_down)


def product_kernel(left, right, spread, total, gathered, own, arrived, sems, *gather_sems):
    line = Line(own, arrived, total, sems)
    place = Place()
    gather = Gather(spread, gathered, place, *gather_sems, pieces=GATHER_PIECES)
    greet(place.neighbours() + line.neighbours())
    gather.start()
    width = right.shape[1]
    tile = min(512, width)
    for start in range(0, width, tile):
        columns = slice(start, start + tile)
        own[:, columns] = wide_dot(left[...], right[:, columns]).astype(jnp.bfloat16)
    steps = line.pieces + 2 * (line.size - 1)
    done = 0
    for piece in range(GATHER_PIECES):
        upto = steps * (piece + 1) * 2 // (3 * GATHER_PIECES)
        lax.fori_loop(done, upto, line.step_body, 0)
        done = upto
        gather.near(piece)
    lax.fori_loop(done, steps, line.step_body, 0)
    for piece in range(GATHER_PIECES):
        gather.far(piece)
    for kind in range(4):
        for piece in range(GATHER_PIECES):
            gather.paired(kind, piece)
    gather.finish_sends()
    line.finish()


GATHER_PIECES = 4


def summed_product(left, right, spread, collective_id):
    rows, width = left.shape[0], right.shape[1]
    vmem = pl.BlockSpec(memory_space=pltpu.VMEM)
    any_space = pl.BlockSpec(memory_space=pl.ANY)
    return pl.pallas_call(
        product_kernel,
        out_shape=(
            jax.ShapeDtypeStruct((rows, width), jnp.bfloat16),
            jax.ShapeDtypeStruct((lax.axis_size("expert"),) + spread.shape, spread.dtype),
        ),
        in_specs=[vmem, vmem, any_space],
        out_specs=(vmem, any_space),
        scratch_shapes=[
            pltpu.VMEM((rows, width), jnp.bfloat16),
            pltpu.VMEM((rows, width), jnp.bfloat16),
            Line.semaphores(rows),
            *Gather.semaphores(GATHER_PIECES),
        ],
        compiler_params=pltpu.CompilerParams(
            collective_id=collective_id, has_side_effects=True, vmem_limit_bytes=40 * 2**20
        ),
    )(left, right, spread)


def crossed_dot(left, right):
    return lax.dot_general(left, right, (((0,), (0,)), ((), ())), preferred_element_type=jnp.float32)


def closing_kernel(
    normed, query_grad, key_grad, value_grad, attended, attention_grad, extras,
    w_query, w_key, w_value, mixed, x_all, g_all, gated_all, gate_all, up_all,
    total, sums, mixture, gate_out, up_out, down_out,
    line_own, line_in, part, paired, from_x, from_y,
    mix_own, mix_paired, mix_x, mix_y, mix_in, tiles, factors, results, downs,
    line_sems, pair_sems, x_sems, y_sems, mix_line_sems, mix_pair_sems, mix_x_sems, mix_y_sems,
    load_sems, weight_sems, factor_sems, tile_sems, out_sems,
):
    width = normed.shape[1]
    heads = query_grad.shape[1]
    share = part.shape[2]
    experts, _, hidden = gate_out.shape
    column_tile = min(512, width // 2)
    tile = tiles.shape[2]
    count = width // tile
    line = Line(line_own, line_in, total, line_sems)
    plane = Plane(part.at[1], part.at[0], paired, from_x, from_y, pair_sems, x_sems, y_sems)
    mix = Plane(mix_own, mixed, mix_paired, mix_x, mix_y, mix_pair_sems, mix_x_sems, mix_y_sems, by_device=True)
    mix_line = Line(mix_own.at[3], mix_in, mixture, mix_line_sems)
    half = width // 2

    def load_own(chip):
        return pltpu.make_async_copy(mixed.at[mix.block(chip, mix.core)], mix_own.at[chip], load_sems.at[chip])

    weight_loads = [
        pltpu.make_async_copy(w_query, factors.at[0, 0:width], weight_sems.at[0]),
        pltpu.make_async_copy(w_key, factors.at[1, 0:width], weight_sems.at[1]),
        pltpu.make_async_copy(w_value.at[0:half], factors.at[0, width : width + half], weight_sems.at[2]),
        pltpu.make_async_copy(w_value.at[half:], factors.at[1, width : width + half], weight_sems.at[3]),
    ]

    def factor_load(matrix):
        return pltpu.make_async_copy(
            (gate_all, up_all, gated_all)[matrix], factors.at[matrix % 2], factor_sems.at[matrix]
        )

    def tile_copy(source, s):
        columns = pl.ds(pl.multiple_of(s % count * tile, tile), tile)
        return pltpu.make_async_copy(source.at[:, columns], tiles.at[s % 2], tile_sems.at[s % 2])

    def start_tile(s):
        @pl.when(s < 2 * count)
        def _():
            tile_copy(x_all, s).start()

        @pl.when(s >= 2 * count)
        def _():
            tile_copy(g_all, s).start()

    def across(target, s):
        rows = pl.ds(pl.multiple_of(s % count * tile, tile), tile)
        return [
            pltpu.make_async_copy(
                results.at[s % 2, :, j * hidden : (j + 1) * hidden], target.at[j, rows], out_sems.at[0, s % 2, j]
            )
            for j in range(experts)
        ]

    def down(s):
        columns = pl.ds(pl.multiple_of(s % count * tile, tile), tile)
        return [
            pltpu.make_async_copy(
                downs.at[s % 2, j * hidden : (j + 1) * hidden], down_out.at[j, :, columns], out_sems.at[1, s % 2, j]
            )
            for j in range(experts)
        ]

    def expert_tile(s):
        @pl.when(s + 1 < 3 * count)
        def _():
            start_tile(s + 1)

        for matrix in range(3):

            @pl.when(s == matrix * count)
            def _():
                factor_load(matrix).wait()

        tile_copy(x_all, s).wait()

        @pl.when(s < 2 * count)
        def _():
            @pl.when(s >= 2)
            def _():
                for copy in across(gate_out, s):
                    copy.wait()

            results[s % 2] = crossed_dot(tiles[s % 2], factors[s // count])

            @pl.when(s < count)
            def _():
                for copy in across(gate_out, s):
                    copy.start()

            @pl.when(s >= count)
            def _():
                for copy in across(up_out, s):
                    copy.start()

        @pl.when(s >= 2 * count)
        def _():
            @pl.when(s >= 2 * count + 2)
            def _():
                for copy in down(s):
                    copy.wait()

            downs[s % 2] = crossed_dot(factors[0], tiles[s % 2])
            for copy in down(s):
                copy.start()

        @pl.when(s == count - 1)
        def _():
            factor_load(2).start()

    def dense_block(i):
        chip, sub = i // 2, i % 2
        block = plane.block(chip, (plane.core + 1 - sub) % 2)
        columns = pl.ds(pl.multiple_of(block * share, share), share)
        source = normed[:, columns]
        part[sub, chip, :, 0:heads] = crossed_dot(source, query_grad[...]).astype(jnp.bfloat16)
        part[sub, chip, :, heads : 2 * heads] = crossed_dot(source, key_grad[...]).astype(jnp.bfloat16)
        part[sub, chip, :, 2 * heads : 3 * heads] = crossed_dot(source, value_grad[...]).astype(jnp.bfloat16)
        part[sub, chip, :, 3 * heads : 4 * heads] = crossed_dot(
            attention_grad[:, columns], attended[...]
        ).astype(jnp.bfloat16)
        part[sub, chip, :, 4 * heads :] = extras[block]

        @pl.when(sub == 0)
        def _():
            plane.pair_copy(chip).start()

    for copy in weight_loads:
        copy.start()
    for chip in range(4):
        load_own(chip).start()
    greet(plane.neighbours() + line.neighbours())
    for chip in range(4):
        mix.pair_copy(chip).start()
    for copy in weight_loads:
        copy.wait()
    for start in range(0, width, column_tile):
        columns = slice(start, start + column_tile)
        later = width + start % half
        line_own[:, columns] = (
            turned_dot(query_grad[...], factors[0, columns])
            + turned_dot(key_grad[...], factors[1, columns])
            + turned_dot(value_grad[...], factors[start // half, later : later + column_tile])
        ).astype(jnp.bfloat16)
    factor_load(0).start()
    factor_load(1).start()
    start_tile(0)
    mix_last = mix.pieces + 1
    dense_first = 8 + 5
    dense_second = dense_first + plane.pieces // 2 + 2
    dense_last = dense_second + plane.pieces // 2 + 1

    def step(s, carry):
        line.advance(s)
        for chip in range(4):

            @pl.when(s == chip)
            def _():
                load_own(chip).wait()
                mix.pair_copy(chip).wait_recv()
                if chip < 3:
                    mix.send_first(chip)

        @pl.when((s >= 3) & (s - 3 < mix.pieces))
        def _():
            mix.second_piece(s - 3)

        @pl.when((s >= mix_last) & (s - mix_last < mix.pieces))
        def _():
            piece = s - mix_last
            for side, summed in enumerate(mix.last_sum(piece)):
                mix_own[3, mix.rows(side, piece)] = summed.astype(jnp.bfloat16)

        mix_line.advance(s - mix_last)

        @pl.when((s >= 4) & (s < 12))
        def _():
            dense_block(s - 4)

        @pl.when(s == dense_first)
        def _():
            for chip in range(4):
                plane.pair_copy(chip).wait_recv()
            for chip in range(3):
                plane.send_first(chip)

        @pl.when((s >= dense_second) & (s - dense_second < plane.pieces))
        def _():
            plane.second_piece(s - dense_second)

        @pl.when((s >= dense_last) & (s - dense_last < plane.pieces))
        def _():
            piece = s - dense_last
            for side, summed in enumerate(plane.last_sum(piece)):
                sums[plane.rows(side, piece)] = summed

        @pl.when(s < 3 * count)
        def _():
            expert_tile(s)

        return carry

    steps = jnp.maximum(mix_last + mix_line.steps(), jnp.maximum(3 * count, dense_last + plane.pieces))
    lax.fori_loop(0, steps, step, 0)
    for s in (2 * count - 2, 2 * count - 1):
        for copy in across(up_out, s):
            copy.wait()
    for s in (3 * count - 2, 3 * count - 1):
        for copy in down(s):
            copy.wait()
    for each in (plane, line, mix, mix_line):
        each.finish()


TILE = 256


def closing(
    normed, query_grad, key_grad, value_grad, attended, attention_grad, extras, w_query, w_key, w_value,
    mixed, arrived, arrived_grad, gated, gate_grad, up_grad, experts,
):
    rows, width = normed.shape
    heads = query_grad.shape[1]
    ranks, share, more = extras.shape
    wide = 4 * heads + more
    inner = gated.shape[2]
    hidden = inner // experts
    low = jnp.bfloat16
    tile = min(TILE, width // 2)
    vmem = pl.BlockSpec(memory_space=pltpu.VMEM)
    any_space = pl.BlockSpec(memory_space=pl.ANY)
    every = ranks * rows
    return pl.pallas_call(
        closing_kernel,
        out_shape=(
            jax.ShapeDtypeStruct((rows, width), low),
            jax.ShapeDtypeStruct((share, wide), jnp.float32),
            jax.ShapeDtypeStruct((rows, width), low),
            jax.ShapeDtypeStruct((experts, width, hidden), jnp.float32),
            jax.ShapeDtypeStruct((experts, width, hidden), jnp.float32),
            jax.ShapeDtypeStruct((experts, hidden, width), jnp.float32),
        ),
        in_specs=[vmem] * 7 + [any_space] * 9,
        out_specs=(vmem,) * 3 + (any_space,) * 3,
        scratch_shapes=[
            pltpu.VMEM((rows, width), low),
            pltpu.VMEM((rows, width), low),
            pltpu.VMEM((2, 4, share, wide), low),
            pltpu.VMEM((4, share, wide), low),
            pltpu.VMEM((3, share // 2, wide), low),
            pltpu.VMEM((3, share // 2, wide), low),
            pltpu.VMEM((4, rows, width), low),
            pltpu.VMEM((4, rows, width), low),
            pltpu.VMEM((3, rows // 2, width), low),
            pltpu.VMEM((3, rows // 2, width), low),
            pltpu.VMEM((rows, width), low),
            pltpu.VMEM((2, every, tile), low),
            pltpu.VMEM((2, every, inner), low),
            pltpu.VMEM((2, tile, inner), jnp.float32),
            pltpu.VMEM((2, inner, tile), jnp.float32),
            Line.semaphores(rows),
            *Plane.semaphores(share),
            Line.semaphores(rows),
            *Plane.semaphores(rows),
            pltpu.SemaphoreType.DMA((4,)),
            pltpu.SemaphoreType.DMA((4,)),
            pltpu.SemaphoreType.DMA((3,)),
            pltpu.SemaphoreType.DMA((2,)),
            pltpu.SemaphoreType.DMA((2, 2, experts)),
        ],
        compiler_params=pltpu.CompilerParams(
            collective_id=2, has_side_effects=True, vmem_limit_bytes=63 * 2**20
        ),
    )(
        normed, query_grad, key_grad, value_grad, attended, attention_grad, extras, w_query, w_key, w_value,
        mixed, arrived.reshape(every, width), arrived_grad.reshape(every, width),
        gated.reshape(every, inner), gate_grad.reshape(every, inner), up_grad.reshape(every, inner),
    )


epsilon = 1e-05
masked_value = -1e30


def rotate(field, cosine, sine):
    half = field.shape[-1] // 2
    first = field[..., :half]
    second = field[..., half:]
    return jnp.concatenate(
        [first * cosine - second * sine, second * cosine + first * sine], axis=-1
    )


def unrotate(grad, cosine, sine):
    half = grad.shape[-1] // 2
    first = grad[..., :half]
    second = grad[..., half:]
    return jnp.concatenate(
        [first * cosine + second * sine, second * cosine - first * sine], axis=-1
    )


def experts(normed_two, cotangent, gates, w_gate, w_up, w_down, experts_total):
    local_experts = w_gate.shape[0]
    device = lax.axis_index("expert")
    arrived = lax.all_gather(normed_two, "expert", axis=0, tiled=True)
    arrived_grad = lax.all_gather(cotangent, "expert", axis=0, tiled=True)
    gate_pre = jnp.einsum("rd,jdf->jrf", arrived, w_gate, preferred_element_type=jnp.float32)
    up_pre = jnp.einsum("rd,jdf->jrf", arrived, w_up, preferred_element_type=jnp.float32)
    raw_grad = jnp.einsum("rd,jfd->jrf", arrived_grad, w_down, preferred_element_type=jnp.float32)
    sigma = jax.nn.sigmoid(gate_pre)
    activated = gate_pre * sigma
    inner = activated * up_pre
    gated = (gates[:, :, None] * inner).astype(jnp.bfloat16)
    mixed_part = jnp.einsum("jrf,jfd->rd", gated, w_down, preferred_element_type=jnp.float32)
    mixture = lax.psum(
        lax.psum_scatter(
            mixed_part.astype(jnp.bfloat16), "expert", scatter_dimension=0, tiled=True
        ),
        "tensor",
    ).astype(jnp.float32)
    gate_grad_part = jnp.sum(raw_grad * inner, axis=2)
    act_grad = gates[:, :, None] * raw_grad
    up_grad = (act_grad * activated).astype(jnp.bfloat16)
    gate_grad = (act_grad * up_pre * sigma * (1.0 + gate_pre * (1.0 - sigma))).astype(jnp.bfloat16)
    grad_w_down = jnp.einsum("jrf,rd->jfd", gated, arrived_grad, preferred_element_type=jnp.float32)
    grad_w_gate = jnp.einsum("rd,jrf->jdf", arrived, gate_grad, preferred_element_type=jnp.float32)
    grad_w_up = jnp.einsum("rd,jrf->jdf", arrived, up_grad, preferred_element_type=jnp.float32)
    slot_grad = jnp.einsum("jrf,jdf->rd", gate_grad, w_gate, preferred_element_type=jnp.float32)
    slot_grad = slot_grad + jnp.einsum(
        "jrf,jdf->rd", up_grad, w_up, preferred_element_type=jnp.float32
    )
    moe_input_grad = lax.psum(
        lax.psum_scatter(
            slot_grad.astype(jnp.bfloat16), "expert", scatter_dimension=0, tiled=True
        ),
        "tensor",
    ).astype(jnp.float32)
    placed = jnp.zeros((arrived.shape[0], experts_total), jnp.float32)
    placed = lax.dynamic_update_slice_in_dim(placed, gate_grad_part.T, device * local_experts, 1)
    chance_grad = lax.psum(
        lax.psum_scatter(placed, "expert", scatter_dimension=0, tiled=True), "tensor"
    )
    return mixture, moe_input_grad, chance_grad, [grad_w_gate, grad_w_up, grad_w_down]


def body(
    tokens,
    w_query,
    w_key,
    w_value,
    w_out,
    attn_gain,
    ffn_gain,
    qk_gain,
    router,
    w_gate,
    w_up,
    w_down,
    routes,
    cont_group,
    cotangent,
):
    rows, width = tokens.shape
    local_width = w_query.shape[1]
    head_count = local_width // HD
    experts_total = router.shape[1]
    local_experts = w_gate.shape[0]
    ranks = lax.axis_size("expert")
    device = lax.axis_index("expert")
    span = ranks // 2
    compact = ranks == 8
    prompt_len = PROMPT_DEV * span
    factor = HD ** (-0.5)
    local = jnp.arange(rows, dtype=jnp.int32)
    is_prompt = local < PROMPT_DEV
    after = jnp.maximum(local - PROMPT_DEV, 0)
    slot_cont = after // CLEN
    cont_pick = jnp.sum(
        jnp.where(
            slot_cont[:, None] == jnp.arange(CONT_DEV, dtype=jnp.int32)[None, :],
            cont_group[None, :],
            0,
        ),
        axis=1,
    )
    group = jnp.where(is_prompt, device // span, cont_pick)
    position = jnp.where(is_prompt, device % span * PROMPT_DEV + local, prompt_len + after % CLEN)
    tag = jnp.where(is_prompt, -1, slot_cont)
    frequency = 10000.0 ** (-jnp.arange(HD // 2, dtype=jnp.float32) * 2.0 / HD)
    angle = position.astype(jnp.float32)[:, None] * frequency[None, :]
    cosine = jnp.cos(angle)[:, None, :]
    sine = jnp.sin(angle)[:, None, :]
    if compact:
        routes_all = lax.all_gather(routes, "expert", axis=0)
        own_expert = device * local_experts + jnp.arange(local_experts, dtype=jnp.int32)
        expert_mask = jnp.any(routes_all[:, :, :, None] == own_expert, axis=2).astype(jnp.float32)
        expert_mask = jnp.pad(expert_mask, ((0, 0), (0, 0), (0, LANE - local_experts)))
        own_first = jnp.roll(router, -device * local_experts, axis=1)
        own_first = jnp.pad(own_first, ((0, 0), (0, LANE - experts_total)))
        bias = jnp.where(jnp.arange(LANE) < experts_total, 0.0, masked_value)
        bias = bias.astype(jnp.float32)[None]
    source = tokens.astype(jnp.float32)
    scale_one = lax.rsqrt(jnp.mean(source * source, axis=1, keepdims=True) + epsilon)
    normed = (source * scale_one * attn_gain).astype(jnp.bfloat16)
    query_raw = jnp.dot(normed, w_query, preferred_element_type=jnp.float32)
    key_raw = jnp.dot(normed, w_key, preferred_element_type=jnp.float32)
    value_raw = jnp.dot(normed, w_value, preferred_element_type=jnp.float32)
    squares = lax.psum(
        jnp.stack(
            [jnp.sum(query_raw * query_raw, axis=1), jnp.sum(key_raw * key_raw, axis=1)], axis=1
        ),
        "tensor",
    )
    scale_query = lax.rsqrt(squares[:, 0:1] / width + epsilon)
    scale_key = lax.rsqrt(squares[:, 1:2] / width + epsilon)
    query_rot = (
        rotate((query_raw * scale_query * qk_gain[0]).reshape(rows, head_count, HD), cosine, sine)
        .reshape(rows, local_width)
        .astype(jnp.bfloat16)
    )
    key_rot = (
        rotate((key_raw * scale_key * qk_gain[1]).reshape(rows, head_count, HD), cosine, sine)
        .reshape(rows, local_width)
        .astype(jnp.bfloat16)
    )
    value_low = value_raw.astype(jnp.bfloat16)
    prompts = lax.all_gather(
        jnp.concatenate([key_rot[:PROMPT_DEV], value_low[:PROMPT_DEV]], axis=1),
        "expert",
        axis=0,
        tiled=True,
    )
    prompt_keys, prompt_values = prompts[:, :local_width], prompts[:, local_width:]
    prompt_count = prompt_keys.shape[0]
    all_keys = jnp.concatenate([prompt_keys, key_rot[PROMPT_DEV:]], axis=0)
    all_values = jnp.concatenate([prompt_values, value_low[PROMPT_DEV:]], axis=0)
    key_index = jnp.arange(prompt_count, dtype=jnp.int32)
    prompt_mask = (group[:, None] == (key_index // prompt_len)[None, :]) & (
        (key_index % prompt_len)[None, :] <= position[:, None]
    )
    own_mask = (tag[:, None] == tag[None, PROMPT_DEV:]) & (
        position[None, PROMPT_DEV:] <= position[:, None]
    )
    mask = jnp.concatenate([prompt_mask, own_mask], axis=1)

    def head_scores(query_head, key_head):
        scores = (
            jnp.einsum("qd,kd->qk", query_head, key_head, preferred_element_type=jnp.float32)
            * factor
        )
        return jnp.where(mask, scores, masked_value)

    outputs = []
    log_totals = []
    for head in range(head_count):
        start = head * HD
        scores = head_scores(query_rot[:, start : start + HD], all_keys[:, start : start + HD])
        top = jnp.max(scores, axis=1, keepdims=True)
        weights = jnp.exp(scores - top)
        total = jnp.sum(weights, axis=1, keepdims=True)
        shares = (weights / total).astype(jnp.bfloat16)
        outputs.append(
            jnp.dot(shares, all_values[:, start : start + HD], preferred_element_type=jnp.float32)
        )
        log_totals.append(top + jnp.log(total))
    attended = jnp.concatenate(outputs, axis=1).astype(jnp.bfloat16)
    if compact:
        attention, arrived_grad = summed_product(attended, w_out, cotangent, 1)
        attention = attention.astype(jnp.float32)
    else:
        attention = lax.psum(
            jnp.dot(attended, w_out, preferred_element_type=jnp.float32), "tensor"
        )
    hidden = source + attention
    scale_two = lax.rsqrt(jnp.mean(hidden * hidden, axis=1, keepdims=True) + epsilon)
    normed_two = (hidden * scale_two * ffn_gain).astype(jnp.bfloat16)
    logits = jnp.dot(normed_two, router, preferred_element_type=jnp.float32)
    top = jnp.max(logits, axis=1, keepdims=True)
    weights = jnp.exp(logits - top)
    chances = weights / jnp.sum(weights, axis=1, keepdims=True)
    hits = (routes[:, :, None] == jnp.arange(experts_total, dtype=jnp.int32)[None, None, :]).astype(
        jnp.float32
    )
    rows_mask = jnp.sum(hits, axis=1)
    grad_out = cotangent.astype(jnp.float32)
    if compact:
        arrived = lax.all_gather(normed_two, "expert", axis=0)
        reduced, gated, gate_grad, up_grad, mixed_part = experts_fused(
            arrived, arrived_grad, expert_mask, own_first, bias, w_gate, w_up, w_down
        )
        moe_input_grad = reduced[:, :width].astype(jnp.float32)
        chance_grad = reduced[:, width : width + experts_total].astype(jnp.float32)
    else:
        routed = lax.all_gather(
            (rows_mask * chances).astype(jnp.float32), "expert", axis=0, tiled=True
        )
        gates = lax.dynamic_slice_in_dim(routed, device * local_experts, local_experts, 1).T
        pieces = max(1, ranks * rows // 4096)
        piece = rows // pieces
        split_gates = gates.reshape(local_experts, ranks, rows)
        results = []
        weight_grads = None
        for number in range(pieces):
            part = slice(number * piece, (number + 1) * piece)
            sources = (normed_two[part], cotangent[part])
            if results:
                sources, results, weight_grads = lax.optimization_barrier(
                    (sources, results, weight_grads)
                )
            *result, grads = experts(
                *sources,
                split_gates[:, :, part].reshape(local_experts, ranks * piece),
                w_gate,
                w_up,
                w_down,
                experts_total,
            )
            results.append(result)
            weight_grads = grads if weight_grads is None else [a + b for a, b in zip(weight_grads, grads)]
        mixture, moe_input_grad, chance_grad = (
            jnp.concatenate(list(group_of), axis=0) for group_of in zip(*results)
        )
        grad_w_gate, grad_w_up, grad_w_down = weight_grads
    chance_grad = rows_mask * chance_grad
    logit_grad = (
        chances * (chance_grad - jnp.sum(chances * chance_grad, axis=1, keepdims=True))
    ).astype(jnp.bfloat16)
    grad_router = jnp.einsum(
        "td,te->de", normed_two, logit_grad, preferred_element_type=jnp.float32
    )
    normed_two_grad = moe_input_grad + jnp.einsum(
        "te,de->td", logit_grad, router, preferred_element_type=jnp.float32
    )
    weighted_two = ffn_gain * normed_two_grad
    grad_ffn_gain = jnp.sum(normed_two_grad * hidden * scale_two, axis=0)
    hidden_grad = (
        grad_out
        + scale_two * weighted_two
        - hidden * (scale_two**3 / width) * jnp.sum(weighted_two * hidden, axis=1, keepdims=True)
    )
    attention_grad = hidden_grad.astype(jnp.bfloat16)
    attended_grad = jnp.einsum(
        "te,de->td", attention_grad, w_out, preferred_element_type=jnp.float32
    ).astype(jnp.bfloat16)
    query_grads = []
    key_grads = []
    value_grads = []
    for head in range(head_count):
        start = head * HD
        query_head = query_rot[:, start : start + HD]
        key_head = all_keys[:, start : start + HD]
        value_head = all_values[:, start : start + HD]
        out_grad_head = attended_grad[:, start : start + HD]
        recomputed = jnp.exp(head_scores(query_head, key_head) - log_totals[head])
        share_grad = jnp.einsum(
            "qd,kd->qk", out_grad_head, value_head, preferred_element_type=jnp.float32
        )
        delta = jnp.sum(recomputed * share_grad, axis=1, keepdims=True)
        score_grad = (recomputed * (share_grad - delta)).astype(jnp.bfloat16)
        query_grads.append(
            jnp.dot(score_grad, key_head, preferred_element_type=jnp.float32) * factor
        )
        key_grads.append(
            jnp.einsum("qk,qd->kd", score_grad, query_head, preferred_element_type=jnp.float32)
            * factor
        )
        value_grads.append(
            jnp.einsum(
                "qk,qd->kd",
                recomputed.astype(jnp.bfloat16),
                out_grad_head,
                preferred_element_type=jnp.float32,
            )
        )
    key_grad_all = jnp.concatenate(key_grads, axis=1)
    value_grad_all = jnp.concatenate(value_grads, axis=1)
    prompt_grads = lax.psum_scatter(
        jnp.concatenate(
            [key_grad_all[:prompt_count], value_grad_all[:prompt_count]], axis=1
        ).astype(jnp.bfloat16),
        "expert",
        scatter_dimension=0,
        tiled=True,
    ).astype(jnp.float32)
    prompt_key_grad, prompt_value_grad = prompt_grads[:, :local_width], prompt_grads[:, local_width:]
    key_grad = jnp.concatenate([prompt_key_grad, key_grad_all[prompt_count:]], axis=0)
    value_grad = jnp.concatenate([prompt_value_grad, value_grad_all[prompt_count:]], axis=0)
    query_grad = unrotate(
        jnp.concatenate(query_grads, axis=1).reshape(rows, head_count, HD), cosine, sine
    ).reshape(rows, local_width)
    key_grad = unrotate(key_grad.reshape(rows, head_count, HD), cosine, sine).reshape(
        rows, local_width
    )
    grad_qk_gain = jnp.stack(
        [
            jnp.sum(query_grad * query_raw * scale_query, axis=0),
            jnp.sum(key_grad * key_raw * scale_key, axis=0),
        ],
        axis=0,
    )
    weighted_query = qk_gain[0] * query_grad
    weighted_key = qk_gain[1] * key_grad
    inner_sums = lax.psum(
        jnp.stack(
            [jnp.sum(weighted_query * query_raw, axis=1), jnp.sum(weighted_key * key_raw, axis=1)],
            axis=1,
        ),
        "tensor",
    )
    query_raw_grad = (
        scale_query * weighted_query - query_raw * (scale_query**3 / width) * inner_sums[:, 0:1]
    ).astype(jnp.bfloat16)
    key_raw_grad = (
        scale_key * weighted_key - key_raw * (scale_key**3 / width) * inner_sums[:, 1:2]
    ).astype(jnp.bfloat16)
    value_raw_grad = value_grad.astype(jnp.bfloat16)
    if compact:
        small_part = local_width // ranks
        gains = jnp.pad(
            grad_qk_gain.reshape(2, ranks, small_part).transpose(1, 2, 0),
            ((0, 0), (0, width // ranks - small_part), (0, 0)),
        )
        extras = jnp.concatenate(
            [
                grad_router.reshape(ranks, width // ranks, experts_total),
                grad_ffn_gain.reshape(ranks, width // ranks, 1),
                gains,
            ],
            axis=2,
        ).astype(jnp.bfloat16)
        extras = jnp.pad(extras, ((0, 0), (0, 0), (0, LANE - experts_total - 3)))
        normed_grad, sums, mixture, grad_w_gate, grad_w_up, grad_w_down = closing(
            normed,
            query_raw_grad,
            key_raw_grad,
            value_raw_grad,
            attended,
            attention_grad,
            extras,
            w_query,
            w_key,
            w_value,
            mixed_part,
            arrived,
            arrived_grad,
            gated,
            gate_grad,
            up_grad,
            local_experts,
        )
        mixture = mixture.astype(jnp.float32)
        normed_grad = normed_grad.astype(jnp.float32)
    else:
        grad_w_out = jnp.einsum(
            "td,te->de", attended, attention_grad, preferred_element_type=jnp.float32
        )
        grad_w_query = jnp.einsum(
            "td,te->de", normed, query_raw_grad, preferred_element_type=jnp.float32
        )
        grad_w_key = jnp.einsum("td,te->de", normed, key_raw_grad, preferred_element_type=jnp.float32)
        grad_w_value = jnp.einsum(
            "td,te->de", normed, value_raw_grad, preferred_element_type=jnp.float32
        )
        normed_part = jnp.einsum(
            "te,de->td", query_raw_grad, w_query, preferred_element_type=jnp.float32
        )
        normed_part = normed_part + jnp.einsum(
            "te,de->td", key_raw_grad, w_key, preferred_element_type=jnp.float32
        )
        normed_part = normed_part + jnp.einsum(
            "te,de->td", value_raw_grad, w_value, preferred_element_type=jnp.float32
        )
        normed_grad = lax.psum(normed_part.astype(jnp.bfloat16), "tensor").astype(jnp.float32)
    weighted_one = attn_gain * normed_grad
    grad_attn_gain = jnp.sum(normed_grad * source * scale_one, axis=0)
    input_grad = (
        hidden_grad
        + scale_one * weighted_one
        - source * (scale_one**3 / width) * jnp.sum(weighted_one * source, axis=1, keepdims=True)
    )
    if compact:
        edge = 4 * local_width
        summed = (
            sums[:, :local_width],
            sums[:, local_width : 2 * local_width],
            sums[:, 2 * local_width : 3 * local_width],
            sums[:, 3 * local_width : edge].T,
            lax.psum_scatter(
                grad_attn_gain.astype(jnp.bfloat16), "expert", scatter_dimension=0, tiled=True
            ).astype(jnp.float32),
            sums[:, edge + experts_total],
            sums[:small_part, edge + experts_total + 1 : edge + experts_total + 3].T,
            sums[:, edge : edge + experts_total],
        )
    else:
        summed = (
            lax.psum_scatter(
                grad_w_query.astype(jnp.bfloat16), "expert", scatter_dimension=0, tiled=True
            ).astype(jnp.float32),
            lax.psum_scatter(
                grad_w_key.astype(jnp.bfloat16), "expert", scatter_dimension=0, tiled=True
            ).astype(jnp.float32),
            lax.psum_scatter(
                grad_w_value.astype(jnp.bfloat16), "expert", scatter_dimension=0, tiled=True
            ).astype(jnp.float32),
            lax.psum_scatter(
                grad_w_out.astype(jnp.bfloat16), "expert", scatter_dimension=1, tiled=True
            ).astype(jnp.float32),
            lax.psum_scatter(
                grad_attn_gain.astype(jnp.bfloat16), "expert", scatter_dimension=0, tiled=True
            ).astype(jnp.float32),
            lax.psum_scatter(
                grad_ffn_gain.astype(jnp.bfloat16), "expert", scatter_dimension=0, tiled=True
            ).astype(jnp.float32),
            lax.psum_scatter(
                grad_qk_gain.astype(jnp.bfloat16), "expert", scatter_dimension=1, tiled=True
            ).astype(jnp.float32),
            lax.psum_scatter(
                grad_router.astype(jnp.bfloat16), "expert", scatter_dimension=0, tiled=True
            ).astype(jnp.float32),
        )
    output = (hidden + mixture).astype(jnp.bfloat16)
    return (
        output,
        input_grad,
        summed[0],
        summed[1],
        summed[2],
        summed[3],
        summed[4],
        summed[5],
        summed[6],
        summed[7],
        grad_w_gate,
        grad_w_up,
        grad_w_down,
    )


def solution(mesh):
    return jax.shard_map(
        body,
        mesh=mesh,
        in_specs=(
            P("expert", None),
            P(None, "tensor"),
            P(None, "tensor"),
            P(None, "tensor"),
            P("tensor", None),
            P(),
            P(),
            P(None, "tensor"),
            P(),
            P("expert", None, "tensor"),
            P("expert", None, "tensor"),
            P("expert", "tensor", None),
            P("expert", None),
            P("expert"),
            P("expert", None),
        ),
        out_specs=(
            P("expert", None),
            P("expert", None),
            P("expert", "tensor"),
            P("expert", "tensor"),
            P("expert", "tensor"),
            P("tensor", "expert"),
            P("expert"),
            P("expert"),
            P(None, ("tensor", "expert")),
            P("expert", None),
            P("expert", None, "tensor"),
            P("expert", None, "tensor"),
            P("expert", "tensor", None),
        ),
        check_vma=False,
    )
```

```python
import jax
import jax.numpy as jnp
from jax import lax
from jax.experimental import pallas as pl
from jax.experimental.pallas import tpu as pltpu
from jax.sharding import PartitionSpec as P

HD = 128
PROMPT_DEV = 128
CLEN = 256
CONT_DEV = 1


epsilon = 1e-05
masked_value = -1e30


MESH = pl.DeviceIdType.MESH
STEP = 16
LANE = 128


def remote(source, target, sent, received, **where):
    return pltpu.make_async_remote_copy(
        src_ref=source,
        dst_ref=target,
        send_sem=sent,
        recv_sem=received,
        device_id=where,
        device_id_type=MESH,
    )


def greet(places):
    barrier = pltpu.get_barrier_semaphore()
    for condition, where in places:
        def signal(where=where):
            pl.semaphore_signal(barrier, inc=1, device_id=where, device_id_type=MESH)
        if condition is None:
            signal()
        else:
            pl.when(condition)(signal)
    count = 0
    for condition, _ in places:
        count = count + (1 if condition is None else jnp.where(condition, 1, 0))
    pl.semaphore_wait(barrier, count)


class Line:
    def __init__(self, own, arrived, total, sems):
        self.own, self.arrived, self.total = own, arrived, total
        self.up_sent, self.up_got, self.down_sent, self.down_got = (sems.at[i] for i in range(4))
        self.size = lax.axis_size("tensor")
        self.here = lax.axis_index("tensor")
        self.half = own.shape[0] // 2
        self.pieces = self.half // STEP

    @staticmethod
    def semaphores(rows):
        return pltpu.SemaphoreType.DMA((4, 2, rows // 2 // STEP))

    def neighbours(self):
        here, size = self.here, self.size
        return [
            (here > 0, {"tensor": jnp.maximum(here - 1, 0)}),
            (here < size - 1, {"tensor": jnp.minimum(here + 1, size - 1)}),
        ]

    def lane(self, lane):
        here, size = self.here, self.size
        if lane == 0:
            return here, here + 1, here - 1
        return size - 1 - here, here - 1, here + 1

    def rows(self, lane, piece):
        return pl.ds(pl.multiple_of(lane * self.half + piece * STEP, STEP), STEP)

    def up_copy(self, lane, piece):
        rows = self.rows(lane, piece)
        onward = self.lane(lane)[1]
        return remote(
            self.own.at[rows], self.arrived.at[rows],
            self.up_sent.at[lane, piece], self.up_got.at[lane, piece], tensor=onward,
        )

    def down_copy(self, lane, piece):
        rows = self.rows(lane, piece)
        back = self.lane(lane)[2]
        return remote(
            self.total.at[rows], self.total.at[rows],
            self.down_sent.at[lane, piece], self.down_got.at[lane, piece], tensor=back,
        )

    def rise(self, lane, piece):
        place = self.lane(lane)[0]
        rows = self.rows(lane, piece)

        @pl.when(place > 0)
        def _():
            self.up_copy(lane, piece).wait_recv()
            summed = (
                self.own[rows].astype(jnp.float32) + self.arrived[rows].astype(jnp.float32)
            ).astype(jnp.bfloat16)

            @pl.when(place < self.size - 1)
            def _():
                self.own[rows] = summed

            @pl.when(place == self.size - 1)
            def _():
                self.total[rows] = summed
                self.down_copy(lane, piece).start()

        @pl.when(place < self.size - 1)
        def _():
            self.up_copy(lane, piece).start()

    def fall(self, lane, piece):
        place = self.lane(lane)[0]

        @pl.when(place < self.size - 1)
        def _():
            self.down_copy(lane, piece).wait_recv()

            @pl.when(place > 0)
            def _():
                self.down_copy(lane, piece).start()

    def advance(self, step, skew=1):
        for act, far in ((self.rise, False), (self.fall, True)):
            for lane in range(2):
                place = self.lane(lane)[0]
                piece = step - skew * (2 * (self.size - 1) - place if far else place)

                @pl.when((piece >= 0) & (piece < self.pieces))
                def _():
                    act(lane, piece)

    def step_body(self, step, carry):
        self.advance(step)
        return carry

    def steps(self, skew=1):
        return self.pieces + skew * 2 * (self.size - 1)

    def finish(self):
        def one(piece, carry):
            for lane in range(2):
                place = self.lane(lane)[0]

                @pl.when(place < self.size - 1)
                def _():
                    self.up_copy(lane, piece).wait_send()

                @pl.when(place > 0)
                def _():
                    self.down_copy(lane, piece).wait_send()
            return carry

        lax.fori_loop(0, self.pieces, one, 0)


class Place:
    def __init__(self):
        here = lax.axis_index("expert")
        self.here = here
        self.core, self.x, self.y = here % 2, here // 2 % 2, here // 4
        self.sibling = here + 1 - 2 * self.core
        self.x_chip = here + 2 - 4 * self.x
        self.y_chip = here + 4 - 8 * self.y

    def neighbours(self):
        return [(None, {"expert": i}) for i in (self.sibling, self.x_chip, self.y_chip)]

    def block(self, chip, core):
        x = self.x + (1 - chip // 2) * (1 - 2 * self.x)
        y = self.y + (1 - chip % 2) * (1 - 2 * self.y)
        return 4 * y + 2 * x + core


class Plane(Place):
    def __init__(self, own, spare, paired, from_x, from_y, pair_sems, x_sems, y_sems, by_device=False):
        self.by_device = by_device
        self.own, self.spare, self.paired, self.from_x, self.from_y = own, spare, paired, from_x, from_y
        self.pair_sems, self.x_sems, self.y_sems = pair_sems, x_sems, y_sems
        super().__init__()
        self.half = own.shape[1] // 2
        self.pieces = self.half // STEP

    @staticmethod
    def semaphores(rows):
        pieces = rows // 2 // STEP
        return [
            pltpu.SemaphoreType.DMA((2, 4)),
            pltpu.SemaphoreType.DMA((2, 3, pieces)),
            pltpu.SemaphoreType.DMA((2, 3, pieces)),
        ]

    def pair_copy(self, chip):
        place = self.block(chip, 1 - self.core) if self.by_device else chip
        return remote(
            self.spare.at[place], self.paired.at[chip],
            self.pair_sems.at[0, chip], self.pair_sems.at[1, chip], expert=self.sibling,
        )

    def rows(self, side, piece):
        return pl.ds(pl.multiple_of(side * self.half + piece * STEP, STEP), STEP)

    def landing(self, piece):
        return pl.ds(pl.multiple_of(piece * STEP, STEP), STEP)

    def x_copy(self, kind, piece):
        chip, side = ((0, 0), (1, 0), (1, 1))[kind]
        return remote(
            self.own.at[chip, self.rows(side, piece)], self.from_x.at[kind, self.landing(piece)],
            self.x_sems.at[0, kind, piece], self.x_sems.at[1, kind, piece], expert=self.x_chip,
        )

    def y_copy(self, kind, piece):
        chip, side = ((0, 1), (2, 1), (2, 0))[kind]
        return remote(
            self.own.at[chip, self.rows(side, piece)], self.from_y.at[kind, self.landing(piece)],
            self.y_sems.at[0, kind, piece], self.y_sems.at[1, kind, piece], expert=self.y_chip,
        )

    def add_pair(self, chip, side, piece):
        rows = self.rows(side, piece)
        self.own[chip, rows] = (
            self.own[chip, rows].astype(jnp.float32) + self.paired[chip, rows].astype(jnp.float32)
        ).astype(jnp.bfloat16)

    def each(self, step):
        def one(piece, carry):
            step(piece)
            return carry

        lax.fori_loop(0, self.pieces, one, 0)

    def send_first(self, chip):
        def step(piece):
            if chip in (0, 1):
                self.add_pair(chip, 0, piece)
                self.x_copy(chip, piece).start()
            if chip in (0, 2):
                self.add_pair(chip, 1, piece)
                self.y_copy(chip // 2, piece).start()

        self.each(step)

    def second_piece(self, piece):
        landed = self.landing(piece)
        self.y_copy(0, piece).wait_recv()
        rows = self.rows(1, piece)
        self.own[1, rows] = (
            self.own[1, rows].astype(jnp.float32)
            + self.paired[1, rows].astype(jnp.float32)
            + self.from_y[0, landed].astype(jnp.float32)
        ).astype(jnp.bfloat16)
        self.x_copy(2, piece).start()
        self.x_copy(0, piece).wait_recv()
        rows = self.rows(0, piece)
        self.own[2, rows] = (
            self.own[2, rows].astype(jnp.float32)
            + self.paired[2, rows].astype(jnp.float32)
            + self.from_x[0, landed].astype(jnp.float32)
        ).astype(jnp.bfloat16)
        self.y_copy(2, piece).start()

    def send_second(self):
        self.each(self.second_piece)

    def last_sum(self, piece):
        landed = self.landing(piece)
        sums = []
        for side in range(2):
            first, second = (self.x_copy(1, piece), self.y_copy(2, piece)) if side == 0 else (self.y_copy(1, piece), self.x_copy(2, piece))
            first.wait_recv()
            second.wait_recv()
            a, b = (self.from_x[1, landed], self.from_y[2, landed]) if side == 0 else (self.from_y[1, landed], self.from_x[2, landed])
            rows = self.rows(side, piece)
            sums.append(
                self.own[3, rows].astype(jnp.float32)
                + self.paired[3, rows].astype(jnp.float32)
                + a.astype(jnp.float32)
                + b.astype(jnp.float32)
            )
        return sums

    def finish(self):
        for chip in range(4):
            self.pair_copy(chip).wait_send()

        def step(piece):
            for kind in range(3):
                self.x_copy(kind, piece).wait_send()
                self.y_copy(kind, piece).wait_send()

        self.each(step)


class Gather:
    def __init__(self, source, target, place, x_sems, y_sems, far_sems, pair_sems, own_sem, pieces):
        self.source, self.target = source, target
        self.place = place
        self.x_sems, self.y_sems, self.far_sems, self.pair_sems, self.own_sem = x_sems, y_sems, far_sems, pair_sems, own_sem
        self.pieces = pieces
        self.rows_each = source.shape[0] // pieces

    @staticmethod
    def semaphores(pieces):
        return [
            pltpu.SemaphoreType.DMA((2, pieces)),
            pltpu.SemaphoreType.DMA((2, pieces)),
            pltpu.SemaphoreType.DMA((2, pieces)),
            pltpu.SemaphoreType.DMA((2, 4, pieces)),
            pltpu.SemaphoreType.DMA,
        ]

    def rows(self, piece):
        return pl.ds(piece * self.rows_each, self.rows_each)

    def own_copy(self):
        return pltpu.make_async_copy(self.source, self.target.at[self.place.here], self.own_sem)

    def x_copy(self, piece):
        rows = self.rows(piece)
        return remote(
            self.source.at[rows], self.target.at[self.place.here, rows],
            self.x_sems.at[0, piece], self.x_sems.at[1, piece], expert=self.place.x_chip,
        )

    def y_copy(self, piece):
        rows = self.rows(piece)
        return remote(
            self.source.at[rows], self.target.at[self.place.here, rows],
            self.y_sems.at[0, piece], self.y_sems.at[1, piece], expert=self.place.y_chip,
        )

    def far_copy(self, piece):
        rows = self.rows(piece)
        came, goes = (
            (self.place.x_chip, self.place.y_chip) if piece < self.pieces // 2 else (self.place.y_chip, self.place.x_chip)
        )
        return remote(
            self.target.at[came, rows], self.target.at[came, rows],
            self.far_sems.at[0, piece], self.far_sems.at[1, piece], expert=goes,
        )

    def pair_copy(self, kind, piece):
        rows = self.rows(piece)
        block = self.place.block(kind, self.place.core)
        source = self.source.at[rows] if kind == 3 else self.target.at[block, rows]
        return remote(
            source, self.target.at[block, rows],
            self.pair_sems.at[0, kind, piece], self.pair_sems.at[1, kind, piece], expert=self.place.sibling,
        )

    def start_piece(self, piece):
        self.x_copy(piece).start()
        self.y_copy(piece).start()
        self.pair_copy(3, piece).start()

    def start(self):
        self.own_copy().start()
        for piece in range(self.pieces):
            self.start_piece(piece)

    def near(self, piece):
        self.x_copy(piece).wait_recv()
        if piece < self.pieces // 2:
            self.far_copy(piece).start()
        self.pair_copy(1, piece).start()
        self.y_copy(piece).wait_recv()
        if piece >= self.pieces // 2:
            self.far_copy(piece).start()
        self.pair_copy(2, piece).start()

    def far(self, piece):
        self.far_copy(piece).wait_recv()
        self.pair_copy(0, piece).start()

    def paired(self, kind, piece):
        self.pair_copy(kind, piece).wait_recv()

    def finish(self):
        for piece in range(self.pieces):
            self.x_copy(piece).wait_send()
            self.y_copy(piece).wait_send()
            self.far_copy(piece).wait_send()
            for kind in range(4):
                self.pair_copy(kind, piece).wait_send()


def wide_dot(left, right):
    return jnp.dot(left, right, preferred_element_type=jnp.float32)


def turned_dot(left, right):
    return lax.dot_general(left, right, (((1,), (1,)), ((), ())), preferred_element_type=jnp.float32)


def expert_kernel(
    x_all, g_all, mask, router, bias, w_gate, w_up, w_down,
    reduced, gated_all, gate_all, up_all, mixed_all,
    x_buf, g_buf, part, paired, from_x, from_y, line_in, small, mixed,
    in_sems, out_sems, pair_sems, x_sems, y_sems, line_sems,
):
    experts, width, hidden = w_gate.shape
    rows = x_buf.shape[1]
    tile = min(512, width)
    plane = Plane(part.at[1], part.at[0], paired, from_x, from_y, pair_sems, x_sems, y_sems)
    line = Line(part.at[1, 3], line_in, reduced, line_sems)
    first_expert = lax.axis_index("expert") * experts
    outs = (gated_all, gate_all, up_all)

    def block_of(i):
        return plane.block(i // 2, (plane.core + 1 - i % 2) % 2)

    def fetch(i):
        slot, block = i % 2, block_of(i)
        return (
            pltpu.make_async_copy(x_all.at[block], x_buf.at[slot], in_sems.at[0, slot]),
            pltpu.make_async_copy(g_all.at[block], g_buf.at[slot], in_sems.at[1, slot]),
        )

    def store(i):
        slot, block = i % 2, block_of(i)
        return [
            pltpu.make_async_copy(small.at[slot, n], outs[n].at[block], out_sems.at[n, slot])
            for n in range(3)
        ] + [pltpu.make_async_copy(mixed.at[slot], mixed_all.at[block], out_sems.at[3, slot])]

    def compute(i):
        slot = i % 2
        block = block_of(i)
        x = x_buf.at[slot]
        g = g_buf.at[slot]
        logits = wide_dot(x[...], router[...]) + bias[...]
        weights = jnp.exp(logits - jnp.max(logits, axis=1, keepdims=True))
        gates = weights / jnp.sum(weights, axis=1, keepdims=True) * mask[block]
        column = lax.broadcasted_iota(jnp.int32, (rows, LANE), 1)
        extra = jnp.zeros((rows, LANE), jnp.float32)
        for j in range(experts):
            gate_pre = wide_dot(x[...], w_gate[j])
            up_pre = wide_dot(x[...], w_up[j])
            raw = turned_dot(g[...], w_down[j])
            gate = gates[:, j : j + 1]
            sigma = jax.nn.sigmoid(gate_pre)
            activated = gate_pre * sigma
            inner = activated * up_pre
            act = gate * raw
            span = slice(j * hidden, (j + 1) * hidden)
            small[slot, 0, :, span] = (gate * inner).astype(jnp.bfloat16)
            small[slot, 1, :, span] = (
                act * up_pre * sigma * (1.0 + gate_pre * (1.0 - sigma))
            ).astype(jnp.bfloat16)
            small[slot, 2, :, span] = (act * activated).astype(jnp.bfloat16)
            gain = jnp.sum(raw * inner, axis=1, keepdims=True)
            extra = jnp.where(column == first_expert + j, gain, extra)
        for start in range(0, width, tile):
            columns = slice(start, start + tile)
            slot_grad = None
            mix = None
            for j in range(experts):
                span = slice(j * hidden, (j + 1) * hidden)
                term = turned_dot(small[slot, 1, :, span], w_gate[j, columns]) + turned_dot(
                    small[slot, 2, :, span], w_up[j, columns]
                )
                more = wide_dot(small[slot, 0, :, span], w_down[j, :, columns])
                slot_grad = term if slot_grad is None else slot_grad + term
                mix = more if mix is None else mix + more
            part[i % 2, i // 2, :, columns] = slot_grad.astype(jnp.bfloat16)
            mixed[slot, :, columns] = mix.astype(jnp.bfloat16)
        part[i % 2, i // 2, :, width:] = extra.astype(jnp.bfloat16)

    for copy in fetch(0):
        copy.start()
    greet(plane.neighbours() + line.neighbours())

    def step(i, carry):
        @pl.when(i < 7)
        def _():
            for copy in fetch(i + 1):
                copy.start()

        for copy in fetch(i):
            copy.wait()

        @pl.when(i >= 2)
        def _():
            for copy in store(i - 2):
                copy.wait()

        compute(i)
        for copy in store(i):
            copy.start()

        @pl.when(i % 2 == 0)
        def _():
            plane.pair_copy(i // 2).start()

        @pl.when(i % 2 == 1)
        def _():
            plane.pair_copy(i // 2).wait_recv()

        for chip in range(3):

            @pl.when(i == 2 * chip + 1)
            def _():
                plane.send_first(chip)
                if chip == 2:
                    plane.send_second()

        return carry

    lax.fori_loop(0, 8, step, 0)

    def last(step, carry):
        @pl.when(step < plane.pieces)
        def _():
            for side, total in enumerate(plane.last_sum(step)):
                plane.own[3, plane.rows(side, step)] = total.astype(jnp.bfloat16)

        line.advance(step)
        return carry

    lax.fori_loop(0, line.steps(), last, 0)
    for i in (6, 7):
        for copy in store(i):
            copy.wait()
    plane.finish()
    line.finish()


def experts_fused(arrived, arrived_grad, mask, router, bias, w_gate, w_up, w_down):
    ranks, rows, width = arrived.shape
    experts, _, hidden = w_gate.shape
    wide = width + LANE
    inner = experts * hidden
    half = rows // 2
    low = jnp.bfloat16
    any_space = pl.BlockSpec(memory_space=pl.ANY)
    vmem = pl.BlockSpec(memory_space=pltpu.VMEM)
    small_shape = jax.ShapeDtypeStruct((ranks, rows, inner), low)
    return pl.pallas_call(
        expert_kernel,
        out_shape=(
            jax.ShapeDtypeStruct((rows, wide), low), small_shape, small_shape, small_shape,
            jax.ShapeDtypeStruct((ranks, rows, width), low),
        ),
        in_specs=[any_space, any_space] + [vmem] * 6,
        out_specs=(vmem, any_space, any_space, any_space, any_space),
        scratch_shapes=[
            pltpu.VMEM((2, rows, width), low),
            pltpu.VMEM((2, rows, width), low),
            pltpu.VMEM((2, 4, rows, wide), low),
            pltpu.VMEM((4, rows, wide), low),
            pltpu.VMEM((3, half, wide), low),
            pltpu.VMEM((3, half, wide), low),
            pltpu.VMEM((rows, wide), low),
            pltpu.VMEM((2, 3, rows, inner), low),
            pltpu.VMEM((2, rows, width), low),
            pltpu.SemaphoreType.DMA((2, 2)),
            pltpu.SemaphoreType.DMA((4, 2)),
            *Plane.semaphores(rows),
            Line.semaphores(rows),
        ],
        compiler_params=pltpu.CompilerParams(
            collective_id=0, has_side_effects=True, vmem_limit_bytes=61 * 2**20
        ),
        cost_estimate=pl.CostEstimate(
            flops=12 * ranks * rows * width * inner, bytes_accessed=8 * ranks * rows * width, transcendentals=0
        ),
    )(arrived, arrived_grad, mask, router, bias, w_gate, w_up, w_down)


GATHER_PIECES = 4


def crossed_dot(left, right):
    return lax.dot_general(left, right, (((0,), (0,)), ((), ())), preferred_element_type=jnp.float32)


def closing_kernel(
    normed, query_grad, key_grad, value_grad, attended, attention_grad, extras,
    w_query, w_key, w_value, mixed, x_all, g_all, gated_all, gate_all, up_all,
    total, sums, mixture, gate_out, up_out, down_out,
    line_own, line_in, part, paired, from_x, from_y,
    mix_own, mix_paired, mix_x, mix_y, mix_in, tiles, factors, results, downs,
    line_sems, pair_sems, x_sems, y_sems, mix_line_sems, mix_pair_sems, mix_x_sems, mix_y_sems,
    load_sems, weight_sems, factor_sems, tile_sems, out_sems,
):
    width = normed.shape[1]
    heads = query_grad.shape[1]
    share = part.shape[2]
    experts, _, hidden = gate_out.shape
    column_tile = min(512, width // 2)
    tile = tiles.shape[2]
    count = width // tile
    line = Line(line_own, line_in, total, line_sems)
    plane = Plane(part.at[1], part.at[0], paired, from_x, from_y, pair_sems, x_sems, y_sems)
    mix = Plane(mix_own, mixed, mix_paired, mix_x, mix_y, mix_pair_sems, mix_x_sems, mix_y_sems, by_device=True)
    mix_line = Line(mix_own.at[3], mix_in, mixture, mix_line_sems)
    half = width // 2

    def load_own(chip):
        return pltpu.make_async_copy(mixed.at[mix.block(chip, mix.core)], mix_own.at[chip], load_sems.at[chip])

    weight_loads = [
        pltpu.make_async_copy(w_query, factors.at[0, 0:width], weight_sems.at[0]),
        pltpu.make_async_copy(w_key, factors.at[1, 0:width], weight_sems.at[1]),
        pltpu.make_async_copy(w_value.at[0:half], factors.at[0, width : width + half], weight_sems.at[2]),
        pltpu.make_async_copy(w_value.at[half:], factors.at[1, width : width + half], weight_sems.at[3]),
    ]

    def factor_load(matrix):
        return pltpu.make_async_copy(
            (gate_all, up_all, gated_all)[matrix], factors.at[matrix % 2], factor_sems.at[matrix]
        )

    def tile_copy(source, s):
        columns = pl.ds(pl.multiple_of(s % count * tile, tile), tile)
        return pltpu.make_async_copy(source.at[:, columns], tiles.at[s % 2], tile_sems.at[s % 2])

    def start_tile(s):
        @pl.when(s < 2 * count)
        def _():
            tile_copy(x_all, s).start()

        @pl.when(s >= 2 * count)
        def _():
            tile_copy(g_all, s).start()

    def across(target, s):
        rows = pl.ds(pl.multiple_of(s % count * tile, tile), tile)
        return [
            pltpu.make_async_copy(
                results.at[s % 2, :, j * hidden : (j + 1) * hidden], target.at[j, rows], out_sems.at[0, s % 2, j]
            )
            for j in range(experts)
        ]

    def down(s):
        columns = pl.ds(pl.multiple_of(s % count * tile, tile), tile)
        return [
            pltpu.make_async_copy(
                downs.at[s % 2, j * hidden : (j + 1) * hidden], down_out.at[j, :, columns], out_sems.at[1, s % 2, j]
            )
            for j in range(experts)
        ]

    def expert_tile(s):
        @pl.when(s + 1 < 3 * count)
        def _():
            start_tile(s + 1)

        for matrix in range(3):

            @pl.when(s == matrix * count)
            def _():
                factor_load(matrix).wait()

        tile_copy(x_all, s).wait()

        @pl.when(s < 2 * count)
        def _():
            @pl.when(s >= 2)
            def _():
                for copy in across(gate_out, s):
                    copy.wait()

            results[s % 2] = crossed_dot(tiles[s % 2], factors[s // count])

            @pl.when(s < count)
            def _():
                for copy in across(gate_out, s):
                    copy.start()

            @pl.when(s >= count)
            def _():
                for copy in across(up_out, s):
                    copy.start()

        @pl.when(s >= 2 * count)
        def _():
            @pl.when(s >= 2 * count + 2)
            def _():
                for copy in down(s):
                    copy.wait()

            downs[s % 2] = crossed_dot(factors[0], tiles[s % 2])
            for copy in down(s):
                copy.start()

        @pl.when(s == count - 1)
        def _():
            factor_load(2).start()

    def dense_block(i):
        chip, sub = i // 2, i % 2
        block = plane.block(chip, (plane.core + 1 - sub) % 2)
        columns = pl.ds(pl.multiple_of(block * share, share), share)
        source = normed[:, columns]
        part[sub, chip, :, 0:heads] = crossed_dot(source, query_grad[...]).astype(jnp.bfloat16)
        part[sub, chip, :, heads : 2 * heads] = crossed_dot(source, key_grad[...]).astype(jnp.bfloat16)
        part[sub, chip, :, 2 * heads : 3 * heads] = crossed_dot(source, value_grad[...]).astype(jnp.bfloat16)
        part[sub, chip, :, 3 * heads : 4 * heads] = crossed_dot(
            attention_grad[:, columns], attended[...]
        ).astype(jnp.bfloat16)
        part[sub, chip, :, 4 * heads :] = extras[block]

        @pl.when(sub == 0)
        def _():
            plane.pair_copy(chip).start()

    for copy in weight_loads:
        copy.start()
    for chip in range(4):
        load_own(chip).start()
    greet(plane.neighbours() + line.neighbours())
    for chip in range(4):
        mix.pair_copy(chip).start()
    for copy in weight_loads:
        copy.wait()
    for start in range(0, width, column_tile):
        columns = slice(start, start + column_tile)
        later = width + start % half
        line_own[:, columns] = (
            turned_dot(query_grad[...], factors[0, columns])
            + turned_dot(key_grad[...], factors[1, columns])
            + turned_dot(value_grad[...], factors[start // half, later : later + column_tile])
        ).astype(jnp.bfloat16)
    factor_load(0).start()
    factor_load(1).start()
    start_tile(0)
    mix_last = mix.pieces + 1
    dense_first = 8 + 5
    dense_second = dense_first + plane.pieces // 2 + 2
    dense_last = dense_second + plane.pieces // 2 + 1

    def step(s, carry):
        line.advance(s)
        for chip in range(4):

            @pl.when(s == chip)
            def _():
                load_own(chip).wait()
                mix.pair_copy(chip).wait_recv()
                if chip < 3:
                    mix.send_first(chip)

        @pl.when((s >= 3) & (s - 3 < mix.pieces))
        def _():
            mix.second_piece(s - 3)

        @pl.when((s >= mix_last) & (s - mix_last < mix.pieces))
        def _():
            piece = s - mix_last
            for side, summed in enumerate(mix.last_sum(piece)):
                mix_own[3, mix.rows(side, piece)] = summed.astype(jnp.bfloat16)

        mix_line.advance(s - mix_last)

        @pl.when((s >= 4) & (s < 12))
        def _():
            dense_block(s - 4)

        @pl.when(s == dense_first)
        def _():
            for chip in range(4):
                plane.pair_copy(chip).wait_recv()
            for chip in range(3):
                plane.send_first(chip)

        @pl.when((s >= dense_second) & (s - dense_second < plane.pieces))
        def _():
            plane.second_piece(s - dense_second)

        @pl.when((s >= dense_last) & (s - dense_last < plane.pieces))
        def _():
            piece = s - dense_last
            for side, summed in enumerate(plane.last_sum(piece)):
                sums[plane.rows(side, piece)] = summed

        @pl.when(s < 3 * count)
        def _():
            expert_tile(s)

        return carry

    steps = jnp.maximum(mix_last + mix_line.steps(), jnp.maximum(3 * count, dense_last + plane.pieces))
    lax.fori_loop(0, steps, step, 0)
    for s in (2 * count - 2, 2 * count - 1):
        for copy in across(up_out, s):
            copy.wait()
    for s in (3 * count - 2, 3 * count - 1):
        for copy in down(s):
            copy.wait()
    for each in (plane, line, mix, mix_line):
        each.finish()


TILE = 256


def closing(
    normed, query_grad, key_grad, value_grad, attended, attention_grad, extras, w_query, w_key, w_value,
    mixed, arrived, arrived_grad, gated, gate_grad, up_grad, experts,
):
    rows, width = normed.shape
    heads = query_grad.shape[1]
    ranks, share, more = extras.shape
    wide = 4 * heads + more
    inner = gated.shape[2]
    hidden = inner // experts
    low = jnp.bfloat16
    tile = min(TILE, width // 2)
    vmem = pl.BlockSpec(memory_space=pltpu.VMEM)
    any_space = pl.BlockSpec(memory_space=pl.ANY)
    every = ranks * rows
    return pl.pallas_call(
        closing_kernel,
        out_shape=(
            jax.ShapeDtypeStruct((rows, width), low),
            jax.ShapeDtypeStruct((share, wide), jnp.float32),
            jax.ShapeDtypeStruct((rows, width), low),
            jax.ShapeDtypeStruct((experts, width, hidden), jnp.float32),
            jax.ShapeDtypeStruct((experts, width, hidden), jnp.float32),
            jax.ShapeDtypeStruct((experts, hidden, width), jnp.float32),
        ),
        in_specs=[vmem] * 7 + [any_space] * 9,
        out_specs=(vmem,) * 3 + (any_space,) * 3,
        scratch_shapes=[
            pltpu.VMEM((rows, width), low),
            pltpu.VMEM((rows, width), low),
            pltpu.VMEM((2, 4, share, wide), low),
            pltpu.VMEM((4, share, wide), low),
            pltpu.VMEM((3, share // 2, wide), low),
            pltpu.VMEM((3, share // 2, wide), low),
            pltpu.VMEM((4, rows, width), low),
            pltpu.VMEM((4, rows, width), low),
            pltpu.VMEM((3, rows // 2, width), low),
            pltpu.VMEM((3, rows // 2, width), low),
            pltpu.VMEM((rows, width), low),
            pltpu.VMEM((2, every, tile), low),
            pltpu.VMEM((2, every, inner), low),
            pltpu.VMEM((2, tile, inner), jnp.float32),
            pltpu.VMEM((2, inner, tile), jnp.float32),
            Line.semaphores(rows),
            *Plane.semaphores(share),
            Line.semaphores(rows),
            *Plane.semaphores(rows),
            pltpu.SemaphoreType.DMA((4,)),
            pltpu.SemaphoreType.DMA((4,)),
            pltpu.SemaphoreType.DMA((3,)),
            pltpu.SemaphoreType.DMA((2,)),
            pltpu.SemaphoreType.DMA((2, 2, experts)),
        ],
        compiler_params=pltpu.CompilerParams(
            collective_id=2, has_side_effects=True, vmem_limit_bytes=63 * 2**20
        ),
    )(
        normed, query_grad, key_grad, value_grad, attended, attention_grad, extras, w_query, w_key, w_value,
        mixed, arrived.reshape(every, width), arrived_grad.reshape(every, width),
        gated.reshape(every, inner), gate_grad.reshape(every, inner), up_grad.reshape(every, inner),
    )


class Peers:
    def __init__(self, mine, theirs, sent, got):
        self.mine, self.theirs, self.sent, self.got = mine, theirs, sent, got
        self.size = lax.axis_size("tensor")
        self.here = lax.axis_index("tensor")

    def neighbours(self):
        return [(None, {"tensor": (self.here + d) % self.size}) for d in range(1, self.size)]

    def copies(self):
        return [
            remote(
                self.mine, self.theirs.at[d - 1], self.sent.at[d - 1], self.got.at[d - 1],
                tensor=(self.here + d) % self.size,
            )
            for d in range(1, self.size)
        ]

    def start(self):
        for copy in self.copies():
            copy.start()

    def total(self):
        result = self.mine[...]
        for d, copy in enumerate(self.copies()):
            copy.wait_recv()
            result = result + self.theirs[d]
        return result

    def finish(self):
        for copy in self.copies():
            copy.wait_send()


def to_rows(columns, rows):
    lane = lax.broadcasted_iota(jnp.int32, (rows, LANE), 1)
    field = jnp.zeros((rows, LANE), jnp.float32)
    for i, column in enumerate(columns):
        field = jnp.where(lane == i, column, field)
    return field.T[:8]


def to_columns(sums):
    padded = jnp.concatenate([sums, jnp.zeros((LANE - 8, sums.shape[1]), jnp.float32)], axis=0)
    return padded.T


def swapped(field):
    half = HD // 2
    return jnp.concatenate([field[:, half:], field[:, :half]], axis=1)


def front_kernel(
    tokens, attn_gain, ffn_gain, w_query, w_key, w_value, w_out, qk_gain, cosine, sine, bias, routes, cotangent,
    total, normed, normed_two, attended, query_rot, keys_values, query_raw, key_raw, stats, routes_all, spread_all,
    line_own, line_in, prompt, mine, theirs,
    line_sems, peer_sent, peer_got, *gather_sems,
):
    rows, width = tokens.shape
    local = w_query.shape[1]
    heads = local // HD
    factor = HD ** (-0.5)
    own_blocks = rows // PROMPT_DEV - 1
    devices = keys_values.shape[0] - own_blocks
    place = Place()
    line = Line(line_own, line_in, total, line_sems)
    peers = Peers(mine, theirs, peer_sent, peer_got)
    spread = Gather(cotangent, spread_all, place, *gather_sems[0:5], pieces=GATHER_PIECES)
    names = Gather(routes, routes_all, place, *gather_sems[5:10], pieces=2)
    prompts = Gather(prompt, keys_values, place, *gather_sems[10:15], pieces=2)
    greet(place.neighbours() + peers.neighbours())
    names.start()
    spread.own_copy().start()
    spread.start_piece(0)
    source = tokens[...].astype(jnp.float32)
    scale_one = lax.rsqrt(jnp.sum(source * source, axis=1, keepdims=True) / width + epsilon)
    normed[...] = (source * scale_one * attn_gain[...]).astype(jnp.bfloat16)
    query_raw[...] = wide_dot(normed[...], w_query[...])
    key_raw[...] = wide_dot(normed[...], w_key[...])
    mine[...] = to_rows(
        [
            jnp.sum(query_raw[...] * query_raw[...], axis=1, keepdims=True),
            jnp.sum(key_raw[...] * key_raw[...], axis=1, keepdims=True),
        ],
        rows,
    )
    peers.start()
    value = wide_dot(normed[...], w_value[...]).astype(jnp.bfloat16)
    prompt[:, local:] = value[:PROMPT_DEV]
    for i in range(own_blocks):
        keys_values[devices + i, :, local:] = value[(i + 1) * PROMPT_DEV : (i + 2) * PROMPT_DEV]
    squares = to_columns(peers.total())
    scale_query = lax.rsqrt(squares[:, 0:1] / width + epsilon)
    scale_key = lax.rsqrt(squares[:, 1:2] / width + epsilon)
    for head in range(heads):
        columns = slice(head * HD, (head + 1) * HD)
        turned = key_raw[:, columns] * scale_key * qk_gain[1:2, columns]
        turned = (turned * cosine[...] + swapped(turned) * sine[...]).astype(jnp.bfloat16)
        prompt[:, columns] = turned[:PROMPT_DEV]
        for i in range(own_blocks):
            keys_values[devices + i, :, columns] = turned[(i + 1) * PROMPT_DEV : (i + 2) * PROMPT_DEV]
    prompts.own_copy().start()
    for piece in range(2):
        prompts.start_piece(piece)
    for piece in range(1, GATHER_PIECES):
        spread.start_piece(piece)
    for head in range(heads):
        columns = slice(head * HD, (head + 1) * HD)
        turned = query_raw[:, columns] * scale_query * qk_gain[0:1, columns]
        turned = turned * cosine[...] + swapped(turned) * sine[...]
        query_rot[:, columns] = turned.astype(jnp.bfloat16)
    for piece in range(2):
        prompts.near(piece)
    for piece in range(2):
        names.near(piece)
    for piece in range(2):
        prompts.far(piece)
        names.far(piece)
    prompts.own_copy().wait()
    for kind in range(4):
        for piece in range(2):
            prompts.paired(kind, piece)
            names.paired(kind, piece)
    lane = lax.broadcasted_iota(jnp.int32, (rows, LANE), 1)
    kept = jnp.where(lane == 0, scale_one, 0.0)
    kept = jnp.where(lane == 1, scale_query, kept)
    kept = jnp.where(lane == 2, scale_key, kept)
    count = keys_values.shape[0] * PROMPT_DEV
    for head in range(heads):
        columns = slice(head * HD, (head + 1) * HD)
        keys = keys_values[:, :, columns].reshape(count, HD)
        values = keys_values[:, :, local + head * HD : local + (head + 1) * HD].reshape(count, HD)
        scores = turned_dot(query_rot[:, columns], keys) * factor + bias[...]
        top = jnp.max(scores, axis=1, keepdims=True)
        weights = jnp.exp(scores - top)
        whole = jnp.sum(weights, axis=1, keepdims=True)
        shares = (weights / whole).astype(jnp.bfloat16)
        attended[:, columns] = wide_dot(shares, values).astype(jnp.bfloat16)
        kept = jnp.where(lane == 8 + head, top + jnp.log(whole), kept)
    tile = min(512, width)
    for start in range(0, width, tile):
        columns = slice(start, start + tile)
        line_own[:, columns] = wide_dot(attended[...], w_out[:, columns]).astype(jnp.bfloat16)
    steps = line.pieces + 2 * (line.size - 1)
    done = 0
    for piece in range(GATHER_PIECES):
        upto = steps * (piece + 1) // (2 * GATHER_PIECES)
        lax.fori_loop(done, upto, line.step_body, 0)
        done = upto
        spread.near(piece)
    for piece in range(GATHER_PIECES):
        upto = done + (steps - done) * (piece + 1) // GATHER_PIECES
        lax.fori_loop(done, upto, line.step_body, 0)
        done = upto
        spread.far(piece)
    hidden = tokens[...].astype(jnp.float32) + total[...].astype(jnp.float32)
    scale_two = lax.rsqrt(jnp.sum(hidden * hidden, axis=1, keepdims=True) / width + epsilon)
    normed_two[...] = (hidden * scale_two * ffn_gain[...]).astype(jnp.bfloat16)
    stats[...] = jnp.where(lane == 3, scale_two, kept)
    for kind in range(4):
        for piece in range(GATHER_PIECES):
            spread.paired(kind, piece)
    names.own_copy().wait()
    spread.own_copy().wait()
    for each in (names, prompts, spread, line, peers):
        each.finish()


def front(tokens, attn_gain, ffn_gain, w_query, w_key, w_value, w_out, qk_gain, cosine, sine, bias, routes, cotangent):
    rows, width = tokens.shape
    local = w_query.shape[1]
    ranks = lax.axis_size("expert")
    size = lax.axis_size("tensor")
    low, full = jnp.bfloat16, jnp.float32
    vmem = pl.BlockSpec(memory_space=pltpu.VMEM)
    any_space = pl.BlockSpec(memory_space=pl.ANY)
    blocks = ranks + rows // PROMPT_DEV - 1
    return pl.pallas_call(
        front_kernel,
        out_shape=(
            jax.ShapeDtypeStruct((rows, width), low),
            jax.ShapeDtypeStruct((rows, width), low),
            jax.ShapeDtypeStruct((rows, width), low),
            jax.ShapeDtypeStruct((rows, local), low),
            jax.ShapeDtypeStruct((rows, local), low),
            jax.ShapeDtypeStruct((blocks, PROMPT_DEV, 2 * local), low),
            jax.ShapeDtypeStruct((rows, local), full),
            jax.ShapeDtypeStruct((rows, local), full),
            jax.ShapeDtypeStruct((rows, LANE), full),
            jax.ShapeDtypeStruct((ranks,) + routes.shape, jnp.int32),
            jax.ShapeDtypeStruct((ranks, rows, width), low),
        ),
        in_specs=[vmem] * 12 + [any_space],
        out_specs=(vmem,) * 10 + (any_space,),
        scratch_shapes=[
            pltpu.VMEM((rows, width), low),
            pltpu.VMEM((rows, width), low),
            pltpu.VMEM((PROMPT_DEV, 2 * local), low),
            pltpu.VMEM((8, rows), full),
            pltpu.VMEM((size - 1, 8, rows), full),
            Line.semaphores(rows),
            pltpu.SemaphoreType.DMA((size - 1,)),
            pltpu.SemaphoreType.DMA((size - 1,)),
            *Gather.semaphores(GATHER_PIECES),
            *Gather.semaphores(2),
            *Gather.semaphores(2),
        ],
        compiler_params=pltpu.CompilerParams(
            collective_id=1, has_side_effects=True, vmem_limit_bytes=60 * 2**20
        ),
    )(tokens, attn_gain, ffn_gain, w_query, w_key, w_value, w_out, qk_gain, cosine, sine, bias, routes, cotangent)


def backward_kernel(
    attention_grad, w_out, query_rot, keys_values, bias, stats, query_raw, key_raw, cosine, sine, qk_gain,
    query_out, key_out, value_out, gain_out,
    out_grad, query_grad, prompt_grads, own_grads, own, paired, from_x, from_y, mine, theirs,
    pair_sems, x_sems, y_sems, peer_sent, peer_got,
):
    rows, local = query_rot.shape
    width = attention_grad.shape[1]
    heads = local // HD
    factor = HD ** (-0.5)
    own_blocks = rows // PROMPT_DEV - 1
    devices = keys_values.shape[0] - own_blocks
    count = keys_values.shape[0] * PROMPT_DEV
    reach = devices * PROMPT_DEV
    plane = Plane(own, prompt_grads, paired, from_x, from_y, pair_sems, x_sems, y_sems, by_device=True)
    peers = Peers(mine, theirs, peer_sent, peer_got)
    greet(plane.neighbours() + peers.neighbours())
    out_grad[...] = turned_dot(attention_grad[...], w_out[...]).astype(jnp.bfloat16)
    for head in range(heads):
        columns = slice(head * HD, (head + 1) * HD)
        other = slice(local + head * HD, local + (head + 1) * HD)
        keys = keys_values[:, :, columns].reshape(count, HD)
        values = keys_values[:, :, other].reshape(count, HD)
        query, above = query_rot[:, columns], out_grad[:, columns]
        scores = turned_dot(query, keys) * factor + bias[...]
        shares = jnp.exp(scores - stats[:, 8 + head : 9 + head])
        share_grad = turned_dot(above, values)
        delta = jnp.sum(shares * share_grad, axis=1, keepdims=True)
        score_grad = (shares * (share_grad - delta)).astype(jnp.bfloat16)
        query_grad[:, columns] = wide_dot(score_grad, keys) * factor
        key_grad = crossed_dot(score_grad, query) * factor
        value_grad = crossed_dot(shares.astype(jnp.bfloat16), above)
        prompt_grads[:, :, columns] = key_grad[:reach].astype(jnp.bfloat16).reshape(devices, PROMPT_DEV, HD)
        prompt_grads[:, :, other] = value_grad[:reach].astype(jnp.bfloat16).reshape(devices, PROMPT_DEV, HD)
        own_grads[PROMPT_DEV:, columns] = key_grad[reach:]
        own_grads[PROMPT_DEV:, other] = value_grad[reach:]
    for chip in range(4):
        plane.pair_copy(chip).start()
    for chip in range(4):
        own[chip] = prompt_grads[plane.block(chip, plane.core)]
    for chip in range(4):
        plane.pair_copy(chip).wait_recv()
        if chip < 3:
            plane.send_first(chip)

    def normed_part(source, raw, row, scale):
        inner = jnp.zeros((rows, 1), jnp.float32)
        for head in range(heads):
            columns = slice(head * HD, (head + 1) * HD)
            grad = source[:, columns]
            grad = grad * cosine[...] - swapped(grad) * sine[...]
            gain_out[row : row + 1, columns] = jnp.sum(grad * raw[:, columns] * scale, axis=0, keepdims=True)
            grad = qk_gain[row : row + 1, columns] * grad
            source[:, columns] = grad
            inner = inner + jnp.sum(grad * raw[:, columns], axis=1, keepdims=True)
        return inner

    scale_query, scale_key = stats[:, 1:2], stats[:, 2:3]
    query_inner = normed_part(query_grad, query_raw, 0, scale_query)
    plane.send_second()

    def last(piece, carry):
        for side, summed in enumerate(plane.last_sum(piece)):
            own_grads[plane.rows(side, piece)] = summed
        return carry

    lax.fori_loop(0, plane.pieces, last, 0)
    key_inner = normed_part(own_grads, key_raw, 1, scale_key)
    mine[...] = to_rows([query_inner, key_inner], rows)
    peers.start()
    value_out[...] = own_grads[:, local:].astype(jnp.bfloat16)
    inner = to_columns(peers.total())
    for out, source, raw, scale, i in (
        (query_out, query_grad, query_raw, scale_query, 0),
        (key_out, own_grads, key_raw, scale_key, 1),
    ):
        pull = scale * scale * scale / width * inner[:, i : i + 1]
        out[...] = (scale * source[:, :local] - raw[...] * pull).astype(jnp.bfloat16)
    plane.finish()
    peers.finish()


def backward(attention_grad, w_out, query_rot, keys_values, bias, stats, query_raw, key_raw, cosine, sine, qk_gain):
    rows, local = query_rot.shape
    size = lax.axis_size("tensor")
    ranks = lax.axis_size("expert")
    low, full = jnp.bfloat16, jnp.float32
    vmem = pl.BlockSpec(memory_space=pltpu.VMEM)
    small = jax.ShapeDtypeStruct((rows, local), low)
    return pl.pallas_call(
        backward_kernel,
        out_shape=(small, small, small, jax.ShapeDtypeStruct((2, local), full)),
        in_specs=[vmem] * 11,
        out_specs=(vmem,) * 4,
        scratch_shapes=[
            pltpu.VMEM((rows, local), low),
            pltpu.VMEM((rows, local), full),
            pltpu.VMEM((ranks, PROMPT_DEV, 2 * local), low),
            pltpu.VMEM((rows, 2 * local), full),
            pltpu.VMEM((4, PROMPT_DEV, 2 * local), low),
            pltpu.VMEM((4, PROMPT_DEV, 2 * local), low),
            pltpu.VMEM((3, PROMPT_DEV // 2, 2 * local), low),
            pltpu.VMEM((3, PROMPT_DEV // 2, 2 * local), low),
            pltpu.VMEM((8, rows), full),
            pltpu.VMEM((size - 1, 8, rows), full),
            *Plane.semaphores(PROMPT_DEV),
            pltpu.SemaphoreType.DMA((size - 1,)),
            pltpu.SemaphoreType.DMA((size - 1,)),
        ],
        compiler_params=pltpu.CompilerParams(
            collective_id=3, has_side_effects=True, vmem_limit_bytes=60 * 2**20
        ),
    )(attention_grad, w_out, query_rot, keys_values, bias, stats, query_raw, key_raw, cosine, sine, qk_gain)


def rotate(field, cosine, sine):
    half = field.shape[-1] // 2
    first = field[..., :half]
    second = field[..., half:]
    return jnp.concatenate(
        [first * cosine - second * sine, second * cosine + first * sine], axis=-1
    )


def unrotate(grad, cosine, sine):
    half = grad.shape[-1] // 2
    first = grad[..., :half]
    second = grad[..., half:]
    return jnp.concatenate(
        [first * cosine + second * sine, second * cosine - first * sine], axis=-1
    )


def experts(normed_two, cotangent, gates, w_gate, w_up, w_down, experts_total):
    local_experts = w_gate.shape[0]
    device = lax.axis_index("expert")
    arrived = lax.all_gather(normed_two, "expert", axis=0, tiled=True)
    arrived_grad = lax.all_gather(cotangent, "expert", axis=0, tiled=True)
    gate_pre = jnp.einsum("rd,jdf->jrf", arrived, w_gate, preferred_element_type=jnp.float32)
    up_pre = jnp.einsum("rd,jdf->jrf", arrived, w_up, preferred_element_type=jnp.float32)
    raw_grad = jnp.einsum("rd,jfd->jrf", arrived_grad, w_down, preferred_element_type=jnp.float32)
    sigma = jax.nn.sigmoid(gate_pre)
    activated = gate_pre * sigma
    inner = activated * up_pre
    gated = (gates[:, :, None] * inner).astype(jnp.bfloat16)
    mixed_part = jnp.einsum("jrf,jfd->rd", gated, w_down, preferred_element_type=jnp.float32)
    mixture = lax.psum(
        lax.psum_scatter(
            mixed_part.astype(jnp.bfloat16), "expert", scatter_dimension=0, tiled=True
        ),
        "tensor",
    ).astype(jnp.float32)
    gate_grad_part = jnp.sum(raw_grad * inner, axis=2)
    act_grad = gates[:, :, None] * raw_grad
    up_grad = (act_grad * activated).astype(jnp.bfloat16)
    gate_grad = (act_grad * up_pre * sigma * (1.0 + gate_pre * (1.0 - sigma))).astype(jnp.bfloat16)
    grad_w_down = jnp.einsum("jrf,rd->jfd", gated, arrived_grad, preferred_element_type=jnp.float32)
    grad_w_gate = jnp.einsum("rd,jrf->jdf", arrived, gate_grad, preferred_element_type=jnp.float32)
    grad_w_up = jnp.einsum("rd,jrf->jdf", arrived, up_grad, preferred_element_type=jnp.float32)
    slot_grad = jnp.einsum("jrf,jdf->rd", gate_grad, w_gate, preferred_element_type=jnp.float32)
    slot_grad = slot_grad + jnp.einsum(
        "jrf,jdf->rd", up_grad, w_up, preferred_element_type=jnp.float32
    )
    moe_input_grad = lax.psum(
        lax.psum_scatter(
            slot_grad.astype(jnp.bfloat16), "expert", scatter_dimension=0, tiled=True
        ),
        "tensor",
    ).astype(jnp.float32)
    placed = jnp.zeros((arrived.shape[0], experts_total), jnp.float32)
    placed = lax.dynamic_update_slice_in_dim(placed, gate_grad_part.T, device * local_experts, 1)
    chance_grad = lax.psum(
        lax.psum_scatter(placed, "expert", scatter_dimension=0, tiled=True), "tensor"
    )
    return mixture, moe_input_grad, chance_grad, [grad_w_gate, grad_w_up, grad_w_down]


def body(
    tokens,
    w_query,
    w_key,
    w_value,
    w_out,
    attn_gain,
    ffn_gain,
    qk_gain,
    router,
    w_gate,
    w_up,
    w_down,
    routes,
    cont_group,
    cotangent,
):
    rows, width = tokens.shape
    local_width = w_query.shape[1]
    head_count = local_width // HD
    experts_total = router.shape[1]
    local_experts = w_gate.shape[0]
    ranks = lax.axis_size("expert")
    device = lax.axis_index("expert")
    span = ranks // 2
    prompt_len = PROMPT_DEV * span
    factor = HD ** (-0.5)
    local = jnp.arange(rows, dtype=jnp.int32)
    is_prompt = local < PROMPT_DEV
    after = jnp.maximum(local - PROMPT_DEV, 0)
    slot_cont = after // CLEN
    cont_pick = jnp.sum(
        jnp.where(
            slot_cont[:, None] == jnp.arange(CONT_DEV, dtype=jnp.int32)[None, :],
            cont_group[None, :],
            0,
        ),
        axis=1,
    )
    group = jnp.where(is_prompt, device // span, cont_pick)
    position = jnp.where(is_prompt, device % span * PROMPT_DEV + local, prompt_len + after % CLEN)
    tag = jnp.where(is_prompt, -1, slot_cont)
    frequency = 10000.0 ** (-jnp.arange(HD // 2, dtype=jnp.float32) * 2.0 / HD)
    angle = position.astype(jnp.float32)[:, None] * frequency[None, :]
    cosine = jnp.cos(angle)[:, None, :]
    sine = jnp.sin(angle)[:, None, :]
    source = tokens.astype(jnp.float32)
    scale_one = lax.rsqrt(jnp.mean(source * source, axis=1, keepdims=True) + epsilon)
    normed = (source * scale_one * attn_gain).astype(jnp.bfloat16)
    query_raw = jnp.dot(normed, w_query, preferred_element_type=jnp.float32)
    key_raw = jnp.dot(normed, w_key, preferred_element_type=jnp.float32)
    value_raw = jnp.dot(normed, w_value, preferred_element_type=jnp.float32)
    squares = lax.psum(
        jnp.stack(
            [jnp.sum(query_raw * query_raw, axis=1), jnp.sum(key_raw * key_raw, axis=1)], axis=1
        ),
        "tensor",
    )
    scale_query = lax.rsqrt(squares[:, 0:1] / width + epsilon)
    scale_key = lax.rsqrt(squares[:, 1:2] / width + epsilon)
    query_rot = (
        rotate((query_raw * scale_query * qk_gain[0]).reshape(rows, head_count, HD), cosine, sine)
        .reshape(rows, local_width)
        .astype(jnp.bfloat16)
    )
    key_rot = (
        rotate((key_raw * scale_key * qk_gain[1]).reshape(rows, head_count, HD), cosine, sine)
        .reshape(rows, local_width)
        .astype(jnp.bfloat16)
    )
    value_low = value_raw.astype(jnp.bfloat16)
    prompt_keys, prompt_values = (
        lax.all_gather(key_rot[:PROMPT_DEV], "expert", axis=0, tiled=True),
        lax.all_gather(value_low[:PROMPT_DEV], "expert", axis=0, tiled=True),
    )
    prompt_count = prompt_keys.shape[0]
    all_keys = jnp.concatenate([prompt_keys, key_rot[PROMPT_DEV:]], axis=0)
    all_values = jnp.concatenate([prompt_values, value_low[PROMPT_DEV:]], axis=0)
    key_index = jnp.arange(prompt_count, dtype=jnp.int32)
    prompt_mask = (group[:, None] == (key_index // prompt_len)[None, :]) & (
        (key_index % prompt_len)[None, :] <= position[:, None]
    )
    own_mask = (tag[:, None] == tag[None, PROMPT_DEV:]) & (
        position[None, PROMPT_DEV:] <= position[:, None]
    )
    mask = jnp.concatenate([prompt_mask, own_mask], axis=1)

    def head_scores(query_head, key_head):
        scores = (
            jnp.einsum("qd,kd->qk", query_head, key_head, preferred_element_type=jnp.float32)
            * factor
        )
        return jnp.where(mask, scores, masked_value)

    outputs = []
    log_totals = []
    for head in range(head_count):
        start = head * HD
        scores = head_scores(query_rot[:, start : start + HD], all_keys[:, start : start + HD])
        top = jnp.max(scores, axis=1, keepdims=True)
        weights = jnp.exp(scores - top)
        total = jnp.sum(weights, axis=1, keepdims=True)
        shares = (weights / total).astype(jnp.bfloat16)
        outputs.append(
            jnp.dot(shares, all_values[:, start : start + HD], preferred_element_type=jnp.float32)
        )
        log_totals.append(top + jnp.log(total))
    attended = jnp.concatenate(outputs, axis=1).astype(jnp.bfloat16)
    attention = lax.psum(jnp.dot(attended, w_out, preferred_element_type=jnp.float32), "tensor")
    hidden = source + attention
    scale_two = lax.rsqrt(jnp.mean(hidden * hidden, axis=1, keepdims=True) + epsilon)
    normed_two = (hidden * scale_two * ffn_gain).astype(jnp.bfloat16)
    logits = jnp.dot(normed_two, router, preferred_element_type=jnp.float32)
    top = jnp.max(logits, axis=1, keepdims=True)
    weights = jnp.exp(logits - top)
    chances = weights / jnp.sum(weights, axis=1, keepdims=True)
    hits = (routes[:, :, None] == jnp.arange(experts_total, dtype=jnp.int32)[None, None, :]).astype(
        jnp.float32
    )
    rows_mask = jnp.sum(hits, axis=1)
    routed = lax.all_gather(
        (rows_mask * chances).astype(jnp.float32), "expert", axis=0, tiled=True
    )
    gates = lax.dynamic_slice_in_dim(routed, device * local_experts, local_experts, 1).T
    grad_out = cotangent.astype(jnp.float32)
    pieces = max(1, ranks * rows // 4096)
    piece = rows // pieces
    split_gates = gates.reshape(local_experts, ranks, rows)
    results = []
    weight_grads = None
    for number in range(pieces):
        part = slice(number * piece, (number + 1) * piece)
        sources = (normed_two[part], cotangent[part])
        if results:
            sources, results, weight_grads = lax.optimization_barrier(
                (sources, results, weight_grads)
            )
        *result, grads = experts(
            *sources,
            split_gates[:, :, part].reshape(local_experts, ranks * piece),
            w_gate,
            w_up,
            w_down,
            experts_total,
        )
        results.append(result)
        weight_grads = grads if weight_grads is None else [a + b for a, b in zip(weight_grads, grads)]
    mixture, moe_input_grad, chance_grad = (
        jnp.concatenate(list(group_of), axis=0) for group_of in zip(*results)
    )
    grad_w_gate, grad_w_up, grad_w_down = weight_grads
    chance_grad = rows_mask * chance_grad
    output = (hidden + mixture).astype(jnp.bfloat16)
    logit_grad = (
        chances * (chance_grad - jnp.sum(chances * chance_grad, axis=1, keepdims=True))
    ).astype(jnp.bfloat16)
    grad_router = jnp.einsum(
        "td,te->de", normed_two, logit_grad, preferred_element_type=jnp.float32
    )
    normed_two_grad = moe_input_grad + jnp.einsum(
        "te,de->td", logit_grad, router, preferred_element_type=jnp.float32
    )
    weighted_two = ffn_gain * normed_two_grad
    grad_ffn_gain = jnp.sum(normed_two_grad * hidden * scale_two, axis=0)
    hidden_grad = (
        grad_out
        + scale_two * weighted_two
        - hidden * (scale_two**3 / width) * jnp.sum(weighted_two * hidden, axis=1, keepdims=True)
    )
    attention_grad = hidden_grad.astype(jnp.bfloat16)
    grad_w_out = jnp.einsum(
        "td,te->de", attended, attention_grad, preferred_element_type=jnp.float32
    )
    attended_grad = jnp.einsum(
        "te,de->td", attention_grad, w_out, preferred_element_type=jnp.float32
    ).astype(jnp.bfloat16)
    query_grads = []
    key_grads = []
    value_grads = []
    for head in range(head_count):
        start = head * HD
        query_head = query_rot[:, start : start + HD]
        key_head = all_keys[:, start : start + HD]
        value_head = all_values[:, start : start + HD]
        out_grad_head = attended_grad[:, start : start + HD]
        recomputed = jnp.exp(head_scores(query_head, key_head) - log_totals[head])
        share_grad = jnp.einsum(
            "qd,kd->qk", out_grad_head, value_head, preferred_element_type=jnp.float32
        )
        delta = jnp.sum(recomputed * share_grad, axis=1, keepdims=True)
        score_grad = (recomputed * (share_grad - delta)).astype(jnp.bfloat16)
        query_grads.append(
            jnp.dot(score_grad, key_head, preferred_element_type=jnp.float32) * factor
        )
        key_grads.append(
            jnp.einsum("qk,qd->kd", score_grad, query_head, preferred_element_type=jnp.float32)
            * factor
        )
        value_grads.append(
            jnp.einsum(
                "qk,qd->kd",
                recomputed.astype(jnp.bfloat16),
                out_grad_head,
                preferred_element_type=jnp.float32,
            )
        )
    key_grad_all = jnp.concatenate(key_grads, axis=1)
    value_grad_all = jnp.concatenate(value_grads, axis=1)
    prompt_key_grad, prompt_value_grad = (
        lax.psum_scatter(
            key_grad_all[:prompt_count].astype(jnp.bfloat16),
            "expert",
            scatter_dimension=0,
            tiled=True,
        ).astype(jnp.float32),
        lax.psum_scatter(
            value_grad_all[:prompt_count].astype(jnp.bfloat16),
            "expert",
            scatter_dimension=0,
            tiled=True,
        ).astype(jnp.float32),
    )
    key_grad = jnp.concatenate([prompt_key_grad, key_grad_all[prompt_count:]], axis=0)
    value_grad = jnp.concatenate([prompt_value_grad, value_grad_all[prompt_count:]], axis=0)
    query_grad = unrotate(
        jnp.concatenate(query_grads, axis=1).reshape(rows, head_count, HD), cosine, sine
    ).reshape(rows, local_width)
    key_grad = unrotate(key_grad.reshape(rows, head_count, HD), cosine, sine).reshape(
        rows, local_width
    )
    grad_qk_gain = jnp.stack(
        [
            jnp.sum(query_grad * query_raw * scale_query, axis=0),
            jnp.sum(key_grad * key_raw * scale_key, axis=0),
        ],
        axis=0,
    )
    weighted_query = qk_gain[0] * query_grad
    weighted_key = qk_gain[1] * key_grad
    inner_sums = lax.psum(
        jnp.stack(
            [jnp.sum(weighted_query * query_raw, axis=1), jnp.sum(weighted_key * key_raw, axis=1)],
            axis=1,
        ),
        "tensor",
    )
    query_raw_grad = (
        scale_query * weighted_query - query_raw * (scale_query**3 / width) * inner_sums[:, 0:1]
    ).astype(jnp.bfloat16)
    key_raw_grad = (
        scale_key * weighted_key - key_raw * (scale_key**3 / width) * inner_sums[:, 1:2]
    ).astype(jnp.bfloat16)
    value_raw_grad = value_grad.astype(jnp.bfloat16)
    grad_w_query = jnp.einsum(
        "td,te->de", normed, query_raw_grad, preferred_element_type=jnp.float32
    )
    grad_w_key = jnp.einsum("td,te->de", normed, key_raw_grad, preferred_element_type=jnp.float32)
    grad_w_value = jnp.einsum(
        "td,te->de", normed, value_raw_grad, preferred_element_type=jnp.float32
    )
    normed_part = jnp.einsum(
        "te,de->td", query_raw_grad, w_query, preferred_element_type=jnp.float32
    )
    normed_part = normed_part + jnp.einsum(
        "te,de->td", key_raw_grad, w_key, preferred_element_type=jnp.float32
    )
    normed_part = normed_part + jnp.einsum(
        "te,de->td", value_raw_grad, w_value, preferred_element_type=jnp.float32
    )
    normed_grad = lax.psum(normed_part.astype(jnp.bfloat16), "tensor").astype(jnp.float32)
    weighted_one = attn_gain * normed_grad
    grad_attn_gain = jnp.sum(normed_grad * source * scale_one, axis=0)
    input_grad = (
        hidden_grad
        + scale_one * weighted_one
        - source * (scale_one**3 / width) * jnp.sum(weighted_one * source, axis=1, keepdims=True)
    )
    summed = (
        lax.psum_scatter(
            grad_w_query.astype(jnp.bfloat16), "expert", scatter_dimension=0, tiled=True
        ).astype(jnp.float32),
        lax.psum_scatter(
            grad_w_key.astype(jnp.bfloat16), "expert", scatter_dimension=0, tiled=True
        ).astype(jnp.float32),
        lax.psum_scatter(
            grad_w_value.astype(jnp.bfloat16), "expert", scatter_dimension=0, tiled=True
        ).astype(jnp.float32),
        lax.psum_scatter(
            grad_w_out.astype(jnp.bfloat16), "expert", scatter_dimension=1, tiled=True
        ).astype(jnp.float32),
        lax.psum_scatter(
            grad_attn_gain.astype(jnp.bfloat16), "expert", scatter_dimension=0, tiled=True
        ).astype(jnp.float32),
        lax.psum_scatter(
            grad_ffn_gain.astype(jnp.bfloat16), "expert", scatter_dimension=0, tiled=True
        ).astype(jnp.float32),
        lax.psum_scatter(
            grad_qk_gain.astype(jnp.bfloat16), "expert", scatter_dimension=1, tiled=True
        ).astype(jnp.float32),
        lax.psum_scatter(
            grad_router.astype(jnp.bfloat16), "expert", scatter_dimension=0, tiled=True
        ).astype(jnp.float32),
    )
    return (
        output,
        input_grad,
        summed[0],
        summed[1],
        summed[2],
        summed[3],
        summed[4],
        summed[5],
        summed[6],
        summed[7],
        grad_w_gate,
        grad_w_up,
        grad_w_down,
    )


def compact(
    tokens, w_query, w_key, w_value, w_out, attn_gain, ffn_gain, qk_gain, router, w_gate, w_up, w_down,
    routes, cont_group, cotangent,
):
    rows, width = tokens.shape
    local_width = w_query.shape[1]
    head_count = local_width // HD
    experts_total = router.shape[1]
    local_experts = w_gate.shape[0]
    ranks = lax.axis_size("expert")
    device = lax.axis_index("expert")
    full = jnp.float32
    group, position, tag = layout(rows, ranks, device, cont_group)
    frequency = 10000.0 ** (-jnp.arange(HD // 2, dtype=full) * 2.0 / HD)
    angle = position.astype(full)[:, None] * frequency[None, :]
    cosine, sine = jnp.cos(angle), jnp.sin(angle)
    cosine = jnp.concatenate([cosine, cosine], axis=1)
    sine = jnp.concatenate([-sine, sine], axis=1)
    bias = jnp.where(attention_mask(group, position, tag, ranks), 0.0, masked_value).astype(full)
    own_first = jnp.roll(router, -device * local_experts, axis=1)
    own_first = jnp.pad(own_first, ((0, 0), (0, LANE - experts_total)))
    expert_bias = jnp.where(jnp.arange(LANE) < experts_total, 0.0, masked_value).astype(full)[None]
    turned_routes = jnp.tile(jnp.pad(routes.T, ((0, -routes.shape[1] % 8), (0, 0)), constant_values=-1), (2, 1))
    hits = routes[:, :, None] == jnp.arange(experts_total, dtype=jnp.int32)
    routed = jnp.any(hits, axis=1).astype(full)
    (
        attention, normed, normed_two, attended, query_rot, keys_values, query_raw, key_raw, stats, routes_all, arrived_grad,
    ) = front(
        tokens, attn_gain[None], ffn_gain[None], w_query, w_key, w_value, w_out, qk_gain, cosine, sine, bias,
        turned_routes, cotangent,
    )
    own_expert = device * local_experts + jnp.arange(local_experts, dtype=jnp.int32)
    names = routes_all[:, : turned_routes.shape[0] // 2]
    expert_mask = jnp.any(names[:, :, :, None] == own_expert, axis=1).astype(full)
    expert_mask = jnp.pad(expert_mask, ((0, 0), (0, 0), (0, LANE - local_experts)))
    arrived = lax.all_gather(normed_two, "expert", axis=0)
    reduced, gated, gate_grad, up_grad, mixed_part = experts_fused(
        arrived, arrived_grad, expert_mask, own_first, expert_bias, w_gate, w_up, w_down
    )
    source = tokens.astype(full)
    hidden = source + attention.astype(full)
    scale_one, scale_two = stats[:, 0:1], stats[:, 3:4]
    logits = jnp.dot(normed_two, router, preferred_element_type=full)
    weights = jnp.exp(logits - jnp.max(logits, axis=1, keepdims=True))
    chances = weights / jnp.sum(weights, axis=1, keepdims=True)
    chance_grad = routed * reduced[:, width : width + experts_total].astype(full)
    logit_grad = (
        chances * (chance_grad - jnp.sum(chances * chance_grad, axis=1, keepdims=True))
    ).astype(jnp.bfloat16)
    grad_router = jnp.einsum("td,te->de", normed_two, logit_grad, preferred_element_type=full)
    normed_two_grad = reduced[:, :width].astype(full) + jnp.einsum(
        "te,de->td", logit_grad, router, preferred_element_type=full
    )
    grad_out = cotangent.astype(full)
    weighted_two = ffn_gain * normed_two_grad
    grad_ffn_gain = jnp.sum(normed_two_grad * hidden * scale_two, axis=0)
    hidden_grad = (
        grad_out
        + scale_two * weighted_two
        - hidden * (scale_two**3 / width) * jnp.sum(weighted_two * hidden, axis=1, keepdims=True)
    )
    attention_grad = hidden_grad.astype(jnp.bfloat16)
    query_raw_grad, key_raw_grad, value_raw_grad, grad_qk_gain = backward(
        attention_grad, w_out, query_rot, keys_values, bias, stats, query_raw, key_raw, cosine, sine, qk_gain
    )
    small_part = local_width // ranks
    share = width // ranks
    gains = jnp.pad(
        grad_qk_gain.reshape(2, ranks, small_part).transpose(1, 2, 0), ((0, 0), (0, share - small_part), (0, 0))
    )
    extras = jnp.concatenate(
        [grad_router.reshape(ranks, share, experts_total), grad_ffn_gain.reshape(ranks, share, 1), gains], axis=2
    ).astype(jnp.bfloat16)
    extras = jnp.pad(extras, ((0, 0), (0, 0), (0, LANE - experts_total - 3)))
    normed_grad, sums, mixture, grad_w_gate, grad_w_up, grad_w_down = closing(
        normed, query_raw_grad, key_raw_grad, value_raw_grad, attended, attention_grad, extras, w_query, w_key, w_value,
        mixed_part, arrived, arrived_grad, gated, gate_grad, up_grad, local_experts,
    )
    normed_grad = normed_grad.astype(full)
    output = (hidden + mixture.astype(full)).astype(jnp.bfloat16)
    weighted_one = attn_gain * normed_grad
    grad_attn_gain = jnp.sum(normed_grad * source * scale_one, axis=0)
    input_grad = (
        hidden_grad
        + scale_one * weighted_one
        - source * (scale_one**3 / width) * jnp.sum(weighted_one * source, axis=1, keepdims=True)
    )
    edge = 4 * local_width
    return (
        output,
        input_grad,
        sums[:, :local_width],
        sums[:, local_width : 2 * local_width],
        sums[:, 2 * local_width : 3 * local_width],
        sums[:, 3 * local_width : edge].T,
        lax.psum_scatter(
            grad_attn_gain.astype(jnp.bfloat16), "expert", scatter_dimension=0, tiled=True
        ).astype(full),
        sums[:, edge + experts_total],
        sums[:small_part, edge + experts_total + 1 : edge + experts_total + 3].T,
        sums[:, edge : edge + experts_total],
        grad_w_gate,
        grad_w_up,
        grad_w_down,
    )


def layout(rows, ranks, device, cont_group):
    span = ranks // 2
    prompt_len = PROMPT_DEV * span
    local = jnp.arange(rows, dtype=jnp.int32)
    is_prompt = local < PROMPT_DEV
    after = jnp.maximum(local - PROMPT_DEV, 0)
    slot_cont = after // CLEN
    cont_pick = jnp.sum(
        jnp.where(
            slot_cont[:, None] == jnp.arange(CONT_DEV, dtype=jnp.int32)[None, :], cont_group[None, :], 0
        ),
        axis=1,
    )
    group = jnp.where(is_prompt, device // span, cont_pick)
    position = jnp.where(is_prompt, device % span * PROMPT_DEV + local, prompt_len + after % CLEN)
    tag = jnp.where(is_prompt, -1, slot_cont)
    return group, position, tag


def attention_mask(group, position, tag, ranks):
    prompt_len = PROMPT_DEV * (ranks // 2)
    key_index = jnp.arange(ranks * PROMPT_DEV, dtype=jnp.int32)
    prompt_mask = (group[:, None] == (key_index // prompt_len)[None, :]) & (
        (key_index % prompt_len)[None, :] <= position[:, None]
    )
    own_mask = (tag[:, None] == tag[None, PROMPT_DEV:]) & (
        position[None, PROMPT_DEV:] <= position[:, None]
    )
    return jnp.concatenate([prompt_mask, own_mask], axis=1)


def solution(mesh):
    small = mesh.shape["expert"] == 8
    return jax.shard_map(
        compact if small else body,
        mesh=mesh,
        in_specs=(
            P("expert", None),
            P(None, "tensor"),
            P(None, "tensor"),
            P(None, "tensor"),
            P("tensor", None),
            P(),
            P(),
            P(None, "tensor"),
            P(),
            P("expert", None, "tensor"),
            P("expert", None, "tensor"),
            P("expert", "tensor", None),
            P("expert", None),
            P("expert"),
            P("expert", None),
        ),
        out_specs=(
            P("expert", None),
            P("expert", None),
            P("expert", "tensor"),
            P("expert", "tensor"),
            P("expert", "tensor"),
            P("tensor", "expert"),
            P("expert"),
            P("expert"),
            P(None, ("tensor", "expert")),
            P("expert", None),
            P("expert", None, "tensor"),
            P("expert", None, "tensor"),
            P("expert", "tensor", None),
        ),
        check_vma=False,
    )
```

```python
import functools

import jax
import jax.numpy as jnp
from jax import lax
from jax.experimental import pallas as pl
from jax.experimental.pallas import tpu as pltpu
from jax.sharding import PartitionSpec as P

HD = 128
PROMPT_DEV = 128
CLEN = 256
CONT_DEV = 1


epsilon = 1e-05
masked_value = -1e30


MESH = pl.DeviceIdType.MESH
STEP = 16
LANE = 128


def remote(source, target, sent, received, **where):
    return pltpu.make_async_remote_copy(
        src_ref=source,
        dst_ref=target,
        send_sem=sent,
        recv_sem=received,
        device_id=where,
        device_id_type=MESH,
    )


def greet(places):
    barrier = pltpu.get_barrier_semaphore()
    for condition, where in places:
        def signal(where=where):
            pl.semaphore_signal(barrier, inc=1, device_id=where, device_id_type=MESH)
        if condition is None:
            signal()
        else:
            pl.when(condition)(signal)
    count = 0
    for condition, _ in places:
        count = count + (1 if condition is None else jnp.where(condition, 1, 0))
    pl.semaphore_wait(barrier, count)


class Line:
    def __init__(self, own, arrived, total, sems):
        self.own, self.arrived, self.total = own, arrived, total
        self.up_sent, self.up_got, self.down_sent, self.down_got = (sems.at[i] for i in range(4))
        self.size = lax.axis_size("tensor")
        self.here = lax.axis_index("tensor")
        self.half = own.shape[0] // 2
        self.pieces = self.half // STEP

    @staticmethod
    def semaphores(rows):
        return pltpu.SemaphoreType.DMA((4, 2, rows // 2 // STEP))

    def neighbours(self):
        here, size = self.here, self.size
        return [
            (here > 0, {"tensor": jnp.maximum(here - 1, 0)}),
            (here < size - 1, {"tensor": jnp.minimum(here + 1, size - 1)}),
        ]

    def lane(self, lane):
        here, size = self.here, self.size
        if lane == 0:
            return here, here + 1, here - 1
        return size - 1 - here, here - 1, here + 1

    def rows(self, lane, piece):
        return pl.ds(pl.multiple_of(lane * self.half + piece * STEP, STEP), STEP)

    def up_copy(self, lane, piece):
        rows = self.rows(lane, piece)
        onward = self.lane(lane)[1]
        return remote(
            self.own.at[rows], self.arrived.at[rows],
            self.up_sent.at[lane, piece], self.up_got.at[lane, piece], tensor=onward,
        )

    def down_copy(self, lane, piece):
        rows = self.rows(lane, piece)
        back = self.lane(lane)[2]
        return remote(
            self.total.at[rows], self.total.at[rows],
            self.down_sent.at[lane, piece], self.down_got.at[lane, piece], tensor=back,
        )

    def rise(self, lane, piece):
        place = self.lane(lane)[0]
        rows = self.rows(lane, piece)

        @pl.when(place > 0)
        def _():
            self.up_copy(lane, piece).wait_recv()
            summed = (
                self.own[rows].astype(jnp.float32) + self.arrived[rows].astype(jnp.float32)
            ).astype(jnp.bfloat16)

            @pl.when(place < self.size - 1)
            def _():
                self.own[rows] = summed

            @pl.when(place == self.size - 1)
            def _():
                self.total[rows] = summed
                self.down_copy(lane, piece).start()

        @pl.when(place < self.size - 1)
        def _():
            self.up_copy(lane, piece).start()

    def fall(self, lane, piece):
        place = self.lane(lane)[0]

        @pl.when(place < self.size - 1)
        def _():
            self.down_copy(lane, piece).wait_recv()

            @pl.when(place > 0)
            def _():
                self.down_copy(lane, piece).start()

    def advance(self, step, skew=1):
        for act, far in ((self.rise, False), (self.fall, True)):
            for lane in range(2):
                place = self.lane(lane)[0]
                piece = step - skew * (2 * (self.size - 1) - place if far else place)

                @pl.when((piece >= 0) & (piece < self.pieces))
                def _():
                    act(lane, piece)

    def step_body(self, step, carry):
        self.advance(step)
        return carry

    def steps(self, skew=1):
        return self.pieces + skew * 2 * (self.size - 1)

    def finish(self):
        def one(piece, carry):
            for lane in range(2):
                place = self.lane(lane)[0]

                @pl.when(place < self.size - 1)
                def _():
                    self.up_copy(lane, piece).wait_send()

                @pl.when(place > 0)
                def _():
                    self.down_copy(lane, piece).wait_send()
            return carry

        lax.fori_loop(0, self.pieces, one, 0)


class Place:
    def __init__(self):
        here = lax.axis_index("expert")
        self.here = here
        self.core, self.x, self.y = here % 2, here // 2 % 2, here // 4
        self.sibling = here + 1 - 2 * self.core
        self.x_chip = here + 2 - 4 * self.x
        self.y_chip = here + 4 - 8 * self.y

    def neighbours(self):
        return [(None, {"expert": i}) for i in (self.sibling, self.x_chip, self.y_chip)]

    def block(self, chip, core):
        x = self.x + (1 - chip // 2) * (1 - 2 * self.x)
        y = self.y + (1 - chip % 2) * (1 - 2 * self.y)
        return 4 * y + 2 * x + core


class Plane(Place):
    def __init__(self, own, spare, paired, from_x, from_y, pair_sems, x_sems, y_sems, by_device=False):
        self.by_device = by_device
        self.own, self.spare, self.paired, self.from_x, self.from_y = own, spare, paired, from_x, from_y
        self.pair_sems, self.x_sems, self.y_sems = pair_sems, x_sems, y_sems
        super().__init__()
        self.half = own.shape[1] // 2
        self.pieces = self.half // STEP

    @staticmethod
    def semaphores(rows):
        pieces = rows // 2 // STEP
        return [
            pltpu.SemaphoreType.DMA((2, 4)),
            pltpu.SemaphoreType.DMA((2, 3, pieces)),
            pltpu.SemaphoreType.DMA((2, 3, pieces)),
        ]

    def pair_copy(self, chip):
        place = self.block(chip, 1 - self.core) if self.by_device else chip
        return remote(
            self.spare.at[place], self.paired.at[chip],
            self.pair_sems.at[0, chip], self.pair_sems.at[1, chip], expert=self.sibling,
        )

    def rows(self, side, piece):
        return pl.ds(pl.multiple_of(side * self.half + piece * STEP, STEP), STEP)

    def landing(self, piece):
        return pl.ds(pl.multiple_of(piece * STEP, STEP), STEP)

    def x_copy(self, kind, piece):
        chip, side = ((0, 0), (1, 0), (1, 1))[kind]
        return remote(
            self.own.at[chip, self.rows(side, piece)], self.from_x.at[kind, self.landing(piece)],
            self.x_sems.at[0, kind, piece], self.x_sems.at[1, kind, piece], expert=self.x_chip,
        )

    def y_copy(self, kind, piece):
        chip, side = ((0, 1), (2, 1), (2, 0))[kind]
        return remote(
            self.own.at[chip, self.rows(side, piece)], self.from_y.at[kind, self.landing(piece)],
            self.y_sems.at[0, kind, piece], self.y_sems.at[1, kind, piece], expert=self.y_chip,
        )

    def add_pair(self, chip, side, piece):
        rows = self.rows(side, piece)
        self.own[chip, rows] = (
            self.own[chip, rows].astype(jnp.float32) + self.paired[chip, rows].astype(jnp.float32)
        ).astype(jnp.bfloat16)

    def each(self, step):
        def one(piece, carry):
            step(piece)
            return carry

        lax.fori_loop(0, self.pieces, one, 0)

    def send_first(self, chip):
        def step(piece):
            if chip in (0, 1):
                self.add_pair(chip, 0, piece)
                self.x_copy(chip, piece).start()
            if chip in (0, 2):
                self.add_pair(chip, 1, piece)
                self.y_copy(chip // 2, piece).start()

        self.each(step)

    def second_piece(self, piece):
        landed = self.landing(piece)
        self.y_copy(0, piece).wait_recv()
        rows = self.rows(1, piece)
        self.own[1, rows] = (
            self.own[1, rows].astype(jnp.float32)
            + self.paired[1, rows].astype(jnp.float32)
            + self.from_y[0, landed].astype(jnp.float32)
        ).astype(jnp.bfloat16)
        self.x_copy(2, piece).start()
        self.x_copy(0, piece).wait_recv()
        rows = self.rows(0, piece)
        self.own[2, rows] = (
            self.own[2, rows].astype(jnp.float32)
            + self.paired[2, rows].astype(jnp.float32)
            + self.from_x[0, landed].astype(jnp.float32)
        ).astype(jnp.bfloat16)
        self.y_copy(2, piece).start()

    def send_second(self):
        self.each(self.second_piece)

    def last_sum(self, piece):
        landed = self.landing(piece)
        sums = []
        for side in range(2):
            first, second = (self.x_copy(1, piece), self.y_copy(2, piece)) if side == 0 else (self.y_copy(1, piece), self.x_copy(2, piece))
            first.wait_recv()
            second.wait_recv()
            a, b = (self.from_x[1, landed], self.from_y[2, landed]) if side == 0 else (self.from_y[1, landed], self.from_x[2, landed])
            rows = self.rows(side, piece)
            sums.append(
                self.own[3, rows].astype(jnp.float32)
                + self.paired[3, rows].astype(jnp.float32)
                + a.astype(jnp.float32)
                + b.astype(jnp.float32)
            )
        return sums

    def finish(self):
        for chip in range(4):
            self.pair_copy(chip).wait_send()

        def step(piece):
            for kind in range(3):
                self.x_copy(kind, piece).wait_send()
                self.y_copy(kind, piece).wait_send()

        self.each(step)


class Gather:
    def __init__(self, source, target, place, x_sems, y_sems, far_sems, pair_sems, own_sem, pieces):
        self.source, self.target = source, target
        self.place = place
        self.x_sems, self.y_sems, self.far_sems, self.pair_sems, self.own_sem = x_sems, y_sems, far_sems, pair_sems, own_sem
        self.pieces = pieces
        self.rows_each = source.shape[0] // pieces

    @staticmethod
    def semaphores(pieces):
        return [
            pltpu.SemaphoreType.DMA((2, pieces)),
            pltpu.SemaphoreType.DMA((2, pieces)),
            pltpu.SemaphoreType.DMA((2, pieces)),
            pltpu.SemaphoreType.DMA((2, 4, pieces)),
            pltpu.SemaphoreType.DMA,
        ]

    def rows(self, piece):
        return pl.ds(piece * self.rows_each, self.rows_each)

    def own_copy(self):
        return pltpu.make_async_copy(self.source, self.target.at[self.place.here], self.own_sem)

    def x_copy(self, piece):
        rows = self.rows(piece)
        return remote(
            self.source.at[rows], self.target.at[self.place.here, rows],
            self.x_sems.at[0, piece], self.x_sems.at[1, piece], expert=self.place.x_chip,
        )

    def y_copy(self, piece):
        rows = self.rows(piece)
        return remote(
            self.source.at[rows], self.target.at[self.place.here, rows],
            self.y_sems.at[0, piece], self.y_sems.at[1, piece], expert=self.place.y_chip,
        )

    def far_copy(self, piece):
        rows = self.rows(piece)
        came, goes = (
            (self.place.x_chip, self.place.y_chip) if piece % 2 == 0 else (self.place.y_chip, self.place.x_chip)
        )
        return remote(
            self.target.at[came, rows], self.target.at[came, rows],
            self.far_sems.at[0, piece], self.far_sems.at[1, piece], expert=goes,
        )

    def pair_copy(self, kind, piece):
        rows = self.rows(piece)
        block = self.place.block(kind, self.place.core)
        source = self.source.at[rows] if kind == 3 else self.target.at[block, rows]
        return remote(
            source, self.target.at[block, rows],
            self.pair_sems.at[0, kind, piece], self.pair_sems.at[1, kind, piece], expert=self.place.sibling,
        )

    def start_piece(self, piece):
        self.x_copy(piece).start()
        self.y_copy(piece).start()
        self.pair_copy(3, piece).start()

    def start(self):
        self.own_copy().start()
        for piece in range(self.pieces):
            self.start_piece(piece)

    def near(self, piece):
        self.x_copy(piece).wait_recv()
        if piece % 2 == 0:
            self.far_copy(piece).start()
        self.pair_copy(1, piece).start()
        self.y_copy(piece).wait_recv()
        if piece % 2 == 1:
            self.far_copy(piece).start()
        self.pair_copy(2, piece).start()

    def far(self, piece):
        self.far_copy(piece).wait_recv()
        self.pair_copy(0, piece).start()

    def paired(self, kind, piece):
        self.pair_copy(kind, piece).wait_recv()

    def finish(self):
        for piece in range(self.pieces):
            self.x_copy(piece).wait_send()
            self.y_copy(piece).wait_send()
            self.far_copy(piece).wait_send()
            for kind in range(4):
                self.pair_copy(kind, piece).wait_send()


def wide_dot(left, right):
    return jnp.dot(left, right, preferred_element_type=jnp.float32)


def turned_dot(left, right):
    return lax.dot_general(left, right, (((1,), (1,)), ((), ())), preferred_element_type=jnp.float32)


def expert_kernel(
    x_all, g_all, mask, router, bias, w_gate, w_up, w_down,
    reduced, gated_all, gate_all, up_all, mixed_all,
    x_buf, g_buf, part, paired, from_x, from_y, line_in, small, mixed,
    in_sems, out_sems, pair_sems, x_sems, y_sems, line_sems,
):
    experts, width, hidden = w_gate.shape
    rows = x_buf.shape[1]
    tile = min(512, width)
    plane = Plane(part.at[1], part.at[0], paired, from_x, from_y, pair_sems, x_sems, y_sems)
    line = Line(part.at[1, 3], line_in, reduced, line_sems)
    first_expert = lax.axis_index("expert") * experts
    outs = (gated_all, gate_all, up_all)

    def block_of(i):
        return plane.block(i // 2, (plane.core + 1 - i % 2) % 2)

    def fetch(i):
        slot, block = i % 2, block_of(i)
        return (
            pltpu.make_async_copy(x_all.at[block], x_buf.at[slot], in_sems.at[0, slot]),
            pltpu.make_async_copy(g_all.at[block], g_buf.at[slot], in_sems.at[1, slot]),
        )

    def store(i):
        slot, block = i % 2, block_of(i)
        return [
            pltpu.make_async_copy(small.at[slot, n], outs[n].at[block], out_sems.at[n, slot])
            for n in range(3)
        ] + [pltpu.make_async_copy(mixed.at[slot], mixed_all.at[block], out_sems.at[3, slot])]

    def compute(i):
        slot = i % 2
        block = block_of(i)
        x = x_buf.at[slot]
        g = g_buf.at[slot]
        logits = wide_dot(x[...], router[...]) + bias[...]
        weights = jnp.exp(logits - jnp.max(logits, axis=1, keepdims=True))
        gates = weights / jnp.sum(weights, axis=1, keepdims=True) * mask[block]
        column = lax.broadcasted_iota(jnp.int32, (rows, LANE), 1)
        extra = jnp.zeros((rows, LANE), jnp.float32)
        for j in range(experts):
            gate_pre = wide_dot(x[...], w_gate[j])
            up_pre = wide_dot(x[...], w_up[j])
            raw = turned_dot(g[...], w_down[j])
            gate = gates[:, j : j + 1]
            sigma = jax.nn.sigmoid(gate_pre)
            activated = gate_pre * sigma
            inner = activated * up_pre
            act = gate * raw
            span = slice(j * hidden, (j + 1) * hidden)
            small[slot, 0, :, span] = (gate * inner).astype(jnp.bfloat16)
            small[slot, 1, :, span] = (
                act * up_pre * sigma * (1.0 + gate_pre * (1.0 - sigma))
            ).astype(jnp.bfloat16)
            small[slot, 2, :, span] = (act * activated).astype(jnp.bfloat16)
            gain = jnp.sum(raw * inner, axis=1, keepdims=True)
            extra = jnp.where(column == first_expert + j, gain, extra)
        for start in range(0, width, tile):
            columns = slice(start, start + tile)
            slot_grad = None
            mix = None
            for j in range(experts):
                span = slice(j * hidden, (j + 1) * hidden)
                term = turned_dot(small[slot, 1, :, span], w_gate[j, columns]) + turned_dot(
                    small[slot, 2, :, span], w_up[j, columns]
                )
                more = wide_dot(small[slot, 0, :, span], w_down[j, :, columns])
                slot_grad = term if slot_grad is None else slot_grad + term
                mix = more if mix is None else mix + more
            part[i % 2, i // 2, :, columns] = slot_grad.astype(jnp.bfloat16)
            mixed[slot, :, columns] = mix.astype(jnp.bfloat16)
        part[i % 2, i // 2, :, width:] = extra.astype(jnp.bfloat16)

    for copy in fetch(0):
        copy.start()
    greet(plane.neighbours() + line.neighbours())

    def step(i, carry):
        @pl.when(i < 7)
        def _():
            for copy in fetch(i + 1):
                copy.start()

        for copy in fetch(i):
            copy.wait()

        @pl.when(i >= 2)
        def _():
            for copy in store(i - 2):
                copy.wait()

        compute(i)
        for copy in store(i):
            copy.start()

        @pl.when(i % 2 == 0)
        def _():
            plane.pair_copy(i // 2).start()

        @pl.when(i % 2 == 1)
        def _():
            plane.pair_copy(i // 2).wait_recv()

        for chip in range(3):

            @pl.when(i == 2 * chip + 1)
            def _():
                plane.send_first(chip)
                if chip == 2:
                    plane.send_second()

        return carry

    lax.fori_loop(0, 8, step, 0)

    def last(step, carry):
        @pl.when(step < plane.pieces)
        def _():
            for side, total in enumerate(plane.last_sum(step)):
                plane.own[3, plane.rows(side, step)] = total.astype(jnp.bfloat16)

        line.advance(step)
        return carry

    lax.fori_loop(0, line.steps(), last, 0)
    for i in (6, 7):
        for copy in store(i):
            copy.wait()
    plane.finish()
    line.finish()


def experts_fused(arrived, arrived_grad, mask, router, bias, w_gate, w_up, w_down):
    ranks, rows, width = arrived.shape
    experts, _, hidden = w_gate.shape
    wide = width + LANE
    inner = experts * hidden
    half = rows // 2
    low = jnp.bfloat16
    any_space = pl.BlockSpec(memory_space=pl.ANY)
    vmem = pl.BlockSpec(memory_space=pltpu.VMEM)
    small_shape = jax.ShapeDtypeStruct((ranks, rows, inner), low)
    return pl.pallas_call(
        expert_kernel,
        out_shape=(
            jax.ShapeDtypeStruct((rows, wide), low), small_shape, small_shape, small_shape,
            jax.ShapeDtypeStruct((ranks, rows, width), low),
        ),
        in_specs=[any_space, any_space] + [vmem] * 6,
        out_specs=(vmem, any_space, any_space, any_space, any_space),
        scratch_shapes=[
            pltpu.VMEM((2, rows, width), low),
            pltpu.VMEM((2, rows, width), low),
            pltpu.VMEM((2, 4, rows, wide), low),
            pltpu.VMEM((4, rows, wide), low),
            pltpu.VMEM((3, half, wide), low),
            pltpu.VMEM((3, half, wide), low),
            pltpu.VMEM((rows, wide), low),
            pltpu.VMEM((2, 3, rows, inner), low),
            pltpu.VMEM((2, rows, width), low),
            pltpu.SemaphoreType.DMA((2, 2)),
            pltpu.SemaphoreType.DMA((4, 2)),
            *Plane.semaphores(rows),
            Line.semaphores(rows),
        ],
        compiler_params=pltpu.CompilerParams(
            collective_id=0, has_side_effects=True, vmem_limit_bytes=61 * 2**20
        ),
        cost_estimate=pl.CostEstimate(
            flops=12 * ranks * rows * width * inner, bytes_accessed=8 * ranks * rows * width, transcendentals=0
        ),
    )(arrived, arrived_grad, mask, router, bias, w_gate, w_up, w_down)


def crossed_dot(left, right):
    return lax.dot_general(left, right, (((0,), (0,)), ((), ())), preferred_element_type=jnp.float32)


def closing_kernel(
    normed, query_grad, key_grad, value_grad, attended, attention_grad, extras,
    w_query, w_key, w_value, mixed, x_all, g_all, gated_all, gate_all, up_all,
    total, sums, gain, mixture, gate_out, up_out, down_out,
    line_own, line_in, part, paired, from_x, from_y,
    mix_own, mix_paired, mix_x, mix_y, mix_in, tiles, factors, results, downs,
    line_sems, pair_sems, x_sems, y_sems, mix_line_sems, mix_pair_sems, mix_x_sems, mix_y_sems,
    load_sems, weight_sems, factor_sems, tile_sems, out_sems,
    gains, mine, theirs, peer_sent, peer_got,
    *,
    gain_column,
):
    width = normed.shape[1]
    heads = query_grad.shape[1]
    share = part.shape[2]
    experts, _, hidden = gate_out.shape
    column_tile = min(512, width // 2)
    tile = tiles.shape[2]
    count = width // tile
    line = Line(line_own, line_in, total, line_sems)
    plane = Plane(part.at[1], part.at[0], paired, from_x, from_y, pair_sems, x_sems, y_sems)
    mix = Plane(mix_own, mixed, mix_paired, mix_x, mix_y, mix_pair_sems, mix_x_sems, mix_y_sems, by_device=True)
    mix_line = Line(mix_own.at[3], mix_in, mixture, mix_line_sems)
    peers = Peers(mine, theirs, peer_sent, peer_got)
    half = width // 2

    def load_own(chip):
        return pltpu.make_async_copy(mixed.at[mix.block(chip, mix.core)], mix_own.at[chip], load_sems.at[chip])

    weight_loads = [
        pltpu.make_async_copy(w_query, factors.at[0, 0:width], weight_sems.at[0]),
        pltpu.make_async_copy(w_key, factors.at[1, 0:width], weight_sems.at[1]),
        pltpu.make_async_copy(w_value.at[0:half], factors.at[0, width : width + half], weight_sems.at[2]),
        pltpu.make_async_copy(w_value.at[half:], factors.at[1, width : width + half], weight_sems.at[3]),
    ]

    def factor_load(matrix):
        return pltpu.make_async_copy(
            (gate_all, up_all, gated_all)[matrix], factors.at[matrix % 2], factor_sems.at[matrix]
        )

    def tile_copy(source, s):
        columns = pl.ds(pl.multiple_of(s % count * tile, tile), tile)
        return pltpu.make_async_copy(source.at[:, columns], tiles.at[s % 2], tile_sems.at[s % 2])

    def start_tile(s):
        @pl.when(s < 2 * count)
        def _():
            tile_copy(x_all, s).start()

        @pl.when(s >= 2 * count)
        def _():
            tile_copy(g_all, s).start()

    def across(target, s):
        rows = pl.ds(pl.multiple_of(s % count * tile, tile), tile)
        return [
            pltpu.make_async_copy(
                results.at[s % 2, :, j * hidden : (j + 1) * hidden], target.at[j, rows], out_sems.at[0, s % 2, j]
            )
            for j in range(experts)
        ]

    def down(s):
        columns = pl.ds(pl.multiple_of(s % count * tile, tile), tile)
        return [
            pltpu.make_async_copy(
                downs.at[s % 2, j * hidden : (j + 1) * hidden], down_out.at[j, :, columns], out_sems.at[1, s % 2, j]
            )
            for j in range(experts)
        ]

    def expert_tile(s):
        @pl.when(s + 1 < 3 * count)
        def _():
            start_tile(s + 1)

        for matrix in range(3):

            @pl.when(s == matrix * count)
            def _():
                factor_load(matrix).wait()

        tile_copy(x_all, s).wait()

        @pl.when(s < 2 * count)
        def _():
            @pl.when(s >= 2)
            def _():
                for copy in across(gate_out, s):
                    copy.wait()

            results[s % 2] = crossed_dot(tiles[s % 2], factors[s // count])

            @pl.when(s < count)
            def _():
                for copy in across(gate_out, s):
                    copy.start()

            @pl.when(s >= count)
            def _():
                for copy in across(up_out, s):
                    copy.start()

        @pl.when(s >= 2 * count)
        def _():
            @pl.when(s >= 2 * count + 2)
            def _():
                for copy in down(s):
                    copy.wait()

            downs[s % 2] = crossed_dot(factors[0], tiles[s % 2])
            for copy in down(s):
                copy.start()

        @pl.when(s == count - 1)
        def _():
            factor_load(2).start()

    def dense_block(i):
        chip, sub = i // 2, i % 2
        block = plane.block(chip, (plane.core + 1 - sub) % 2)
        columns = pl.ds(pl.multiple_of(block * share, share), share)
        source = normed[:, columns]
        part[sub, chip, :, 0:heads] = crossed_dot(source, query_grad[...]).astype(jnp.bfloat16)
        part[sub, chip, :, heads : 2 * heads] = crossed_dot(source, key_grad[...]).astype(jnp.bfloat16)
        part[sub, chip, :, 2 * heads : 3 * heads] = crossed_dot(source, value_grad[...]).astype(jnp.bfloat16)
        part[sub, chip, :, 3 * heads : 4 * heads] = crossed_dot(
            attention_grad[:, columns], attended[...]
        ).astype(jnp.bfloat16)
        part[sub, chip, :, 4 * heads :] = extras[block] + gains[columns]

        @pl.when(sub == 0)
        def _():
            plane.pair_copy(chip).start()

    for copy in weight_loads:
        copy.start()
    for chip in range(4):
        load_own(chip).start()
    greet(plane.neighbours() + peers.neighbours())
    for chip in range(4):
        mix.pair_copy(chip).start()
    for copy in weight_loads:
        copy.wait()
    for start in range(0, width, column_tile):
        columns = slice(start, start + column_tile)
        later = width + start % half
        line_own[:, columns] = (
            turned_dot(query_grad[...], factors[0, columns])
            + turned_dot(key_grad[...], factors[1, columns])
            + turned_dot(value_grad[...], factors[start // half, later : later + column_tile])
        ).astype(jnp.bfloat16)
    place = lax.broadcasted_iota(jnp.int32, (normed.shape[0], LANE), 1)
    chosen = jnp.where(place == gain_column, 1.0, 0.0).astype(jnp.bfloat16)
    for start in range(0, width, column_tile):
        columns = slice(start, start + column_tile)
        pull = line_own[:, columns].astype(jnp.float32) * normed[:, columns].astype(jnp.float32)
        gains[columns] = crossed_dot(pull.astype(jnp.bfloat16), chosen).astype(jnp.bfloat16)
    factor_load(0).start()
    factor_load(1).start()
    start_tile(0)
    mix_last = mix.pieces + 1
    dense_first = 8 + 5
    dense_second = dense_first + plane.pieces // 2 + 2
    dense_last = dense_second + plane.pieces // 2 + 1

    def step(s, carry):
        line.advance(s)
        for chip in range(4):

            @pl.when(s == chip)
            def _():
                load_own(chip).wait()
                mix.pair_copy(chip).wait_recv()
                if chip < 3:
                    mix.send_first(chip)

        @pl.when((s >= 3) & (s - 3 < mix.pieces))
        def _():
            mix.second_piece(s - 3)

        @pl.when((s >= mix_last) & (s - mix_last < mix.pieces))
        def _():
            piece = s - mix_last
            for side, summed in enumerate(mix.last_sum(piece)):
                mix_own[3, mix.rows(side, piece)] = summed.astype(jnp.bfloat16)

        mix_line.advance(s - mix_last)

        @pl.when((s >= 4) & (s < 12))
        def _():
            dense_block(s - 4)

        @pl.when(s == dense_first)
        def _():
            for chip in range(4):
                plane.pair_copy(chip).wait_recv()
            for chip in range(3):
                plane.send_first(chip)

        @pl.when((s >= dense_second) & (s - dense_second < plane.pieces))
        def _():
            plane.second_piece(s - dense_second)

        @pl.when((s >= dense_last) & (s - dense_last < plane.pieces))
        def _():
            piece = s - dense_last
            for side, summed in enumerate(plane.last_sum(piece)):
                sums[plane.rows(side, piece)] = summed

        @pl.when(s < 3 * count)
        def _():
            expert_tile(s)

        return carry

    steps = jnp.maximum(mix_last + mix_line.steps(), jnp.maximum(3 * count, dense_last + plane.pieces))
    lax.fori_loop(0, steps, step, 0)
    column = 4 * heads + gain_column
    mine[...] = to_rows([sums[:, column : column + 1]], share)
    peers.start()
    for s in (2 * count - 2, 2 * count - 1):
        for copy in across(up_out, s):
            copy.wait()
    for s in (3 * count - 2, 3 * count - 1):
        for copy in down(s):
            copy.wait()
    gain[...] = peers.total()
    for each in (plane, line, mix, mix_line, peers):
        each.finish()


TILE = 256


def closing(
    normed, query_grad, key_grad, value_grad, attended, attention_grad, extras, w_query, w_key, w_value,
    mixed, arrived, arrived_grad, gated, gate_grad, up_grad, experts, gain_column,
):
    rows, width = normed.shape
    heads = query_grad.shape[1]
    ranks, share, more = extras.shape
    wide = 4 * heads + more
    inner = gated.shape[2]
    hidden = inner // experts
    low = jnp.bfloat16
    tile = min(TILE, width // 2)
    vmem = pl.BlockSpec(memory_space=pltpu.VMEM)
    any_space = pl.BlockSpec(memory_space=pl.ANY)
    every = ranks * rows
    size = lax.axis_size("tensor")
    return pl.pallas_call(
        functools.partial(closing_kernel, gain_column=gain_column),
        out_shape=(
            jax.ShapeDtypeStruct((rows, width), low),
            jax.ShapeDtypeStruct((share, wide), jnp.float32),
            jax.ShapeDtypeStruct((8, share), jnp.float32),
            jax.ShapeDtypeStruct((rows, width), low),
            jax.ShapeDtypeStruct((experts, width, hidden), jnp.float32),
            jax.ShapeDtypeStruct((experts, width, hidden), jnp.float32),
            jax.ShapeDtypeStruct((experts, hidden, width), jnp.float32),
        ),
        in_specs=[vmem] * 7 + [any_space] * 9,
        out_specs=(vmem,) * 4 + (any_space,) * 3,
        scratch_shapes=[
            pltpu.VMEM((rows, width), low),
            pltpu.VMEM((rows, width), low),
            pltpu.VMEM((2, 4, share, wide), low),
            pltpu.VMEM((4, share, wide), low),
            pltpu.VMEM((3, share // 2, wide), low),
            pltpu.VMEM((3, share // 2, wide), low),
            pltpu.VMEM((4, rows, width), low),
            pltpu.VMEM((4, rows, width), low),
            pltpu.VMEM((3, rows // 2, width), low),
            pltpu.VMEM((3, rows // 2, width), low),
            pltpu.VMEM((rows, width), low),
            pltpu.VMEM((2, every, tile), low),
            pltpu.VMEM((2, every, inner), low),
            pltpu.VMEM((2, tile, inner), jnp.float32),
            pltpu.VMEM((2, inner, tile), jnp.float32),
            Line.semaphores(rows),
            *Plane.semaphores(share),
            Line.semaphores(rows),
            *Plane.semaphores(rows),
            pltpu.SemaphoreType.DMA((4,)),
            pltpu.SemaphoreType.DMA((4,)),
            pltpu.SemaphoreType.DMA((3,)),
            pltpu.SemaphoreType.DMA((2,)),
            pltpu.SemaphoreType.DMA((2, 2, experts)),
            pltpu.VMEM((width, LANE), low),
            pltpu.VMEM((8, share), jnp.float32),
            pltpu.VMEM((size - 1, 8, share), jnp.float32),
            pltpu.SemaphoreType.DMA((size - 1,)),
            pltpu.SemaphoreType.DMA((size - 1,)),
        ],
        compiler_params=pltpu.CompilerParams(
            collective_id=2, has_side_effects=True, vmem_limit_bytes=63 * 2**20
        ),
    )(
        normed, query_grad, key_grad, value_grad, attended, attention_grad, extras, w_query, w_key, w_value,
        mixed, arrived.reshape(every, width), arrived_grad.reshape(every, width),
        gated.reshape(every, inner), gate_grad.reshape(every, inner), up_grad.reshape(every, inner),
    )


class Peers:
    def __init__(self, mine, theirs, sent, got):
        self.mine, self.theirs, self.sent, self.got = mine, theirs, sent, got
        self.size = lax.axis_size("tensor")
        self.here = lax.axis_index("tensor")

    def neighbours(self):
        return [(None, {"tensor": (self.here + d) % self.size}) for d in range(1, self.size)]

    def copies(self):
        return [
            remote(
                self.mine, self.theirs.at[d - 1], self.sent.at[d - 1], self.got.at[d - 1],
                tensor=(self.here + d) % self.size,
            )
            for d in range(1, self.size)
        ]

    def start(self):
        for copy in self.copies():
            copy.start()

    def total(self):
        result = self.mine[...]
        for d, copy in enumerate(self.copies()):
            copy.wait_recv()
            result = result + self.theirs[d]
        return result

    def finish(self):
        for copy in self.copies():
            copy.wait_send()


def to_rows(columns, rows):
    lane = lax.broadcasted_iota(jnp.int32, (rows, LANE), 1)
    field = jnp.zeros((rows, LANE), jnp.float32)
    for i, column in enumerate(columns):
        field = jnp.where(lane == i, column, field)
    return field.T[:8]


def to_columns(sums):
    padded = jnp.concatenate([sums, jnp.zeros((LANE - 8, sums.shape[1]), jnp.float32)], axis=0)
    return padded.T


def swapped(field):
    half = HD // 2
    return jnp.concatenate([field[:, half:], field[:, :half]], axis=1)


SPREAD = 32
SPREAD_LAG = 2


def front_kernel(
    tokens, attn_gain, ffn_gain, w_query, w_key, w_value, w_out, qk_gain, cosine, sine, bias, routes,
    total, normed, normed_two, attended, query_rot, keys_values, query_raw, key_raw, stats, routes_all, arrived,
    line_own, line_in, prompt, mine, theirs, two,
    line_sems, peer_sent, peer_got, *gather_sems,
):
    rows, width = tokens.shape
    local = w_query.shape[1]
    heads = local // HD
    factor = HD ** (-0.5)
    own_blocks = rows // PROMPT_DEV - 1
    devices = keys_values.shape[0] - own_blocks
    place = Place()
    line = Line(line_own, line_in, total, line_sems)
    peers = Peers(mine, theirs, peer_sent, peer_got)
    names = Gather(routes, routes_all, place, *gather_sems[0:5], pieces=2)
    prompts = Gather(prompt, keys_values, place, *gather_sems[5:10], pieces=2)
    spread = Gather(normed_two, arrived, place, *gather_sems[10:15], pieces=rows // SPREAD)
    greet(place.neighbours() + peers.neighbours())
    names.start()
    source = tokens[...].astype(jnp.float32)
    scale_one = lax.rsqrt(jnp.sum(source * source, axis=1, keepdims=True) / width + epsilon)
    normed[...] = (source * scale_one * attn_gain[...]).astype(jnp.bfloat16)
    query_raw[...] = wide_dot(normed[...], w_query[...])
    key_raw[...] = wide_dot(normed[...], w_key[...])
    mine[...] = to_rows(
        [
            jnp.sum(query_raw[...] * query_raw[...], axis=1, keepdims=True),
            jnp.sum(key_raw[...] * key_raw[...], axis=1, keepdims=True),
        ],
        rows,
    )
    peers.start()
    value = wide_dot(normed[...], w_value[...]).astype(jnp.bfloat16)
    prompt[:, local:] = value[:PROMPT_DEV]
    for i in range(own_blocks):
        keys_values[devices + i, :, local:] = value[(i + 1) * PROMPT_DEV : (i + 2) * PROMPT_DEV]
    squares = to_columns(peers.total())
    scale_query = lax.rsqrt(squares[:, 0:1] / width + epsilon)
    scale_key = lax.rsqrt(squares[:, 1:2] / width + epsilon)
    for head in range(heads):
        columns = slice(head * HD, (head + 1) * HD)
        turned = key_raw[:, columns] * scale_key * qk_gain[1:2, columns]
        turned = (turned * cosine[...] + swapped(turned) * sine[...]).astype(jnp.bfloat16)
        prompt[:, columns] = turned[:PROMPT_DEV]
        for i in range(own_blocks):
            keys_values[devices + i, :, columns] = turned[(i + 1) * PROMPT_DEV : (i + 2) * PROMPT_DEV]
    prompts.own_copy().start()
    for piece in range(2):
        prompts.start_piece(piece)
    for head in range(heads):
        columns = slice(head * HD, (head + 1) * HD)
        turned = query_raw[:, columns] * scale_query * qk_gain[0:1, columns]
        turned = turned * cosine[...] + swapped(turned) * sine[...]
        query_rot[:, columns] = turned.astype(jnp.bfloat16)
    for piece in range(2):
        prompts.near(piece)
    for piece in range(2):
        names.near(piece)
    for piece in range(2):
        prompts.far(piece)
        names.far(piece)
    prompts.own_copy().wait()
    for kind in range(4):
        for piece in range(2):
            prompts.paired(kind, piece)
            names.paired(kind, piece)
    lane = lax.broadcasted_iota(jnp.int32, (rows, LANE), 1)
    kept = jnp.where(lane == 0, scale_one, 0.0)
    kept = jnp.where(lane == 1, scale_query, kept)
    kept = jnp.where(lane == 2, scale_key, kept)
    count = keys_values.shape[0] * PROMPT_DEV
    for head in range(heads):
        columns = slice(head * HD, (head + 1) * HD)
        keys = keys_values[:, :, columns].reshape(count, HD)
        values = keys_values[:, :, local + head * HD : local + (head + 1) * HD].reshape(count, HD)
        scores = turned_dot(query_rot[:, columns], keys) * factor + bias[...]
        top = jnp.max(scores, axis=1, keepdims=True)
        weights = jnp.exp(scores - top)
        whole = jnp.sum(weights, axis=1, keepdims=True)
        shares = (weights / whole).astype(jnp.bfloat16)
        attended[:, columns] = wide_dot(shares, values).astype(jnp.bfloat16)
        kept = jnp.where(lane == 8 + head, top + jnp.log(whole), kept)
    tile = min(512, width)
    for start in range(0, width, tile):
        columns = slice(start, start + tile)
        line_own[:, columns] = wide_dot(attended[...], w_out[:, columns]).astype(jnp.bfloat16)
    steps = line.pieces + 2 * (line.size - 1)
    ratio = SPREAD // STEP
    groups = line.pieces // ratio

    def norm_rows(piece):
        span = slice(piece * SPREAD, (piece + 1) * SPREAD)
        hidden = tokens[span].astype(jnp.float32) + total[span].astype(jnp.float32)
        scale = lax.rsqrt(jnp.sum(hidden * hidden, axis=1, keepdims=True) / width + epsilon)
        normed_two[span] = (hidden * scale * ffn_gain[...]).astype(jnp.bfloat16)
        two[span] = jnp.broadcast_to(scale, (SPREAD, LANE))

    done = 0
    passed = 0
    for group in range(groups):
        ready = 2 * (line.size - 1) + (group + 1) * ratio
        lax.fori_loop(done, ready, line.step_body, 0)
        done = ready
        for piece in (group, groups + group):
            norm_rows(piece)
            spread.start_piece(piece)
        if group >= SPREAD_LAG:
            for piece in (passed, groups + passed):
                spread.near(piece)
            passed += 1
    spread.own_copy().start()
    for group in range(passed, groups):
        for piece in (group, groups + group):
            spread.near(piece)
    for group in range(groups):
        for piece in (group, groups + group):
            spread.far(piece)
    stats[...] = jnp.where(lane == 3, two[...], kept)
    for kind in range(4):
        for piece in range(spread.pieces):
            spread.paired(kind, piece)
    spread.own_copy().wait()
    names.own_copy().wait()
    for each in (names, prompts, spread, line, peers):
        each.finish()


def front(tokens, attn_gain, ffn_gain, w_query, w_key, w_value, w_out, qk_gain, cosine, sine, bias, routes):
    rows, width = tokens.shape
    local = w_query.shape[1]
    ranks = lax.axis_size("expert")
    size = lax.axis_size("tensor")
    low, full = jnp.bfloat16, jnp.float32
    vmem = pl.BlockSpec(memory_space=pltpu.VMEM)
    blocks = ranks + rows // PROMPT_DEV - 1
    return pl.pallas_call(
        front_kernel,
        out_shape=(
            jax.ShapeDtypeStruct((rows, width), low),
            jax.ShapeDtypeStruct((rows, width), low),
            jax.ShapeDtypeStruct((rows, width), low),
            jax.ShapeDtypeStruct((rows, local), low),
            jax.ShapeDtypeStruct((rows, local), low),
            jax.ShapeDtypeStruct((blocks, PROMPT_DEV, 2 * local), low),
            jax.ShapeDtypeStruct((rows, local), full),
            jax.ShapeDtypeStruct((rows, local), full),
            jax.ShapeDtypeStruct((rows, LANE), full),
            jax.ShapeDtypeStruct((ranks,) + routes.shape, jnp.int32),
            jax.ShapeDtypeStruct((ranks, rows, width), low),
        ),
        in_specs=[vmem] * 12,
        out_specs=(vmem,) * 10 + (pl.BlockSpec(memory_space=pl.ANY),),
        scratch_shapes=[
            pltpu.VMEM((rows, width), low),
            pltpu.VMEM((rows, width), low),
            pltpu.VMEM((PROMPT_DEV, 2 * local), low),
            pltpu.VMEM((8, rows), full),
            pltpu.VMEM((size - 1, 8, rows), full),
            pltpu.VMEM((rows, LANE), full),
            Line.semaphores(rows),
            pltpu.SemaphoreType.DMA((size - 1,)),
            pltpu.SemaphoreType.DMA((size - 1,)),
            *Gather.semaphores(2),
            *Gather.semaphores(2),
            *Gather.semaphores(rows // SPREAD),
        ],
        compiler_params=pltpu.CompilerParams(
            collective_id=1, has_side_effects=True, vmem_limit_bytes=60 * 2**20
        ),
        cost_estimate=pl.CostEstimate(flops=100 * 10**9, bytes_accessed=200 * 10**6, transcendentals=0),
    )(tokens, attn_gain, ffn_gain, w_query, w_key, w_value, w_out, qk_gain, cosine, sine, bias, routes)


def backward_kernel(
    attention_grad, w_out, query_rot, keys_values, bias, stats, query_raw, key_raw, cosine, sine, qk_gain,
    query_out, key_out, value_out, gain_out,
    out_grad, query_grad, prompt_grads, own_grads, own, paired, from_x, from_y, mine, theirs,
    pair_sems, x_sems, y_sems, peer_sent, peer_got,
):
    rows, local = query_rot.shape
    width = attention_grad.shape[1]
    heads = local // HD
    factor = HD ** (-0.5)
    own_blocks = rows // PROMPT_DEV - 1
    devices = keys_values.shape[0] - own_blocks
    count = keys_values.shape[0] * PROMPT_DEV
    reach = devices * PROMPT_DEV
    plane = Plane(own, prompt_grads, paired, from_x, from_y, pair_sems, x_sems, y_sems, by_device=True)
    peers = Peers(mine, theirs, peer_sent, peer_got)
    greet(plane.neighbours() + peers.neighbours())
    out_grad[...] = turned_dot(attention_grad[...], w_out[...]).astype(jnp.bfloat16)
    for head in range(heads):
        columns = slice(head * HD, (head + 1) * HD)
        other = slice(local + head * HD, local + (head + 1) * HD)
        keys = keys_values[:, :, columns].reshape(count, HD)
        values = keys_values[:, :, other].reshape(count, HD)
        query, above = query_rot[:, columns], out_grad[:, columns]
        scores = turned_dot(query, keys) * factor + bias[...]
        shares = jnp.exp(scores - stats[:, 8 + head : 9 + head])
        share_grad = turned_dot(above, values)
        delta = jnp.sum(shares * share_grad, axis=1, keepdims=True)
        score_grad = (shares * (share_grad - delta)).astype(jnp.bfloat16)
        query_grad[:, columns] = wide_dot(score_grad, keys) * factor
        key_grad = crossed_dot(score_grad, query) * factor
        value_grad = crossed_dot(shares.astype(jnp.bfloat16), above)
        prompt_grads[:, :, columns] = key_grad[:reach].astype(jnp.bfloat16).reshape(devices, PROMPT_DEV, HD)
        prompt_grads[:, :, other] = value_grad[:reach].astype(jnp.bfloat16).reshape(devices, PROMPT_DEV, HD)
        own_grads[PROMPT_DEV:, columns] = key_grad[reach:]
        own_grads[PROMPT_DEV:, other] = value_grad[reach:]
    for chip in range(4):
        plane.pair_copy(chip).start()
    for chip in range(4):
        own[chip] = prompt_grads[plane.block(chip, plane.core)]
    for chip in range(4):
        plane.pair_copy(chip).wait_recv()
        if chip < 3:
            plane.send_first(chip)

    def normed_part(source, raw, row, scale):
        inner = jnp.zeros((rows, 1), jnp.float32)
        for head in range(heads):
            columns = slice(head * HD, (head + 1) * HD)
            grad = source[:, columns]
            grad = grad * cosine[...] - swapped(grad) * sine[...]
            gain_out[row : row + 1, columns] = jnp.sum(grad * raw[:, columns] * scale, axis=0, keepdims=True)
            grad = qk_gain[row : row + 1, columns] * grad
            source[:, columns] = grad
            inner = inner + jnp.sum(grad * raw[:, columns], axis=1, keepdims=True)
        return inner

    scale_query, scale_key = stats[:, 1:2], stats[:, 2:3]
    query_inner = normed_part(query_grad, query_raw, 0, scale_query)
    plane.send_second()

    def last(piece, carry):
        for side, summed in enumerate(plane.last_sum(piece)):
            own_grads[plane.rows(side, piece)] = summed
        return carry

    lax.fori_loop(0, plane.pieces, last, 0)
    key_inner = normed_part(own_grads, key_raw, 1, scale_key)
    mine[...] = to_rows([query_inner, key_inner], rows)
    peers.start()
    value_out[...] = own_grads[:, local:].astype(jnp.bfloat16)
    inner = to_columns(peers.total())
    for out, source, raw, scale, i in (
        (query_out, query_grad, query_raw, scale_query, 0),
        (key_out, own_grads, key_raw, scale_key, 1),
    ):
        pull = scale * scale * scale / width * inner[:, i : i + 1]
        out[...] = (scale * source[:, :local] - raw[...] * pull).astype(jnp.bfloat16)
    plane.finish()
    peers.finish()


def backward(attention_grad, w_out, query_rot, keys_values, bias, stats, query_raw, key_raw, cosine, sine, qk_gain):
    rows, local = query_rot.shape
    size = lax.axis_size("tensor")
    ranks = lax.axis_size("expert")
    low, full = jnp.bfloat16, jnp.float32
    vmem = pl.BlockSpec(memory_space=pltpu.VMEM)
    small = jax.ShapeDtypeStruct((rows, local), low)
    return pl.pallas_call(
        backward_kernel,
        out_shape=(small, small, small, jax.ShapeDtypeStruct((2, local), full)),
        in_specs=[vmem] * 11,
        out_specs=(vmem,) * 4,
        scratch_shapes=[
            pltpu.VMEM((rows, local), low),
            pltpu.VMEM((rows, local), full),
            pltpu.VMEM((ranks, PROMPT_DEV, 2 * local), low),
            pltpu.VMEM((rows, 2 * local), full),
            pltpu.VMEM((4, PROMPT_DEV, 2 * local), low),
            pltpu.VMEM((4, PROMPT_DEV, 2 * local), low),
            pltpu.VMEM((3, PROMPT_DEV // 2, 2 * local), low),
            pltpu.VMEM((3, PROMPT_DEV // 2, 2 * local), low),
            pltpu.VMEM((8, rows), full),
            pltpu.VMEM((size - 1, 8, rows), full),
            *Plane.semaphores(PROMPT_DEV),
            pltpu.SemaphoreType.DMA((size - 1,)),
            pltpu.SemaphoreType.DMA((size - 1,)),
        ],
        compiler_params=pltpu.CompilerParams(
            collective_id=3, has_side_effects=True, vmem_limit_bytes=60 * 2**20
        ),
    )(attention_grad, w_out, query_rot, keys_values, bias, stats, query_raw, key_raw, cosine, sine, qk_gain)


def rotate(field, cosine, sine):
    half = field.shape[-1] // 2
    first = field[..., :half]
    second = field[..., half:]
    return jnp.concatenate(
        [first * cosine - second * sine, second * cosine + first * sine], axis=-1
    )


def unrotate(grad, cosine, sine):
    half = grad.shape[-1] // 2
    first = grad[..., :half]
    second = grad[..., half:]
    return jnp.concatenate(
        [first * cosine + second * sine, second * cosine - first * sine], axis=-1
    )


def experts(normed_two, cotangent, gates, w_gate, w_up, w_down, experts_total):
    local_experts = w_gate.shape[0]
    device = lax.axis_index("expert")
    arrived = lax.all_gather(normed_two, "expert", axis=0, tiled=True)
    arrived_grad = lax.all_gather(cotangent, "expert", axis=0, tiled=True)
    gate_pre = jnp.einsum("rd,jdf->jrf", arrived, w_gate, preferred_element_type=jnp.float32)
    up_pre = jnp.einsum("rd,jdf->jrf", arrived, w_up, preferred_element_type=jnp.float32)
    raw_grad = jnp.einsum("rd,jfd->jrf", arrived_grad, w_down, preferred_element_type=jnp.float32)
    sigma = jax.nn.sigmoid(gate_pre)
    activated = gate_pre * sigma
    inner = activated * up_pre
    gated = (gates[:, :, None] * inner).astype(jnp.bfloat16)
    mixed_part = jnp.einsum("jrf,jfd->rd", gated, w_down, preferred_element_type=jnp.float32)
    mixture = lax.psum(
        lax.psum_scatter(
            mixed_part.astype(jnp.bfloat16), "expert", scatter_dimension=0, tiled=True
        ),
        "tensor",
    ).astype(jnp.float32)
    gate_grad_part = jnp.sum(raw_grad * inner, axis=2)
    act_grad = gates[:, :, None] * raw_grad
    up_grad = (act_grad * activated).astype(jnp.bfloat16)
    gate_grad = (act_grad * up_pre * sigma * (1.0 + gate_pre * (1.0 - sigma))).astype(jnp.bfloat16)
    grad_w_down = jnp.einsum("jrf,rd->jfd", gated, arrived_grad, preferred_element_type=jnp.float32)
    grad_w_gate = jnp.einsum("rd,jrf->jdf", arrived, gate_grad, preferred_element_type=jnp.float32)
    grad_w_up = jnp.einsum("rd,jrf->jdf", arrived, up_grad, preferred_element_type=jnp.float32)
    slot_grad = jnp.einsum("jrf,jdf->rd", gate_grad, w_gate, preferred_element_type=jnp.float32)
    slot_grad = slot_grad + jnp.einsum(
        "jrf,jdf->rd", up_grad, w_up, preferred_element_type=jnp.float32
    )
    moe_input_grad = lax.psum(
        lax.psum_scatter(
            slot_grad.astype(jnp.bfloat16), "expert", scatter_dimension=0, tiled=True
        ),
        "tensor",
    ).astype(jnp.float32)
    placed = jnp.zeros((arrived.shape[0], experts_total), jnp.float32)
    placed = lax.dynamic_update_slice_in_dim(placed, gate_grad_part.T, device * local_experts, 1)
    chance_grad = lax.psum(
        lax.psum_scatter(placed, "expert", scatter_dimension=0, tiled=True), "tensor"
    )
    return mixture, moe_input_grad, chance_grad, [grad_w_gate, grad_w_up, grad_w_down]


def body(
    tokens,
    w_query,
    w_key,
    w_value,
    w_out,
    attn_gain,
    ffn_gain,
    qk_gain,
    router,
    w_gate,
    w_up,
    w_down,
    routes,
    cont_group,
    cotangent,
):
    rows, width = tokens.shape
    local_width = w_query.shape[1]
    head_count = local_width // HD
    experts_total = router.shape[1]
    local_experts = w_gate.shape[0]
    ranks = lax.axis_size("expert")
    device = lax.axis_index("expert")
    span = ranks // 2
    prompt_len = PROMPT_DEV * span
    factor = HD ** (-0.5)
    local = jnp.arange(rows, dtype=jnp.int32)
    is_prompt = local < PROMPT_DEV
    after = jnp.maximum(local - PROMPT_DEV, 0)
    slot_cont = after // CLEN
    cont_pick = jnp.sum(
        jnp.where(
            slot_cont[:, None] == jnp.arange(CONT_DEV, dtype=jnp.int32)[None, :],
            cont_group[None, :],
            0,
        ),
        axis=1,
    )
    group = jnp.where(is_prompt, device // span, cont_pick)
    position = jnp.where(is_prompt, device % span * PROMPT_DEV + local, prompt_len + after % CLEN)
    tag = jnp.where(is_prompt, -1, slot_cont)
    frequency = 10000.0 ** (-jnp.arange(HD // 2, dtype=jnp.float32) * 2.0 / HD)
    angle = position.astype(jnp.float32)[:, None] * frequency[None, :]
    cosine = jnp.cos(angle)[:, None, :]
    sine = jnp.sin(angle)[:, None, :]
    source = tokens.astype(jnp.float32)
    scale_one = lax.rsqrt(jnp.mean(source * source, axis=1, keepdims=True) + epsilon)
    normed = (source * scale_one * attn_gain).astype(jnp.bfloat16)
    query_raw = jnp.dot(normed, w_query, preferred_element_type=jnp.float32)
    key_raw = jnp.dot(normed, w_key, preferred_element_type=jnp.float32)
    value_raw = jnp.dot(normed, w_value, preferred_element_type=jnp.float32)
    squares = lax.psum(
        jnp.stack(
            [jnp.sum(query_raw * query_raw, axis=1), jnp.sum(key_raw * key_raw, axis=1)], axis=1
        ),
        "tensor",
    )
    scale_query = lax.rsqrt(squares[:, 0:1] / width + epsilon)
    scale_key = lax.rsqrt(squares[:, 1:2] / width + epsilon)
    query_rot = (
        rotate((query_raw * scale_query * qk_gain[0]).reshape(rows, head_count, HD), cosine, sine)
        .reshape(rows, local_width)
        .astype(jnp.bfloat16)
    )
    key_rot = (
        rotate((key_raw * scale_key * qk_gain[1]).reshape(rows, head_count, HD), cosine, sine)
        .reshape(rows, local_width)
        .astype(jnp.bfloat16)
    )
    value_low = value_raw.astype(jnp.bfloat16)
    prompt_keys, prompt_values = (
        lax.all_gather(key_rot[:PROMPT_DEV], "expert", axis=0, tiled=True),
        lax.all_gather(value_low[:PROMPT_DEV], "expert", axis=0, tiled=True),
    )
    prompt_count = prompt_keys.shape[0]
    all_keys = jnp.concatenate([prompt_keys, key_rot[PROMPT_DEV:]], axis=0)
    all_values = jnp.concatenate([prompt_values, value_low[PROMPT_DEV:]], axis=0)
    key_index = jnp.arange(prompt_count, dtype=jnp.int32)
    prompt_mask = (group[:, None] == (key_index // prompt_len)[None, :]) & (
        (key_index % prompt_len)[None, :] <= position[:, None]
    )
    own_mask = (tag[:, None] == tag[None, PROMPT_DEV:]) & (
        position[None, PROMPT_DEV:] <= position[:, None]
    )
    mask = jnp.concatenate([prompt_mask, own_mask], axis=1)

    def head_scores(query_head, key_head):
        scores = (
            jnp.einsum("qd,kd->qk", query_head, key_head, preferred_element_type=jnp.float32)
            * factor
        )
        return jnp.where(mask, scores, masked_value)

    outputs = []
    log_totals = []
    for head in range(head_count):
        start = head * HD
        scores = head_scores(query_rot[:, start : start + HD], all_keys[:, start : start + HD])
        top = jnp.max(scores, axis=1, keepdims=True)
        weights = jnp.exp(scores - top)
        total = jnp.sum(weights, axis=1, keepdims=True)
        shares = (weights / total).astype(jnp.bfloat16)
        outputs.append(
            jnp.dot(shares, all_values[:, start : start + HD], preferred_element_type=jnp.float32)
        )
        log_totals.append(top + jnp.log(total))
    attended = jnp.concatenate(outputs, axis=1).astype(jnp.bfloat16)
    attention = lax.psum(jnp.dot(attended, w_out, preferred_element_type=jnp.float32), "tensor")
    hidden = source + attention
    scale_two = lax.rsqrt(jnp.mean(hidden * hidden, axis=1, keepdims=True) + epsilon)
    normed_two = (hidden * scale_two * ffn_gain).astype(jnp.bfloat16)
    logits = jnp.dot(normed_two, router, preferred_element_type=jnp.float32)
    top = jnp.max(logits, axis=1, keepdims=True)
    weights = jnp.exp(logits - top)
    chances = weights / jnp.sum(weights, axis=1, keepdims=True)
    hits = (routes[:, :, None] == jnp.arange(experts_total, dtype=jnp.int32)[None, None, :]).astype(
        jnp.float32
    )
    rows_mask = jnp.sum(hits, axis=1)
    routed = lax.all_gather(
        (rows_mask * chances).astype(jnp.float32), "expert", axis=0, tiled=True
    )
    gates = lax.dynamic_slice_in_dim(routed, device * local_experts, local_experts, 1).T
    grad_out = cotangent.astype(jnp.float32)
    pieces = max(1, ranks * rows // 4096)
    piece = rows // pieces
    split_gates = gates.reshape(local_experts, ranks, rows)
    results = []
    weight_grads = None
    for number in range(pieces):
        part = slice(number * piece, (number + 1) * piece)
        sources = (normed_two[part], cotangent[part])
        if results:
            sources, results, weight_grads = lax.optimization_barrier(
                (sources, results, weight_grads)
            )
        *result, grads = experts(
            *sources,
            split_gates[:, :, part].reshape(local_experts, ranks * piece),
            w_gate,
            w_up,
            w_down,
            experts_total,
        )
        results.append(result)
        weight_grads = grads if weight_grads is None else [a + b for a, b in zip(weight_grads, grads)]
    mixture, moe_input_grad, chance_grad = (
        jnp.concatenate(list(group_of), axis=0) for group_of in zip(*results)
    )
    grad_w_gate, grad_w_up, grad_w_down = weight_grads
    chance_grad = rows_mask * chance_grad
    output = (hidden + mixture).astype(jnp.bfloat16)
    logit_grad = (
        chances * (chance_grad - jnp.sum(chances * chance_grad, axis=1, keepdims=True))
    ).astype(jnp.bfloat16)
    grad_router = jnp.einsum(
        "td,te->de", normed_two, logit_grad, preferred_element_type=jnp.float32
    )
    normed_two_grad = moe_input_grad + jnp.einsum(
        "te,de->td", logit_grad, router, preferred_element_type=jnp.float32
    )
    weighted_two = ffn_gain * normed_two_grad
    grad_ffn_gain = jnp.sum(normed_two_grad * hidden * scale_two, axis=0)
    hidden_grad = (
        grad_out
        + scale_two * weighted_two
        - hidden * (scale_two**3 / width) * jnp.sum(weighted_two * hidden, axis=1, keepdims=True)
    )
    attention_grad = hidden_grad.astype(jnp.bfloat16)
    grad_w_out = jnp.einsum(
        "td,te->de", attended, attention_grad, preferred_element_type=jnp.float32
    )
    attended_grad = jnp.einsum(
        "te,de->td", attention_grad, w_out, preferred_element_type=jnp.float32
    ).astype(jnp.bfloat16)
    query_grads = []
    key_grads = []
    value_grads = []
    for head in range(head_count):
        start = head * HD
        query_head = query_rot[:, start : start + HD]
        key_head = all_keys[:, start : start + HD]
        value_head = all_values[:, start : start + HD]
        out_grad_head = attended_grad[:, start : start + HD]
        recomputed = jnp.exp(head_scores(query_head, key_head) - log_totals[head])
        share_grad = jnp.einsum(
            "qd,kd->qk", out_grad_head, value_head, preferred_element_type=jnp.float32
        )
        delta = jnp.sum(recomputed * share_grad, axis=1, keepdims=True)
        score_grad = (recomputed * (share_grad - delta)).astype(jnp.bfloat16)
        query_grads.append(
            jnp.dot(score_grad, key_head, preferred_element_type=jnp.float32) * factor
        )
        key_grads.append(
            jnp.einsum("qk,qd->kd", score_grad, query_head, preferred_element_type=jnp.float32)
            * factor
        )
        value_grads.append(
            jnp.einsum(
                "qk,qd->kd",
                recomputed.astype(jnp.bfloat16),
                out_grad_head,
                preferred_element_type=jnp.float32,
            )
        )
    key_grad_all = jnp.concatenate(key_grads, axis=1)
    value_grad_all = jnp.concatenate(value_grads, axis=1)
    prompt_key_grad, prompt_value_grad = (
        lax.psum_scatter(
            key_grad_all[:prompt_count].astype(jnp.bfloat16),
            "expert",
            scatter_dimension=0,
            tiled=True,
        ).astype(jnp.float32),
        lax.psum_scatter(
            value_grad_all[:prompt_count].astype(jnp.bfloat16),
            "expert",
            scatter_dimension=0,
            tiled=True,
        ).astype(jnp.float32),
    )
    key_grad = jnp.concatenate([prompt_key_grad, key_grad_all[prompt_count:]], axis=0)
    value_grad = jnp.concatenate([prompt_value_grad, value_grad_all[prompt_count:]], axis=0)
    query_grad = unrotate(
        jnp.concatenate(query_grads, axis=1).reshape(rows, head_count, HD), cosine, sine
    ).reshape(rows, local_width)
    key_grad = unrotate(key_grad.reshape(rows, head_count, HD), cosine, sine).reshape(
        rows, local_width
    )
    grad_qk_gain = jnp.stack(
        [
            jnp.sum(query_grad * query_raw * scale_query, axis=0),
            jnp.sum(key_grad * key_raw * scale_key, axis=0),
        ],
        axis=0,
    )
    weighted_query = qk_gain[0] * query_grad
    weighted_key = qk_gain[1] * key_grad
    inner_sums = lax.psum(
        jnp.stack(
            [jnp.sum(weighted_query * query_raw, axis=1), jnp.sum(weighted_key * key_raw, axis=1)],
            axis=1,
        ),
        "tensor",
    )
    query_raw_grad = (
        scale_query * weighted_query - query_raw * (scale_query**3 / width) * inner_sums[:, 0:1]
    ).astype(jnp.bfloat16)
    key_raw_grad = (
        scale_key * weighted_key - key_raw * (scale_key**3 / width) * inner_sums[:, 1:2]
    ).astype(jnp.bfloat16)
    value_raw_grad = value_grad.astype(jnp.bfloat16)
    grad_w_query = jnp.einsum(
        "td,te->de", normed, query_raw_grad, preferred_element_type=jnp.float32
    )
    grad_w_key = jnp.einsum("td,te->de", normed, key_raw_grad, preferred_element_type=jnp.float32)
    grad_w_value = jnp.einsum(
        "td,te->de", normed, value_raw_grad, preferred_element_type=jnp.float32
    )
    normed_part = jnp.einsum(
        "te,de->td", query_raw_grad, w_query, preferred_element_type=jnp.float32
    )
    normed_part = normed_part + jnp.einsum(
        "te,de->td", key_raw_grad, w_key, preferred_element_type=jnp.float32
    )
    normed_part = normed_part + jnp.einsum(
        "te,de->td", value_raw_grad, w_value, preferred_element_type=jnp.float32
    )
    normed_grad = lax.psum(normed_part.astype(jnp.bfloat16), "tensor").astype(jnp.float32)
    weighted_one = attn_gain * normed_grad
    grad_attn_gain = jnp.sum(normed_grad * source * scale_one, axis=0)
    input_grad = (
        hidden_grad
        + scale_one * weighted_one
        - source * (scale_one**3 / width) * jnp.sum(weighted_one * source, axis=1, keepdims=True)
    )
    summed = (
        lax.psum_scatter(
            grad_w_query.astype(jnp.bfloat16), "expert", scatter_dimension=0, tiled=True
        ).astype(jnp.float32),
        lax.psum_scatter(
            grad_w_key.astype(jnp.bfloat16), "expert", scatter_dimension=0, tiled=True
        ).astype(jnp.float32),
        lax.psum_scatter(
            grad_w_value.astype(jnp.bfloat16), "expert", scatter_dimension=0, tiled=True
        ).astype(jnp.float32),
        lax.psum_scatter(
            grad_w_out.astype(jnp.bfloat16), "expert", scatter_dimension=1, tiled=True
        ).astype(jnp.float32),
        lax.psum_scatter(
            grad_attn_gain.astype(jnp.bfloat16), "expert", scatter_dimension=0, tiled=True
        ).astype(jnp.float32),
        lax.psum_scatter(
            grad_ffn_gain.astype(jnp.bfloat16), "expert", scatter_dimension=0, tiled=True
        ).astype(jnp.float32),
        lax.psum_scatter(
            grad_qk_gain.astype(jnp.bfloat16), "expert", scatter_dimension=1, tiled=True
        ).astype(jnp.float32),
        lax.psum_scatter(
            grad_router.astype(jnp.bfloat16), "expert", scatter_dimension=0, tiled=True
        ).astype(jnp.float32),
    )
    return (
        output,
        input_grad,
        summed[0],
        summed[1],
        summed[2],
        summed[3],
        summed[4],
        summed[5],
        summed[6],
        summed[7],
        grad_w_gate,
        grad_w_up,
        grad_w_down,
    )


def compact(
    tokens, w_query, w_key, w_value, w_out, attn_gain, ffn_gain, qk_gain, router, w_gate, w_up, w_down,
    routes, cont_group, cotangent,
):
    rows, width = tokens.shape
    local_width = w_query.shape[1]
    head_count = local_width // HD
    experts_total = router.shape[1]
    local_experts = w_gate.shape[0]
    ranks = lax.axis_size("expert")
    device = lax.axis_index("expert")
    full = jnp.float32
    group, position, tag = layout(rows, ranks, device, cont_group)
    frequency = 10000.0 ** (-jnp.arange(HD // 2, dtype=full) * 2.0 / HD)
    angle = position.astype(full)[:, None] * frequency[None, :]
    cosine, sine = jnp.cos(angle), jnp.sin(angle)
    cosine = jnp.concatenate([cosine, cosine], axis=1)
    sine = jnp.concatenate([-sine, sine], axis=1)
    bias = jnp.where(attention_mask(group, position, tag, ranks), 0.0, masked_value).astype(full)
    own_first = jnp.roll(router, -device * local_experts, axis=1)
    own_first = jnp.pad(own_first, ((0, 0), (0, LANE - experts_total)))
    expert_bias = jnp.where(jnp.arange(LANE) < experts_total, 0.0, masked_value).astype(full)[None]
    turned_routes = jnp.tile(jnp.pad(routes.T, ((0, -routes.shape[1] % 8), (0, 0)), constant_values=-1), (2, 1))
    hits = routes[:, :, None] == jnp.arange(experts_total, dtype=jnp.int32)
    routed = jnp.any(hits, axis=1).astype(full)
    (
        attention, normed, normed_two, attended, query_rot, keys_values, query_raw, key_raw, stats, routes_all, arrived,
    ) = front(
        tokens, attn_gain[None], ffn_gain[None], w_query, w_key, w_value, w_out, qk_gain, cosine, sine, bias,
        turned_routes,
    )
    arrived_grad = lax.all_gather(cotangent, "expert", axis=0)
    own_expert = device * local_experts + jnp.arange(local_experts, dtype=jnp.int32)
    names = routes_all[:, : turned_routes.shape[0] // 2]
    expert_mask = jnp.any(names[:, :, :, None] == own_expert, axis=1).astype(full)
    expert_mask = jnp.pad(expert_mask, ((0, 0), (0, 0), (0, LANE - local_experts)))
    reduced, gated, gate_grad, up_grad, mixed_part = experts_fused(
        arrived, arrived_grad, expert_mask, own_first, expert_bias, w_gate, w_up, w_down
    )
    source = tokens.astype(full)
    hidden = source + attention.astype(full)
    scale_one, scale_two = stats[:, 0:1], stats[:, 3:4]
    logits = jnp.dot(normed_two, router, preferred_element_type=full)
    weights = jnp.exp(logits - jnp.max(logits, axis=1, keepdims=True))
    chances = weights / jnp.sum(weights, axis=1, keepdims=True)
    chance_grad = routed * reduced[:, width : width + experts_total].astype(full)
    logit_grad = (
        chances * (chance_grad - jnp.sum(chances * chance_grad, axis=1, keepdims=True))
    ).astype(jnp.bfloat16)
    grad_router = jnp.einsum("td,te->de", normed_two, logit_grad, preferred_element_type=full)
    normed_two_grad = reduced[:, :width].astype(full) + jnp.einsum(
        "te,de->td", logit_grad, router, preferred_element_type=full
    )
    grad_out = cotangent.astype(full)
    weighted_two = ffn_gain * normed_two_grad
    grad_ffn_gain = jnp.sum(normed_two_grad * hidden * scale_two, axis=0)
    hidden_grad = (
        grad_out
        + scale_two * weighted_two
        - hidden * (scale_two**3 / width) * jnp.sum(weighted_two * hidden, axis=1, keepdims=True)
    )
    attention_grad = hidden_grad.astype(jnp.bfloat16)
    query_raw_grad, key_raw_grad, value_raw_grad, grad_qk_gain = backward(
        attention_grad, w_out, query_rot, keys_values, bias, stats, query_raw, key_raw, cosine, sine, qk_gain
    )
    small_part = local_width // ranks
    share = width // ranks
    gains = jnp.pad(
        grad_qk_gain.reshape(2, ranks, small_part).transpose(1, 2, 0), ((0, 0), (0, share - small_part), (0, 0))
    )
    extras = jnp.concatenate(
        [grad_router.reshape(ranks, share, experts_total), grad_ffn_gain.reshape(ranks, share, 1), gains], axis=2
    ).astype(jnp.bfloat16)
    extras = jnp.pad(extras, ((0, 0), (0, 0), (0, LANE - experts_total - 3)))
    normed_grad, sums, gain_total, mixture, grad_w_gate, grad_w_up, grad_w_down = closing(
        normed, query_raw_grad, key_raw_grad, value_raw_grad, attended, attention_grad, extras, w_query, w_key, w_value,
        mixed_part, arrived, arrived_grad, gated, gate_grad, up_grad, local_experts, experts_total + 3,
    )
    normed_grad = normed_grad.astype(full)
    output = (hidden + mixture.astype(full)).astype(jnp.bfloat16)
    weighted_one = attn_gain * normed_grad
    input_grad = (
        hidden_grad
        + scale_one * weighted_one
        - source * (scale_one**3 / width) * jnp.sum(weighted_one * source, axis=1, keepdims=True)
    )
    edge = 4 * local_width
    return (
        output,
        input_grad,
        sums[:, :local_width],
        sums[:, local_width : 2 * local_width],
        sums[:, 2 * local_width : 3 * local_width],
        sums[:, 3 * local_width : edge].T,
        gain_total[0] / lax.dynamic_slice_in_dim(attn_gain, device * share, share),
        sums[:, edge + experts_total],
        sums[:small_part, edge + experts_total + 1 : edge + experts_total + 3].T,
        sums[:, edge : edge + experts_total],
        grad_w_gate,
        grad_w_up,
        grad_w_down,
    )


def layout(rows, ranks, device, cont_group):
    span = ranks // 2
    prompt_len = PROMPT_DEV * span
    local = jnp.arange(rows, dtype=jnp.int32)
    is_prompt = local < PROMPT_DEV
    after = jnp.maximum(local - PROMPT_DEV, 0)
    slot_cont = after // CLEN
    cont_pick = jnp.sum(
        jnp.where(
            slot_cont[:, None] == jnp.arange(CONT_DEV, dtype=jnp.int32)[None, :], cont_group[None, :], 0
        ),
        axis=1,
    )
    group = jnp.where(is_prompt, device // span, cont_pick)
    position = jnp.where(is_prompt, device % span * PROMPT_DEV + local, prompt_len + after % CLEN)
    tag = jnp.where(is_prompt, -1, slot_cont)
    return group, position, tag


def attention_mask(group, position, tag, ranks):
    prompt_len = PROMPT_DEV * (ranks // 2)
    key_index = jnp.arange(ranks * PROMPT_DEV, dtype=jnp.int32)
    prompt_mask = (group[:, None] == (key_index // prompt_len)[None, :]) & (
        (key_index % prompt_len)[None, :] <= position[:, None]
    )
    own_mask = (tag[:, None] == tag[None, PROMPT_DEV:]) & (
        position[None, PROMPT_DEV:] <= position[:, None]
    )
    return jnp.concatenate([prompt_mask, own_mask], axis=1)


def solution(mesh):
    small = mesh.shape["expert"] == 8
    return jax.shard_map(
        compact if small else body,
        mesh=mesh,
        in_specs=(
            P("expert", None),
            P(None, "tensor"),
            P(None, "tensor"),
            P(None, "tensor"),
            P("tensor", None),
            P(),
            P(),
            P(None, "tensor"),
            P(),
            P("expert", None, "tensor"),
            P("expert", None, "tensor"),
            P("expert", "tensor", None),
            P("expert", None),
            P("expert"),
            P("expert", None),
        ),
        out_specs=(
            P("expert", None),
            P("expert", None),
            P("expert", "tensor"),
            P("expert", "tensor"),
            P("expert", "tensor"),
            P("tensor", "expert"),
            P("expert"),
            P("expert"),
            P(None, ("tensor", "expert")),
            P("expert", None),
            P("expert", None, "tensor"),
            P("expert", None, "tensor"),
            P("expert", "tensor", None),
        ),
        check_vma=False,
    )
```

```python
import functools

import jax
import jax.numpy as jnp
from jax import lax
from jax.experimental import pallas as pl
from jax.experimental.pallas import tpu as pltpu
from jax.sharding import PartitionSpec as P

HD = 128
PROMPT_DEV = 128
CLEN = 256
CONT_DEV = 1


epsilon = 1e-05
masked_value = -1e30


MESH = pl.DeviceIdType.MESH
STEP = 16
LANE = 128


def remote(source, target, sent, received, **where):
    return pltpu.make_async_remote_copy(
        src_ref=source,
        dst_ref=target,
        send_sem=sent,
        recv_sem=received,
        device_id=where,
        device_id_type=MESH,
    )


def greet(places):
    barrier = pltpu.get_barrier_semaphore()
    for condition, where in places:
        def signal(where=where):
            pl.semaphore_signal(barrier, inc=1, device_id=where, device_id_type=MESH)
        if condition is None:
            signal()
        else:
            pl.when(condition)(signal)
    count = 0
    for condition, _ in places:
        count = count + (1 if condition is None else jnp.where(condition, 1, 0))
    pl.semaphore_wait(barrier, count)


class Line:
    def __init__(self, own, arrived, spare, total, sems, step=STEP):
        self.step = step
        self.own, self.arrived, self.spare, self.total = own, arrived, spare, total
        self.up_sent, self.far_got, self.near_got, self.far_sent, self.near_sent, self.down_got = (
            sems.at[i] for i in range(6)
        )
        self.size = lax.axis_size("tensor")
        self.here = lax.axis_index("tensor")
        self.root = self.size // 2 - 1
        self.rise_steps = self.size - 1 - self.root
        self.trip = 2 * self.rise_steps
        self.half = own.shape[0] // 2
        self.pieces = self.half // step

    @staticmethod
    def semaphores(rows, step=STEP):
        return pltpu.SemaphoreType.DMA((6, 2, rows // 2 // step))

    @staticmethod
    def spare_shape(rows, width):
        return pltpu.VMEM((rows // 2, width), jnp.bfloat16)

    def neighbours(self):
        here, size = self.here, self.size
        return [
            (here > 0, {"tensor": jnp.maximum(here - 1, 0)}),
            (here < size - 1, {"tensor": jnp.minimum(here + 1, size - 1)}),
        ]

    def place(self, lane):
        return self.here if lane == 0 else self.size - 1 - self.here

    def device(self, lane, place):
        return place if lane == 0 else self.size - 1 - place

    def rows(self, lane, piece):
        return pl.ds(pl.multiple_of(lane * self.half + piece * self.step, self.step), self.step)

    def landing(self, piece):
        return pl.ds(pl.multiple_of(piece * self.step, self.step), self.step)

    def far_up(self, lane, piece):
        rows, place = self.rows(lane, piece), self.place(lane)
        inward = jnp.where(place > self.root, place - 1, place + 1)
        return remote(
            self.own.at[rows], self.arrived.at[rows],
            self.up_sent.at[lane, piece], self.far_got.at[lane, piece], tensor=self.device(lane, inward),
        )

    def near_up(self, lane, piece):
        return remote(
            self.own.at[self.rows(lane, piece)], self.spare.at[self.landing(piece)],
            self.up_sent.at[lane, piece], self.near_got.at[lane, piece], tensor=self.device(lane, self.root),
        )

    def down(self, lane, piece, away):
        rows = self.rows(lane, piece)
        sent = self.far_sent if away == 1 else self.near_sent
        return remote(
            self.total.at[rows], self.total.at[rows],
            sent.at[lane, piece], self.down_got.at[lane, piece], tensor=self.device(lane, self.place(lane) + away),
        )

    def rise(self, lane, piece):
        place, root = self.place(lane), self.root
        rows = self.rows(lane, piece)

        def value(field):
            return field.astype(jnp.float32)

        @pl.when((place > root) & (place < self.size - 1) | (place > 0) & (place < root))
        def _():
            self.far_up(lane, piece).wait_recv()
            self.own[rows] = (value(self.own[rows]) + value(self.arrived[rows])).astype(jnp.bfloat16)

        @pl.when(place == root)
        def _():
            self.far_up(lane, piece).wait_recv()
            summed = value(self.own[rows]) + value(self.arrived[rows])
            if root > 0:
                self.near_up(lane, piece).wait_recv()
                summed = summed + value(self.spare[self.landing(piece)])
            self.total[rows] = summed.astype(jnp.bfloat16)
            self.down(lane, piece, 1).start()
            if root > 0:
                self.down(lane, piece, -1).start()

        if root > 0:

            @pl.when(place == root - 1)
            def _():
                self.near_up(lane, piece).start()

        @pl.when((place > root) | (place < root - 1))
        def _():
            self.far_up(lane, piece).start()

    def fall(self, lane, piece):
        place, root = self.place(lane), self.root

        @pl.when(place != root)
        def _():
            self.down(lane, piece, 1).wait_recv()

        @pl.when((place > root) & (place < self.size - 1))
        def _():
            self.down(lane, piece, 1).start()

        @pl.when((place > 0) & (place < root))
        def _():
            self.down(lane, piece, -1).start()

    def advance(self, step):
        for lane in range(2):
            place = self.place(lane)
            steps_in = self.rise_steps - jnp.abs(place - self.root)
            piece = step - steps_in

            @pl.when((piece >= 0) & (piece < self.pieces))
            def _():
                self.rise(lane, piece)

        for lane in range(2):
            place = self.place(lane)
            piece = step - self.rise_steps - jnp.abs(place - self.root)

            @pl.when((piece >= 0) & (piece < self.pieces))
            def _():
                self.fall(lane, piece)

    def step_body(self, step, carry):
        self.advance(step)
        return carry

    def steps(self):
        return self.pieces + self.trip

    def finish(self):
        def one(piece, carry):
            for lane in range(2):
                place, root = self.place(lane), self.root

                @pl.when(place != root)
                def _():
                    self.far_up(lane, piece).wait_send()

                @pl.when((place >= root) & (place < self.size - 1))
                def _():
                    self.down(lane, piece, 1).wait_send()

                @pl.when((place <= root) & (place > 0))
                def _():
                    self.down(lane, piece, -1).wait_send()
            return carry

        lax.fori_loop(0, self.pieces, one, 0)


class Place:
    def __init__(self):
        here = lax.axis_index("expert")
        self.here = here
        self.core, self.x, self.y = here % 2, here // 2 % 2, here // 4
        self.sibling = here + 1 - 2 * self.core
        self.x_chip = here + 2 - 4 * self.x
        self.y_chip = here + 4 - 8 * self.y

    def neighbours(self):
        return [(None, {"expert": i}) for i in (self.sibling, self.x_chip, self.y_chip)]

    def block(self, chip, core):
        x = self.x + (1 - chip // 2) * (1 - 2 * self.x)
        y = self.y + (1 - chip % 2) * (1 - 2 * self.y)
        return 4 * y + 2 * x + core


class Plane(Place):
    def __init__(self, own, spare, paired, from_x, from_y, pair_sems, x_sems, y_sems, by_device=False, step=STEP):
        self.step = step
        self.by_device = by_device
        self.own, self.spare, self.paired, self.from_x, self.from_y = own, spare, paired, from_x, from_y
        self.pair_sems, self.x_sems, self.y_sems = pair_sems, x_sems, y_sems
        super().__init__()
        self.half = own.shape[1] // 2
        self.pieces = self.half // step

    @staticmethod
    def semaphores(rows, step=STEP):
        pieces = rows // 2 // step
        return [
            pltpu.SemaphoreType.DMA((2, 4)),
            pltpu.SemaphoreType.DMA((2, 3, pieces)),
            pltpu.SemaphoreType.DMA((2, 3, pieces)),
        ]

    def pair_copy(self, chip):
        place = self.block(chip, 1 - self.core) if self.by_device else chip
        return remote(
            self.spare.at[place], self.paired.at[chip],
            self.pair_sems.at[0, chip], self.pair_sems.at[1, chip], expert=self.sibling,
        )

    def rows(self, side, piece):
        return pl.ds(pl.multiple_of(side * self.half + piece * self.step, self.step), self.step)

    def landing(self, piece):
        return pl.ds(pl.multiple_of(piece * self.step, self.step), self.step)

    def x_copy(self, kind, piece):
        chip, side = ((0, 0), (1, 0), (1, 1))[kind]
        return remote(
            self.own.at[chip, self.rows(side, piece)], self.from_x.at[kind, self.landing(piece)],
            self.x_sems.at[0, kind, piece], self.x_sems.at[1, kind, piece], expert=self.x_chip,
        )

    def y_copy(self, kind, piece):
        chip, side = ((0, 1), (2, 1), (2, 0))[kind]
        return remote(
            self.own.at[chip, self.rows(side, piece)], self.from_y.at[kind, self.landing(piece)],
            self.y_sems.at[0, kind, piece], self.y_sems.at[1, kind, piece], expert=self.y_chip,
        )

    def add_pair(self, chip, side, piece):
        rows = self.rows(side, piece)
        self.own[chip, rows] = (
            self.own[chip, rows].astype(jnp.float32) + self.paired[chip, rows].astype(jnp.float32)
        ).astype(jnp.bfloat16)

    def each(self, step):
        def one(piece, carry):
            step(piece)
            return carry

        lax.fori_loop(0, self.pieces, one, 0)

    def send_first(self, chip):
        def step(piece):
            if chip in (0, 1):
                self.add_pair(chip, 0, piece)
                self.x_copy(chip, piece).start()
            if chip in (0, 2):
                self.add_pair(chip, 1, piece)
                self.y_copy(chip // 2, piece).start()

        self.each(step)

    def first_piece(self, piece):
        for chip, side in ((0, 0), (0, 1), (1, 0), (2, 1)):
            self.add_pair(chip, side, piece)
        for kind in range(2):
            self.x_copy(kind, piece).start()
            self.y_copy(kind, piece).start()

    def second_piece(self, piece):
        landed = self.landing(piece)
        self.y_copy(0, piece).wait_recv()
        rows = self.rows(1, piece)
        self.own[1, rows] = (
            self.own[1, rows].astype(jnp.float32)
            + self.paired[1, rows].astype(jnp.float32)
            + self.from_y[0, landed].astype(jnp.float32)
        ).astype(jnp.bfloat16)
        self.x_copy(2, piece).start()
        self.x_copy(0, piece).wait_recv()
        rows = self.rows(0, piece)
        self.own[2, rows] = (
            self.own[2, rows].astype(jnp.float32)
            + self.paired[2, rows].astype(jnp.float32)
            + self.from_x[0, landed].astype(jnp.float32)
        ).astype(jnp.bfloat16)
        self.y_copy(2, piece).start()

    def send_second(self):
        self.each(self.second_piece)

    def last_sum(self, piece):
        landed = self.landing(piece)
        sums = []
        for side in range(2):
            first, second = (self.x_copy(1, piece), self.y_copy(2, piece)) if side == 0 else (self.y_copy(1, piece), self.x_copy(2, piece))
            first.wait_recv()
            second.wait_recv()
            a, b = (self.from_x[1, landed], self.from_y[2, landed]) if side == 0 else (self.from_y[1, landed], self.from_x[2, landed])
            rows = self.rows(side, piece)
            sums.append(
                self.own[3, rows].astype(jnp.float32)
                + self.paired[3, rows].astype(jnp.float32)
                + a.astype(jnp.float32)
                + b.astype(jnp.float32)
            )
        return sums

    def finish(self):
        for chip in range(4):
            self.pair_copy(chip).wait_send()

        def step(piece):
            for kind in range(3):
                self.x_copy(kind, piece).wait_send()
                self.y_copy(kind, piece).wait_send()

        self.each(step)


class Gather:
    def __init__(self, source, target, place, x_sems, y_sems, far_sems, pair_sems, own_sem, pieces):
        self.source, self.target = source, target
        self.place = place
        self.x_sems, self.y_sems, self.far_sems, self.pair_sems, self.own_sem = x_sems, y_sems, far_sems, pair_sems, own_sem
        self.pieces = pieces
        self.rows_each = source.shape[0] // pieces

    @staticmethod
    def semaphores(pieces):
        return [
            pltpu.SemaphoreType.DMA((2, pieces)),
            pltpu.SemaphoreType.DMA((2, pieces)),
            pltpu.SemaphoreType.DMA((2, pieces)),
            pltpu.SemaphoreType.DMA((2, 4, pieces)),
            pltpu.SemaphoreType.DMA,
        ]

    def rows(self, piece):
        return pl.ds(piece * self.rows_each, self.rows_each)

    def own_copy(self):
        return pltpu.make_async_copy(self.source, self.target.at[self.place.here], self.own_sem)

    def x_copy(self, piece):
        rows = self.rows(piece)
        return remote(
            self.source.at[rows], self.target.at[self.place.here, rows],
            self.x_sems.at[0, piece], self.x_sems.at[1, piece], expert=self.place.x_chip,
        )

    def y_copy(self, piece):
        rows = self.rows(piece)
        return remote(
            self.source.at[rows], self.target.at[self.place.here, rows],
            self.y_sems.at[0, piece], self.y_sems.at[1, piece], expert=self.place.y_chip,
        )

    def far_copy(self, piece):
        rows = self.rows(piece)
        came, goes = (
            (self.place.x_chip, self.place.y_chip) if piece % 2 == 0 else (self.place.y_chip, self.place.x_chip)
        )
        return remote(
            self.target.at[came, rows], self.target.at[came, rows],
            self.far_sems.at[0, piece], self.far_sems.at[1, piece], expert=goes,
        )

    def pair_copy(self, kind, piece):
        rows = self.rows(piece)
        block = self.place.block(kind, self.place.core)
        source = self.source.at[rows] if kind == 3 else self.target.at[block, rows]
        return remote(
            source, self.target.at[block, rows],
            self.pair_sems.at[0, kind, piece], self.pair_sems.at[1, kind, piece], expert=self.place.sibling,
        )

    def start_piece(self, piece):
        self.x_copy(piece).start()
        self.y_copy(piece).start()
        self.pair_copy(3, piece).start()

    def start(self):
        self.own_copy().start()
        for piece in range(self.pieces):
            self.start_piece(piece)

    def near(self, piece):
        self.x_copy(piece).wait_recv()
        if piece % 2 == 0:
            self.far_copy(piece).start()
        self.pair_copy(1, piece).start()
        self.y_copy(piece).wait_recv()
        if piece % 2 == 1:
            self.far_copy(piece).start()
        self.pair_copy(2, piece).start()

    def far(self, piece):
        self.far_copy(piece).wait_recv()
        self.pair_copy(0, piece).start()

    def paired(self, kind, piece):
        self.pair_copy(kind, piece).wait_recv()

    def finish(self):
        for piece in range(self.pieces):
            self.x_copy(piece).wait_send()
            self.y_copy(piece).wait_send()
            self.far_copy(piece).wait_send()
            for kind in range(4):
                self.pair_copy(kind, piece).wait_send()


def wide_dot(left, right):
    return jnp.dot(left, right, preferred_element_type=jnp.float32)


def turned_dot(left, right):
    return lax.dot_general(left, right, (((1,), (1,)), ((), ())), preferred_element_type=jnp.float32)


BLOCK_STEP = 32


def expert_kernel(
    x_all, g_all, mask, router, bias, w_gate, w_up, w_down,
    reduced, gated_all, gate_all, up_all, mixed_all,
    x_buf, g_buf, part, paired, from_x, from_y, line_in, line_spare, small, mixed,
    in_sems, out_sems, pair_sems, x_sems, y_sems, line_sems,
):
    experts, width, hidden = w_gate.shape
    rows = x_buf.shape[1]
    tile = min(512, width)
    plane = Plane(part.at[1], part.at[0], paired, from_x, from_y, pair_sems, x_sems, y_sems, step=BLOCK_STEP)
    line = Line(part.at[1, 3], line_in, line_spare, reduced, line_sems, step=BLOCK_STEP)
    first_expert = lax.axis_index("expert") * experts
    outs = (gated_all, gate_all, up_all)

    def block_of(i):
        return plane.block(i // 2, (plane.core + 1 - i % 2) % 2)

    def fetch(i):
        slot, block = i % 2, block_of(i)
        return (
            pltpu.make_async_copy(x_all.at[block], x_buf.at[slot], in_sems.at[0, slot]),
            pltpu.make_async_copy(g_all.at[block], g_buf.at[slot], in_sems.at[1, slot]),
        )

    def store(i):
        slot, block = i % 2, block_of(i)
        return [
            pltpu.make_async_copy(small.at[slot, n], outs[n].at[block], out_sems.at[n, slot])
            for n in range(3)
        ] + [pltpu.make_async_copy(mixed.at[slot], mixed_all.at[block], out_sems.at[3, slot])]

    def compute(i):
        slot = i % 2
        block = block_of(i)
        x = x_buf.at[slot]
        g = g_buf.at[slot]
        logits = wide_dot(x[...], router[...]) + bias[...]
        weights = jnp.exp(logits - jnp.max(logits, axis=1, keepdims=True))
        gates = weights / jnp.sum(weights, axis=1, keepdims=True) * mask[block]
        column = lax.broadcasted_iota(jnp.int32, (rows, LANE), 1)
        extra = jnp.zeros((rows, LANE), jnp.float32)
        for j in range(experts):
            gate_pre = wide_dot(x[...], w_gate[j])
            up_pre = wide_dot(x[...], w_up[j])
            raw = turned_dot(g[...], w_down[j])
            gate = gates[:, j : j + 1]
            sigma = jax.nn.sigmoid(gate_pre)
            activated = gate_pre * sigma
            inner = activated * up_pre
            act = gate * raw
            span = slice(j * hidden, (j + 1) * hidden)
            small[slot, 0, :, span] = (gate * inner).astype(jnp.bfloat16)
            small[slot, 1, :, span] = (
                act * up_pre * sigma * (1.0 + gate_pre * (1.0 - sigma))
            ).astype(jnp.bfloat16)
            small[slot, 2, :, span] = (act * activated).astype(jnp.bfloat16)
            gain = jnp.sum(raw * inner, axis=1, keepdims=True)
            extra = jnp.where(column == first_expert + j, gain, extra)
        for start in range(0, width, tile):
            columns = slice(start, start + tile)
            slot_grad = None
            mix = None
            for j in range(experts):
                span = slice(j * hidden, (j + 1) * hidden)
                term = turned_dot(small[slot, 1, :, span], w_gate[j, columns]) + turned_dot(
                    small[slot, 2, :, span], w_up[j, columns]
                )
                more = wide_dot(small[slot, 0, :, span], w_down[j, :, columns])
                slot_grad = term if slot_grad is None else slot_grad + term
                mix = more if mix is None else mix + more
            part[i % 2, i // 2, :, columns] = slot_grad.astype(jnp.bfloat16)
            mixed[slot, :, columns] = mix.astype(jnp.bfloat16)
        part[i % 2, i // 2, :, width:] = extra.astype(jnp.bfloat16)

    for copy in fetch(0):
        copy.start()
    greet(plane.neighbours() + line.neighbours())

    def step(i, carry):
        @pl.when(i < 7)
        def _():
            for copy in fetch(i + 1):
                copy.start()

        for copy in fetch(i):
            copy.wait()

        @pl.when(i >= 2)
        def _():
            for copy in store(i - 2):
                copy.wait()

        compute(i)
        for copy in store(i):
            copy.start()

        @pl.when(i % 2 == 0)
        def _():
            plane.pair_copy(i // 2).start()

        @pl.when(i % 2 == 1)
        def _():
            plane.pair_copy(i // 2).wait_recv()

        for chip in range(3):

            @pl.when(i == 2 * chip + 1)
            def _():
                plane.send_first(chip)
                if chip == 2:
                    plane.send_second()

        return carry

    lax.fori_loop(0, 8, step, 0)

    def last(step, carry):
        @pl.when(step < plane.pieces)
        def _():
            for side, total in enumerate(plane.last_sum(step)):
                plane.own[3, plane.rows(side, step)] = total.astype(jnp.bfloat16)

        line.advance(step)
        return carry

    lax.fori_loop(0, line.steps(), last, 0)
    for i in (6, 7):
        for copy in store(i):
            copy.wait()
    plane.finish()
    line.finish()


def experts_fused(arrived, arrived_grad, mask, router, bias, w_gate, w_up, w_down):
    ranks, rows, width = arrived.shape
    experts, _, hidden = w_gate.shape
    wide = width + LANE
    inner = experts * hidden
    half = rows // 2
    low = jnp.bfloat16
    any_space = pl.BlockSpec(memory_space=pl.ANY)
    vmem = pl.BlockSpec(memory_space=pltpu.VMEM)
    small_shape = jax.ShapeDtypeStruct((ranks, rows, inner), low)
    return pl.pallas_call(
        expert_kernel,
        out_shape=(
            jax.ShapeDtypeStruct((rows, wide), low), small_shape, small_shape, small_shape,
            jax.ShapeDtypeStruct((ranks, rows, width), low),
        ),
        in_specs=[any_space, any_space] + [vmem] * 6,
        out_specs=(vmem, any_space, any_space, any_space, any_space),
        scratch_shapes=[
            pltpu.VMEM((2, rows, width), low),
            pltpu.VMEM((2, rows, width), low),
            pltpu.VMEM((2, 4, rows, wide), low),
            pltpu.VMEM((4, rows, wide), low),
            pltpu.VMEM((3, half, wide), low),
            pltpu.VMEM((3, half, wide), low),
            pltpu.VMEM((rows, wide), low),
            Line.spare_shape(rows, wide),
            pltpu.VMEM((2, 3, rows, inner), low),
            pltpu.VMEM((2, rows, width), low),
            pltpu.SemaphoreType.DMA((2, 2)),
            pltpu.SemaphoreType.DMA((4, 2)),
            *Plane.semaphores(rows, step=BLOCK_STEP),
            Line.semaphores(rows, step=BLOCK_STEP),
        ],
        compiler_params=pltpu.CompilerParams(
            collective_id=0, has_side_effects=True, vmem_limit_bytes=61 * 2**20
        ),
        cost_estimate=pl.CostEstimate(
            flops=12 * ranks * rows * width * inner, bytes_accessed=8 * ranks * rows * width, transcendentals=0
        ),
    )(arrived, arrived_grad, mask, router, bias, w_gate, w_up, w_down)


def crossed_dot(left, right):
    return lax.dot_general(left, right, (((0,), (0,)), ((), ())), preferred_element_type=jnp.float32)


def closing_kernel(
    normed, query_grad, key_grad, value_grad, attended, attention_grad, extras,
    w_query, w_key, w_value, mixed, x_all, g_all, gated_all, gate_all, up_all,
    total, sums, gain, mixture, gate_out, up_out, down_out,
    line_own, line_in, line_spare, part, paired, from_x, from_y,
    mix_own, mix_paired, mix_x, mix_y, mix_in, mix_spare, tiles, factors, results, downs,
    line_sems, pair_sems, x_sems, y_sems, mix_line_sems, mix_pair_sems, mix_x_sems, mix_y_sems,
    load_sems, weight_sems, factor_sems, tile_sems, out_sems,
    gains, mine, theirs, peer_sent, peer_got,
    *,
    gain_column,
):
    width = normed.shape[1]
    heads = query_grad.shape[1]
    share = part.shape[2]
    experts, _, hidden = gate_out.shape
    column_tile = min(512, width // 2)
    tile = tiles.shape[2]
    count = width // tile
    line = Line(line_own, line_in, line_spare, total, line_sems)
    plane = Plane(part.at[1], part.at[0], paired, from_x, from_y, pair_sems, x_sems, y_sems)
    mix = Plane(mix_own, mixed, mix_paired, mix_x, mix_y, mix_pair_sems, mix_x_sems, mix_y_sems, by_device=True)
    mix_line = Line(mix_own.at[3], mix_in, mix_spare, mixture, mix_line_sems)
    peers = Peers(mine, theirs, peer_sent, peer_got)
    half = width // 2

    def load_own(chip):
        return pltpu.make_async_copy(mixed.at[mix.block(chip, mix.core)], mix_own.at[chip], load_sems.at[chip])

    weight_loads = [
        pltpu.make_async_copy(w_query, factors.at[0, 0:width], weight_sems.at[0]),
        pltpu.make_async_copy(w_key, factors.at[1, 0:width], weight_sems.at[1]),
        pltpu.make_async_copy(w_value.at[0:half], factors.at[0, width : width + half], weight_sems.at[2]),
        pltpu.make_async_copy(w_value.at[half:], factors.at[1, width : width + half], weight_sems.at[3]),
    ]

    def factor_load(matrix):
        return pltpu.make_async_copy(
            (gate_all, up_all, gated_all)[matrix], factors.at[matrix % 2], factor_sems.at[matrix]
        )

    def tile_copy(source, s):
        columns = pl.ds(pl.multiple_of(s % count * tile, tile), tile)
        return pltpu.make_async_copy(source.at[:, columns], tiles.at[s % 2], tile_sems.at[s % 2])

    def start_tile(s):
        @pl.when(s < 2 * count)
        def _():
            tile_copy(x_all, s).start()

        @pl.when(s >= 2 * count)
        def _():
            tile_copy(g_all, s).start()

    def across(target, s):
        rows = pl.ds(pl.multiple_of(s % count * tile, tile), tile)
        return [
            pltpu.make_async_copy(
                results.at[s % 2, :, j * hidden : (j + 1) * hidden], target.at[j, rows], out_sems.at[0, s % 2, j]
            )
            for j in range(experts)
        ]

    def down(s):
        columns = pl.ds(pl.multiple_of(s % count * tile, tile), tile)
        return [
            pltpu.make_async_copy(
                downs.at[s % 2, j * hidden : (j + 1) * hidden], down_out.at[j, :, columns], out_sems.at[1, s % 2, j]
            )
            for j in range(experts)
        ]

    def expert_tile(s):
        @pl.when(s + 1 < 3 * count)
        def _():
            start_tile(s + 1)

        for matrix in range(3):

            @pl.when(s == matrix * count)
            def _():
                factor_load(matrix).wait()

        tile_copy(x_all, s).wait()

        @pl.when(s < 2 * count)
        def _():
            @pl.when(s >= 2)
            def _():
                for copy in across(gate_out, s):
                    copy.wait()

            results[s % 2] = crossed_dot(tiles[s % 2], factors[s // count])

            @pl.when(s < count)
            def _():
                for copy in across(gate_out, s):
                    copy.start()

            @pl.when(s >= count)
            def _():
                for copy in across(up_out, s):
                    copy.start()

        @pl.when(s >= 2 * count)
        def _():
            @pl.when(s >= 2 * count + 2)
            def _():
                for copy in down(s):
                    copy.wait()

            downs[s % 2] = crossed_dot(factors[0], tiles[s % 2])
            for copy in down(s):
                copy.start()

        @pl.when(s == count - 1)
        def _():
            factor_load(2).start()

    def dense_block(i):
        chip, sub = i // 2, i % 2
        block = plane.block(chip, (plane.core + 1 - sub) % 2)
        columns = pl.ds(pl.multiple_of(block * share, share), share)
        source = normed[:, columns]
        part[sub, chip, :, 0:heads] = crossed_dot(source, query_grad[...]).astype(jnp.bfloat16)
        part[sub, chip, :, heads : 2 * heads] = crossed_dot(source, key_grad[...]).astype(jnp.bfloat16)
        part[sub, chip, :, 2 * heads : 3 * heads] = crossed_dot(source, value_grad[...]).astype(jnp.bfloat16)
        part[sub, chip, :, 3 * heads : 4 * heads] = crossed_dot(
            attention_grad[:, columns], attended[...]
        ).astype(jnp.bfloat16)
        part[sub, chip, :, 4 * heads :] = extras[block] + gains[columns]

        @pl.when(sub == 0)
        def _():
            plane.pair_copy(chip).start()

    for copy in weight_loads:
        copy.start()
    for chip in range(4):
        load_own(chip).start()
    greet(plane.neighbours() + peers.neighbours())
    for chip in range(4):
        mix.pair_copy(chip).start()
    for copy in weight_loads:
        copy.wait()
    for start in range(0, width, column_tile):
        columns = slice(start, start + column_tile)
        later = width + start % half
        line_own[:, columns] = (
            turned_dot(query_grad[...], factors[0, columns])
            + turned_dot(key_grad[...], factors[1, columns])
            + turned_dot(value_grad[...], factors[start // half, later : later + column_tile])
        ).astype(jnp.bfloat16)
    place = lax.broadcasted_iota(jnp.int32, (normed.shape[0], LANE), 1)
    chosen = jnp.where(place == gain_column, 1.0, 0.0).astype(jnp.bfloat16)
    for start in range(0, width, column_tile):
        columns = slice(start, start + column_tile)
        pull = line_own[:, columns].astype(jnp.float32) * normed[:, columns].astype(jnp.float32)
        gains[columns] = crossed_dot(pull.astype(jnp.bfloat16), chosen).astype(jnp.bfloat16)
    factor_load(0).start()
    factor_load(1).start()
    start_tile(0)
    mix_second, mix_last, dense_first, dense_second, dense_last = PLAN

    def step(s, carry):
        line.advance(s)

        @pl.when(s == 0)
        def _():
            for chip in range(4):
                load_own(chip).wait()
                mix.pair_copy(chip).wait_recv()
            for piece in range(AHEAD):
                mix.first_piece(piece)

        @pl.when((s > 0) & (s + AHEAD - 1 < mix.pieces))
        def _():
            mix.first_piece(s + AHEAD - 1)

        @pl.when((s >= mix_second) & (s - mix_second < mix.pieces))
        def _():
            mix.second_piece(s - mix_second)

        @pl.when((s >= mix_last) & (s - mix_last < mix.pieces))
        def _():
            piece = s - mix_last
            for side, summed in enumerate(mix.last_sum(piece)):
                mix_own[3, mix.rows(side, piece)] = summed.astype(jnp.bfloat16)

        mix_line.advance(s - mix_last)

        @pl.when((s >= 4) & (s < 12))
        def _():
            dense_block(s - 4)

        @pl.when(s == dense_first)
        def _():
            for chip in range(4):
                plane.pair_copy(chip).wait_recv()
            for chip in range(3):
                plane.send_first(chip)

        @pl.when((s >= dense_second) & (s - dense_second < plane.pieces))
        def _():
            plane.second_piece(s - dense_second)

        @pl.when((s >= dense_last) & (s - dense_last < plane.pieces))
        def _():
            piece = s - dense_last
            for side, summed in enumerate(plane.last_sum(piece)):
                sums[plane.rows(side, piece)] = summed

        @pl.when(s < 3 * count)
        def _():
            expert_tile(s)

        return carry

    steps = jnp.maximum(mix_last + mix_line.steps(), jnp.maximum(3 * count, dense_last + plane.pieces))
    lax.fori_loop(0, steps, step, 0)
    column = 4 * heads + gain_column
    mine[...] = to_rows([sums[:, column : column + 1]], share)
    peers.start()
    for s in (2 * count - 2, 2 * count - 1):
        for copy in across(up_out, s):
            copy.wait()
    for s in (3 * count - 2, 3 * count - 1):
        for copy in down(s):
            copy.wait()
    gain[...] = peers.total()
    for each in (plane, line, mix, mix_line, peers):
        each.finish()


PLAN = (1, 3, 12, 15, 18)
AHEAD = 2
TILE = 256


def closing(
    normed, query_grad, key_grad, value_grad, attended, attention_grad, extras, w_query, w_key, w_value,
    mixed, arrived, arrived_grad, gated, gate_grad, up_grad, experts, gain_column,
):
    rows, width = normed.shape
    heads = query_grad.shape[1]
    ranks, share, more = extras.shape
    wide = 4 * heads + more
    inner = gated.shape[2]
    hidden = inner // experts
    low = jnp.bfloat16
    tile = min(TILE, width // 2)
    vmem = pl.BlockSpec(memory_space=pltpu.VMEM)
    any_space = pl.BlockSpec(memory_space=pl.ANY)
    every = ranks * rows
    size = lax.axis_size("tensor")
    return pl.pallas_call(
        functools.partial(closing_kernel, gain_column=gain_column),
        out_shape=(
            jax.ShapeDtypeStruct((rows, width), low),
            jax.ShapeDtypeStruct((share, wide), jnp.float32),
            jax.ShapeDtypeStruct((8, share), jnp.float32),
            jax.ShapeDtypeStruct((rows, width), low),
            jax.ShapeDtypeStruct((experts, width, hidden), jnp.float32),
            jax.ShapeDtypeStruct((experts, width, hidden), jnp.float32),
            jax.ShapeDtypeStruct((experts, hidden, width), jnp.float32),
        ),
        in_specs=[vmem] * 7 + [any_space] * 9,
        out_specs=(vmem,) * 4 + (any_space,) * 3,
        scratch_shapes=[
            pltpu.VMEM((rows, width), low),
            pltpu.VMEM((rows, width), low),
            Line.spare_shape(rows, width),
            pltpu.VMEM((2, 4, share, wide), low),
            pltpu.VMEM((4, share, wide), low),
            pltpu.VMEM((3, share // 2, wide), low),
            pltpu.VMEM((3, share // 2, wide), low),
            pltpu.VMEM((4, rows, width), low),
            pltpu.VMEM((4, rows, width), low),
            pltpu.VMEM((3, rows // 2, width), low),
            pltpu.VMEM((3, rows // 2, width), low),
            pltpu.VMEM((rows, width), low),
            Line.spare_shape(rows, width),
            pltpu.VMEM((2, every, tile), low),
            pltpu.VMEM((2, every, inner), low),
            pltpu.VMEM((2, tile, inner), jnp.float32),
            pltpu.VMEM((2, inner, tile), jnp.float32),
            Line.semaphores(rows),
            *Plane.semaphores(share),
            Line.semaphores(rows),
            *Plane.semaphores(rows),
            pltpu.SemaphoreType.DMA((4,)),
            pltpu.SemaphoreType.DMA((4,)),
            pltpu.SemaphoreType.DMA((3,)),
            pltpu.SemaphoreType.DMA((2,)),
            pltpu.SemaphoreType.DMA((2, 2, experts)),
            pltpu.VMEM((width, LANE), low),
            pltpu.VMEM((8, share), jnp.float32),
            pltpu.VMEM((size - 1, 8, share), jnp.float32),
            pltpu.SemaphoreType.DMA((size - 1,)),
            pltpu.SemaphoreType.DMA((size - 1,)),
        ],
        compiler_params=pltpu.CompilerParams(
            collective_id=2, has_side_effects=True, vmem_limit_bytes=63 * 2**20
        ),
    )(
        normed, query_grad, key_grad, value_grad, attended, attention_grad, extras, w_query, w_key, w_value,
        mixed, arrived.reshape(every, width), arrived_grad.reshape(every, width),
        gated.reshape(every, inner), gate_grad.reshape(every, inner), up_grad.reshape(every, inner),
    )


class Peers:
    def __init__(self, mine, theirs, sent, got):
        self.mine, self.theirs, self.sent, self.got = mine, theirs, sent, got
        self.size = lax.axis_size("tensor")
        self.here = lax.axis_index("tensor")

    def neighbours(self):
        return [(None, {"tensor": (self.here + d) % self.size}) for d in range(1, self.size)]

    def copies(self):
        return [
            remote(
                self.mine, self.theirs.at[d - 1], self.sent.at[d - 1], self.got.at[d - 1],
                tensor=(self.here + d) % self.size,
            )
            for d in range(1, self.size)
        ]

    def start(self):
        for copy in self.copies():
            copy.start()

    def total(self):
        result = self.mine[...]
        for d, copy in enumerate(self.copies()):
            copy.wait_recv()
            result = result + self.theirs[d]
        return result

    def finish(self):
        for copy in self.copies():
            copy.wait_send()


def to_rows(columns, rows):
    lane = lax.broadcasted_iota(jnp.int32, (rows, LANE), 1)
    field = jnp.zeros((rows, LANE), jnp.float32)
    for i, column in enumerate(columns):
        field = jnp.where(lane == i, column, field)
    return field.T[:8]


def to_columns(sums):
    padded = jnp.concatenate([sums, jnp.zeros((LANE - 8, sums.shape[1]), jnp.float32)], axis=0)
    return padded.T


def swapped(field):
    half = HD // 2
    return jnp.concatenate([field[:, half:], field[:, :half]], axis=1)


SPREAD = 32
SPREAD_LAG = 2


def front_kernel(
    tokens, attn_gain, ffn_gain, w_query, w_key, w_value, w_out, qk_gain, cosine, sine, bias, routes,
    total, normed, normed_two, attended, query_rot, keys_values, query_raw, key_raw, stats, routes_all, arrived,
    line_own, line_in, line_spare, prompt, mine, theirs, two,
    line_sems, peer_sent, peer_got, *gather_sems,
):
    rows, width = tokens.shape
    local = w_query.shape[1]
    heads = local // HD
    factor = HD ** (-0.5)
    own_blocks = rows // PROMPT_DEV - 1
    devices = keys_values.shape[0] - own_blocks
    place = Place()
    line = Line(line_own, line_in, line_spare, total, line_sems)
    peers = Peers(mine, theirs, peer_sent, peer_got)
    names = Gather(routes, routes_all, place, *gather_sems[0:5], pieces=2)
    prompts = Gather(prompt, keys_values, place, *gather_sems[5:10], pieces=2)
    spread = Gather(normed_two, arrived, place, *gather_sems[10:15], pieces=rows // SPREAD)
    greet(place.neighbours() + peers.neighbours())
    names.start()
    source = tokens[...].astype(jnp.float32)
    scale_one = lax.rsqrt(jnp.sum(source * source, axis=1, keepdims=True) / width + epsilon)
    normed[...] = (source * scale_one * attn_gain[...]).astype(jnp.bfloat16)
    query_raw[...] = wide_dot(normed[...], w_query[...])
    key_raw[...] = wide_dot(normed[...], w_key[...])
    mine[...] = to_rows(
        [
            jnp.sum(query_raw[...] * query_raw[...], axis=1, keepdims=True),
            jnp.sum(key_raw[...] * key_raw[...], axis=1, keepdims=True),
        ],
        rows,
    )
    peers.start()
    value = wide_dot(normed[...], w_value[...]).astype(jnp.bfloat16)
    prompt[:, local:] = value[:PROMPT_DEV]
    for i in range(own_blocks):
        keys_values[devices + i, :, local:] = value[(i + 1) * PROMPT_DEV : (i + 2) * PROMPT_DEV]
    squares = to_columns(peers.total())
    scale_query = lax.rsqrt(squares[:, 0:1] / width + epsilon)
    scale_key = lax.rsqrt(squares[:, 1:2] / width + epsilon)
    for head in range(heads):
        columns = slice(head * HD, (head + 1) * HD)
        turned = key_raw[:, columns] * scale_key * qk_gain[1:2, columns]
        turned = (turned * cosine[...] + swapped(turned) * sine[...]).astype(jnp.bfloat16)
        prompt[:, columns] = turned[:PROMPT_DEV]
        for i in range(own_blocks):
            keys_values[devices + i, :, columns] = turned[(i + 1) * PROMPT_DEV : (i + 2) * PROMPT_DEV]
    prompts.own_copy().start()
    for piece in range(2):
        prompts.start_piece(piece)
    for head in range(heads):
        columns = slice(head * HD, (head + 1) * HD)
        turned = query_raw[:, columns] * scale_query * qk_gain[0:1, columns]
        turned = turned * cosine[...] + swapped(turned) * sine[...]
        query_rot[:, columns] = turned.astype(jnp.bfloat16)
    for piece in range(2):
        prompts.near(piece)
    for piece in range(2):
        names.near(piece)
    for piece in range(2):
        prompts.far(piece)
        names.far(piece)
    prompts.own_copy().wait()
    for kind in range(4):
        for piece in range(2):
            prompts.paired(kind, piece)
            names.paired(kind, piece)
    lane = lax.broadcasted_iota(jnp.int32, (rows, LANE), 1)
    kept = jnp.where(lane == 0, scale_one, 0.0)
    kept = jnp.where(lane == 1, scale_query, kept)
    kept = jnp.where(lane == 2, scale_key, kept)
    count = keys_values.shape[0] * PROMPT_DEV
    for head in range(heads):
        columns = slice(head * HD, (head + 1) * HD)
        keys = keys_values[:, :, columns].reshape(count, HD)
        values = keys_values[:, :, local + head * HD : local + (head + 1) * HD].reshape(count, HD)
        scores = turned_dot(query_rot[:, columns], keys) * factor + bias[...]
        top = jnp.max(scores, axis=1, keepdims=True)
        weights = jnp.exp(scores - top)
        whole = jnp.sum(weights, axis=1, keepdims=True)
        shares = (weights / whole).astype(jnp.bfloat16)
        attended[:, columns] = wide_dot(shares, values).astype(jnp.bfloat16)
        kept = jnp.where(lane == 8 + head, top + jnp.log(whole), kept)
    tile = min(512, width)
    for start in range(0, width, tile):
        columns = slice(start, start + tile)
        line_own[:, columns] = wide_dot(attended[...], w_out[:, columns]).astype(jnp.bfloat16)
    ratio = SPREAD // STEP
    groups = line.pieces // ratio

    def norm_rows(piece):
        span = slice(piece * SPREAD, (piece + 1) * SPREAD)
        hidden = tokens[span].astype(jnp.float32) + total[span].astype(jnp.float32)
        scale = lax.rsqrt(jnp.sum(hidden * hidden, axis=1, keepdims=True) / width + epsilon)
        normed_two[span] = (hidden * scale * ffn_gain[...]).astype(jnp.bfloat16)
        two[span] = jnp.broadcast_to(scale, (SPREAD, LANE))

    done = 0
    passed = 0
    for group in range(groups):
        ready = line.trip + (group + 1) * ratio
        lax.fori_loop(done, ready, line.step_body, 0)
        done = ready
        for piece in (group, groups + group):
            norm_rows(piece)
            spread.start_piece(piece)
        if group >= SPREAD_LAG:
            for piece in (passed, groups + passed):
                spread.near(piece)
            passed += 1
    spread.own_copy().start()
    for group in range(passed, groups):
        for piece in (group, groups + group):
            spread.near(piece)
    for group in range(groups):
        for piece in (group, groups + group):
            spread.far(piece)
    stats[...] = jnp.where(lane == 3, two[...], kept)
    for kind in range(4):
        for piece in range(spread.pieces):
            spread.paired(kind, piece)
    spread.own_copy().wait()
    names.own_copy().wait()
    for each in (names, prompts, spread, line, peers):
        each.finish()


def front(tokens, attn_gain, ffn_gain, w_query, w_key, w_value, w_out, qk_gain, cosine, sine, bias, routes):
    rows, width = tokens.shape
    local = w_query.shape[1]
    ranks = lax.axis_size("expert")
    size = lax.axis_size("tensor")
    low, full = jnp.bfloat16, jnp.float32
    vmem = pl.BlockSpec(memory_space=pltpu.VMEM)
    blocks = ranks + rows // PROMPT_DEV - 1
    return pl.pallas_call(
        front_kernel,
        out_shape=(
            jax.ShapeDtypeStruct((rows, width), low),
            jax.ShapeDtypeStruct((rows, width), low),
            jax.ShapeDtypeStruct((rows, width), low),
            jax.ShapeDtypeStruct((rows, local), low),
            jax.ShapeDtypeStruct((rows, local), low),
            jax.ShapeDtypeStruct((blocks, PROMPT_DEV, 2 * local), low),
            jax.ShapeDtypeStruct((rows, local), full),
            jax.ShapeDtypeStruct((rows, local), full),
            jax.ShapeDtypeStruct((rows, LANE), full),
            jax.ShapeDtypeStruct((ranks,) + routes.shape, jnp.int32),
            jax.ShapeDtypeStruct((ranks, rows, width), low),
        ),
        in_specs=[vmem] * 12,
        out_specs=(vmem,) * 10 + (pl.BlockSpec(memory_space=pl.ANY),),
        scratch_shapes=[
            pltpu.VMEM((rows, width), low),
            pltpu.VMEM((rows, width), low),
            Line.spare_shape(rows, width),
            pltpu.VMEM((PROMPT_DEV, 2 * local), low),
            pltpu.VMEM((8, rows), full),
            pltpu.VMEM((size - 1, 8, rows), full),
            pltpu.VMEM((rows, LANE), full),
            Line.semaphores(rows),
            pltpu.SemaphoreType.DMA((size - 1,)),
            pltpu.SemaphoreType.DMA((size - 1,)),
            *Gather.semaphores(2),
            *Gather.semaphores(2),
            *Gather.semaphores(rows // SPREAD),
        ],
        compiler_params=pltpu.CompilerParams(
            collective_id=1, has_side_effects=True, vmem_limit_bytes=60 * 2**20
        ),
        cost_estimate=pl.CostEstimate(flops=100 * 10**9, bytes_accessed=200 * 10**6, transcendentals=0),
    )(tokens, attn_gain, ffn_gain, w_query, w_key, w_value, w_out, qk_gain, cosine, sine, bias, routes)


def backward_kernel(
    attention_grad, w_out, query_rot, keys_values, bias, stats, query_raw, key_raw, cosine, sine, qk_gain,
    query_out, key_out, value_out, gain_out,
    out_grad, query_grad, prompt_grads, own_grads, own, paired, from_x, from_y, mine, theirs,
    pair_sems, x_sems, y_sems, peer_sent, peer_got,
):
    rows, local = query_rot.shape
    width = attention_grad.shape[1]
    heads = local // HD
    factor = HD ** (-0.5)
    own_blocks = rows // PROMPT_DEV - 1
    devices = keys_values.shape[0] - own_blocks
    count = keys_values.shape[0] * PROMPT_DEV
    reach = devices * PROMPT_DEV
    plane = Plane(own, prompt_grads, paired, from_x, from_y, pair_sems, x_sems, y_sems, by_device=True)
    peers = Peers(mine, theirs, peer_sent, peer_got)
    greet(plane.neighbours() + peers.neighbours())
    out_grad[...] = turned_dot(attention_grad[...], w_out[...]).astype(jnp.bfloat16)
    for head in range(heads):
        columns = slice(head * HD, (head + 1) * HD)
        other = slice(local + head * HD, local + (head + 1) * HD)
        keys = keys_values[:, :, columns].reshape(count, HD)
        values = keys_values[:, :, other].reshape(count, HD)
        query, above = query_rot[:, columns], out_grad[:, columns]
        scores = turned_dot(query, keys) * factor + bias[...]
        shares = jnp.exp(scores - stats[:, 8 + head : 9 + head])
        share_grad = turned_dot(above, values)
        delta = jnp.sum(shares * share_grad, axis=1, keepdims=True)
        score_grad = (shares * (share_grad - delta)).astype(jnp.bfloat16)
        query_grad[:, columns] = wide_dot(score_grad, keys) * factor
        key_grad = crossed_dot(score_grad, query) * factor
        value_grad = crossed_dot(shares.astype(jnp.bfloat16), above)
        prompt_grads[:, :, columns] = key_grad[:reach].astype(jnp.bfloat16).reshape(devices, PROMPT_DEV, HD)
        prompt_grads[:, :, other] = value_grad[:reach].astype(jnp.bfloat16).reshape(devices, PROMPT_DEV, HD)
        own_grads[PROMPT_DEV:, columns] = key_grad[reach:]
        own_grads[PROMPT_DEV:, other] = value_grad[reach:]
    for chip in range(4):
        plane.pair_copy(chip).start()
    for chip in range(4):
        own[chip] = prompt_grads[plane.block(chip, plane.core)]
    for chip in range(4):
        plane.pair_copy(chip).wait_recv()
        if chip < 3:
            plane.send_first(chip)

    def normed_part(source, raw, row, scale):
        inner = jnp.zeros((rows, 1), jnp.float32)
        for head in range(heads):
            columns = slice(head * HD, (head + 1) * HD)
            grad = source[:, columns]
            grad = grad * cosine[...] - swapped(grad) * sine[...]
            gain_out[row : row + 1, columns] = jnp.sum(grad * raw[:, columns] * scale, axis=0, keepdims=True)
            grad = qk_gain[row : row + 1, columns] * grad
            source[:, columns] = grad
            inner = inner + jnp.sum(grad * raw[:, columns], axis=1, keepdims=True)
        return inner

    scale_query, scale_key = stats[:, 1:2], stats[:, 2:3]
    query_inner = normed_part(query_grad, query_raw, 0, scale_query)
    plane.send_second()

    def last(piece, carry):
        for side, summed in enumerate(plane.last_sum(piece)):
            own_grads[plane.rows(side, piece)] = summed
        return carry

    lax.fori_loop(0, plane.pieces, last, 0)
    key_inner = normed_part(own_grads, key_raw, 1, scale_key)
    mine[...] = to_rows([query_inner, key_inner], rows)
    peers.start()
    value_out[...] = own_grads[:, local:].astype(jnp.bfloat16)
    inner = to_columns(peers.total())
    for out, source, raw, scale, i in (
        (query_out, query_grad, query_raw, scale_query, 0),
        (key_out, own_grads, key_raw, scale_key, 1),
    ):
        pull = scale * scale * scale / width * inner[:, i : i + 1]
        out[...] = (scale * source[:, :local] - raw[...] * pull).astype(jnp.bfloat16)
    plane.finish()
    peers.finish()


def backward(attention_grad, w_out, query_rot, keys_values, bias, stats, query_raw, key_raw, cosine, sine, qk_gain):
    rows, local = query_rot.shape
    size = lax.axis_size("tensor")
    ranks = lax.axis_size("expert")
    low, full = jnp.bfloat16, jnp.float32
    vmem = pl.BlockSpec(memory_space=pltpu.VMEM)
    small = jax.ShapeDtypeStruct((rows, local), low)
    return pl.pallas_call(
        backward_kernel,
        out_shape=(small, small, small, jax.ShapeDtypeStruct((2, local), full)),
        in_specs=[vmem] * 11,
        out_specs=(vmem,) * 4,
        scratch_shapes=[
            pltpu.VMEM((rows, local), low),
            pltpu.VMEM((rows, local), full),
            pltpu.VMEM((ranks, PROMPT_DEV, 2 * local), low),
            pltpu.VMEM((rows, 2 * local), full),
            pltpu.VMEM((4, PROMPT_DEV, 2 * local), low),
            pltpu.VMEM((4, PROMPT_DEV, 2 * local), low),
            pltpu.VMEM((3, PROMPT_DEV // 2, 2 * local), low),
            pltpu.VMEM((3, PROMPT_DEV // 2, 2 * local), low),
            pltpu.VMEM((8, rows), full),
            pltpu.VMEM((size - 1, 8, rows), full),
            *Plane.semaphores(PROMPT_DEV),
            pltpu.SemaphoreType.DMA((size - 1,)),
            pltpu.SemaphoreType.DMA((size - 1,)),
        ],
        compiler_params=pltpu.CompilerParams(
            collective_id=3, has_side_effects=True, vmem_limit_bytes=60 * 2**20
        ),
    )(attention_grad, w_out, query_rot, keys_values, bias, stats, query_raw, key_raw, cosine, sine, qk_gain)


def rotate(field, cosine, sine):
    half = field.shape[-1] // 2
    first = field[..., :half]
    second = field[..., half:]
    return jnp.concatenate(
        [first * cosine - second * sine, second * cosine + first * sine], axis=-1
    )


def unrotate(grad, cosine, sine):
    half = grad.shape[-1] // 2
    first = grad[..., :half]
    second = grad[..., half:]
    return jnp.concatenate(
        [first * cosine + second * sine, second * cosine - first * sine], axis=-1
    )


def experts(normed_two, cotangent, gates, w_gate, w_up, w_down, experts_total):
    local_experts = w_gate.shape[0]
    device = lax.axis_index("expert")
    arrived = lax.all_gather(normed_two, "expert", axis=0, tiled=True)
    arrived_grad = lax.all_gather(cotangent, "expert", axis=0, tiled=True)
    gate_pre = jnp.einsum("rd,jdf->jrf", arrived, w_gate, preferred_element_type=jnp.float32)
    up_pre = jnp.einsum("rd,jdf->jrf", arrived, w_up, preferred_element_type=jnp.float32)
    raw_grad = jnp.einsum("rd,jfd->jrf", arrived_grad, w_down, preferred_element_type=jnp.float32)
    sigma = jax.nn.sigmoid(gate_pre)
    activated = gate_pre * sigma
    inner = activated * up_pre
    gated = (gates[:, :, None] * inner).astype(jnp.bfloat16)
    mixed_part = jnp.einsum("jrf,jfd->rd", gated, w_down, preferred_element_type=jnp.float32)
    mixture = lax.psum(
        lax.psum_scatter(
            mixed_part.astype(jnp.bfloat16), "expert", scatter_dimension=0, tiled=True
        ),
        "tensor",
    ).astype(jnp.float32)
    gate_grad_part = jnp.sum(raw_grad * inner, axis=2)
    act_grad = gates[:, :, None] * raw_grad
    up_grad = (act_grad * activated).astype(jnp.bfloat16)
    gate_grad = (act_grad * up_pre * sigma * (1.0 + gate_pre * (1.0 - sigma))).astype(jnp.bfloat16)
    grad_w_down = jnp.einsum("jrf,rd->jfd", gated, arrived_grad, preferred_element_type=jnp.float32)
    grad_w_gate = jnp.einsum("rd,jrf->jdf", arrived, gate_grad, preferred_element_type=jnp.float32)
    grad_w_up = jnp.einsum("rd,jrf->jdf", arrived, up_grad, preferred_element_type=jnp.float32)
    slot_grad = jnp.einsum("jrf,jdf->rd", gate_grad, w_gate, preferred_element_type=jnp.float32)
    slot_grad = slot_grad + jnp.einsum(
        "jrf,jdf->rd", up_grad, w_up, preferred_element_type=jnp.float32
    )
    moe_input_grad = lax.psum(
        lax.psum_scatter(
            slot_grad.astype(jnp.bfloat16), "expert", scatter_dimension=0, tiled=True
        ),
        "tensor",
    ).astype(jnp.float32)
    placed = jnp.zeros((arrived.shape[0], experts_total), jnp.float32)
    placed = lax.dynamic_update_slice_in_dim(placed, gate_grad_part.T, device * local_experts, 1)
    chance_grad = lax.psum(
        lax.psum_scatter(placed, "expert", scatter_dimension=0, tiled=True), "tensor"
    )
    return mixture, moe_input_grad, chance_grad, [grad_w_gate, grad_w_up, grad_w_down]


def body(
    tokens,
    w_query,
    w_key,
    w_value,
    w_out,
    attn_gain,
    ffn_gain,
    qk_gain,
    router,
    w_gate,
    w_up,
    w_down,
    routes,
    cont_group,
    cotangent,
):
    rows, width = tokens.shape
    local_width = w_query.shape[1]
    head_count = local_width // HD
    experts_total = router.shape[1]
    local_experts = w_gate.shape[0]
    ranks = lax.axis_size("expert")
    device = lax.axis_index("expert")
    span = ranks // 2
    prompt_len = PROMPT_DEV * span
    factor = HD ** (-0.5)
    local = jnp.arange(rows, dtype=jnp.int32)
    is_prompt = local < PROMPT_DEV
    after = jnp.maximum(local - PROMPT_DEV, 0)
    slot_cont = after // CLEN
    cont_pick = jnp.sum(
        jnp.where(
            slot_cont[:, None] == jnp.arange(CONT_DEV, dtype=jnp.int32)[None, :],
            cont_group[None, :],
            0,
        ),
        axis=1,
    )
    group = jnp.where(is_prompt, device // span, cont_pick)
    position = jnp.where(is_prompt, device % span * PROMPT_DEV + local, prompt_len + after % CLEN)
    tag = jnp.where(is_prompt, -1, slot_cont)
    frequency = 10000.0 ** (-jnp.arange(HD // 2, dtype=jnp.float32) * 2.0 / HD)
    angle = position.astype(jnp.float32)[:, None] * frequency[None, :]
    cosine = jnp.cos(angle)[:, None, :]
    sine = jnp.sin(angle)[:, None, :]
    source = tokens.astype(jnp.float32)
    scale_one = lax.rsqrt(jnp.mean(source * source, axis=1, keepdims=True) + epsilon)
    normed = (source * scale_one * attn_gain).astype(jnp.bfloat16)
    query_raw = jnp.dot(normed, w_query, preferred_element_type=jnp.float32)
    key_raw = jnp.dot(normed, w_key, preferred_element_type=jnp.float32)
    value_raw = jnp.dot(normed, w_value, preferred_element_type=jnp.float32)
    squares = lax.psum(
        jnp.stack(
            [jnp.sum(query_raw * query_raw, axis=1), jnp.sum(key_raw * key_raw, axis=1)], axis=1
        ),
        "tensor",
    )
    scale_query = lax.rsqrt(squares[:, 0:1] / width + epsilon)
    scale_key = lax.rsqrt(squares[:, 1:2] / width + epsilon)
    query_rot = (
        rotate((query_raw * scale_query * qk_gain[0]).reshape(rows, head_count, HD), cosine, sine)
        .reshape(rows, local_width)
        .astype(jnp.bfloat16)
    )
    key_rot = (
        rotate((key_raw * scale_key * qk_gain[1]).reshape(rows, head_count, HD), cosine, sine)
        .reshape(rows, local_width)
        .astype(jnp.bfloat16)
    )
    value_low = value_raw.astype(jnp.bfloat16)
    prompt_keys, prompt_values = (
        lax.all_gather(key_rot[:PROMPT_DEV], "expert", axis=0, tiled=True),
        lax.all_gather(value_low[:PROMPT_DEV], "expert", axis=0, tiled=True),
    )
    prompt_count = prompt_keys.shape[0]
    all_keys = jnp.concatenate([prompt_keys, key_rot[PROMPT_DEV:]], axis=0)
    all_values = jnp.concatenate([prompt_values, value_low[PROMPT_DEV:]], axis=0)
    key_index = jnp.arange(prompt_count, dtype=jnp.int32)
    prompt_mask = (group[:, None] == (key_index // prompt_len)[None, :]) & (
        (key_index % prompt_len)[None, :] <= position[:, None]
    )
    own_mask = (tag[:, None] == tag[None, PROMPT_DEV:]) & (
        position[None, PROMPT_DEV:] <= position[:, None]
    )
    mask = jnp.concatenate([prompt_mask, own_mask], axis=1)

    def head_scores(query_head, key_head):
        scores = (
            jnp.einsum("qd,kd->qk", query_head, key_head, preferred_element_type=jnp.float32)
            * factor
        )
        return jnp.where(mask, scores, masked_value)

    outputs = []
    log_totals = []
    for head in range(head_count):
        start = head * HD
        scores = head_scores(query_rot[:, start : start + HD], all_keys[:, start : start + HD])
        top = jnp.max(scores, axis=1, keepdims=True)
        weights = jnp.exp(scores - top)
        total = jnp.sum(weights, axis=1, keepdims=True)
        shares = (weights / total).astype(jnp.bfloat16)
        outputs.append(
            jnp.dot(shares, all_values[:, start : start + HD], preferred_element_type=jnp.float32)
        )
        log_totals.append(top + jnp.log(total))
    attended = jnp.concatenate(outputs, axis=1).astype(jnp.bfloat16)
    attention = lax.psum(jnp.dot(attended, w_out, preferred_element_type=jnp.float32), "tensor")
    hidden = source + attention
    scale_two = lax.rsqrt(jnp.mean(hidden * hidden, axis=1, keepdims=True) + epsilon)
    normed_two = (hidden * scale_two * ffn_gain).astype(jnp.bfloat16)
    logits = jnp.dot(normed_two, router, preferred_element_type=jnp.float32)
    top = jnp.max(logits, axis=1, keepdims=True)
    weights = jnp.exp(logits - top)
    chances = weights / jnp.sum(weights, axis=1, keepdims=True)
    hits = (routes[:, :, None] == jnp.arange(experts_total, dtype=jnp.int32)[None, None, :]).astype(
        jnp.float32
    )
    rows_mask = jnp.sum(hits, axis=1)
    routed = lax.all_gather(
        (rows_mask * chances).astype(jnp.float32), "expert", axis=0, tiled=True
    )
    gates = lax.dynamic_slice_in_dim(routed, device * local_experts, local_experts, 1).T
    grad_out = cotangent.astype(jnp.float32)
    pieces = max(1, ranks * rows // 4096)
    piece = rows // pieces
    split_gates = gates.reshape(local_experts, ranks, rows)
    results = []
    weight_grads = None
    for number in range(pieces):
        part = slice(number * piece, (number + 1) * piece)
        sources = (normed_two[part], cotangent[part])
        if results:
            sources, results, weight_grads = lax.optimization_barrier(
                (sources, results, weight_grads)
            )
        *result, grads = experts(
            *sources,
            split_gates[:, :, part].reshape(local_experts, ranks * piece),
            w_gate,
            w_up,
            w_down,
            experts_total,
        )
        results.append(result)
        weight_grads = grads if weight_grads is None else [a + b for a, b in zip(weight_grads, grads)]
    mixture, moe_input_grad, chance_grad = (
        jnp.concatenate(list(group_of), axis=0) for group_of in zip(*results)
    )
    grad_w_gate, grad_w_up, grad_w_down = weight_grads
    chance_grad = rows_mask * chance_grad
    output = (hidden + mixture).astype(jnp.bfloat16)
    logit_grad = (
        chances * (chance_grad - jnp.sum(chances * chance_grad, axis=1, keepdims=True))
    ).astype(jnp.bfloat16)
    grad_router = jnp.einsum(
        "td,te->de", normed_two, logit_grad, preferred_element_type=jnp.float32
    )
    normed_two_grad = moe_input_grad + jnp.einsum(
        "te,de->td", logit_grad, router, preferred_element_type=jnp.float32
    )
    weighted_two = ffn_gain * normed_two_grad
    grad_ffn_gain = jnp.sum(normed_two_grad * hidden * scale_two, axis=0)
    hidden_grad = (
        grad_out
        + scale_two * weighted_two
        - hidden * (scale_two**3 / width) * jnp.sum(weighted_two * hidden, axis=1, keepdims=True)
    )
    attention_grad = hidden_grad.astype(jnp.bfloat16)
    grad_w_out = jnp.einsum(
        "td,te->de", attended, attention_grad, preferred_element_type=jnp.float32
    )
    attended_grad = jnp.einsum(
        "te,de->td", attention_grad, w_out, preferred_element_type=jnp.float32
    ).astype(jnp.bfloat16)
    query_grads = []
    key_grads = []
    value_grads = []
    for head in range(head_count):
        start = head * HD
        query_head = query_rot[:, start : start + HD]
        key_head = all_keys[:, start : start + HD]
        value_head = all_values[:, start : start + HD]
        out_grad_head = attended_grad[:, start : start + HD]
        recomputed = jnp.exp(head_scores(query_head, key_head) - log_totals[head])
        share_grad = jnp.einsum(
            "qd,kd->qk", out_grad_head, value_head, preferred_element_type=jnp.float32
        )
        delta = jnp.sum(recomputed * share_grad, axis=1, keepdims=True)
        score_grad = (recomputed * (share_grad - delta)).astype(jnp.bfloat16)
        query_grads.append(
            jnp.dot(score_grad, key_head, preferred_element_type=jnp.float32) * factor
        )
        key_grads.append(
            jnp.einsum("qk,qd->kd", score_grad, query_head, preferred_element_type=jnp.float32)
            * factor
        )
        value_grads.append(
            jnp.einsum(
                "qk,qd->kd",
                recomputed.astype(jnp.bfloat16),
                out_grad_head,
                preferred_element_type=jnp.float32,
            )
        )
    key_grad_all = jnp.concatenate(key_grads, axis=1)
    value_grad_all = jnp.concatenate(value_grads, axis=1)
    prompt_key_grad, prompt_value_grad = (
        lax.psum_scatter(
            key_grad_all[:prompt_count].astype(jnp.bfloat16),
            "expert",
            scatter_dimension=0,
            tiled=True,
        ).astype(jnp.float32),
        lax.psum_scatter(
            value_grad_all[:prompt_count].astype(jnp.bfloat16),
            "expert",
            scatter_dimension=0,
            tiled=True,
        ).astype(jnp.float32),
    )
    key_grad = jnp.concatenate([prompt_key_grad, key_grad_all[prompt_count:]], axis=0)
    value_grad = jnp.concatenate([prompt_value_grad, value_grad_all[prompt_count:]], axis=0)
    query_grad = unrotate(
        jnp.concatenate(query_grads, axis=1).reshape(rows, head_count, HD), cosine, sine
    ).reshape(rows, local_width)
    key_grad = unrotate(key_grad.reshape(rows, head_count, HD), cosine, sine).reshape(
        rows, local_width
    )
    grad_qk_gain = jnp.stack(
        [
            jnp.sum(query_grad * query_raw * scale_query, axis=0),
            jnp.sum(key_grad * key_raw * scale_key, axis=0),
        ],
        axis=0,
    )
    weighted_query = qk_gain[0] * query_grad
    weighted_key = qk_gain[1] * key_grad
    inner_sums = lax.psum(
        jnp.stack(
            [jnp.sum(weighted_query * query_raw, axis=1), jnp.sum(weighted_key * key_raw, axis=1)],
            axis=1,
        ),
        "tensor",
    )
    query_raw_grad = (
        scale_query * weighted_query - query_raw * (scale_query**3 / width) * inner_sums[:, 0:1]
    ).astype(jnp.bfloat16)
    key_raw_grad = (
        scale_key * weighted_key - key_raw * (scale_key**3 / width) * inner_sums[:, 1:2]
    ).astype(jnp.bfloat16)
    value_raw_grad = value_grad.astype(jnp.bfloat16)
    grad_w_query = jnp.einsum(
        "td,te->de", normed, query_raw_grad, preferred_element_type=jnp.float32
    )
    grad_w_key = jnp.einsum("td,te->de", normed, key_raw_grad, preferred_element_type=jnp.float32)
    grad_w_value = jnp.einsum(
        "td,te->de", normed, value_raw_grad, preferred_element_type=jnp.float32
    )
    normed_part = jnp.einsum(
        "te,de->td", query_raw_grad, w_query, preferred_element_type=jnp.float32
    )
    normed_part = normed_part + jnp.einsum(
        "te,de->td", key_raw_grad, w_key, preferred_element_type=jnp.float32
    )
    normed_part = normed_part + jnp.einsum(
        "te,de->td", value_raw_grad, w_value, preferred_element_type=jnp.float32
    )
    normed_grad = lax.psum(normed_part.astype(jnp.bfloat16), "tensor").astype(jnp.float32)
    weighted_one = attn_gain * normed_grad
    grad_attn_gain = jnp.sum(normed_grad * source * scale_one, axis=0)
    input_grad = (
        hidden_grad
        + scale_one * weighted_one
        - source * (scale_one**3 / width) * jnp.sum(weighted_one * source, axis=1, keepdims=True)
    )
    summed = (
        lax.psum_scatter(
            grad_w_query.astype(jnp.bfloat16), "expert", scatter_dimension=0, tiled=True
        ).astype(jnp.float32),
        lax.psum_scatter(
            grad_w_key.astype(jnp.bfloat16), "expert", scatter_dimension=0, tiled=True
        ).astype(jnp.float32),
        lax.psum_scatter(
            grad_w_value.astype(jnp.bfloat16), "expert", scatter_dimension=0, tiled=True
        ).astype(jnp.float32),
        lax.psum_scatter(
            grad_w_out.astype(jnp.bfloat16), "expert", scatter_dimension=1, tiled=True
        ).astype(jnp.float32),
        lax.psum_scatter(
            grad_attn_gain.astype(jnp.bfloat16), "expert", scatter_dimension=0, tiled=True
        ).astype(jnp.float32),
        lax.psum_scatter(
            grad_ffn_gain.astype(jnp.bfloat16), "expert", scatter_dimension=0, tiled=True
        ).astype(jnp.float32),
        lax.psum_scatter(
            grad_qk_gain.astype(jnp.bfloat16), "expert", scatter_dimension=1, tiled=True
        ).astype(jnp.float32),
        lax.psum_scatter(
            grad_router.astype(jnp.bfloat16), "expert", scatter_dimension=0, tiled=True
        ).astype(jnp.float32),
    )
    return (
        output,
        input_grad,
        summed[0],
        summed[1],
        summed[2],
        summed[3],
        summed[4],
        summed[5],
        summed[6],
        summed[7],
        grad_w_gate,
        grad_w_up,
        grad_w_down,
    )


def compact(
    tokens, w_query, w_key, w_value, w_out, attn_gain, ffn_gain, qk_gain, router, w_gate, w_up, w_down,
    routes, cont_group, cotangent,
):
    rows, width = tokens.shape
    local_width = w_query.shape[1]
    head_count = local_width // HD
    experts_total = router.shape[1]
    local_experts = w_gate.shape[0]
    ranks = lax.axis_size("expert")
    device = lax.axis_index("expert")
    full = jnp.float32
    group, position, tag = layout(rows, ranks, device, cont_group)
    frequency = 10000.0 ** (-jnp.arange(HD // 2, dtype=full) * 2.0 / HD)
    angle = position.astype(full)[:, None] * frequency[None, :]
    cosine, sine = jnp.cos(angle), jnp.sin(angle)
    cosine = jnp.concatenate([cosine, cosine], axis=1)
    sine = jnp.concatenate([-sine, sine], axis=1)
    bias = jnp.where(attention_mask(group, position, tag, ranks), 0.0, masked_value).astype(full)
    own_first = jnp.roll(router, -device * local_experts, axis=1)
    own_first = jnp.pad(own_first, ((0, 0), (0, LANE - experts_total)))
    expert_bias = jnp.where(jnp.arange(LANE) < experts_total, 0.0, masked_value).astype(full)[None]
    turned_routes = jnp.tile(jnp.pad(routes.T, ((0, -routes.shape[1] % 8), (0, 0)), constant_values=-1), (2, 1))
    hits = routes[:, :, None] == jnp.arange(experts_total, dtype=jnp.int32)
    routed = jnp.any(hits, axis=1).astype(full)
    (
        attention, normed, normed_two, attended, query_rot, keys_values, query_raw, key_raw, stats, routes_all, arrived,
    ) = front(
        tokens, attn_gain[None], ffn_gain[None], w_query, w_key, w_value, w_out, qk_gain, cosine, sine, bias,
        turned_routes,
    )
    arrived_grad = lax.all_gather(cotangent, "expert", axis=0)
    own_expert = device * local_experts + jnp.arange(local_experts, dtype=jnp.int32)
    names = routes_all[:, : turned_routes.shape[0] // 2]
    expert_mask = jnp.any(names[:, :, :, None] == own_expert, axis=1).astype(full)
    expert_mask = jnp.pad(expert_mask, ((0, 0), (0, 0), (0, LANE - local_experts)))
    reduced, gated, gate_grad, up_grad, mixed_part = experts_fused(
        arrived, arrived_grad, expert_mask, own_first, expert_bias, w_gate, w_up, w_down
    )
    source = tokens.astype(full)
    hidden = source + attention.astype(full)
    scale_one, scale_two = stats[:, 0:1], stats[:, 3:4]
    logits = jnp.dot(normed_two, router, preferred_element_type=full)
    weights = jnp.exp(logits - jnp.max(logits, axis=1, keepdims=True))
    chances = weights / jnp.sum(weights, axis=1, keepdims=True)
    chance_grad = routed * reduced[:, width : width + experts_total].astype(full)
    logit_grad = (
        chances * (chance_grad - jnp.sum(chances * chance_grad, axis=1, keepdims=True))
    ).astype(jnp.bfloat16)
    grad_router = jnp.einsum("td,te->de", normed_two, logit_grad, preferred_element_type=full)
    normed_two_grad = reduced[:, :width].astype(full) + jnp.einsum(
        "te,de->td", logit_grad, router, preferred_element_type=full
    )
    grad_out = cotangent.astype(full)
    weighted_two = ffn_gain * normed_two_grad
    grad_ffn_gain = jnp.sum(normed_two_grad * hidden * scale_two, axis=0)
    hidden_grad = (
        grad_out
        + scale_two * weighted_two
        - hidden * (scale_two**3 / width) * jnp.sum(weighted_two * hidden, axis=1, keepdims=True)
    )
    attention_grad = hidden_grad.astype(jnp.bfloat16)
    query_raw_grad, key_raw_grad, value_raw_grad, grad_qk_gain = backward(
        attention_grad, w_out, query_rot, keys_values, bias, stats, query_raw, key_raw, cosine, sine, qk_gain
    )
    small_part = local_width // ranks
    share = width // ranks
    gains = jnp.pad(
        grad_qk_gain.reshape(2, ranks, small_part).transpose(1, 2, 0), ((0, 0), (0, share - small_part), (0, 0))
    )
    extras = jnp.concatenate(
        [grad_router.reshape(ranks, share, experts_total), grad_ffn_gain.reshape(ranks, share, 1), gains], axis=2
    ).astype(jnp.bfloat16)
    extras = jnp.pad(extras, ((0, 0), (0, 0), (0, LANE - experts_total - 3)))
    normed_grad, sums, gain_total, mixture, grad_w_gate, grad_w_up, grad_w_down = closing(
        normed, query_raw_grad, key_raw_grad, value_raw_grad, attended, attention_grad, extras, w_query, w_key, w_value,
        mixed_part, arrived, arrived_grad, gated, gate_grad, up_grad, local_experts, experts_total + 3,
    )
    normed_grad = normed_grad.astype(full)
    output = (hidden + mixture.astype(full)).astype(jnp.bfloat16)
    weighted_one = attn_gain * normed_grad
    input_grad = (
        hidden_grad
        + scale_one * weighted_one
        - source * (scale_one**3 / width) * jnp.sum(weighted_one * source, axis=1, keepdims=True)
    )
    edge = 4 * local_width
    return (
        output,
        input_grad,
        sums[:, :local_width],
        sums[:, local_width : 2 * local_width],
        sums[:, 2 * local_width : 3 * local_width],
        sums[:, 3 * local_width : edge].T,
        gain_total[0] / lax.dynamic_slice_in_dim(attn_gain, device * share, share),
        sums[:, edge + experts_total],
        sums[:small_part, edge + experts_total + 1 : edge + experts_total + 3].T,
        sums[:, edge : edge + experts_total],
        grad_w_gate,
        grad_w_up,
        grad_w_down,
    )


def layout(rows, ranks, device, cont_group):
    span = ranks // 2
    prompt_len = PROMPT_DEV * span
    local = jnp.arange(rows, dtype=jnp.int32)
    is_prompt = local < PROMPT_DEV
    after = jnp.maximum(local - PROMPT_DEV, 0)
    slot_cont = after // CLEN
    cont_pick = jnp.sum(
        jnp.where(
            slot_cont[:, None] == jnp.arange(CONT_DEV, dtype=jnp.int32)[None, :], cont_group[None, :], 0
        ),
        axis=1,
    )
    group = jnp.where(is_prompt, device // span, cont_pick)
    position = jnp.where(is_prompt, device % span * PROMPT_DEV + local, prompt_len + after % CLEN)
    tag = jnp.where(is_prompt, -1, slot_cont)
    return group, position, tag


def attention_mask(group, position, tag, ranks):
    prompt_len = PROMPT_DEV * (ranks // 2)
    key_index = jnp.arange(ranks * PROMPT_DEV, dtype=jnp.int32)
    prompt_mask = (group[:, None] == (key_index // prompt_len)[None, :]) & (
        (key_index % prompt_len)[None, :] <= position[:, None]
    )
    own_mask = (tag[:, None] == tag[None, PROMPT_DEV:]) & (
        position[None, PROMPT_DEV:] <= position[:, None]
    )
    return jnp.concatenate([prompt_mask, own_mask], axis=1)


def solution(mesh):
    small = mesh.shape["expert"] == 8
    return jax.shard_map(
        compact if small else body,
        mesh=mesh,
        in_specs=(
            P("expert", None),
            P(None, "tensor"),
            P(None, "tensor"),
            P(None, "tensor"),
            P("tensor", None),
            P(),
            P(),
            P(None, "tensor"),
            P(),
            P("expert", None, "tensor"),
            P("expert", None, "tensor"),
            P("expert", "tensor", None),
            P("expert", None),
            P("expert"),
            P("expert", None),
        ),
        out_specs=(
            P("expert", None),
            P("expert", None),
            P("expert", "tensor"),
            P("expert", "tensor"),
            P("expert", "tensor"),
            P("tensor", "expert"),
            P("expert"),
            P("expert"),
            P(None, ("tensor", "expert")),
            P("expert", None),
            P("expert", None, "tensor"),
            P("expert", None, "tensor"),
            P("expert", "tensor", None),
        ),
        check_vma=False,
    )
```

```python
import functools

import jax
import jax.numpy as jnp
from jax import lax
from jax.experimental import pallas as pl
from jax.experimental.pallas import tpu as pltpu
from jax.sharding import PartitionSpec as P

HD = 128
PROMPT_DEV = 128
CLEN = 256
CONT_DEV = 1


epsilon = 1e-05
masked_value = -1e30


MESH = pl.DeviceIdType.MESH
STEP = 16
LANE = 128


def remote(source, target, sent, received, **where):
    return pltpu.make_async_remote_copy(
        src_ref=source,
        dst_ref=target,
        send_sem=sent,
        recv_sem=received,
        device_id=where,
        device_id_type=MESH,
    )


def greet(places):
    barrier = pltpu.get_barrier_semaphore()
    for condition, where in places:
        def signal(where=where):
            pl.semaphore_signal(barrier, inc=1, device_id=where, device_id_type=MESH)
        if condition is None:
            signal()
        else:
            pl.when(condition)(signal)
    count = 0
    for condition, _ in places:
        count = count + (1 if condition is None else jnp.where(condition, 1, 0))
    pl.semaphore_wait(barrier, count)


class Line:
    def __init__(self, own, arrived, spare, total, sems, step=STEP):
        self.step = step
        self.own, self.arrived, self.spare, self.total = own, arrived, spare, total
        self.up_sent, self.far_got, self.near_got, self.far_sent, self.near_sent, self.down_got = (
            sems.at[i] for i in range(6)
        )
        self.size = lax.axis_size("tensor")
        self.here = lax.axis_index("tensor")
        self.root = self.size // 2 - 1
        self.rise_steps = self.size - 1 - self.root
        self.trip = 2 * self.rise_steps
        self.half = own.shape[0] // 2
        self.pieces = self.half // step

    @staticmethod
    def semaphores(rows, step=STEP):
        return pltpu.SemaphoreType.DMA((6, 2, rows // 2 // step))

    @staticmethod
    def spare_shape(rows, width):
        return pltpu.VMEM((rows // 2, width), jnp.bfloat16)

    def neighbours(self):
        here, size = self.here, self.size
        return [
            (here > 0, {"tensor": jnp.maximum(here - 1, 0)}),
            (here < size - 1, {"tensor": jnp.minimum(here + 1, size - 1)}),
        ]

    def place(self, lane):
        return self.here if lane == 0 else self.size - 1 - self.here

    def device(self, lane, place):
        return place if lane == 0 else self.size - 1 - place

    def rows(self, lane, piece):
        return pl.ds(pl.multiple_of(lane * self.half + piece * self.step, self.step), self.step)

    def landing(self, piece):
        return pl.ds(pl.multiple_of(piece * self.step, self.step), self.step)

    def far_up(self, lane, piece):
        rows, place = self.rows(lane, piece), self.place(lane)
        inward = jnp.where(place > self.root, place - 1, place + 1)
        return remote(
            self.own.at[rows], self.arrived.at[rows],
            self.up_sent.at[lane, piece], self.far_got.at[lane, piece], tensor=self.device(lane, inward),
        )

    def near_up(self, lane, piece):
        return remote(
            self.own.at[self.rows(lane, piece)], self.spare.at[self.landing(piece)],
            self.up_sent.at[lane, piece], self.near_got.at[lane, piece], tensor=self.device(lane, self.root),
        )

    def down(self, lane, piece, away):
        rows = self.rows(lane, piece)
        sent = self.far_sent if away == 1 else self.near_sent
        return remote(
            self.total.at[rows], self.total.at[rows],
            sent.at[lane, piece], self.down_got.at[lane, piece], tensor=self.device(lane, self.place(lane) + away),
        )

    def rise(self, lane, piece):
        place, root = self.place(lane), self.root
        rows = self.rows(lane, piece)

        def value(field):
            return field.astype(jnp.float32)

        @pl.when((place > root) & (place < self.size - 1) | (place > 0) & (place < root))
        def _():
            self.far_up(lane, piece).wait_recv()
            self.own[rows] = (value(self.own[rows]) + value(self.arrived[rows])).astype(jnp.bfloat16)

        @pl.when(place == root)
        def _():
            self.far_up(lane, piece).wait_recv()
            summed = value(self.own[rows]) + value(self.arrived[rows])
            if root > 0:
                self.near_up(lane, piece).wait_recv()
                summed = summed + value(self.spare[self.landing(piece)])
            self.total[rows] = summed.astype(jnp.bfloat16)
            self.down(lane, piece, 1).start()
            if root > 0:
                self.down(lane, piece, -1).start()

        if root > 0:

            @pl.when(place == root - 1)
            def _():
                self.near_up(lane, piece).start()

        @pl.when((place > root) | (place < root - 1))
        def _():
            self.far_up(lane, piece).start()

    def fall(self, lane, piece):
        place, root = self.place(lane), self.root

        @pl.when(place != root)
        def _():
            self.down(lane, piece, 1).wait_recv()

        @pl.when((place > root) & (place < self.size - 1))
        def _():
            self.down(lane, piece, 1).start()

        @pl.when((place > 0) & (place < root))
        def _():
            self.down(lane, piece, -1).start()

    def advance(self, step):
        for lane in range(2):
            place = self.place(lane)
            steps_in = self.rise_steps - jnp.abs(place - self.root)
            piece = step - steps_in

            @pl.when((piece >= 0) & (piece < self.pieces))
            def _():
                self.rise(lane, piece)

        for lane in range(2):
            place = self.place(lane)
            piece = step - self.rise_steps - jnp.abs(place - self.root)

            @pl.when((piece >= 0) & (piece < self.pieces))
            def _():
                self.fall(lane, piece)

    def step_body(self, step, carry):
        self.advance(step)
        return carry

    def steps(self):
        return self.pieces + self.trip

    def finish(self):
        def one(piece, carry):
            for lane in range(2):
                place, root = self.place(lane), self.root

                @pl.when(place != root)
                def _():
                    self.far_up(lane, piece).wait_send()

                @pl.when((place >= root) & (place < self.size - 1))
                def _():
                    self.down(lane, piece, 1).wait_send()

                @pl.when((place <= root) & (place > 0))
                def _():
                    self.down(lane, piece, -1).wait_send()
            return carry

        lax.fori_loop(0, self.pieces, one, 0)


class Place:
    def __init__(self):
        here = lax.axis_index("expert")
        self.here = here
        self.core, self.x, self.y = here % 2, here // 2 % 2, here // 4
        self.sibling = here + 1 - 2 * self.core
        self.x_chip = here + 2 - 4 * self.x
        self.y_chip = here + 4 - 8 * self.y

    def neighbours(self):
        return [(None, {"expert": i}) for i in (self.sibling, self.x_chip, self.y_chip)]

    def block(self, chip, core):
        x = self.x + (1 - chip // 2) * (1 - 2 * self.x)
        y = self.y + (1 - chip % 2) * (1 - 2 * self.y)
        return 4 * y + 2 * x + core


class Plane(Place):
    def __init__(self, own, spare, paired, from_x, from_y, pair_sems, x_sems, y_sems, by_device=False, step=STEP):
        self.step = step
        self.by_device = by_device
        self.own, self.spare, self.paired, self.from_x, self.from_y = own, spare, paired, from_x, from_y
        self.pair_sems, self.x_sems, self.y_sems = pair_sems, x_sems, y_sems
        super().__init__()
        self.half = own.shape[1] // 2
        self.pieces = self.half // step

    @staticmethod
    def semaphores(rows, step=STEP):
        pieces = rows // 2 // step
        return [
            pltpu.SemaphoreType.DMA((2, 4)),
            pltpu.SemaphoreType.DMA((2, 3, pieces)),
            pltpu.SemaphoreType.DMA((2, 3, pieces)),
        ]

    def pair_copy(self, chip):
        place = self.block(chip, 1 - self.core) if self.by_device else chip
        return remote(
            self.spare.at[place], self.paired.at[chip],
            self.pair_sems.at[0, chip], self.pair_sems.at[1, chip], expert=self.sibling,
        )

    def rows(self, side, piece):
        return pl.ds(pl.multiple_of(side * self.half + piece * self.step, self.step), self.step)

    def landing(self, piece):
        return pl.ds(pl.multiple_of(piece * self.step, self.step), self.step)

    def x_copy(self, kind, piece):
        chip, side = ((0, 0), (1, 0), (1, 1))[kind]
        return remote(
            self.own.at[chip, self.rows(side, piece)], self.from_x.at[kind, self.landing(piece)],
            self.x_sems.at[0, kind, piece], self.x_sems.at[1, kind, piece], expert=self.x_chip,
        )

    def y_copy(self, kind, piece):
        chip, side = ((0, 1), (2, 1), (2, 0))[kind]
        return remote(
            self.own.at[chip, self.rows(side, piece)], self.from_y.at[kind, self.landing(piece)],
            self.y_sems.at[0, kind, piece], self.y_sems.at[1, kind, piece], expert=self.y_chip,
        )

    def add_pair(self, chip, side, piece):
        rows = self.rows(side, piece)
        self.own[chip, rows] = (
            self.own[chip, rows].astype(jnp.float32) + self.paired[chip, rows].astype(jnp.float32)
        ).astype(jnp.bfloat16)

    def each(self, step):
        def one(piece, carry):
            step(piece)
            return carry

        lax.fori_loop(0, self.pieces, one, 0)

    def send_first(self, chip):
        def step(piece):
            if chip in (0, 1):
                self.add_pair(chip, 0, piece)
                self.x_copy(chip, piece).start()
            if chip in (0, 2):
                self.add_pair(chip, 1, piece)
                self.y_copy(chip // 2, piece).start()

        self.each(step)

    def first_piece(self, piece):
        for chip, side in ((0, 0), (0, 1), (1, 0), (2, 1)):
            self.add_pair(chip, side, piece)
        for kind in range(2):
            self.x_copy(kind, piece).start()
            self.y_copy(kind, piece).start()

    def second_piece(self, piece):
        landed = self.landing(piece)
        self.y_copy(0, piece).wait_recv()
        rows = self.rows(1, piece)
        self.own[1, rows] = (
            self.own[1, rows].astype(jnp.float32)
            + self.paired[1, rows].astype(jnp.float32)
            + self.from_y[0, landed].astype(jnp.float32)
        ).astype(jnp.bfloat16)
        self.x_copy(2, piece).start()
        self.x_copy(0, piece).wait_recv()
        rows = self.rows(0, piece)
        self.own[2, rows] = (
            self.own[2, rows].astype(jnp.float32)
            + self.paired[2, rows].astype(jnp.float32)
            + self.from_x[0, landed].astype(jnp.float32)
        ).astype(jnp.bfloat16)
        self.y_copy(2, piece).start()

    def send_second(self):
        self.each(self.second_piece)

    def last_sum(self, piece):
        landed = self.landing(piece)
        sums = []
        for side in range(2):
            first, second = (self.x_copy(1, piece), self.y_copy(2, piece)) if side == 0 else (self.y_copy(1, piece), self.x_copy(2, piece))
            first.wait_recv()
            second.wait_recv()
            a, b = (self.from_x[1, landed], self.from_y[2, landed]) if side == 0 else (self.from_y[1, landed], self.from_x[2, landed])
            rows = self.rows(side, piece)
            sums.append(
                self.own[3, rows].astype(jnp.float32)
                + self.paired[3, rows].astype(jnp.float32)
                + a.astype(jnp.float32)
                + b.astype(jnp.float32)
            )
        return sums

    def finish(self):
        for chip in range(4):
            self.pair_copy(chip).wait_send()

        def step(piece):
            for kind in range(3):
                self.x_copy(kind, piece).wait_send()
                self.y_copy(kind, piece).wait_send()

        self.each(step)


class Gather:
    def __init__(self, source, target, place, x_sems, y_sems, far_sems, pair_sems, own_sem, pieces):
        self.source, self.target = source, target
        self.place = place
        self.x_sems, self.y_sems, self.far_sems, self.pair_sems, self.own_sem = x_sems, y_sems, far_sems, pair_sems, own_sem
        self.pieces = pieces
        self.rows_each = source.shape[0] // pieces

    @staticmethod
    def semaphores(pieces):
        return [
            pltpu.SemaphoreType.DMA((2, pieces)),
            pltpu.SemaphoreType.DMA((2, pieces)),
            pltpu.SemaphoreType.DMA((2, pieces)),
            pltpu.SemaphoreType.DMA((2, 4, pieces)),
            pltpu.SemaphoreType.DMA,
        ]

    def rows(self, piece):
        return pl.ds(piece * self.rows_each, self.rows_each)

    def own_copy(self):
        return pltpu.make_async_copy(self.source, self.target.at[self.place.here], self.own_sem)

    def x_copy(self, piece):
        rows = self.rows(piece)
        return remote(
            self.source.at[rows], self.target.at[self.place.here, rows],
            self.x_sems.at[0, piece], self.x_sems.at[1, piece], expert=self.place.x_chip,
        )

    def y_copy(self, piece):
        rows = self.rows(piece)
        return remote(
            self.source.at[rows], self.target.at[self.place.here, rows],
            self.y_sems.at[0, piece], self.y_sems.at[1, piece], expert=self.place.y_chip,
        )

    def far_copy(self, piece):
        rows = self.rows(piece)
        came, goes = (
            (self.place.x_chip, self.place.y_chip) if piece % 2 == 0 else (self.place.y_chip, self.place.x_chip)
        )
        return remote(
            self.target.at[came, rows], self.target.at[came, rows],
            self.far_sems.at[0, piece], self.far_sems.at[1, piece], expert=goes,
        )

    def pair_copy(self, kind, piece):
        rows = self.rows(piece)
        block = self.place.block(kind, self.place.core)
        source = self.source.at[rows] if kind == 3 else self.target.at[block, rows]
        return remote(
            source, self.target.at[block, rows],
            self.pair_sems.at[0, kind, piece], self.pair_sems.at[1, kind, piece], expert=self.place.sibling,
        )

    def start_piece(self, piece):
        self.x_copy(piece).start()
        self.y_copy(piece).start()
        self.pair_copy(3, piece).start()

    def start(self):
        self.own_copy().start()
        for piece in range(self.pieces):
            self.start_piece(piece)

    def near(self, piece):
        self.x_copy(piece).wait_recv()
        if piece % 2 == 0:
            self.far_copy(piece).start()
        self.pair_copy(1, piece).start()
        self.y_copy(piece).wait_recv()
        if piece % 2 == 1:
            self.far_copy(piece).start()
        self.pair_copy(2, piece).start()

    def far(self, piece):
        self.far_copy(piece).wait_recv()
        self.pair_copy(0, piece).start()

    def paired(self, kind, piece):
        self.pair_copy(kind, piece).wait_recv()

    def finish(self):
        for piece in range(self.pieces):
            self.x_copy(piece).wait_send()
            self.y_copy(piece).wait_send()
            self.far_copy(piece).wait_send()
            for kind in range(4):
                self.pair_copy(kind, piece).wait_send()


def wide_dot(left, right):
    return jnp.dot(left, right, preferred_element_type=jnp.float32)


def turned_dot(left, right):
    return lax.dot_general(left, right, (((1,), (1,)), ((), ())), preferred_element_type=jnp.float32)


BLOCK_STEP = 32


def expert_kernel(
    x_all, g_all, mask, router, bias, w_gate, w_up, w_down,
    reduced, gated_all, gate_all, up_all, mixed_all,
    x_buf, g_buf, part, paired, from_x, from_y, line_in, line_spare, small, mixed,
    in_sems, out_sems, pair_sems, x_sems, y_sems, line_sems,
):
    experts, width, hidden = w_gate.shape
    rows = x_buf.shape[1]
    tile = min(512, width)
    plane = Plane(part.at[1], part.at[0], paired, from_x, from_y, pair_sems, x_sems, y_sems, step=BLOCK_STEP)
    line = Line(part.at[1, 3], line_in, line_spare, reduced, line_sems, step=BLOCK_STEP)
    first_expert = lax.axis_index("expert") * experts
    outs = (gated_all, gate_all, up_all)

    def block_of(i):
        return plane.block(i // 2, (plane.core + 1 - i % 2) % 2)

    def fetch(i):
        slot, block = i % 2, block_of(i)
        return (
            pltpu.make_async_copy(x_all.at[block], x_buf.at[slot], in_sems.at[0, slot]),
            pltpu.make_async_copy(g_all.at[block], g_buf.at[slot], in_sems.at[1, slot]),
        )

    def store(i):
        slot, block = i % 2, block_of(i)
        return [
            pltpu.make_async_copy(small.at[slot, n], outs[n].at[block], out_sems.at[n, slot])
            for n in range(3)
        ] + [pltpu.make_async_copy(mixed.at[slot], mixed_all.at[block], out_sems.at[3, slot])]

    def compute(i):
        slot = i % 2
        block = block_of(i)
        x = x_buf.at[slot]
        g = g_buf.at[slot]
        logits = wide_dot(x[...], router[...]) + bias[...]
        weights = jnp.exp(logits - jnp.max(logits, axis=1, keepdims=True))
        gates = weights / jnp.sum(weights, axis=1, keepdims=True) * mask[block]
        column = lax.broadcasted_iota(jnp.int32, (rows, LANE), 1)
        extra = jnp.zeros((rows, LANE), jnp.float32)
        for j in range(experts):
            gate_pre = wide_dot(x[...], w_gate[j])
            up_pre = wide_dot(x[...], w_up[j])
            raw = turned_dot(g[...], w_down[j])
            gate = gates[:, j : j + 1]
            sigma = jax.nn.sigmoid(gate_pre)
            activated = gate_pre * sigma
            inner = activated * up_pre
            act = gate * raw
            span = slice(j * hidden, (j + 1) * hidden)
            small[slot, 0, :, span] = (gate * inner).astype(jnp.bfloat16)
            small[slot, 1, :, span] = (
                act * up_pre * sigma * (1.0 + gate_pre * (1.0 - sigma))
            ).astype(jnp.bfloat16)
            small[slot, 2, :, span] = (act * activated).astype(jnp.bfloat16)
            gain = jnp.sum(raw * inner, axis=1, keepdims=True)
            extra = jnp.where(column == first_expert + j, gain, extra)
        for start in range(0, width, tile):
            columns = slice(start, start + tile)
            slot_grad = None
            mix = None
            for j in range(experts):
                span = slice(j * hidden, (j + 1) * hidden)
                term = turned_dot(small[slot, 1, :, span], w_gate[j, columns]) + turned_dot(
                    small[slot, 2, :, span], w_up[j, columns]
                )
                more = wide_dot(small[slot, 0, :, span], w_down[j, :, columns])
                slot_grad = term if slot_grad is None else slot_grad + term
                mix = more if mix is None else mix + more
            part[i % 2, i // 2, :, columns] = slot_grad.astype(jnp.bfloat16)
            mixed[slot, :, columns] = mix.astype(jnp.bfloat16)
        part[i % 2, i // 2, :, width:] = extra.astype(jnp.bfloat16)

    for copy in fetch(0):
        copy.start()
    greet(plane.neighbours() + line.neighbours())

    def step(i, carry):
        @pl.when(i < 7)
        def _():
            for copy in fetch(i + 1):
                copy.start()

        for copy in fetch(i):
            copy.wait()

        @pl.when(i >= 2)
        def _():
            for copy in store(i - 2):
                copy.wait()

        compute(i)
        for copy in store(i):
            copy.start()

        @pl.when(i % 2 == 0)
        def _():
            plane.pair_copy(i // 2).start()

        @pl.when(i % 2 == 1)
        def _():
            plane.pair_copy(i // 2).wait_recv()

        for chip in range(3):

            @pl.when(i == 2 * chip + 1)
            def _():
                plane.send_first(chip)
                if chip == 2:
                    plane.send_second()

        return carry

    lax.fori_loop(0, 8, step, 0)

    def last(step, carry):
        @pl.when(step < plane.pieces)
        def _():
            for side, total in enumerate(plane.last_sum(step)):
                plane.own[3, plane.rows(side, step)] = total.astype(jnp.bfloat16)

        line.advance(step)
        return carry

    lax.fori_loop(0, line.steps(), last, 0)
    for i in (6, 7):
        for copy in store(i):
            copy.wait()
    plane.finish()
    line.finish()


def experts_fused(arrived, arrived_grad, mask, router, bias, w_gate, w_up, w_down):
    ranks, rows, width = arrived.shape
    experts, _, hidden = w_gate.shape
    wide = width + LANE
    inner = experts * hidden
    half = rows // 2
    low = jnp.bfloat16
    any_space = pl.BlockSpec(memory_space=pl.ANY)
    vmem = pl.BlockSpec(memory_space=pltpu.VMEM)
    small_shape = jax.ShapeDtypeStruct((ranks, rows, inner), low)
    return pl.pallas_call(
        expert_kernel,
        out_shape=(
            jax.ShapeDtypeStruct((rows, wide), low), small_shape, small_shape, small_shape,
            jax.ShapeDtypeStruct((ranks, rows, width), low),
        ),
        in_specs=[any_space, any_space] + [vmem] * 6,
        out_specs=(vmem, any_space, any_space, any_space, any_space),
        scratch_shapes=[
            pltpu.VMEM((2, rows, width), low),
            pltpu.VMEM((2, rows, width), low),
            pltpu.VMEM((2, 4, rows, wide), low),
            pltpu.VMEM((4, rows, wide), low),
            pltpu.VMEM((3, half, wide), low),
            pltpu.VMEM((3, half, wide), low),
            pltpu.VMEM((rows, wide), low),
            Line.spare_shape(rows, wide),
            pltpu.VMEM((2, 3, rows, inner), low),
            pltpu.VMEM((2, rows, width), low),
            pltpu.SemaphoreType.DMA((2, 2)),
            pltpu.SemaphoreType.DMA((4, 2)),
            *Plane.semaphores(rows, step=BLOCK_STEP),
            Line.semaphores(rows, step=BLOCK_STEP),
        ],
        compiler_params=pltpu.CompilerParams(
            collective_id=0, has_side_effects=True, vmem_limit_bytes=61 * 2**20
        ),
        cost_estimate=pl.CostEstimate(
            flops=12 * ranks * rows * width * inner, bytes_accessed=8 * ranks * rows * width, transcendentals=0
        ),
    )(arrived, arrived_grad, mask, router, bias, w_gate, w_up, w_down)


def crossed_dot(left, right):
    return lax.dot_general(left, right, (((0,), (0,)), ((), ())), preferred_element_type=jnp.float32)


def closing_kernel(
    normed, query_grad, key_grad, value_grad, attended, attention_grad, extras,
    w_query, w_key, w_value, mixed, x_all, g_all, gated_all, gate_all, up_all,
    total, sums, gain, mixture, gate_out, up_out, down_out,
    line_own, line_in, line_spare, part, paired, from_x, from_y,
    mix_own, mix_paired, mix_x, mix_y, mix_in, mix_spare, tiles, factors, results, downs,
    line_sems, pair_sems, x_sems, y_sems, mix_line_sems, mix_pair_sems, mix_x_sems, mix_y_sems,
    load_sems, weight_sems, factor_sems, tile_sems, out_sems,
    gains, mine, theirs, peer_sent, peer_got,
    *,
    gain_column,
):
    width = normed.shape[1]
    heads = query_grad.shape[1]
    share = part.shape[2]
    experts, _, hidden = gate_out.shape
    column_tile = min(512, width // 2)
    tile = tiles.shape[2]
    count = width // tile
    line = Line(line_own, line_in, line_spare, total, line_sems)
    plane = Plane(part.at[1], part.at[0], paired, from_x, from_y, pair_sems, x_sems, y_sems)
    mix = Plane(mix_own, mixed, mix_paired, mix_x, mix_y, mix_pair_sems, mix_x_sems, mix_y_sems, by_device=True)
    mix_line = Line(mix_own.at[3], mix_in, mix_spare, mixture, mix_line_sems)
    peers = Peers(mine, theirs, peer_sent, peer_got)
    half = width // 2

    def load_own(chip):
        return pltpu.make_async_copy(mixed.at[mix.block(chip, mix.core)], mix_own.at[chip], load_sems.at[chip])

    weight_loads = [
        pltpu.make_async_copy(w_query, factors.at[0, 0:width], weight_sems.at[0]),
        pltpu.make_async_copy(w_key, factors.at[1, 0:width], weight_sems.at[1]),
        pltpu.make_async_copy(w_value.at[0:half], factors.at[0, width : width + half], weight_sems.at[2]),
        pltpu.make_async_copy(w_value.at[half:], factors.at[1, width : width + half], weight_sems.at[3]),
    ]

    def factor_load(matrix):
        return pltpu.make_async_copy(
            (gate_all, up_all, gated_all)[matrix], factors.at[matrix % 2], factor_sems.at[matrix]
        )

    def tile_copy(source, s):
        columns = pl.ds(pl.multiple_of(s % count * tile, tile), tile)
        return pltpu.make_async_copy(source.at[:, columns], tiles.at[s % 2], tile_sems.at[s % 2])

    def start_tile(s):
        @pl.when(s < 2 * count)
        def _():
            tile_copy(x_all, s).start()

        @pl.when(s >= 2 * count)
        def _():
            tile_copy(g_all, s).start()

    def across(target, s):
        rows = pl.ds(pl.multiple_of(s % count * tile, tile), tile)
        return [
            pltpu.make_async_copy(
                results.at[s % 2, :, j * hidden : (j + 1) * hidden], target.at[j, rows], out_sems.at[0, s % 2, j]
            )
            for j in range(experts)
        ]

    def down(s):
        columns = pl.ds(pl.multiple_of(s % count * tile, tile), tile)
        return [
            pltpu.make_async_copy(
                downs.at[s % 2, j * hidden : (j + 1) * hidden], down_out.at[j, :, columns], out_sems.at[1, s % 2, j]
            )
            for j in range(experts)
        ]

    def expert_tile(s):
        @pl.when(s + 1 < 3 * count)
        def _():
            start_tile(s + 1)

        for matrix in range(3):

            @pl.when(s == matrix * count)
            def _():
                factor_load(matrix).wait()

        tile_copy(x_all, s).wait()

        @pl.when(s < 2 * count)
        def _():
            @pl.when(s >= 2)
            def _():
                for copy in across(gate_out, s):
                    copy.wait()

            results[s % 2] = crossed_dot(tiles[s % 2], factors[s // count]).astype(jnp.bfloat16)

            @pl.when(s < count)
            def _():
                for copy in across(gate_out, s):
                    copy.start()

            @pl.when(s >= count)
            def _():
                for copy in across(up_out, s):
                    copy.start()

        @pl.when(s >= 2 * count)
        def _():
            @pl.when(s >= 2 * count + 2)
            def _():
                for copy in down(s):
                    copy.wait()

            downs[s % 2] = crossed_dot(factors[0], tiles[s % 2]).astype(jnp.bfloat16)
            for copy in down(s):
                copy.start()

        @pl.when(s == count - 1)
        def _():
            factor_load(2).start()

    def dense_block(i):
        chip, sub = i // 2, i % 2
        block = plane.block(chip, (plane.core + 1 - sub) % 2)
        columns = pl.ds(pl.multiple_of(block * share, share), share)
        source = normed[:, columns]
        part[sub, chip, :, 0:heads] = crossed_dot(source, query_grad[...]).astype(jnp.bfloat16)
        part[sub, chip, :, heads : 2 * heads] = crossed_dot(source, key_grad[...]).astype(jnp.bfloat16)
        part[sub, chip, :, 2 * heads : 3 * heads] = crossed_dot(source, value_grad[...]).astype(jnp.bfloat16)
        part[sub, chip, :, 3 * heads : 4 * heads] = crossed_dot(
            attention_grad[:, columns], attended[...]
        ).astype(jnp.bfloat16)
        part[sub, chip, :, 4 * heads :] = extras[block] + gains[columns]

        @pl.when(sub == 0)
        def _():
            plane.pair_copy(chip).start()

    for copy in weight_loads:
        copy.start()
    for chip in range(4):
        load_own(chip).start()
    greet(plane.neighbours() + peers.neighbours())
    for chip in range(4):
        mix.pair_copy(chip).start()
    for copy in weight_loads:
        copy.wait()
    for start in range(0, width, column_tile):
        columns = slice(start, start + column_tile)
        later = width + start % half
        line_own[:, columns] = (
            turned_dot(query_grad[...], factors[0, columns])
            + turned_dot(key_grad[...], factors[1, columns])
            + turned_dot(value_grad[...], factors[start // half, later : later + column_tile])
        ).astype(jnp.bfloat16)
    place = lax.broadcasted_iota(jnp.int32, (normed.shape[0], LANE), 1)
    chosen = jnp.where(place == gain_column, 1.0, 0.0).astype(jnp.bfloat16)
    for start in range(0, width, column_tile):
        columns = slice(start, start + column_tile)
        pull = line_own[:, columns].astype(jnp.float32) * normed[:, columns].astype(jnp.float32)
        gains[columns] = crossed_dot(pull.astype(jnp.bfloat16), chosen).astype(jnp.bfloat16)
    factor_load(0).start()
    factor_load(1).start()
    start_tile(0)
    mix_second, mix_last, dense_first, dense_second, dense_last = PLAN

    def step(s, carry):
        line.advance(s)

        @pl.when(s == 0)
        def _():
            for chip in range(3):
                load_own(chip).wait()
                mix.pair_copy(chip).wait_recv()
            for piece in range(AHEAD):
                mix.first_piece(piece)

        @pl.when(s == mix_last - 1)
        def _():
            load_own(3).wait()
            mix.pair_copy(3).wait_recv()

        @pl.when((s > 0) & (s + AHEAD - 1 < mix.pieces))
        def _():
            mix.first_piece(s + AHEAD - 1)

        @pl.when((s >= mix_second) & (s - mix_second < mix.pieces))
        def _():
            mix.second_piece(s - mix_second)

        @pl.when((s >= mix_last) & (s - mix_last < mix.pieces))
        def _():
            piece = s - mix_last
            for side, summed in enumerate(mix.last_sum(piece)):
                mix_own[3, mix.rows(side, piece)] = summed.astype(jnp.bfloat16)

        mix_line.advance(s - mix_last)

        @pl.when((s >= 4) & (s < 12))
        def _():
            dense_block(s - 4)

        @pl.when(s == dense_first)
        def _():
            for chip in range(4):
                plane.pair_copy(chip).wait_recv()
            for chip in range(3):
                plane.send_first(chip)

        @pl.when((s >= dense_second) & (s - dense_second < plane.pieces))
        def _():
            plane.second_piece(s - dense_second)

        @pl.when((s >= dense_last) & (s - dense_last < plane.pieces))
        def _():
            piece = s - dense_last
            for side, summed in enumerate(plane.last_sum(piece)):
                sums[plane.rows(side, piece)] = summed

        @pl.when(s < 3 * count)
        def _():
            expert_tile(s)

        return carry

    steps = jnp.maximum(mix_last + mix_line.steps(), jnp.maximum(3 * count, dense_last + plane.pieces))
    lax.fori_loop(0, steps, step, 0)
    column = 4 * heads + gain_column
    mine[...] = to_rows([sums[:, column : column + 1]], share)
    peers.start()
    for s in (2 * count - 2, 2 * count - 1):
        for copy in across(up_out, s):
            copy.wait()
    for s in (3 * count - 2, 3 * count - 1):
        for copy in down(s):
            copy.wait()
    gain[...] = peers.total()
    for each in (plane, line, mix, mix_line, peers):
        each.finish()


PLAN = (1, 3, 12, 15, 18)
AHEAD = 2
TILE = 256


def closing(
    normed, query_grad, key_grad, value_grad, attended, attention_grad, extras, w_query, w_key, w_value,
    mixed, arrived, arrived_grad, gated, gate_grad, up_grad, experts, gain_column,
):
    rows, width = normed.shape
    heads = query_grad.shape[1]
    ranks, share, more = extras.shape
    wide = 4 * heads + more
    inner = gated.shape[2]
    hidden = inner // experts
    low = jnp.bfloat16
    tile = min(TILE, width // 2)
    vmem = pl.BlockSpec(memory_space=pltpu.VMEM)
    any_space = pl.BlockSpec(memory_space=pl.ANY)
    every = ranks * rows
    size = lax.axis_size("tensor")
    return pl.pallas_call(
        functools.partial(closing_kernel, gain_column=gain_column),
        out_shape=(
            jax.ShapeDtypeStruct((rows, width), low),
            jax.ShapeDtypeStruct((share, wide), jnp.float32),
            jax.ShapeDtypeStruct((8, share), jnp.float32),
            jax.ShapeDtypeStruct((rows, width), low),
            jax.ShapeDtypeStruct((experts, width, hidden), low),
            jax.ShapeDtypeStruct((experts, width, hidden), low),
            jax.ShapeDtypeStruct((experts, hidden, width), low),
        ),
        in_specs=[vmem] * 7 + [any_space] * 9,
        out_specs=(vmem,) * 4 + (any_space,) * 3,
        scratch_shapes=[
            pltpu.VMEM((rows, width), low),
            pltpu.VMEM((rows, width), low),
            Line.spare_shape(rows, width),
            pltpu.VMEM((2, 4, share, wide), low),
            pltpu.VMEM((4, share, wide), low),
            pltpu.VMEM((3, share // 2, wide), low),
            pltpu.VMEM((3, share // 2, wide), low),
            pltpu.VMEM((4, rows, width), low),
            pltpu.VMEM((4, rows, width), low),
            pltpu.VMEM((3, rows // 2, width), low),
            pltpu.VMEM((3, rows // 2, width), low),
            pltpu.VMEM((rows, width), low),
            Line.spare_shape(rows, width),
            pltpu.VMEM((2, every, tile), low),
            pltpu.VMEM((2, every, inner), low),
            pltpu.VMEM((2, tile, inner), low),
            pltpu.VMEM((2, inner, tile), low),
            Line.semaphores(rows),
            *Plane.semaphores(share),
            Line.semaphores(rows),
            *Plane.semaphores(rows),
            pltpu.SemaphoreType.DMA((4,)),
            pltpu.SemaphoreType.DMA((4,)),
            pltpu.SemaphoreType.DMA((3,)),
            pltpu.SemaphoreType.DMA((2,)),
            pltpu.SemaphoreType.DMA((2, 2, experts)),
            pltpu.VMEM((width, LANE), low),
            pltpu.VMEM((8, share), jnp.float32),
            pltpu.VMEM((size - 1, 8, share), jnp.float32),
            pltpu.SemaphoreType.DMA((size - 1,)),
            pltpu.SemaphoreType.DMA((size - 1,)),
        ],
        compiler_params=pltpu.CompilerParams(
            collective_id=2, has_side_effects=True, vmem_limit_bytes=63 * 2**20
        ),
    )(
        normed, query_grad, key_grad, value_grad, attended, attention_grad, extras, w_query, w_key, w_value,
        mixed, arrived.reshape(every, width), arrived_grad.reshape(every, width),
        gated.reshape(every, inner), gate_grad.reshape(every, inner), up_grad.reshape(every, inner),
    )


class Peers:
    def __init__(self, mine, theirs, sent, got):
        self.mine, self.theirs, self.sent, self.got = mine, theirs, sent, got
        self.size = lax.axis_size("tensor")
        self.here = lax.axis_index("tensor")

    def neighbours(self):
        return [(None, {"tensor": (self.here + d) % self.size}) for d in range(1, self.size)]

    def copies(self):
        return [
            remote(
                self.mine, self.theirs.at[d - 1], self.sent.at[d - 1], self.got.at[d - 1],
                tensor=(self.here + d) % self.size,
            )
            for d in range(1, self.size)
        ]

    def start(self):
        for copy in self.copies():
            copy.start()

    def total(self):
        result = self.mine[...]
        for d, copy in enumerate(self.copies()):
            copy.wait_recv()
            result = result + self.theirs[d]
        return result

    def finish(self):
        for copy in self.copies():
            copy.wait_send()


def to_rows(columns, rows):
    lane = lax.broadcasted_iota(jnp.int32, (rows, LANE), 1)
    field = jnp.zeros((rows, LANE), jnp.float32)
    for i, column in enumerate(columns):
        field = jnp.where(lane == i, column, field)
    return field.T[:8]


def to_columns(sums):
    padded = jnp.concatenate([sums, jnp.zeros((LANE - 8, sums.shape[1]), jnp.float32)], axis=0)
    return padded.T


def swapped(field):
    half = HD // 2
    return jnp.concatenate([field[:, half:], field[:, :half]], axis=1)


SPREAD = 32
SPREAD_LAG = 2


def front_kernel(
    tokens, attn_gain, ffn_gain, w_query, w_key, w_value, w_out, qk_gain, cosine, sine, bias, routes,
    total, normed, normed_two, attended, query_rot, keys_values, query_raw, key_raw, stats, routes_all, arrived,
    line_own, line_in, line_spare, prompt, mine, theirs, two,
    line_sems, peer_sent, peer_got, *gather_sems,
):
    rows, width = tokens.shape
    local = w_query.shape[1]
    heads = local // HD
    factor = HD ** (-0.5)
    own_blocks = rows // PROMPT_DEV - 1
    devices = keys_values.shape[0] - own_blocks
    place = Place()
    line = Line(line_own, line_in, line_spare, total, line_sems)
    peers = Peers(mine, theirs, peer_sent, peer_got)
    names = Gather(routes, routes_all, place, *gather_sems[0:5], pieces=2)
    prompts = Gather(prompt, keys_values, place, *gather_sems[5:10], pieces=2)
    spread = Gather(normed_two, arrived, place, *gather_sems[10:15], pieces=rows // SPREAD)
    greet(place.neighbours() + peers.neighbours())
    names.start()
    source = tokens[...].astype(jnp.float32)
    scale_one = lax.rsqrt(jnp.sum(source * source, axis=1, keepdims=True) / width + epsilon)
    normed[...] = (source * scale_one * attn_gain[...]).astype(jnp.bfloat16)
    query_raw[...] = wide_dot(normed[...], w_query[...])
    key_raw[...] = wide_dot(normed[...], w_key[...])
    mine[...] = to_rows(
        [
            jnp.sum(query_raw[...] * query_raw[...], axis=1, keepdims=True),
            jnp.sum(key_raw[...] * key_raw[...], axis=1, keepdims=True),
        ],
        rows,
    )
    peers.start()
    value = wide_dot(normed[...], w_value[...]).astype(jnp.bfloat16)
    prompt[:, local:] = value[:PROMPT_DEV]
    for i in range(own_blocks):
        keys_values[devices + i, :, local:] = value[(i + 1) * PROMPT_DEV : (i + 2) * PROMPT_DEV]
    squares = to_columns(peers.total())
    scale_query = lax.rsqrt(squares[:, 0:1] / width + epsilon)
    scale_key = lax.rsqrt(squares[:, 1:2] / width + epsilon)
    for head in range(heads):
        columns = slice(head * HD, (head + 1) * HD)
        turned = key_raw[:, columns] * scale_key * qk_gain[1:2, columns]
        turned = (turned * cosine[...] + swapped(turned) * sine[...]).astype(jnp.bfloat16)
        prompt[:, columns] = turned[:PROMPT_DEV]
        for i in range(own_blocks):
            keys_values[devices + i, :, columns] = turned[(i + 1) * PROMPT_DEV : (i + 2) * PROMPT_DEV]
    prompts.own_copy().start()
    for piece in range(2):
        prompts.start_piece(piece)
    for head in range(heads):
        columns = slice(head * HD, (head + 1) * HD)
        turned = query_raw[:, columns] * scale_query * qk_gain[0:1, columns]
        turned = turned * cosine[...] + swapped(turned) * sine[...]
        query_rot[:, columns] = turned.astype(jnp.bfloat16)
    for piece in range(2):
        prompts.near(piece)
    for piece in range(2):
        names.near(piece)
    for piece in range(2):
        prompts.far(piece)
        names.far(piece)
    prompts.own_copy().wait()
    for kind in range(4):
        for piece in range(2):
            prompts.paired(kind, piece)
            names.paired(kind, piece)
    lane = lax.broadcasted_iota(jnp.int32, (rows, LANE), 1)
    kept = jnp.where(lane == 0, scale_one, 0.0)
    kept = jnp.where(lane == 1, scale_query, kept)
    kept = jnp.where(lane == 2, scale_key, kept)
    count = keys_values.shape[0] * PROMPT_DEV
    for head in range(heads):
        columns = slice(head * HD, (head + 1) * HD)
        keys = keys_values[:, :, columns].reshape(count, HD)
        values = keys_values[:, :, local + head * HD : local + (head + 1) * HD].reshape(count, HD)
        scores = turned_dot(query_rot[:, columns], keys) * factor + bias[...]
        top = jnp.max(scores, axis=1, keepdims=True)
        weights = jnp.exp(scores - top)
        whole = jnp.sum(weights, axis=1, keepdims=True)
        shares = (weights / whole).astype(jnp.bfloat16)
        attended[:, columns] = wide_dot(shares, values).astype(jnp.bfloat16)
        kept = jnp.where(lane == 8 + head, top + jnp.log(whole), kept)
    tile = min(512, width)
    for start in range(0, width, tile):
        columns = slice(start, start + tile)
        line_own[:, columns] = wide_dot(attended[...], w_out[:, columns]).astype(jnp.bfloat16)
    ratio = SPREAD // STEP
    groups = line.pieces // ratio

    def norm_rows(piece):
        span = slice(piece * SPREAD, (piece + 1) * SPREAD)
        hidden = tokens[span].astype(jnp.float32) + total[span].astype(jnp.float32)
        scale = lax.rsqrt(jnp.sum(hidden * hidden, axis=1, keepdims=True) / width + epsilon)
        normed_two[span] = (hidden * scale * ffn_gain[...]).astype(jnp.bfloat16)
        two[span] = jnp.broadcast_to(scale, (SPREAD, LANE))

    done = 0
    passed = 0
    for group in range(groups):
        ready = line.trip + (group + 1) * ratio
        lax.fori_loop(done, ready, line.step_body, 0)
        done = ready
        for piece in (group, groups + group):
            norm_rows(piece)
            spread.start_piece(piece)
        if group >= SPREAD_LAG:
            for piece in (passed, groups + passed):
                spread.near(piece)
            passed += 1
    spread.own_copy().start()
    for group in range(passed, groups):
        for piece in (group, groups + group):
            spread.near(piece)
    for group in range(groups):
        for piece in (group, groups + group):
            spread.far(piece)
    stats[...] = jnp.where(lane == 3, two[...], kept)
    for kind in range(4):
        for piece in range(spread.pieces):
            spread.paired(kind, piece)
    spread.own_copy().wait()
    names.own_copy().wait()
    for each in (names, prompts, spread, line, peers):
        each.finish()


def front(tokens, attn_gain, ffn_gain, w_query, w_key, w_value, w_out, qk_gain, cosine, sine, bias, routes):
    rows, width = tokens.shape
    local = w_query.shape[1]
    ranks = lax.axis_size("expert")
    size = lax.axis_size("tensor")
    low, full = jnp.bfloat16, jnp.float32
    vmem = pl.BlockSpec(memory_space=pltpu.VMEM)
    blocks = ranks + rows // PROMPT_DEV - 1
    return pl.pallas_call(
        front_kernel,
        out_shape=(
            jax.ShapeDtypeStruct((rows, width), low),
            jax.ShapeDtypeStruct((rows, width), low),
            jax.ShapeDtypeStruct((rows, width), low),
            jax.ShapeDtypeStruct((rows, local), low),
            jax.ShapeDtypeStruct((rows, local), low),
            jax.ShapeDtypeStruct((blocks, PROMPT_DEV, 2 * local), low),
            jax.ShapeDtypeStruct((rows, local), full),
            jax.ShapeDtypeStruct((rows, local), full),
            jax.ShapeDtypeStruct((rows, LANE), full),
            jax.ShapeDtypeStruct((ranks,) + routes.shape, jnp.int32),
            jax.ShapeDtypeStruct((ranks, rows, width), low),
        ),
        in_specs=[vmem] * 12,
        out_specs=(vmem,) * 10 + (pl.BlockSpec(memory_space=pl.ANY),),
        scratch_shapes=[
            pltpu.VMEM((rows, width), low),
            pltpu.VMEM((rows, width), low),
            Line.spare_shape(rows, width),
            pltpu.VMEM((PROMPT_DEV, 2 * local), low),
            pltpu.VMEM((8, rows), full),
            pltpu.VMEM((size - 1, 8, rows), full),
            pltpu.VMEM((rows, LANE), full),
            Line.semaphores(rows),
            pltpu.SemaphoreType.DMA((size - 1,)),
            pltpu.SemaphoreType.DMA((size - 1,)),
            *Gather.semaphores(2),
            *Gather.semaphores(2),
            *Gather.semaphores(rows // SPREAD),
        ],
        compiler_params=pltpu.CompilerParams(
            collective_id=1, has_side_effects=True, vmem_limit_bytes=60 * 2**20
        ),
        cost_estimate=pl.CostEstimate(flops=100 * 10**9, bytes_accessed=200 * 10**6, transcendentals=0),
    )(tokens, attn_gain, ffn_gain, w_query, w_key, w_value, w_out, qk_gain, cosine, sine, bias, routes)


def backward_kernel(
    reduced, tokens, attention, cotangent, normed_two, router, expert_bias, routed, ffn_gain,
    w_out, query_rot, keys_values, bias, stats, query_raw, key_raw, cosine, sine, qk_gain,
    query_out, key_out, value_out, gain_out, hidden_grad, attention_grad, extras,
    out_grad, query_grad, prompt_grads, own_grads, own, paired, from_x, from_y, mine, theirs,
    pair_sems, x_sems, y_sems, peer_sent, peer_got,
    *,
    gain_column,
):
    rows, local = query_rot.shape
    width = attention_grad.shape[1]
    heads = local // HD
    factor = HD ** (-0.5)
    own_blocks = rows // PROMPT_DEV - 1
    devices = keys_values.shape[0] - own_blocks
    count = keys_values.shape[0] * PROMPT_DEV
    reach = devices * PROMPT_DEV
    plane = Plane(own, prompt_grads, paired, from_x, from_y, pair_sems, x_sems, y_sems, by_device=True)
    peers = Peers(mine, theirs, peer_sent, peer_got)
    greet(plane.neighbours() + peers.neighbours())
    tile = min(512, width)
    starts = range(0, width, tile)
    scale_two = stats[:, 3:4]
    logits = wide_dot(normed_two[...], router[...]) + expert_bias[...]
    weights = jnp.exp(logits - jnp.max(logits, axis=1, keepdims=True))
    chances = weights / jnp.sum(weights, axis=1, keepdims=True)
    chance_grad = routed[...] * reduced[:, width:].astype(jnp.float32)
    logit_grad = (
        chances * (chance_grad - jnp.sum(chances * chance_grad, axis=1, keepdims=True))
    ).astype(jnp.bfloat16)

    def hidden_of(columns):
        return tokens[:, columns].astype(jnp.float32) + attention[:, columns].astype(jnp.float32)

    def input_part(columns):
        return reduced[:, columns].astype(jnp.float32) + turned_dot(logit_grad, router[columns])

    pull = jnp.zeros((rows, 1), jnp.float32)
    for start in starts:
        columns = slice(start, start + tile)
        weighted = ffn_gain[:, columns] * input_part(columns)
        hidden_grad[:, columns] = weighted
        pull = pull + jnp.sum(weighted * hidden_of(columns), axis=1, keepdims=True)
    pull = scale_two * scale_two * scale_two / width * pull
    for start in starts:
        columns = slice(start, start + tile)
        grad = (
            cotangent[:, columns].astype(jnp.float32)
            + scale_two * hidden_grad[:, columns]
            - hidden_of(columns) * pull
        )
        hidden_grad[:, columns] = grad
        attention_grad[:, columns] = grad.astype(jnp.bfloat16)
    out_grad[...] = turned_dot(attention_grad[...], w_out[...]).astype(jnp.bfloat16)
    for head in range(heads):
        columns = slice(head * HD, (head + 1) * HD)
        other = slice(local + head * HD, local + (head + 1) * HD)
        keys = keys_values[:, :, columns].reshape(count, HD)
        values = keys_values[:, :, other].reshape(count, HD)
        query, above = query_rot[:, columns], out_grad[:, columns]
        scores = turned_dot(query, keys) * factor + bias[...]
        shares = jnp.exp(scores - stats[:, 8 + head : 9 + head])
        share_grad = turned_dot(above, values)
        delta = jnp.sum(shares * share_grad, axis=1, keepdims=True)
        score_grad = (shares * (share_grad - delta)).astype(jnp.bfloat16)
        query_grad[:, columns] = wide_dot(score_grad, keys) * factor
        key_grad = crossed_dot(score_grad, query) * factor
        value_grad = crossed_dot(shares.astype(jnp.bfloat16), above)
        prompt_grads[:, :, columns] = key_grad[:reach].astype(jnp.bfloat16).reshape(devices, PROMPT_DEV, HD)
        prompt_grads[:, :, other] = value_grad[:reach].astype(jnp.bfloat16).reshape(devices, PROMPT_DEV, HD)
        own_grads[PROMPT_DEV:, columns] = key_grad[reach:]
        own_grads[PROMPT_DEV:, other] = value_grad[reach:]
    for chip in range(4):
        plane.pair_copy(chip).start()
    for chip in range(4):
        own[chip] = prompt_grads[plane.block(chip, plane.core)]
    for chip in range(4):
        plane.pair_copy(chip).wait_recv()
        if chip < 3:
            plane.send_first(chip)

    def normed_part(source, raw, row, scale):
        inner = jnp.zeros((rows, 1), jnp.float32)
        for head in range(heads):
            columns = slice(head * HD, (head + 1) * HD)
            grad = source[:, columns]
            grad = grad * cosine[...] - swapped(grad) * sine[...]
            gain_out[row : row + 1, columns] = jnp.sum(grad * raw[:, columns] * scale, axis=0, keepdims=True)
            grad = qk_gain[row : row + 1, columns] * grad
            source[:, columns] = grad
            inner = inner + jnp.sum(grad * raw[:, columns], axis=1, keepdims=True)
        return inner

    scale_query, scale_key = stats[:, 1:2], stats[:, 2:3]
    query_inner = normed_part(query_grad, query_raw, 0, scale_query)
    plane.send_second()
    chosen = lax.broadcasted_iota(jnp.int32, (rows, LANE), 1) == gain_column
    chosen = jnp.where(chosen, 1.0, 0.0).astype(jnp.bfloat16)
    for start in starts:
        columns = slice(start, start + tile)
        sway = input_part(columns) * hidden_of(columns) * scale_two
        extras[columns] = (
            crossed_dot(normed_two[:, columns], logit_grad) + crossed_dot(sway.astype(jnp.bfloat16), chosen)
        ).astype(jnp.bfloat16)

    def last(piece, carry):
        for side, summed in enumerate(plane.last_sum(piece)):
            own_grads[plane.rows(side, piece)] = summed
        return carry

    lax.fori_loop(0, plane.pieces, last, 0)
    key_inner = normed_part(own_grads, key_raw, 1, scale_key)
    mine[...] = to_rows([query_inner, key_inner], rows)
    peers.start()
    value_out[...] = own_grads[:, local:].astype(jnp.bfloat16)
    inner = to_columns(peers.total())
    for out, source, raw, scale, i in (
        (query_out, query_grad, query_raw, scale_query, 0),
        (key_out, own_grads, key_raw, scale_key, 1),
    ):
        pull = scale * scale * scale / width * inner[:, i : i + 1]
        out[...] = (scale * source[:, :local] - raw[...] * pull).astype(jnp.bfloat16)
    plane.finish()
    peers.finish()


def backward(
    reduced, tokens, attention, cotangent, normed_two, router, expert_bias, routed, ffn_gain,
    w_out, query_rot, keys_values, bias, stats, query_raw, key_raw, cosine, sine, qk_gain, gain_column,
):
    rows, local = query_rot.shape
    size = lax.axis_size("tensor")
    ranks = lax.axis_size("expert")
    low, full = jnp.bfloat16, jnp.float32
    vmem = pl.BlockSpec(memory_space=pltpu.VMEM)
    small = jax.ShapeDtypeStruct((rows, local), low)
    return pl.pallas_call(
        functools.partial(backward_kernel, gain_column=gain_column),
        out_shape=(
            small, small, small, jax.ShapeDtypeStruct((2, local), full),
            jax.ShapeDtypeStruct(tokens.shape, full), jax.ShapeDtypeStruct(tokens.shape, low),
            jax.ShapeDtypeStruct((tokens.shape[1], LANE), low),
        ),
        in_specs=[vmem] * 19,
        out_specs=(vmem,) * 7,
        scratch_shapes=[
            pltpu.VMEM((rows, local), low),
            pltpu.VMEM((rows, local), full),
            pltpu.VMEM((ranks, PROMPT_DEV, 2 * local), low),
            pltpu.VMEM((rows, 2 * local), full),
            pltpu.VMEM((4, PROMPT_DEV, 2 * local), low),
            pltpu.VMEM((4, PROMPT_DEV, 2 * local), low),
            pltpu.VMEM((3, PROMPT_DEV // 2, 2 * local), low),
            pltpu.VMEM((3, PROMPT_DEV // 2, 2 * local), low),
            pltpu.VMEM((8, rows), full),
            pltpu.VMEM((size - 1, 8, rows), full),
            *Plane.semaphores(PROMPT_DEV),
            pltpu.SemaphoreType.DMA((size - 1,)),
            pltpu.SemaphoreType.DMA((size - 1,)),
        ],
        compiler_params=pltpu.CompilerParams(
            collective_id=3, has_side_effects=True, vmem_limit_bytes=60 * 2**20
        ),
    )(
        reduced, tokens, attention, cotangent, normed_two, router, expert_bias, routed, ffn_gain,
        w_out, query_rot, keys_values, bias, stats, query_raw, key_raw, cosine, sine, qk_gain,
    )


def rotate(field, cosine, sine):
    half = field.shape[-1] // 2
    first = field[..., :half]
    second = field[..., half:]
    return jnp.concatenate(
        [first * cosine - second * sine, second * cosine + first * sine], axis=-1
    )


def unrotate(grad, cosine, sine):
    half = grad.shape[-1] // 2
    first = grad[..., :half]
    second = grad[..., half:]
    return jnp.concatenate(
        [first * cosine + second * sine, second * cosine - first * sine], axis=-1
    )


def experts(normed_two, cotangent, gates, w_gate, w_up, w_down, experts_total):
    local_experts = w_gate.shape[0]
    device = lax.axis_index("expert")
    arrived = lax.all_gather(normed_two, "expert", axis=0, tiled=True)
    arrived_grad = lax.all_gather(cotangent, "expert", axis=0, tiled=True)
    gate_pre = jnp.einsum("rd,jdf->jrf", arrived, w_gate, preferred_element_type=jnp.float32)
    up_pre = jnp.einsum("rd,jdf->jrf", arrived, w_up, preferred_element_type=jnp.float32)
    raw_grad = jnp.einsum("rd,jfd->jrf", arrived_grad, w_down, preferred_element_type=jnp.float32)
    sigma = jax.nn.sigmoid(gate_pre)
    activated = gate_pre * sigma
    inner = activated * up_pre
    gated = (gates[:, :, None] * inner).astype(jnp.bfloat16)
    mixed_part = jnp.einsum("jrf,jfd->rd", gated, w_down, preferred_element_type=jnp.float32)
    mixture = lax.psum(
        lax.psum_scatter(
            mixed_part.astype(jnp.bfloat16), "expert", scatter_dimension=0, tiled=True
        ),
        "tensor",
    ).astype(jnp.float32)
    gate_grad_part = jnp.sum(raw_grad * inner, axis=2)
    act_grad = gates[:, :, None] * raw_grad
    up_grad = (act_grad * activated).astype(jnp.bfloat16)
    gate_grad = (act_grad * up_pre * sigma * (1.0 + gate_pre * (1.0 - sigma))).astype(jnp.bfloat16)
    grad_w_down = jnp.einsum("jrf,rd->jfd", gated, arrived_grad, preferred_element_type=jnp.float32)
    grad_w_gate = jnp.einsum("rd,jrf->jdf", arrived, gate_grad, preferred_element_type=jnp.float32)
    grad_w_up = jnp.einsum("rd,jrf->jdf", arrived, up_grad, preferred_element_type=jnp.float32)
    slot_grad = jnp.einsum("jrf,jdf->rd", gate_grad, w_gate, preferred_element_type=jnp.float32)
    slot_grad = slot_grad + jnp.einsum(
        "jrf,jdf->rd", up_grad, w_up, preferred_element_type=jnp.float32
    )
    moe_input_grad = lax.psum(
        lax.psum_scatter(
            slot_grad.astype(jnp.bfloat16), "expert", scatter_dimension=0, tiled=True
        ),
        "tensor",
    ).astype(jnp.float32)
    placed = jnp.zeros((arrived.shape[0], experts_total), jnp.float32)
    placed = lax.dynamic_update_slice_in_dim(placed, gate_grad_part.T, device * local_experts, 1)
    chance_grad = lax.psum(
        lax.psum_scatter(placed, "expert", scatter_dimension=0, tiled=True), "tensor"
    )
    return mixture, moe_input_grad, chance_grad, [grad_w_gate, grad_w_up, grad_w_down]


def body(
    tokens,
    w_query,
    w_key,
    w_value,
    w_out,
    attn_gain,
    ffn_gain,
    qk_gain,
    router,
    w_gate,
    w_up,
    w_down,
    routes,
    cont_group,
    cotangent,
):
    rows, width = tokens.shape
    local_width = w_query.shape[1]
    head_count = local_width // HD
    experts_total = router.shape[1]
    local_experts = w_gate.shape[0]
    ranks = lax.axis_size("expert")
    device = lax.axis_index("expert")
    span = ranks // 2
    prompt_len = PROMPT_DEV * span
    factor = HD ** (-0.5)
    local = jnp.arange(rows, dtype=jnp.int32)
    is_prompt = local < PROMPT_DEV
    after = jnp.maximum(local - PROMPT_DEV, 0)
    slot_cont = after // CLEN
    cont_pick = jnp.sum(
        jnp.where(
            slot_cont[:, None] == jnp.arange(CONT_DEV, dtype=jnp.int32)[None, :],
            cont_group[None, :],
            0,
        ),
        axis=1,
    )
    group = jnp.where(is_prompt, device // span, cont_pick)
    position = jnp.where(is_prompt, device % span * PROMPT_DEV + local, prompt_len + after % CLEN)
    tag = jnp.where(is_prompt, -1, slot_cont)
    frequency = 10000.0 ** (-jnp.arange(HD // 2, dtype=jnp.float32) * 2.0 / HD)
    angle = position.astype(jnp.float32)[:, None] * frequency[None, :]
    cosine = jnp.cos(angle)[:, None, :]
    sine = jnp.sin(angle)[:, None, :]
    source = tokens.astype(jnp.float32)
    scale_one = lax.rsqrt(jnp.mean(source * source, axis=1, keepdims=True) + epsilon)
    normed = (source * scale_one * attn_gain).astype(jnp.bfloat16)
    query_raw = jnp.dot(normed, w_query, preferred_element_type=jnp.float32)
    key_raw = jnp.dot(normed, w_key, preferred_element_type=jnp.float32)
    value_raw = jnp.dot(normed, w_value, preferred_element_type=jnp.float32)
    squares = lax.psum(
        jnp.stack(
            [jnp.sum(query_raw * query_raw, axis=1), jnp.sum(key_raw * key_raw, axis=1)], axis=1
        ),
        "tensor",
    )
    scale_query = lax.rsqrt(squares[:, 0:1] / width + epsilon)
    scale_key = lax.rsqrt(squares[:, 1:2] / width + epsilon)
    query_rot = (
        rotate((query_raw * scale_query * qk_gain[0]).reshape(rows, head_count, HD), cosine, sine)
        .reshape(rows, local_width)
        .astype(jnp.bfloat16)
    )
    key_rot = (
        rotate((key_raw * scale_key * qk_gain[1]).reshape(rows, head_count, HD), cosine, sine)
        .reshape(rows, local_width)
        .astype(jnp.bfloat16)
    )
    value_low = value_raw.astype(jnp.bfloat16)
    prompt_keys, prompt_values = (
        lax.all_gather(key_rot[:PROMPT_DEV], "expert", axis=0, tiled=True),
        lax.all_gather(value_low[:PROMPT_DEV], "expert", axis=0, tiled=True),
    )
    prompt_count = prompt_keys.shape[0]
    all_keys = jnp.concatenate([prompt_keys, key_rot[PROMPT_DEV:]], axis=0)
    all_values = jnp.concatenate([prompt_values, value_low[PROMPT_DEV:]], axis=0)
    key_index = jnp.arange(prompt_count, dtype=jnp.int32)
    prompt_mask = (group[:, None] == (key_index // prompt_len)[None, :]) & (
        (key_index % prompt_len)[None, :] <= position[:, None]
    )
    own_mask = (tag[:, None] == tag[None, PROMPT_DEV:]) & (
        position[None, PROMPT_DEV:] <= position[:, None]
    )
    mask = jnp.concatenate([prompt_mask, own_mask], axis=1)

    def head_scores(query_head, key_head):
        scores = (
            jnp.einsum("qd,kd->qk", query_head, key_head, preferred_element_type=jnp.float32)
            * factor
        )
        return jnp.where(mask, scores, masked_value)

    outputs = []
    log_totals = []
    for head in range(head_count):
        start = head * HD
        scores = head_scores(query_rot[:, start : start + HD], all_keys[:, start : start + HD])
        top = jnp.max(scores, axis=1, keepdims=True)
        weights = jnp.exp(scores - top)
        total = jnp.sum(weights, axis=1, keepdims=True)
        shares = (weights / total).astype(jnp.bfloat16)
        outputs.append(
            jnp.dot(shares, all_values[:, start : start + HD], preferred_element_type=jnp.float32)
        )
        log_totals.append(top + jnp.log(total))
    attended = jnp.concatenate(outputs, axis=1).astype(jnp.bfloat16)
    attention = lax.psum(jnp.dot(attended, w_out, preferred_element_type=jnp.float32), "tensor")
    hidden = source + attention
    scale_two = lax.rsqrt(jnp.mean(hidden * hidden, axis=1, keepdims=True) + epsilon)
    normed_two = (hidden * scale_two * ffn_gain).astype(jnp.bfloat16)
    logits = jnp.dot(normed_two, router, preferred_element_type=jnp.float32)
    top = jnp.max(logits, axis=1, keepdims=True)
    weights = jnp.exp(logits - top)
    chances = weights / jnp.sum(weights, axis=1, keepdims=True)
    hits = (routes[:, :, None] == jnp.arange(experts_total, dtype=jnp.int32)[None, None, :]).astype(
        jnp.float32
    )
    rows_mask = jnp.sum(hits, axis=1)
    routed = lax.all_gather(
        (rows_mask * chances).astype(jnp.float32), "expert", axis=0, tiled=True
    )
    gates = lax.dynamic_slice_in_dim(routed, device * local_experts, local_experts, 1).T
    grad_out = cotangent.astype(jnp.float32)
    pieces = max(1, ranks * rows // 4096)
    piece = rows // pieces
    split_gates = gates.reshape(local_experts, ranks, rows)
    results = []
    weight_grads = None
    for number in range(pieces):
        part = slice(number * piece, (number + 1) * piece)
        sources = (normed_two[part], cotangent[part])
        if results:
            sources, results, weight_grads = lax.optimization_barrier(
                (sources, results, weight_grads)
            )
        *result, grads = experts(
            *sources,
            split_gates[:, :, part].reshape(local_experts, ranks * piece),
            w_gate,
            w_up,
            w_down,
            experts_total,
        )
        results.append(result)
        weight_grads = grads if weight_grads is None else [a + b for a, b in zip(weight_grads, grads)]
    mixture, moe_input_grad, chance_grad = (
        jnp.concatenate(list(group_of), axis=0) for group_of in zip(*results)
    )
    grad_w_gate, grad_w_up, grad_w_down = weight_grads
    chance_grad = rows_mask * chance_grad
    output = (hidden + mixture).astype(jnp.bfloat16)
    logit_grad = (
        chances * (chance_grad - jnp.sum(chances * chance_grad, axis=1, keepdims=True))
    ).astype(jnp.bfloat16)
    grad_router = jnp.einsum(
        "td,te->de", normed_two, logit_grad, preferred_element_type=jnp.float32
    )
    normed_two_grad = moe_input_grad + jnp.einsum(
        "te,de->td", logit_grad, router, preferred_element_type=jnp.float32
    )
    weighted_two = ffn_gain * normed_two_grad
    grad_ffn_gain = jnp.sum(normed_two_grad * hidden * scale_two, axis=0)
    hidden_grad = (
        grad_out
        + scale_two * weighted_two
        - hidden * (scale_two**3 / width) * jnp.sum(weighted_two * hidden, axis=1, keepdims=True)
    )
    attention_grad = hidden_grad.astype(jnp.bfloat16)
    grad_w_out = jnp.einsum(
        "td,te->de", attended, attention_grad, preferred_element_type=jnp.float32
    )
    attended_grad = jnp.einsum(
        "te,de->td", attention_grad, w_out, preferred_element_type=jnp.float32
    ).astype(jnp.bfloat16)
    query_grads = []
    key_grads = []
    value_grads = []
    for head in range(head_count):
        start = head * HD
        query_head = query_rot[:, start : start + HD]
        key_head = all_keys[:, start : start + HD]
        value_head = all_values[:, start : start + HD]
        out_grad_head = attended_grad[:, start : start + HD]
        recomputed = jnp.exp(head_scores(query_head, key_head) - log_totals[head])
        share_grad = jnp.einsum(
            "qd,kd->qk", out_grad_head, value_head, preferred_element_type=jnp.float32
        )
        delta = jnp.sum(recomputed * share_grad, axis=1, keepdims=True)
        score_grad = (recomputed * (share_grad - delta)).astype(jnp.bfloat16)
        query_grads.append(
            jnp.dot(score_grad, key_head, preferred_element_type=jnp.float32) * factor
        )
        key_grads.append(
            jnp.einsum("qk,qd->kd", score_grad, query_head, preferred_element_type=jnp.float32)
            * factor
        )
        value_grads.append(
            jnp.einsum(
                "qk,qd->kd",
                recomputed.astype(jnp.bfloat16),
                out_grad_head,
                preferred_element_type=jnp.float32,
            )
        )
    key_grad_all = jnp.concatenate(key_grads, axis=1)
    value_grad_all = jnp.concatenate(value_grads, axis=1)
    prompt_key_grad, prompt_value_grad = (
        lax.psum_scatter(
            key_grad_all[:prompt_count].astype(jnp.bfloat16),
            "expert",
            scatter_dimension=0,
            tiled=True,
        ).astype(jnp.float32),
        lax.psum_scatter(
            value_grad_all[:prompt_count].astype(jnp.bfloat16),
            "expert",
            scatter_dimension=0,
            tiled=True,
        ).astype(jnp.float32),
    )
    key_grad = jnp.concatenate([prompt_key_grad, key_grad_all[prompt_count:]], axis=0)
    value_grad = jnp.concatenate([prompt_value_grad, value_grad_all[prompt_count:]], axis=0)
    query_grad = unrotate(
        jnp.concatenate(query_grads, axis=1).reshape(rows, head_count, HD), cosine, sine
    ).reshape(rows, local_width)
    key_grad = unrotate(key_grad.reshape(rows, head_count, HD), cosine, sine).reshape(
        rows, local_width
    )
    grad_qk_gain = jnp.stack(
        [
            jnp.sum(query_grad * query_raw * scale_query, axis=0),
            jnp.sum(key_grad * key_raw * scale_key, axis=0),
        ],
        axis=0,
    )
    weighted_query = qk_gain[0] * query_grad
    weighted_key = qk_gain[1] * key_grad
    inner_sums = lax.psum(
        jnp.stack(
            [jnp.sum(weighted_query * query_raw, axis=1), jnp.sum(weighted_key * key_raw, axis=1)],
            axis=1,
        ),
        "tensor",
    )
    query_raw_grad = (
        scale_query * weighted_query - query_raw * (scale_query**3 / width) * inner_sums[:, 0:1]
    ).astype(jnp.bfloat16)
    key_raw_grad = (
        scale_key * weighted_key - key_raw * (scale_key**3 / width) * inner_sums[:, 1:2]
    ).astype(jnp.bfloat16)
    value_raw_grad = value_grad.astype(jnp.bfloat16)
    grad_w_query = jnp.einsum(
        "td,te->de", normed, query_raw_grad, preferred_element_type=jnp.float32
    )
    grad_w_key = jnp.einsum("td,te->de", normed, key_raw_grad, preferred_element_type=jnp.float32)
    grad_w_value = jnp.einsum(
        "td,te->de", normed, value_raw_grad, preferred_element_type=jnp.float32
    )
    normed_part = jnp.einsum(
        "te,de->td", query_raw_grad, w_query, preferred_element_type=jnp.float32
    )
    normed_part = normed_part + jnp.einsum(
        "te,de->td", key_raw_grad, w_key, preferred_element_type=jnp.float32
    )
    normed_part = normed_part + jnp.einsum(
        "te,de->td", value_raw_grad, w_value, preferred_element_type=jnp.float32
    )
    normed_grad = lax.psum(normed_part.astype(jnp.bfloat16), "tensor").astype(jnp.float32)
    weighted_one = attn_gain * normed_grad
    grad_attn_gain = jnp.sum(normed_grad * source * scale_one, axis=0)
    input_grad = (
        hidden_grad
        + scale_one * weighted_one
        - source * (scale_one**3 / width) * jnp.sum(weighted_one * source, axis=1, keepdims=True)
    )
    summed = (
        lax.psum_scatter(
            grad_w_query.astype(jnp.bfloat16), "expert", scatter_dimension=0, tiled=True
        ).astype(jnp.float32),
        lax.psum_scatter(
            grad_w_key.astype(jnp.bfloat16), "expert", scatter_dimension=0, tiled=True
        ).astype(jnp.float32),
        lax.psum_scatter(
            grad_w_value.astype(jnp.bfloat16), "expert", scatter_dimension=0, tiled=True
        ).astype(jnp.float32),
        lax.psum_scatter(
            grad_w_out.astype(jnp.bfloat16), "expert", scatter_dimension=1, tiled=True
        ).astype(jnp.float32),
        lax.psum_scatter(
            grad_attn_gain.astype(jnp.bfloat16), "expert", scatter_dimension=0, tiled=True
        ).astype(jnp.float32),
        lax.psum_scatter(
            grad_ffn_gain.astype(jnp.bfloat16), "expert", scatter_dimension=0, tiled=True
        ).astype(jnp.float32),
        lax.psum_scatter(
            grad_qk_gain.astype(jnp.bfloat16), "expert", scatter_dimension=1, tiled=True
        ).astype(jnp.float32),
        lax.psum_scatter(
            grad_router.astype(jnp.bfloat16), "expert", scatter_dimension=0, tiled=True
        ).astype(jnp.float32),
    )
    return (
        output,
        input_grad,
        summed[0],
        summed[1],
        summed[2],
        summed[3],
        summed[4],
        summed[5],
        summed[6],
        summed[7],
        grad_w_gate,
        grad_w_up,
        grad_w_down,
    )


def compact(
    tokens, w_query, w_key, w_value, w_out, attn_gain, ffn_gain, qk_gain, router, w_gate, w_up, w_down,
    routes, cont_group, cotangent,
):
    rows, width = tokens.shape
    local_width = w_query.shape[1]
    head_count = local_width // HD
    experts_total = router.shape[1]
    local_experts = w_gate.shape[0]
    ranks = lax.axis_size("expert")
    device = lax.axis_index("expert")
    full = jnp.float32
    group, position, tag = layout(rows, ranks, device, cont_group)
    channel = jnp.arange(HD)
    frequency = 10000.0 ** (-(channel % (HD // 2)).astype(full) * 2.0 / HD)
    angle = position.astype(full)[:, None] * frequency[None, :]
    cosine = jnp.cos(angle)
    sine = jnp.sin(angle) * jnp.where(channel < HD // 2, -1.0, 1.0)
    bias = jnp.where(attention_mask(group, position, tag, ranks), 0.0, masked_value).astype(full)
    own_first = jnp.roll(router, -device * local_experts, axis=1)
    own_first = jnp.pad(own_first, ((0, 0), (0, LANE - experts_total)))
    expert_bias = jnp.where(jnp.arange(LANE) < experts_total, 0.0, masked_value).astype(full)[None]
    turned_routes = jnp.tile(jnp.pad(routes.T, ((0, -routes.shape[1] % 8), (0, 0)), constant_values=-1), (2, 1))
    hits = routes[:, :, None] == jnp.arange(experts_total, dtype=jnp.int32)
    routed = jnp.pad(jnp.any(hits, axis=1).astype(full), ((0, 0), (0, LANE - experts_total)))
    (
        attention, normed, normed_two, attended, query_rot, keys_values, query_raw, key_raw, stats, routes_all, arrived,
    ) = front(
        tokens, attn_gain[None], ffn_gain[None], w_query, w_key, w_value, w_out, qk_gain, cosine, sine, bias,
        turned_routes,
    )
    arrived_grad = lax.all_gather(cotangent, "expert", axis=0)
    own_expert = device * local_experts + jnp.arange(local_experts, dtype=jnp.int32)
    names = routes_all[:, : turned_routes.shape[0] // 2]
    expert_mask = jnp.any(names[:, :, :, None] == own_expert, axis=1).astype(full)
    expert_mask = jnp.pad(expert_mask, ((0, 0), (0, 0), (0, LANE - local_experts)))
    reduced, gated, gate_grad, up_grad, mixed_part = experts_fused(
        arrived, arrived_grad, expert_mask, own_first, expert_bias, w_gate, w_up, w_down
    )
    all_experts = jnp.pad(router, ((0, 0), (0, LANE - experts_total)))
    (
        query_raw_grad, key_raw_grad, value_raw_grad, grad_qk_gain, hidden_grad, attention_grad, extras,
    ) = backward(
        reduced, tokens, attention, cotangent, normed_two, all_experts, expert_bias, routed, ffn_gain[None],
        w_out, query_rot, keys_values, bias, stats, query_raw, key_raw, cosine, sine, qk_gain, experts_total,
    )
    small_part = local_width // ranks
    share = width // ranks
    gains = grad_qk_gain.reshape(2, ranks, small_part).transpose(1, 2, 0).astype(jnp.bfloat16)
    extras = extras.reshape(ranks, share, LANE) + jnp.pad(
        gains, ((0, 0), (0, share - small_part), (experts_total + 1, LANE - experts_total - 3))
    )
    normed_grad, sums, gain_total, mixture, grad_w_gate, grad_w_up, grad_w_down = closing(
        normed, query_raw_grad, key_raw_grad, value_raw_grad, attended, attention_grad, extras, w_query, w_key, w_value,
        mixed_part, arrived, arrived_grad, gated, gate_grad, up_grad, local_experts, experts_total + 3,
    )
    source = tokens.astype(full)
    hidden = source + attention.astype(full)
    scale_one = stats[:, 0:1]
    normed_grad = normed_grad.astype(full)
    output = (hidden + mixture.astype(full)).astype(jnp.bfloat16)
    weighted_one = attn_gain * normed_grad
    input_grad = (
        hidden_grad
        + scale_one * weighted_one
        - source * (scale_one**3 / width) * jnp.sum(weighted_one * source, axis=1, keepdims=True)
    )
    edge = 4 * local_width
    return (
        output,
        input_grad,
        sums[:, :local_width],
        sums[:, local_width : 2 * local_width],
        sums[:, 2 * local_width : 3 * local_width],
        sums[:, 3 * local_width : edge].T,
        gain_total[0] / lax.dynamic_slice_in_dim(attn_gain, device * share, share),
        sums[:, edge + experts_total],
        sums[:small_part, edge + experts_total + 1 : edge + experts_total + 3].T,
        sums[:, edge : edge + experts_total],
        grad_w_gate.astype(full),
        grad_w_up.astype(full),
        grad_w_down.astype(full),
    )


def layout(rows, ranks, device, cont_group):
    span = ranks // 2
    prompt_len = PROMPT_DEV * span
    local = jnp.arange(rows, dtype=jnp.int32)
    is_prompt = local < PROMPT_DEV
    after = jnp.maximum(local - PROMPT_DEV, 0)
    slot_cont = after // CLEN
    cont_pick = jnp.sum(
        jnp.where(
            slot_cont[:, None] == jnp.arange(CONT_DEV, dtype=jnp.int32)[None, :], cont_group[None, :], 0
        ),
        axis=1,
    )
    group = jnp.where(is_prompt, device // span, cont_pick)
    position = jnp.where(is_prompt, device % span * PROMPT_DEV + local, prompt_len + after % CLEN)
    tag = jnp.where(is_prompt, -1, slot_cont)
    return group, position, tag


def attention_mask(group, position, tag, ranks):
    prompt_len = PROMPT_DEV * (ranks // 2)
    key_index = jnp.arange(ranks * PROMPT_DEV, dtype=jnp.int32)
    prompt_mask = (group[:, None] == (key_index // prompt_len)[None, :]) & (
        (key_index % prompt_len)[None, :] <= position[:, None]
    )
    own_mask = (tag[:, None] == tag[None, PROMPT_DEV:]) & (
        position[None, PROMPT_DEV:] <= position[:, None]
    )
    return jnp.concatenate([prompt_mask, own_mask], axis=1)


def solution(mesh):
    small = mesh.shape["expert"] == 8
    return jax.shard_map(
        compact if small else body,
        mesh=mesh,
        in_specs=(
            P("expert", None),
            P(None, "tensor"),
            P(None, "tensor"),
            P(None, "tensor"),
            P("tensor", None),
            P(),
            P(),
            P(None, "tensor"),
            P(),
            P("expert", None, "tensor"),
            P("expert", None, "tensor"),
            P("expert", "tensor", None),
            P("expert", None),
            P("expert"),
            P("expert", None),
        ),
        out_specs=(
            P("expert", None),
            P("expert", None),
            P("expert", "tensor"),
            P("expert", "tensor"),
            P("expert", "tensor"),
            P("tensor", "expert"),
            P("expert"),
            P("expert"),
            P(None, ("tensor", "expert")),
            P("expert", None),
            P("expert", None, "tensor"),
            P("expert", None, "tensor"),
            P("expert", "tensor", None),
        ),
        check_vma=False,
    )
```

```python
import functools

import jax
import jax.numpy as jnp
from jax import lax
from jax.experimental import pallas as pl
from jax.experimental.pallas import tpu as pltpu
from jax.sharding import PartitionSpec as P

HD = 128
PROMPT_DEV = 128
CLEN = 256
CONT_DEV = 1


epsilon = 1e-05
masked_value = -1e30


MESH = pl.DeviceIdType.MESH
STEP = 16
LANE = 128


def remote(source, target, sent, received, **where):
    return pltpu.make_async_remote_copy(
        src_ref=source,
        dst_ref=target,
        send_sem=sent,
        recv_sem=received,
        device_id=where,
        device_id_type=MESH,
    )


def greet(places):
    barrier = pltpu.get_barrier_semaphore()
    for condition, where in places:
        def signal(where=where):
            pl.semaphore_signal(barrier, inc=1, device_id=where, device_id_type=MESH)
        if condition is None:
            signal()
        else:
            pl.when(condition)(signal)
    count = 0
    for condition, _ in places:
        count = count + (1 if condition is None else jnp.where(condition, 1, 0))
    pl.semaphore_wait(barrier, count)


class Line:
    def __init__(self, own, arrived, spare, total, sems, step=STEP):
        self.step = step
        self.own, self.arrived, self.spare, self.total = own, arrived, spare, total
        self.up_sent, self.far_got, self.near_got, self.far_sent, self.near_sent, self.down_got = (
            sems.at[i] for i in range(6)
        )
        self.size = lax.axis_size("tensor")
        self.here = lax.axis_index("tensor")
        self.root = self.size // 2 - 1
        self.rise_steps = self.size - 1 - self.root
        self.trip = 2 * self.rise_steps
        self.half = own.shape[0] // 2
        self.pieces = self.half // step

    @staticmethod
    def semaphores(rows, step=STEP):
        return pltpu.SemaphoreType.DMA((6, 2, rows // 2 // step))

    @staticmethod
    def spare_shape(rows, width):
        return pltpu.VMEM((rows // 2, width), jnp.bfloat16)

    def neighbours(self):
        here, size = self.here, self.size
        return [
            (here > 0, {"tensor": jnp.maximum(here - 1, 0)}),
            (here < size - 1, {"tensor": jnp.minimum(here + 1, size - 1)}),
        ]

    def place(self, lane):
        return self.here if lane == 0 else self.size - 1 - self.here

    def device(self, lane, place):
        return place if lane == 0 else self.size - 1 - place

    def rows(self, lane, piece):
        return pl.ds(pl.multiple_of(lane * self.half + piece * self.step, self.step), self.step)

    def landing(self, piece):
        return pl.ds(pl.multiple_of(piece * self.step, self.step), self.step)

    def far_up(self, lane, piece):
        rows, place = self.rows(lane, piece), self.place(lane)
        inward = jnp.where(place > self.root, place - 1, place + 1)
        return remote(
            self.own.at[rows], self.arrived.at[rows],
            self.up_sent.at[lane, piece], self.far_got.at[lane, piece], tensor=self.device(lane, inward),
        )

    def near_up(self, lane, piece):
        return remote(
            self.own.at[self.rows(lane, piece)], self.spare.at[self.landing(piece)],
            self.up_sent.at[lane, piece], self.near_got.at[lane, piece], tensor=self.device(lane, self.root),
        )

    def down(self, lane, piece, away):
        rows = self.rows(lane, piece)
        sent = self.far_sent if away == 1 else self.near_sent
        return remote(
            self.total.at[rows], self.total.at[rows],
            sent.at[lane, piece], self.down_got.at[lane, piece], tensor=self.device(lane, self.place(lane) + away),
        )

    def rise(self, lane, piece):
        place, root = self.place(lane), self.root
        rows = self.rows(lane, piece)

        def value(field):
            return field.astype(jnp.float32)

        @pl.when((place > root) & (place < self.size - 1) | (place > 0) & (place < root))
        def _():
            self.far_up(lane, piece).wait_recv()
            self.own[rows] = (value(self.own[rows]) + value(self.arrived[rows])).astype(jnp.bfloat16)

        @pl.when(place == root)
        def _():
            self.far_up(lane, piece).wait_recv()
            summed = value(self.own[rows]) + value(self.arrived[rows])
            if root > 0:
                self.near_up(lane, piece).wait_recv()
                summed = summed + value(self.spare[self.landing(piece)])
            self.total[rows] = summed.astype(jnp.bfloat16)
            self.down(lane, piece, 1).start()
            if root > 0:
                self.down(lane, piece, -1).start()

        if root > 0:

            @pl.when(place == root - 1)
            def _():
                self.near_up(lane, piece).start()

        @pl.when((place > root) | (place < root - 1))
        def _():
            self.far_up(lane, piece).start()

    def fall(self, lane, piece):
        place, root = self.place(lane), self.root

        @pl.when(place != root)
        def _():
            self.down(lane, piece, 1).wait_recv()

        @pl.when((place > root) & (place < self.size - 1))
        def _():
            self.down(lane, piece, 1).start()

        @pl.when((place > 0) & (place < root))
        def _():
            self.down(lane, piece, -1).start()

    def advance(self, step):
        for lane in range(2):
            place = self.place(lane)
            steps_in = self.rise_steps - jnp.abs(place - self.root)
            piece = step - steps_in

            @pl.when((piece >= 0) & (piece < self.pieces))
            def _():
                self.rise(lane, piece)

        for lane in range(2):
            place = self.place(lane)
            piece = step - self.rise_steps - jnp.abs(place - self.root)

            @pl.when((piece >= 0) & (piece < self.pieces))
            def _():
                self.fall(lane, piece)

    def step_body(self, step, carry):
        self.advance(step)
        return carry

    def steps(self):
        return self.pieces + self.trip

    def finish(self):
        def one(piece, carry):
            for lane in range(2):
                place, root = self.place(lane), self.root

                @pl.when(place != root)
                def _():
                    self.far_up(lane, piece).wait_send()

                @pl.when((place >= root) & (place < self.size - 1))
                def _():
                    self.down(lane, piece, 1).wait_send()

                @pl.when((place <= root) & (place > 0))
                def _():
                    self.down(lane, piece, -1).wait_send()
            return carry

        lax.fori_loop(0, self.pieces, one, 0)


class Place:
    def __init__(self):
        here = lax.axis_index("expert")
        self.here = here
        self.core, self.x, self.y = here % 2, here // 2 % 2, here // 4
        self.sibling = here + 1 - 2 * self.core
        self.x_chip = here + 2 - 4 * self.x
        self.y_chip = here + 4 - 8 * self.y

    def neighbours(self):
        return [(None, {"expert": i}) for i in (self.sibling, self.x_chip, self.y_chip)]

    def block(self, chip, core):
        x = self.x + (1 - chip // 2) * (1 - 2 * self.x)
        y = self.y + (1 - chip % 2) * (1 - 2 * self.y)
        return 4 * y + 2 * x + core


class Plane(Place):
    def __init__(self, own, spare, paired, from_x, from_y, pair_sems, x_sems, y_sems, by_device=False, step=STEP):
        self.step = step
        self.by_device = by_device
        self.own, self.spare, self.paired, self.from_x, self.from_y = own, spare, paired, from_x, from_y
        self.pair_sems, self.x_sems, self.y_sems = pair_sems, x_sems, y_sems
        super().__init__()
        self.half = own.shape[1] // 2
        self.pieces = self.half // step

    @staticmethod
    def semaphores(rows, step=STEP):
        pieces = rows // 2 // step
        return [
            pltpu.SemaphoreType.DMA((2, 4)),
            pltpu.SemaphoreType.DMA((2, 3, pieces)),
            pltpu.SemaphoreType.DMA((2, 3, pieces)),
        ]

    def pair_copy(self, chip):
        place = self.block(chip, 1 - self.core) if self.by_device else chip
        return remote(
            self.spare.at[place], self.paired.at[chip],
            self.pair_sems.at[0, chip], self.pair_sems.at[1, chip], expert=self.sibling,
        )

    def rows(self, side, piece):
        return pl.ds(pl.multiple_of(side * self.half + piece * self.step, self.step), self.step)

    def landing(self, piece):
        return pl.ds(pl.multiple_of(piece * self.step, self.step), self.step)

    def x_copy(self, kind, piece):
        chip, side = ((0, 0), (1, 0), (1, 1))[kind]
        return remote(
            self.own.at[chip, self.rows(side, piece)], self.from_x.at[kind, self.landing(piece)],
            self.x_sems.at[0, kind, piece], self.x_sems.at[1, kind, piece], expert=self.x_chip,
        )

    def y_copy(self, kind, piece):
        chip, side = ((0, 1), (2, 1), (2, 0))[kind]
        return remote(
            self.own.at[chip, self.rows(side, piece)], self.from_y.at[kind, self.landing(piece)],
            self.y_sems.at[0, kind, piece], self.y_sems.at[1, kind, piece], expert=self.y_chip,
        )

    def add_pair(self, chip, side, piece):
        rows = self.rows(side, piece)
        self.own[chip, rows] = (
            self.own[chip, rows].astype(jnp.float32) + self.paired[chip, rows].astype(jnp.float32)
        ).astype(jnp.bfloat16)

    def each(self, step):
        def one(piece, carry):
            step(piece)
            return carry

        lax.fori_loop(0, self.pieces, one, 0)

    def send_first(self, chip):
        def step(piece):
            if chip in (0, 1):
                self.add_pair(chip, 0, piece)
                self.x_copy(chip, piece).start()
            if chip in (0, 2):
                self.add_pair(chip, 1, piece)
                self.y_copy(chip // 2, piece).start()

        self.each(step)

    def first_piece(self, piece):
        for chip, side in ((0, 0), (0, 1), (1, 0), (2, 1)):
            self.add_pair(chip, side, piece)
        for kind in range(2):
            self.x_copy(kind, piece).start()
            self.y_copy(kind, piece).start()

    def second_piece(self, piece):
        landed = self.landing(piece)
        self.y_copy(0, piece).wait_recv()
        rows = self.rows(1, piece)
        self.own[1, rows] = (
            self.own[1, rows].astype(jnp.float32)
            + self.paired[1, rows].astype(jnp.float32)
            + self.from_y[0, landed].astype(jnp.float32)
        ).astype(jnp.bfloat16)
        self.x_copy(2, piece).start()
        self.x_copy(0, piece).wait_recv()
        rows = self.rows(0, piece)
        self.own[2, rows] = (
            self.own[2, rows].astype(jnp.float32)
            + self.paired[2, rows].astype(jnp.float32)
            + self.from_x[0, landed].astype(jnp.float32)
        ).astype(jnp.bfloat16)
        self.y_copy(2, piece).start()

    def send_second(self):
        self.each(self.second_piece)

    def last_sum(self, piece):
        landed = self.landing(piece)
        sums = []
        for side in range(2):
            first, second = (self.x_copy(1, piece), self.y_copy(2, piece)) if side == 0 else (self.y_copy(1, piece), self.x_copy(2, piece))
            first.wait_recv()
            second.wait_recv()
            a, b = (self.from_x[1, landed], self.from_y[2, landed]) if side == 0 else (self.from_y[1, landed], self.from_x[2, landed])
            rows = self.rows(side, piece)
            sums.append(
                self.own[3, rows].astype(jnp.float32)
                + self.paired[3, rows].astype(jnp.float32)
                + a.astype(jnp.float32)
                + b.astype(jnp.float32)
            )
        return sums

    def finish(self):
        for chip in range(4):
            self.pair_copy(chip).wait_send()

        def step(piece):
            for kind in range(3):
                self.x_copy(kind, piece).wait_send()
                self.y_copy(kind, piece).wait_send()

        self.each(step)


class Gather:
    def __init__(self, source, target, place, x_sems, y_sems, far_sems, pair_sems, own_sem, pieces):
        self.source, self.target = source, target
        self.place = place
        self.x_sems, self.y_sems, self.far_sems, self.pair_sems, self.own_sem = x_sems, y_sems, far_sems, pair_sems, own_sem
        self.pieces = pieces
        self.rows_each = source.shape[0] // pieces

    @staticmethod
    def semaphores(pieces):
        return [
            pltpu.SemaphoreType.DMA((2, pieces)),
            pltpu.SemaphoreType.DMA((2, pieces)),
            pltpu.SemaphoreType.DMA((2, pieces)),
            pltpu.SemaphoreType.DMA((2, 4, pieces)),
            pltpu.SemaphoreType.DMA,
        ]

    def rows(self, piece):
        return pl.ds(piece * self.rows_each, self.rows_each)

    def own_copy(self):
        return pltpu.make_async_copy(self.source, self.target.at[self.place.here], self.own_sem)

    def x_copy(self, piece):
        rows = self.rows(piece)
        return remote(
            self.source.at[rows], self.target.at[self.place.here, rows],
            self.x_sems.at[0, piece], self.x_sems.at[1, piece], expert=self.place.x_chip,
        )

    def y_copy(self, piece):
        rows = self.rows(piece)
        return remote(
            self.source.at[rows], self.target.at[self.place.here, rows],
            self.y_sems.at[0, piece], self.y_sems.at[1, piece], expert=self.place.y_chip,
        )

    def far_copy(self, piece):
        rows = self.rows(piece)
        came, goes = (
            (self.place.x_chip, self.place.y_chip) if piece % 2 == 0 else (self.place.y_chip, self.place.x_chip)
        )
        return remote(
            self.target.at[came, rows], self.target.at[came, rows],
            self.far_sems.at[0, piece], self.far_sems.at[1, piece], expert=goes,
        )

    def pair_copy(self, kind, piece):
        rows = self.rows(piece)
        block = self.place.block(kind, self.place.core)
        source = self.source.at[rows] if kind == 3 else self.target.at[block, rows]
        return remote(
            source, self.target.at[block, rows],
            self.pair_sems.at[0, kind, piece], self.pair_sems.at[1, kind, piece], expert=self.place.sibling,
        )

    def start_piece(self, piece):
        self.x_copy(piece).start()
        self.y_copy(piece).start()
        self.pair_copy(3, piece).start()

    def start(self):
        self.own_copy().start()
        for piece in range(self.pieces):
            self.start_piece(piece)

    def near(self, piece):
        self.x_copy(piece).wait_recv()
        if piece % 2 == 0:
            self.far_copy(piece).start()
        self.pair_copy(1, piece).start()
        self.y_copy(piece).wait_recv()
        if piece % 2 == 1:
            self.far_copy(piece).start()
        self.pair_copy(2, piece).start()

    def far(self, piece):
        self.far_copy(piece).wait_recv()
        self.pair_copy(0, piece).start()

    def paired(self, kind, piece):
        self.pair_copy(kind, piece).wait_recv()

    def finish(self):
        for piece in range(self.pieces):
            self.x_copy(piece).wait_send()
            self.y_copy(piece).wait_send()
            self.far_copy(piece).wait_send()
            for kind in range(4):
                self.pair_copy(kind, piece).wait_send()


def wide_dot(left, right):
    return jnp.dot(left, right, preferred_element_type=jnp.float32)


def turned_dot(left, right):
    return lax.dot_general(left, right, (((1,), (1,)), ((), ())), preferred_element_type=jnp.float32)


BLOCK_STEP = 32


def expert_kernel(
    x_all, g_all, mask, router, bias, w_gate, w_up, w_down,
    reduced, gated_all, gate_all, up_all, mixed_all,
    x_buf, g_buf, part, paired, from_x, from_y, line_in, line_spare, small, mixed,
    in_sems, out_sems, pair_sems, x_sems, y_sems, line_sems,
):
    experts, width, hidden = w_gate.shape
    rows = x_buf.shape[1]
    tile = min(512, width)
    plane = Plane(part.at[1], part.at[0], paired, from_x, from_y, pair_sems, x_sems, y_sems, step=BLOCK_STEP)
    line = Line(part.at[1, 3], line_in, line_spare, reduced, line_sems, step=BLOCK_STEP)
    first_expert = lax.axis_index("expert") * experts
    outs = (gated_all, gate_all, up_all)

    def block_of(i):
        return plane.block(i // 2, (plane.core + 1 - i % 2) % 2)

    def fetch(i):
        slot, block = i % 2, block_of(i)
        return (
            pltpu.make_async_copy(x_all.at[block], x_buf.at[slot], in_sems.at[0, slot]),
            pltpu.make_async_copy(g_all.at[block], g_buf.at[slot], in_sems.at[1, slot]),
        )

    def store(i):
        slot, block = i % 2, block_of(i)
        return [
            pltpu.make_async_copy(small.at[slot, n], outs[n].at[block], out_sems.at[n, slot])
            for n in range(3)
        ] + [pltpu.make_async_copy(mixed.at[slot], mixed_all.at[block], out_sems.at[3, slot])]

    def compute(i):
        slot = i % 2
        block = block_of(i)
        x = x_buf.at[slot]
        g = g_buf.at[slot]
        logits = wide_dot(x[...], router[...]) + bias[...]
        weights = jnp.exp(logits - jnp.max(logits, axis=1, keepdims=True))
        gates = weights / jnp.sum(weights, axis=1, keepdims=True) * mask[block]
        column = lax.broadcasted_iota(jnp.int32, (rows, LANE), 1)
        extra = jnp.zeros((rows, LANE), jnp.float32)
        for j in range(experts):
            gate_pre = wide_dot(x[...], w_gate[j])
            up_pre = wide_dot(x[...], w_up[j])
            raw = turned_dot(g[...], w_down[j])
            gate = jnp.sum(jnp.where(column == first_expert + j, gates, 0.0), axis=1, keepdims=True)
            sigma = jax.nn.sigmoid(gate_pre)
            activated = gate_pre * sigma
            inner = activated * up_pre
            act = gate * raw
            span = slice(j * hidden, (j + 1) * hidden)
            small[slot, 0, :, span] = (gate * inner).astype(jnp.bfloat16)
            small[slot, 1, :, span] = (
                act * up_pre * sigma * (1.0 + gate_pre * (1.0 - sigma))
            ).astype(jnp.bfloat16)
            small[slot, 2, :, span] = (act * activated).astype(jnp.bfloat16)
            gain = jnp.sum(raw * inner, axis=1, keepdims=True)
            extra = jnp.where(column == first_expert + j, gain, extra)
        for start in range(0, width, tile):
            columns = slice(start, start + tile)
            slot_grad = None
            mix = None
            for j in range(experts):
                span = slice(j * hidden, (j + 1) * hidden)
                term = turned_dot(small[slot, 1, :, span], w_gate[j, columns]) + turned_dot(
                    small[slot, 2, :, span], w_up[j, columns]
                )
                more = wide_dot(small[slot, 0, :, span], w_down[j, :, columns])
                slot_grad = term if slot_grad is None else slot_grad + term
                mix = more if mix is None else mix + more
            part[i % 2, i // 2, :, columns] = slot_grad.astype(jnp.bfloat16)
            mixed[slot, :, columns] = mix.astype(jnp.bfloat16)
        part[i % 2, i // 2, :, width:] = extra.astype(jnp.bfloat16)

    for copy in fetch(0):
        copy.start()
    greet(plane.neighbours() + line.neighbours())

    def step(i, carry):
        @pl.when(i < 7)
        def _():
            for copy in fetch(i + 1):
                copy.start()

        for copy in fetch(i):
            copy.wait()

        @pl.when(i >= 2)
        def _():
            for copy in store(i - 2):
                copy.wait()

        compute(i)
        for copy in store(i):
            copy.start()

        @pl.when(i % 2 == 0)
        def _():
            plane.pair_copy(i // 2).start()

        @pl.when(i % 2 == 1)
        def _():
            plane.pair_copy(i // 2).wait_recv()

        for chip in range(3):

            @pl.when(i == 2 * chip + 1)
            def _():
                plane.send_first(chip)
                if chip == 2:
                    plane.send_second()

        return carry

    lax.fori_loop(0, 8, step, 0)

    def last(step, carry):
        @pl.when(step < plane.pieces)
        def _():
            for side, total in enumerate(plane.last_sum(step)):
                plane.own[3, plane.rows(side, step)] = total.astype(jnp.bfloat16)

        line.advance(step)
        return carry

    lax.fori_loop(0, line.steps(), last, 0)
    for i in (6, 7):
        for copy in store(i):
            copy.wait()
    plane.finish()
    line.finish()


def experts_fused(arrived, arrived_grad, mask, router, bias, w_gate, w_up, w_down):
    ranks, rows, width = arrived.shape
    experts, _, hidden = w_gate.shape
    wide = width + LANE
    inner = experts * hidden
    half = rows // 2
    low = jnp.bfloat16
    any_space = pl.BlockSpec(memory_space=pl.ANY)
    vmem = pl.BlockSpec(memory_space=pltpu.VMEM)
    small_shape = jax.ShapeDtypeStruct((ranks, rows, inner), low)
    return pl.pallas_call(
        expert_kernel,
        out_shape=(
            jax.ShapeDtypeStruct((rows, wide), low), small_shape, small_shape, small_shape,
            jax.ShapeDtypeStruct((ranks, rows, width), low),
        ),
        in_specs=[any_space, any_space] + [vmem] * 6,
        out_specs=(vmem, any_space, any_space, any_space, any_space),
        scratch_shapes=[
            pltpu.VMEM((2, rows, width), low),
            pltpu.VMEM((2, rows, width), low),
            pltpu.VMEM((2, 4, rows, wide), low),
            pltpu.VMEM((4, rows, wide), low),
            pltpu.VMEM((3, half, wide), low),
            pltpu.VMEM((3, half, wide), low),
            pltpu.VMEM((rows, wide), low),
            Line.spare_shape(rows, wide),
            pltpu.VMEM((2, 3, rows, inner), low),
            pltpu.VMEM((2, rows, width), low),
            pltpu.SemaphoreType.DMA((2, 2)),
            pltpu.SemaphoreType.DMA((4, 2)),
            *Plane.semaphores(rows, step=BLOCK_STEP),
            Line.semaphores(rows, step=BLOCK_STEP),
        ],
        compiler_params=pltpu.CompilerParams(
            collective_id=0, has_side_effects=True, vmem_limit_bytes=61 * 2**20
        ),
        cost_estimate=pl.CostEstimate(
            flops=12 * ranks * rows * width * inner, bytes_accessed=8 * ranks * rows * width, transcendentals=0
        ),
    )(arrived, arrived_grad, mask, router, bias, w_gate, w_up, w_down)


def crossed_dot(left, right):
    return lax.dot_general(left, right, (((0,), (0,)), ((), ())), preferred_element_type=jnp.float32)


def closing_kernel(
    normed, query_grad, key_grad, value_grad, attended, attention_grad, extras,
    w_query, w_key, w_value, mixed, x_all, g_all, gated_all, gate_all, up_all,
    total, sums, turned, gain, mixture, gate_out, up_out, down_out,
    line_own, line_in, line_spare, part, paired, from_x, from_y,
    mix_own, mix_paired, mix_x, mix_y, mix_in, mix_spare, tiles, factors, results, downs,
    line_sems, pair_sems, x_sems, y_sems, mix_line_sems, mix_pair_sems, mix_x_sems, mix_y_sems,
    load_sems, weight_sems, factor_sems, tile_sems, out_sems,
    gains, mine, theirs, peer_sent, peer_got,
    *,
    gain_column,
):
    width = normed.shape[1]
    heads = query_grad.shape[1]
    share = part.shape[2]
    experts, _, hidden = gate_out.shape
    column_tile = min(512, width // 2)
    tile = tiles.shape[2]
    count = width // tile
    line = Line(line_own, line_in, line_spare, total, line_sems)
    plane = Plane(part.at[1], part.at[0], paired, from_x, from_y, pair_sems, x_sems, y_sems)
    mix = Plane(mix_own, mixed, mix_paired, mix_x, mix_y, mix_pair_sems, mix_x_sems, mix_y_sems, by_device=True)
    mix_line = Line(mix_own.at[3], mix_in, mix_spare, mixture, mix_line_sems)
    peers = Peers(mine, theirs, peer_sent, peer_got)
    half = width // 2

    def load_own(chip):
        return pltpu.make_async_copy(mixed.at[mix.block(chip, mix.core)], mix_own.at[chip], load_sems.at[chip])

    weight_loads = [
        pltpu.make_async_copy(w_query, factors.at[0, 0:width], weight_sems.at[0]),
        pltpu.make_async_copy(w_key, factors.at[1, 0:width], weight_sems.at[1]),
        pltpu.make_async_copy(w_value.at[0:half], factors.at[0, width : width + half], weight_sems.at[2]),
        pltpu.make_async_copy(w_value.at[half:], factors.at[1, width : width + half], weight_sems.at[3]),
    ]

    def factor_load(matrix):
        return pltpu.make_async_copy(
            (gate_all, up_all, gated_all)[matrix], factors.at[matrix % 2], factor_sems.at[matrix]
        )

    def tile_copy(source, s):
        columns = pl.ds(pl.multiple_of(s % count * tile, tile), tile)
        return pltpu.make_async_copy(source.at[:, columns], tiles.at[s % 2], tile_sems.at[s % 2])

    def start_tile(s):
        @pl.when(s < 2 * count)
        def _():
            tile_copy(x_all, s).start()

        @pl.when(s >= 2 * count)
        def _():
            tile_copy(g_all, s).start()

    def across(target, s):
        rows = pl.ds(pl.multiple_of(s % count * tile, tile), tile)
        return [
            pltpu.make_async_copy(
                results.at[s % 2, :, j * hidden : (j + 1) * hidden], target.at[j, rows], out_sems.at[0, s % 2, j]
            )
            for j in range(experts)
        ]

    def down(s):
        columns = pl.ds(pl.multiple_of(s % count * tile, tile), tile)
        return [
            pltpu.make_async_copy(
                downs.at[s % 2, j * hidden : (j + 1) * hidden], down_out.at[j, :, columns], out_sems.at[1, s % 2, j]
            )
            for j in range(experts)
        ]

    def expert_tile(s):
        @pl.when(s + 1 < 3 * count)
        def _():
            start_tile(s + 1)

        for matrix in range(3):

            @pl.when(s == matrix * count)
            def _():
                factor_load(matrix).wait()

        tile_copy(x_all, s).wait()

        @pl.when(s < 2 * count)
        def _():
            @pl.when(s >= 2)
            def _():
                for copy in across(gate_out, s):
                    copy.wait()

            results[s % 2] = crossed_dot(tiles[s % 2], factors[s // count]).astype(jnp.bfloat16)

            @pl.when(s < count)
            def _():
                for copy in across(gate_out, s):
                    copy.start()

            @pl.when(s >= count)
            def _():
                for copy in across(up_out, s):
                    copy.start()

        @pl.when(s >= 2 * count)
        def _():
            @pl.when(s >= 2 * count + 2)
            def _():
                for copy in down(s):
                    copy.wait()

            downs[s % 2] = crossed_dot(factors[0], tiles[s % 2]).astype(jnp.bfloat16)
            for copy in down(s):
                copy.start()

        @pl.when(s == count - 1)
        def _():
            factor_load(2).start()

    def dense_block(i):
        chip, sub = i // 2, i % 2
        block = plane.block(chip, (plane.core + 1 - sub) % 2)
        columns = pl.ds(pl.multiple_of(block * share, share), share)
        source = normed[:, columns]
        part[sub, chip, :, 0:heads] = crossed_dot(source, query_grad[...]).astype(jnp.bfloat16)
        part[sub, chip, :, heads : 2 * heads] = crossed_dot(source, key_grad[...]).astype(jnp.bfloat16)
        part[sub, chip, :, 2 * heads : 3 * heads] = crossed_dot(source, value_grad[...]).astype(jnp.bfloat16)
        part[sub, chip, :, 3 * heads : 4 * heads] = crossed_dot(
            attention_grad[:, columns], attended[...]
        ).astype(jnp.bfloat16)
        part[sub, chip, :, 4 * heads :] = extras[block] + gains[columns]

        @pl.when(sub == 0)
        def _():
            plane.pair_copy(chip).start()

    for copy in weight_loads:
        copy.start()
    for chip in range(4):
        load_own(chip).start()
    greet(plane.neighbours() + peers.neighbours())
    for chip in range(4):
        mix.pair_copy(chip).start()
    for copy in weight_loads:
        copy.wait()
    for start in range(0, width, column_tile):
        columns = slice(start, start + column_tile)
        later = width + start % half
        line_own[:, columns] = (
            turned_dot(query_grad[...], factors[0, columns])
            + turned_dot(key_grad[...], factors[1, columns])
            + turned_dot(value_grad[...], factors[start // half, later : later + column_tile])
        ).astype(jnp.bfloat16)
    place = lax.broadcasted_iota(jnp.int32, (normed.shape[0], LANE), 1)
    chosen = jnp.where(place == gain_column, 1.0, 0.0).astype(jnp.bfloat16)
    for start in range(0, width, column_tile):
        columns = slice(start, start + column_tile)
        pull = line_own[:, columns].astype(jnp.float32) * normed[:, columns].astype(jnp.float32)
        gains[columns] = crossed_dot(pull.astype(jnp.bfloat16), chosen).astype(jnp.bfloat16)
    factor_load(0).start()
    factor_load(1).start()
    start_tile(0)
    mix_second, mix_last, dense_first, dense_second, dense_last = PLAN

    def step(s, carry):
        line.advance(s)

        @pl.when(s == 0)
        def _():
            for chip in range(3):
                load_own(chip).wait()
                mix.pair_copy(chip).wait_recv()
            for piece in range(AHEAD):
                mix.first_piece(piece)

        @pl.when(s == mix_last - 1)
        def _():
            load_own(3).wait()
            mix.pair_copy(3).wait_recv()

        @pl.when((s > 0) & (s + AHEAD - 1 < mix.pieces))
        def _():
            mix.first_piece(s + AHEAD - 1)

        @pl.when((s >= mix_second) & (s - mix_second < mix.pieces))
        def _():
            mix.second_piece(s - mix_second)

        @pl.when((s >= mix_last) & (s - mix_last < mix.pieces))
        def _():
            piece = s - mix_last
            for side, summed in enumerate(mix.last_sum(piece)):
                mix_own[3, mix.rows(side, piece)] = summed.astype(jnp.bfloat16)

        mix_line.advance(s - mix_last)

        @pl.when((s >= 4) & (s < 12))
        def _():
            dense_block(s - 4)

        @pl.when(s == dense_first)
        def _():
            for chip in range(4):
                plane.pair_copy(chip).wait_recv()
            for chip in range(3):
                plane.send_first(chip)

        @pl.when((s >= dense_second) & (s - dense_second < plane.pieces))
        def _():
            plane.second_piece(s - dense_second)

        @pl.when((s >= dense_last) & (s - dense_last < plane.pieces))
        def _():
            piece = s - dense_last
            for side, summed in enumerate(plane.last_sum(piece)):
                sums[plane.rows(side, piece)] = summed

        @pl.when(s < 3 * count)
        def _():
            expert_tile(s)

        return carry

    steps = jnp.maximum(mix_last + mix_line.steps(), jnp.maximum(3 * count, dense_last + plane.pieces))
    lax.fori_loop(0, steps, step, 0)
    column = 4 * heads + gain_column
    mine[...] = to_rows([sums[:, column : column + 1]], share)
    peers.start()
    turned[...] = sums[:, 3 * heads : 4 * heads].T
    for s in (2 * count - 2, 2 * count - 1):
        for copy in across(up_out, s):
            copy.wait()
    for s in (3 * count - 2, 3 * count - 1):
        for copy in down(s):
            copy.wait()
    gain[...] = peers.total()
    for each in (plane, line, mix, mix_line, peers):
        each.finish()


PLAN = (1, 3, 12, 15, 18)
AHEAD = 2
TILE = 256


def closing(
    normed, query_grad, key_grad, value_grad, attended, attention_grad, extras, w_query, w_key, w_value,
    mixed, arrived, arrived_grad, gated, gate_grad, up_grad, experts, gain_column,
):
    rows, width = normed.shape
    heads = query_grad.shape[1]
    ranks, share, more = extras.shape
    wide = 4 * heads + more
    inner = gated.shape[2]
    hidden = inner // experts
    low = jnp.bfloat16
    tile = min(TILE, width // 2)
    vmem = pl.BlockSpec(memory_space=pltpu.VMEM)
    any_space = pl.BlockSpec(memory_space=pl.ANY)
    every = ranks * rows
    size = lax.axis_size("tensor")
    return pl.pallas_call(
        functools.partial(closing_kernel, gain_column=gain_column),
        out_shape=(
            jax.ShapeDtypeStruct((rows, width), low),
            jax.ShapeDtypeStruct((share, wide), jnp.float32),
            jax.ShapeDtypeStruct((heads, share), jnp.float32),
            jax.ShapeDtypeStruct((8, share), jnp.float32),
            jax.ShapeDtypeStruct((rows, width), low),
            jax.ShapeDtypeStruct((experts, width, hidden), low),
            jax.ShapeDtypeStruct((experts, width, hidden), low),
            jax.ShapeDtypeStruct((experts, hidden, width), low),
        ),
        in_specs=[vmem] * 7 + [any_space] * 9,
        out_specs=(vmem,) * 5 + (any_space,) * 3,
        scratch_shapes=[
            pltpu.VMEM((rows, width), low),
            pltpu.VMEM((rows, width), low),
            Line.spare_shape(rows, width),
            pltpu.VMEM((2, 4, share, wide), low),
            pltpu.VMEM((4, share, wide), low),
            pltpu.VMEM((3, share // 2, wide), low),
            pltpu.VMEM((3, share // 2, wide), low),
            pltpu.VMEM((4, rows, width), low),
            pltpu.VMEM((4, rows, width), low),
            pltpu.VMEM((3, rows // 2, width), low),
            pltpu.VMEM((3, rows // 2, width), low),
            pltpu.VMEM((rows, width), low),
            Line.spare_shape(rows, width),
            pltpu.VMEM((2, every, tile), low),
            pltpu.VMEM((2, every, inner), low),
            pltpu.VMEM((2, tile, inner), low),
            pltpu.VMEM((2, inner, tile), low),
            Line.semaphores(rows),
            *Plane.semaphores(share),
            Line.semaphores(rows),
            *Plane.semaphores(rows),
            pltpu.SemaphoreType.DMA((4,)),
            pltpu.SemaphoreType.DMA((4,)),
            pltpu.SemaphoreType.DMA((3,)),
            pltpu.SemaphoreType.DMA((2,)),
            pltpu.SemaphoreType.DMA((2, 2, experts)),
            pltpu.VMEM((width, LANE), low),
            pltpu.VMEM((8, share), jnp.float32),
            pltpu.VMEM((size - 1, 8, share), jnp.float32),
            pltpu.SemaphoreType.DMA((size - 1,)),
            pltpu.SemaphoreType.DMA((size - 1,)),
        ],
        compiler_params=pltpu.CompilerParams(
            collective_id=2, has_side_effects=True, vmem_limit_bytes=63 * 2**20
        ),
    )(
        normed, query_grad, key_grad, value_grad, attended, attention_grad, extras, w_query, w_key, w_value,
        mixed, arrived.reshape(every, width), arrived_grad.reshape(every, width),
        gated.reshape(every, inner), gate_grad.reshape(every, inner), up_grad.reshape(every, inner),
    )


class Peers:
    def __init__(self, mine, theirs, sent, got):
        self.mine, self.theirs, self.sent, self.got = mine, theirs, sent, got
        self.size = lax.axis_size("tensor")
        self.here = lax.axis_index("tensor")

    def neighbours(self):
        return [(None, {"tensor": (self.here + d) % self.size}) for d in range(1, self.size)]

    def copies(self):
        return [
            remote(
                self.mine, self.theirs.at[d - 1], self.sent.at[d - 1], self.got.at[d - 1],
                tensor=(self.here + d) % self.size,
            )
            for d in range(1, self.size)
        ]

    def start(self):
        for copy in self.copies():
            copy.start()

    def total(self):
        result = self.mine[...]
        for d, copy in enumerate(self.copies()):
            copy.wait_recv()
            result = result + self.theirs[d]
        return result

    def finish(self):
        for copy in self.copies():
            copy.wait_send()


def to_rows(columns, rows):
    lane = lax.broadcasted_iota(jnp.int32, (rows, LANE), 1)
    field = jnp.zeros((rows, LANE), jnp.float32)
    for i, column in enumerate(columns):
        field = jnp.where(lane == i, column, field)
    return field.T[:8]


def to_columns(sums):
    padded = jnp.concatenate([sums, jnp.zeros((LANE - 8, sums.shape[1]), jnp.float32)], axis=0)
    return padded.T


def swapped(field):
    half = HD // 2
    return jnp.concatenate([field[:, half:], field[:, :half]], axis=1)


def loads(pairs, sems):
    copies = [pltpu.make_async_copy(source, target, sems.at[i]) for i, (source, target) in enumerate(pairs)]
    for copy in copies:
        copy.start()
    return copies


SPREAD = 32
SPREAD_LAG = 2


def front_kernel(
    tokens, attn_gain, ffn_gain, w_query, key_far, value_far, out_far, qk_gain, cosine, sine, bias_far, routes,
    total, normed, normed_two, attended, query_rot, keys_values, query_raw, key_raw, stats, routes_all, arrived,
    line_own, line_in, line_spare, prompt, mine, theirs, two, w_key, w_value, w_out, bias,
    load_sems, line_sems, peer_sent, peer_got, *gather_sems,
):
    rows, width = tokens.shape
    local = w_query.shape[1]
    heads = local // HD
    factor = HD ** (-0.5)
    own_blocks = rows // PROMPT_DEV - 1
    devices = keys_values.shape[0] - own_blocks
    place = Place()
    line = Line(line_own, line_in, line_spare, total, line_sems)
    peers = Peers(mine, theirs, peer_sent, peer_got)
    names = Gather(routes, routes_all, place, *gather_sems[0:5], pieces=2)
    prompts = Gather(prompt, keys_values, place, *gather_sems[5:10], pieces=2)
    spread = Gather(normed_two, arrived, place, *gather_sems[10:15], pieces=rows // SPREAD)
    load_key, load_value, load_out, load_bias = loads(
        ((key_far, w_key), (value_far, w_value), (out_far, w_out), (bias_far, bias)), load_sems
    )
    greet(place.neighbours() + peers.neighbours())
    names.start()
    source = tokens[...].astype(jnp.float32)
    scale_one = lax.rsqrt(jnp.sum(source * source, axis=1, keepdims=True) / width + epsilon)
    normed[...] = (source * scale_one * attn_gain[...]).astype(jnp.bfloat16)
    query_raw[...] = wide_dot(normed[...], w_query[...])
    load_key.wait()
    key_raw[...] = wide_dot(normed[...], w_key[...])
    mine[...] = to_rows(
        [
            jnp.sum(query_raw[...] * query_raw[...], axis=1, keepdims=True),
            jnp.sum(key_raw[...] * key_raw[...], axis=1, keepdims=True),
        ],
        rows,
    )
    peers.start()
    load_value.wait()
    value = wide_dot(normed[...], w_value[...]).astype(jnp.bfloat16)
    prompt[:, local:] = value[:PROMPT_DEV]
    for i in range(own_blocks):
        keys_values[devices + i, :, local:] = value[(i + 1) * PROMPT_DEV : (i + 2) * PROMPT_DEV]
    squares = to_columns(peers.total())
    scale_query = lax.rsqrt(squares[:, 0:1] / width + epsilon)
    scale_key = lax.rsqrt(squares[:, 1:2] / width + epsilon)
    for head in range(heads):
        columns = slice(head * HD, (head + 1) * HD)
        turned = key_raw[:, columns] * scale_key * qk_gain[1:2, columns]
        turned = (turned * cosine[...] + swapped(turned) * sine[...]).astype(jnp.bfloat16)
        prompt[:, columns] = turned[:PROMPT_DEV]
        for i in range(own_blocks):
            keys_values[devices + i, :, columns] = turned[(i + 1) * PROMPT_DEV : (i + 2) * PROMPT_DEV]
    prompts.own_copy().start()
    for piece in range(2):
        prompts.start_piece(piece)
    for head in range(heads):
        columns = slice(head * HD, (head + 1) * HD)
        turned = query_raw[:, columns] * scale_query * qk_gain[0:1, columns]
        turned = turned * cosine[...] + swapped(turned) * sine[...]
        query_rot[:, columns] = turned.astype(jnp.bfloat16)
    for piece in range(2):
        prompts.near(piece)
    for piece in range(2):
        names.near(piece)
    for piece in range(2):
        prompts.far(piece)
        names.far(piece)
    prompts.own_copy().wait()
    for kind in range(4):
        for piece in range(2):
            prompts.paired(kind, piece)
            names.paired(kind, piece)
    load_bias.wait()
    load_out.wait()
    lane = lax.broadcasted_iota(jnp.int32, (rows, LANE), 1)
    kept = jnp.where(lane == 0, scale_one, 0.0)
    kept = jnp.where(lane == 1, scale_query, kept)
    kept = jnp.where(lane == 2, scale_key, kept)
    count = keys_values.shape[0] * PROMPT_DEV
    for head in range(heads):
        columns = slice(head * HD, (head + 1) * HD)
        keys = keys_values[:, :, columns].reshape(count, HD)
        values = keys_values[:, :, local + head * HD : local + (head + 1) * HD].reshape(count, HD)
        scores = turned_dot(query_rot[:, columns], keys) * factor + bias[...]
        top = jnp.max(scores, axis=1, keepdims=True)
        weights = jnp.exp(scores - top)
        whole = jnp.sum(weights, axis=1, keepdims=True)
        shares = (weights / whole).astype(jnp.bfloat16)
        attended[:, columns] = wide_dot(shares, values).astype(jnp.bfloat16)
        kept = jnp.where(lane == 8 + head, top + jnp.log(whole), kept)
    tile = min(512, width)
    for start in range(0, width, tile):
        columns = slice(start, start + tile)
        line_own[:, columns] = wide_dot(attended[...], w_out[:, columns]).astype(jnp.bfloat16)
    ratio = SPREAD // STEP
    groups = line.pieces // ratio

    def norm_rows(piece):
        span = slice(piece * SPREAD, (piece + 1) * SPREAD)
        hidden = tokens[span].astype(jnp.float32) + total[span].astype(jnp.float32)
        scale = lax.rsqrt(jnp.sum(hidden * hidden, axis=1, keepdims=True) / width + epsilon)
        normed_two[span] = (hidden * scale * ffn_gain[...]).astype(jnp.bfloat16)
        two[span] = jnp.broadcast_to(scale, (SPREAD, LANE))

    done = 0
    passed = 0
    for group in range(groups):
        ready = line.trip + (group + 1) * ratio
        lax.fori_loop(done, ready, line.step_body, 0)
        done = ready
        for piece in (group, groups + group):
            norm_rows(piece)
            spread.start_piece(piece)
        if group >= SPREAD_LAG:
            for piece in (passed, groups + passed):
                spread.near(piece)
            passed += 1
    spread.own_copy().start()
    for group in range(passed, groups):
        for piece in (group, groups + group):
            spread.near(piece)
    for group in range(groups):
        for piece in (group, groups + group):
            spread.far(piece)
    stats[...] = jnp.where(lane == 3, two[...], kept)
    for kind in range(4):
        for piece in range(spread.pieces):
            spread.paired(kind, piece)
    spread.own_copy().wait()
    names.own_copy().wait()
    for each in (names, prompts, spread, line, peers):
        each.finish()


def front(tokens, attn_gain, ffn_gain, w_query, w_key, w_value, w_out, qk_gain, cosine, sine, bias, routes):
    rows, width = tokens.shape
    local = w_query.shape[1]
    ranks = lax.axis_size("expert")
    size = lax.axis_size("tensor")
    low, full = jnp.bfloat16, jnp.float32
    vmem = pl.BlockSpec(memory_space=pltpu.VMEM)
    any_space = pl.BlockSpec(memory_space=pl.ANY)
    blocks = ranks + rows // PROMPT_DEV - 1
    return pl.pallas_call(
        front_kernel,
        out_shape=(
            jax.ShapeDtypeStruct((rows, width), low),
            jax.ShapeDtypeStruct((rows, width), low),
            jax.ShapeDtypeStruct((rows, width), low),
            jax.ShapeDtypeStruct((rows, local), low),
            jax.ShapeDtypeStruct((rows, local), low),
            jax.ShapeDtypeStruct((blocks, PROMPT_DEV, 2 * local), low),
            jax.ShapeDtypeStruct((rows, local), full),
            jax.ShapeDtypeStruct((rows, local), full),
            jax.ShapeDtypeStruct((rows, LANE), full),
            jax.ShapeDtypeStruct((ranks,) + routes.shape, jnp.int32),
            jax.ShapeDtypeStruct((ranks, rows, width), low),
        ),
        in_specs=[vmem] * 4 + [any_space] * 3 + [vmem] * 3 + [any_space, vmem],
        out_specs=(vmem,) * 10 + (any_space,),
        scratch_shapes=[
            pltpu.VMEM((rows, width), low),
            pltpu.VMEM((rows, width), low),
            Line.spare_shape(rows, width),
            pltpu.VMEM((PROMPT_DEV, 2 * local), low),
            pltpu.VMEM((8, rows), full),
            pltpu.VMEM((size - 1, 8, rows), full),
            pltpu.VMEM((rows, LANE), full),
            *(pltpu.VMEM(array.shape, array.dtype) for array in (w_key, w_value, w_out, bias)),
            pltpu.SemaphoreType.DMA((4,)),
            Line.semaphores(rows),
            pltpu.SemaphoreType.DMA((size - 1,)),
            pltpu.SemaphoreType.DMA((size - 1,)),
            *Gather.semaphores(2),
            *Gather.semaphores(2),
            *Gather.semaphores(rows // SPREAD),
        ],
        compiler_params=pltpu.CompilerParams(
            collective_id=1, has_side_effects=True, vmem_limit_bytes=60 * 2**20
        ),
        cost_estimate=pl.CostEstimate(flops=100 * 10**9, bytes_accessed=200 * 10**6, transcendentals=0),
    )(tokens, attn_gain, ffn_gain, w_query, w_key, w_value, w_out, qk_gain, cosine, sine, bias, routes)


def backward_kernel(
    reduced, tokens, attention, cotangent, normed_two, router, expert_bias, routed, ffn_gain,
    out_far, turned_far, keys_far, bias_far, stats, query_far, raw_far, cosine, sine, qk_gain,
    query_out, key_out, value_out, gain_out, hidden_grad, attention_grad, extras,
    out_grad, query_grad, prompt_grads, own_grads, own, paired, from_x, from_y, mine, theirs,
    w_out, query_rot, keys_values, bias, query_raw, key_raw, load_sems,
    pair_sems, x_sems, y_sems, peer_sent, peer_got,
    *,
    gain_column,
):
    rows, local = query_rot.shape
    width = attention_grad.shape[1]
    heads = local // HD
    factor = HD ** (-0.5)
    own_blocks = rows // PROMPT_DEV - 1
    devices = keys_values.shape[0] - own_blocks
    count = keys_values.shape[0] * PROMPT_DEV
    reach = devices * PROMPT_DEV
    plane = Plane(own, prompt_grads, paired, from_x, from_y, pair_sems, x_sems, y_sems, by_device=True)
    peers = Peers(mine, theirs, peer_sent, peer_got)
    load_out, *load_heads, load_query, load_raw = loads(
        (
            (out_far, w_out), (turned_far, query_rot), (keys_far, keys_values), (bias_far, bias),
            (query_far, query_raw), (raw_far, key_raw),
        ),
        load_sems,
    )
    greet(plane.neighbours() + peers.neighbours())
    tile = min(512, width)
    starts = range(0, width, tile)
    scale_two = stats[:, 3:4]
    logits = wide_dot(normed_two[...], router[...]) + expert_bias[...]
    weights = jnp.exp(logits - jnp.max(logits, axis=1, keepdims=True))
    chances = weights / jnp.sum(weights, axis=1, keepdims=True)
    chance_grad = routed[...] * reduced[:, width:].astype(jnp.float32)
    logit_grad = (
        chances * (chance_grad - jnp.sum(chances * chance_grad, axis=1, keepdims=True))
    ).astype(jnp.bfloat16)

    def hidden_of(columns):
        return tokens[:, columns].astype(jnp.float32) + attention[:, columns].astype(jnp.float32)

    def input_part(columns):
        return reduced[:, columns].astype(jnp.float32) + turned_dot(logit_grad, router[columns])

    pull = jnp.zeros((rows, 1), jnp.float32)
    for start in starts:
        columns = slice(start, start + tile)
        weighted = ffn_gain[:, columns] * input_part(columns)
        hidden_grad[:, columns] = weighted
        pull = pull + jnp.sum(weighted * hidden_of(columns), axis=1, keepdims=True)
    pull = scale_two * scale_two * scale_two / width * pull
    for start in starts:
        columns = slice(start, start + tile)
        grad = (
            cotangent[:, columns].astype(jnp.float32)
            + scale_two * hidden_grad[:, columns]
            - hidden_of(columns) * pull
        )
        hidden_grad[:, columns] = grad
        attention_grad[:, columns] = grad.astype(jnp.bfloat16)
    load_out.wait()
    out_grad[...] = turned_dot(attention_grad[...], w_out[...]).astype(jnp.bfloat16)
    for load in load_heads:
        load.wait()
    for head in range(heads):
        columns = slice(head * HD, (head + 1) * HD)
        other = slice(local + head * HD, local + (head + 1) * HD)
        keys = keys_values[:, :, columns].reshape(count, HD)
        values = keys_values[:, :, other].reshape(count, HD)
        query, above = query_rot[:, columns], out_grad[:, columns]
        scores = turned_dot(query, keys) * factor + bias[...]
        shares = jnp.exp(scores - stats[:, 8 + head : 9 + head])
        share_grad = turned_dot(above, values)
        delta = jnp.sum(shares * share_grad, axis=1, keepdims=True)
        score_grad = (shares * (share_grad - delta)).astype(jnp.bfloat16)
        query_grad[:, columns] = wide_dot(score_grad, keys) * factor
        key_grad = crossed_dot(score_grad, query) * factor
        value_grad = crossed_dot(shares.astype(jnp.bfloat16), above)
        prompt_grads[:, :, columns] = key_grad[:reach].astype(jnp.bfloat16).reshape(devices, PROMPT_DEV, HD)
        prompt_grads[:, :, other] = value_grad[:reach].astype(jnp.bfloat16).reshape(devices, PROMPT_DEV, HD)
        own_grads[PROMPT_DEV:, columns] = key_grad[reach:]
        own_grads[PROMPT_DEV:, other] = value_grad[reach:]
    for chip in range(4):
        plane.pair_copy(chip).start()
    for chip in range(4):
        own[chip] = prompt_grads[plane.block(chip, plane.core)]
    for chip in range(4):
        plane.pair_copy(chip).wait_recv()
        if chip < 3:
            plane.send_first(chip)

    def normed_part(source, raw, row, scale):
        inner = jnp.zeros((rows, 1), jnp.float32)
        for head in range(heads):
            columns = slice(head * HD, (head + 1) * HD)
            grad = source[:, columns]
            grad = grad * cosine[...] - swapped(grad) * sine[...]
            gain_out[row : row + 1, columns] = jnp.sum(grad * raw[:, columns] * scale, axis=0, keepdims=True)
            grad = qk_gain[row : row + 1, columns] * grad
            source[:, columns] = grad
            inner = inner + jnp.sum(grad * raw[:, columns], axis=1, keepdims=True)
        return inner

    load_query.wait()
    load_raw.wait()
    scale_query, scale_key = stats[:, 1:2], stats[:, 2:3]
    query_inner = normed_part(query_grad, query_raw, 0, scale_query)
    plane.send_second()
    chosen = lax.broadcasted_iota(jnp.int32, (rows, LANE), 1) == gain_column
    chosen = jnp.where(chosen, 1.0, 0.0).astype(jnp.bfloat16)
    for start in starts:
        columns = slice(start, start + tile)
        sway = input_part(columns) * hidden_of(columns) * scale_two
        extras[columns] = (
            crossed_dot(normed_two[:, columns], logit_grad) + crossed_dot(sway.astype(jnp.bfloat16), chosen)
        ).astype(jnp.bfloat16)

    def last(piece, carry):
        for side, summed in enumerate(plane.last_sum(piece)):
            own_grads[plane.rows(side, piece)] = summed
        return carry

    lax.fori_loop(0, plane.pieces, last, 0)
    key_inner = normed_part(own_grads, key_raw, 1, scale_key)
    mine[...] = to_rows([query_inner, key_inner], rows)
    peers.start()
    value_out[...] = own_grads[:, local:].astype(jnp.bfloat16)
    inner = to_columns(peers.total())
    for out, source, raw, scale, i in (
        (query_out, query_grad, query_raw, scale_query, 0),
        (key_out, own_grads, key_raw, scale_key, 1),
    ):
        pull = scale * scale * scale / width * inner[:, i : i + 1]
        out[...] = (scale * source[:, :local] - raw[...] * pull).astype(jnp.bfloat16)
    plane.finish()
    peers.finish()


def backward(
    reduced, tokens, attention, cotangent, normed_two, router, expert_bias, routed, ffn_gain,
    w_out, query_rot, keys_values, bias, stats, query_raw, key_raw, cosine, sine, qk_gain, gain_column,
):
    rows, local = query_rot.shape
    size = lax.axis_size("tensor")
    ranks = lax.axis_size("expert")
    low, full = jnp.bfloat16, jnp.float32
    vmem = pl.BlockSpec(memory_space=pltpu.VMEM)
    any_space = pl.BlockSpec(memory_space=pl.ANY)
    small = jax.ShapeDtypeStruct((rows, local), low)
    return pl.pallas_call(
        functools.partial(backward_kernel, gain_column=gain_column),
        out_shape=(
            small, small, small, jax.ShapeDtypeStruct((2, local), full),
            jax.ShapeDtypeStruct(tokens.shape, full), jax.ShapeDtypeStruct(tokens.shape, low),
            jax.ShapeDtypeStruct((tokens.shape[1], LANE), low),
        ),
        in_specs=[vmem] * 9 + [any_space] * 4 + [vmem] + [any_space] * 2 + [vmem] * 3,
        out_specs=(vmem,) * 7,
        scratch_shapes=[
            pltpu.VMEM((rows, local), low),
            pltpu.VMEM((rows, local), full),
            pltpu.VMEM((ranks, PROMPT_DEV, 2 * local), low),
            pltpu.VMEM((rows, 2 * local), full),
            pltpu.VMEM((4, PROMPT_DEV, 2 * local), low),
            pltpu.VMEM((4, PROMPT_DEV, 2 * local), low),
            pltpu.VMEM((3, PROMPT_DEV // 2, 2 * local), low),
            pltpu.VMEM((3, PROMPT_DEV // 2, 2 * local), low),
            pltpu.VMEM((8, rows), full),
            pltpu.VMEM((size - 1, 8, rows), full),
            *(
                pltpu.VMEM(array.shape, array.dtype)
                for array in (w_out, query_rot, keys_values, bias, query_raw, key_raw)
            ),
            pltpu.SemaphoreType.DMA((6,)),
            *Plane.semaphores(PROMPT_DEV),
            pltpu.SemaphoreType.DMA((size - 1,)),
            pltpu.SemaphoreType.DMA((size - 1,)),
        ],
        compiler_params=pltpu.CompilerParams(
            collective_id=3, has_side_effects=True, vmem_limit_bytes=60 * 2**20
        ),
    )(
        reduced, tokens, attention, cotangent, normed_two, router, expert_bias, routed, ffn_gain,
        w_out, query_rot, keys_values, bias, stats, query_raw, key_raw, cosine, sine, qk_gain,
    )


def rotate(field, cosine, sine):
    half = field.shape[-1] // 2
    first = field[..., :half]
    second = field[..., half:]
    return jnp.concatenate(
        [first * cosine - second * sine, second * cosine + first * sine], axis=-1
    )


def unrotate(grad, cosine, sine):
    half = grad.shape[-1] // 2
    first = grad[..., :half]
    second = grad[..., half:]
    return jnp.concatenate(
        [first * cosine + second * sine, second * cosine - first * sine], axis=-1
    )


def experts(normed_two, cotangent, gates, w_gate, w_up, w_down, experts_total):
    local_experts = w_gate.shape[0]
    device = lax.axis_index("expert")
    arrived = lax.all_gather(normed_two, "expert", axis=0, tiled=True)
    arrived_grad = lax.all_gather(cotangent, "expert", axis=0, tiled=True)
    gate_pre = jnp.einsum("rd,jdf->jrf", arrived, w_gate, preferred_element_type=jnp.float32)
    up_pre = jnp.einsum("rd,jdf->jrf", arrived, w_up, preferred_element_type=jnp.float32)
    raw_grad = jnp.einsum("rd,jfd->jrf", arrived_grad, w_down, preferred_element_type=jnp.float32)
    sigma = jax.nn.sigmoid(gate_pre)
    activated = gate_pre * sigma
    inner = activated * up_pre
    gated = (gates[:, :, None] * inner).astype(jnp.bfloat16)
    mixed_part = jnp.einsum("jrf,jfd->rd", gated, w_down, preferred_element_type=jnp.float32)
    mixture = lax.psum(
        lax.psum_scatter(
            mixed_part.astype(jnp.bfloat16), "expert", scatter_dimension=0, tiled=True
        ),
        "tensor",
    ).astype(jnp.float32)
    gate_grad_part = jnp.sum(raw_grad * inner, axis=2)
    act_grad = gates[:, :, None] * raw_grad
    up_grad = (act_grad * activated).astype(jnp.bfloat16)
    gate_grad = (act_grad * up_pre * sigma * (1.0 + gate_pre * (1.0 - sigma))).astype(jnp.bfloat16)
    grad_w_down = jnp.einsum("jrf,rd->jfd", gated, arrived_grad, preferred_element_type=jnp.float32)
    grad_w_gate = jnp.einsum("rd,jrf->jdf", arrived, gate_grad, preferred_element_type=jnp.float32)
    grad_w_up = jnp.einsum("rd,jrf->jdf", arrived, up_grad, preferred_element_type=jnp.float32)
    slot_grad = jnp.einsum("jrf,jdf->rd", gate_grad, w_gate, preferred_element_type=jnp.float32)
    slot_grad = slot_grad + jnp.einsum(
        "jrf,jdf->rd", up_grad, w_up, preferred_element_type=jnp.float32
    )
    moe_input_grad = lax.psum(
        lax.psum_scatter(
            slot_grad.astype(jnp.bfloat16), "expert", scatter_dimension=0, tiled=True
        ),
        "tensor",
    ).astype(jnp.float32)
    placed = jnp.zeros((arrived.shape[0], experts_total), jnp.float32)
    placed = lax.dynamic_update_slice_in_dim(placed, gate_grad_part.T, device * local_experts, 1)
    chance_grad = lax.psum(
        lax.psum_scatter(placed, "expert", scatter_dimension=0, tiled=True), "tensor"
    )
    return mixture, moe_input_grad, chance_grad, [grad_w_gate, grad_w_up, grad_w_down]


def body(
    tokens,
    w_query,
    w_key,
    w_value,
    w_out,
    attn_gain,
    ffn_gain,
    qk_gain,
    router,
    w_gate,
    w_up,
    w_down,
    routes,
    cont_group,
    cotangent,
):
    rows, width = tokens.shape
    local_width = w_query.shape[1]
    head_count = local_width // HD
    experts_total = router.shape[1]
    local_experts = w_gate.shape[0]
    ranks = lax.axis_size("expert")
    device = lax.axis_index("expert")
    span = ranks // 2
    prompt_len = PROMPT_DEV * span
    factor = HD ** (-0.5)
    local = jnp.arange(rows, dtype=jnp.int32)
    is_prompt = local < PROMPT_DEV
    after = jnp.maximum(local - PROMPT_DEV, 0)
    slot_cont = after // CLEN
    cont_pick = jnp.sum(
        jnp.where(
            slot_cont[:, None] == jnp.arange(CONT_DEV, dtype=jnp.int32)[None, :],
            cont_group[None, :],
            0,
        ),
        axis=1,
    )
    group = jnp.where(is_prompt, device // span, cont_pick)
    position = jnp.where(is_prompt, device % span * PROMPT_DEV + local, prompt_len + after % CLEN)
    tag = jnp.where(is_prompt, -1, slot_cont)
    frequency = 10000.0 ** (-jnp.arange(HD // 2, dtype=jnp.float32) * 2.0 / HD)
    angle = position.astype(jnp.float32)[:, None] * frequency[None, :]
    cosine = jnp.cos(angle)[:, None, :]
    sine = jnp.sin(angle)[:, None, :]
    source = tokens.astype(jnp.float32)
    scale_one = lax.rsqrt(jnp.mean(source * source, axis=1, keepdims=True) + epsilon)
    normed = (source * scale_one * attn_gain).astype(jnp.bfloat16)
    query_raw = jnp.dot(normed, w_query, preferred_element_type=jnp.float32)
    key_raw = jnp.dot(normed, w_key, preferred_element_type=jnp.float32)
    value_raw = jnp.dot(normed, w_value, preferred_element_type=jnp.float32)
    squares = lax.psum(
        jnp.stack(
            [jnp.sum(query_raw * query_raw, axis=1), jnp.sum(key_raw * key_raw, axis=1)], axis=1
        ),
        "tensor",
    )
    scale_query = lax.rsqrt(squares[:, 0:1] / width + epsilon)
    scale_key = lax.rsqrt(squares[:, 1:2] / width + epsilon)
    query_rot = (
        rotate((query_raw * scale_query * qk_gain[0]).reshape(rows, head_count, HD), cosine, sine)
        .reshape(rows, local_width)
        .astype(jnp.bfloat16)
    )
    key_rot = (
        rotate((key_raw * scale_key * qk_gain[1]).reshape(rows, head_count, HD), cosine, sine)
        .reshape(rows, local_width)
        .astype(jnp.bfloat16)
    )
    value_low = value_raw.astype(jnp.bfloat16)
    prompt_keys, prompt_values = (
        lax.all_gather(key_rot[:PROMPT_DEV], "expert", axis=0, tiled=True),
        lax.all_gather(value_low[:PROMPT_DEV], "expert", axis=0, tiled=True),
    )
    prompt_count = prompt_keys.shape[0]
    all_keys = jnp.concatenate([prompt_keys, key_rot[PROMPT_DEV:]], axis=0)
    all_values = jnp.concatenate([prompt_values, value_low[PROMPT_DEV:]], axis=0)
    key_index = jnp.arange(prompt_count, dtype=jnp.int32)
    prompt_mask = (group[:, None] == (key_index // prompt_len)[None, :]) & (
        (key_index % prompt_len)[None, :] <= position[:, None]
    )
    own_mask = (tag[:, None] == tag[None, PROMPT_DEV:]) & (
        position[None, PROMPT_DEV:] <= position[:, None]
    )
    mask = jnp.concatenate([prompt_mask, own_mask], axis=1)

    def head_scores(query_head, key_head):
        scores = (
            jnp.einsum("qd,kd->qk", query_head, key_head, preferred_element_type=jnp.float32)
            * factor
        )
        return jnp.where(mask, scores, masked_value)

    outputs = []
    log_totals = []
    for head in range(head_count):
        start = head * HD
        scores = head_scores(query_rot[:, start : start + HD], all_keys[:, start : start + HD])
        top = jnp.max(scores, axis=1, keepdims=True)
        weights = jnp.exp(scores - top)
        total = jnp.sum(weights, axis=1, keepdims=True)
        shares = (weights / total).astype(jnp.bfloat16)
        outputs.append(
            jnp.dot(shares, all_values[:, start : start + HD], preferred_element_type=jnp.float32)
        )
        log_totals.append(top + jnp.log(total))
    attended = jnp.concatenate(outputs, axis=1).astype(jnp.bfloat16)
    attention = lax.psum(jnp.dot(attended, w_out, preferred_element_type=jnp.float32), "tensor")
    hidden = source + attention
    scale_two = lax.rsqrt(jnp.mean(hidden * hidden, axis=1, keepdims=True) + epsilon)
    normed_two = (hidden * scale_two * ffn_gain).astype(jnp.bfloat16)
    logits = jnp.dot(normed_two, router, preferred_element_type=jnp.float32)
    top = jnp.max(logits, axis=1, keepdims=True)
    weights = jnp.exp(logits - top)
    chances = weights / jnp.sum(weights, axis=1, keepdims=True)
    hits = (routes[:, :, None] == jnp.arange(experts_total, dtype=jnp.int32)[None, None, :]).astype(
        jnp.float32
    )
    rows_mask = jnp.sum(hits, axis=1)
    routed = lax.all_gather(
        (rows_mask * chances).astype(jnp.float32), "expert", axis=0, tiled=True
    )
    gates = lax.dynamic_slice_in_dim(routed, device * local_experts, local_experts, 1).T
    grad_out = cotangent.astype(jnp.float32)
    pieces = max(1, ranks * rows // 4096)
    piece = rows // pieces
    split_gates = gates.reshape(local_experts, ranks, rows)
    results = []
    weight_grads = None
    for number in range(pieces):
        part = slice(number * piece, (number + 1) * piece)
        sources = (normed_two[part], cotangent[part])
        if results:
            sources, results, weight_grads = lax.optimization_barrier(
                (sources, results, weight_grads)
            )
        *result, grads = experts(
            *sources,
            split_gates[:, :, part].reshape(local_experts, ranks * piece),
            w_gate,
            w_up,
            w_down,
            experts_total,
        )
        results.append(result)
        weight_grads = grads if weight_grads is None else [a + b for a, b in zip(weight_grads, grads)]
    mixture, moe_input_grad, chance_grad = (
        jnp.concatenate(list(group_of), axis=0) for group_of in zip(*results)
    )
    grad_w_gate, grad_w_up, grad_w_down = weight_grads
    chance_grad = rows_mask * chance_grad
    output = (hidden + mixture).astype(jnp.bfloat16)
    logit_grad = (
        chances * (chance_grad - jnp.sum(chances * chance_grad, axis=1, keepdims=True))
    ).astype(jnp.bfloat16)
    grad_router = jnp.einsum(
        "td,te->de", normed_two, logit_grad, preferred_element_type=jnp.float32
    )
    normed_two_grad = moe_input_grad + jnp.einsum(
        "te,de->td", logit_grad, router, preferred_element_type=jnp.float32
    )
    weighted_two = ffn_gain * normed_two_grad
    grad_ffn_gain = jnp.sum(normed_two_grad * hidden * scale_two, axis=0)
    hidden_grad = (
        grad_out
        + scale_two * weighted_two
        - hidden * (scale_two**3 / width) * jnp.sum(weighted_two * hidden, axis=1, keepdims=True)
    )
    attention_grad = hidden_grad.astype(jnp.bfloat16)
    grad_w_out = jnp.einsum(
        "td,te->de", attended, attention_grad, preferred_element_type=jnp.float32
    )
    attended_grad = jnp.einsum(
        "te,de->td", attention_grad, w_out, preferred_element_type=jnp.float32
    ).astype(jnp.bfloat16)
    query_grads = []
    key_grads = []
    value_grads = []
    for head in range(head_count):
        start = head * HD
        query_head = query_rot[:, start : start + HD]
        key_head = all_keys[:, start : start + HD]
        value_head = all_values[:, start : start + HD]
        out_grad_head = attended_grad[:, start : start + HD]
        recomputed = jnp.exp(head_scores(query_head, key_head) - log_totals[head])
        share_grad = jnp.einsum(
            "qd,kd->qk", out_grad_head, value_head, preferred_element_type=jnp.float32
        )
        delta = jnp.sum(recomputed * share_grad, axis=1, keepdims=True)
        score_grad = (recomputed * (share_grad - delta)).astype(jnp.bfloat16)
        query_grads.append(
            jnp.dot(score_grad, key_head, preferred_element_type=jnp.float32) * factor
        )
        key_grads.append(
            jnp.einsum("qk,qd->kd", score_grad, query_head, preferred_element_type=jnp.float32)
            * factor
        )
        value_grads.append(
            jnp.einsum(
                "qk,qd->kd",
                recomputed.astype(jnp.bfloat16),
                out_grad_head,
                preferred_element_type=jnp.float32,
            )
        )
    key_grad_all = jnp.concatenate(key_grads, axis=1)
    value_grad_all = jnp.concatenate(value_grads, axis=1)
    prompt_key_grad, prompt_value_grad = (
        lax.psum_scatter(
            key_grad_all[:prompt_count].astype(jnp.bfloat16),
            "expert",
            scatter_dimension=0,
            tiled=True,
        ).astype(jnp.float32),
        lax.psum_scatter(
            value_grad_all[:prompt_count].astype(jnp.bfloat16),
            "expert",
            scatter_dimension=0,
            tiled=True,
        ).astype(jnp.float32),
    )
    key_grad = jnp.concatenate([prompt_key_grad, key_grad_all[prompt_count:]], axis=0)
    value_grad = jnp.concatenate([prompt_value_grad, value_grad_all[prompt_count:]], axis=0)
    query_grad = unrotate(
        jnp.concatenate(query_grads, axis=1).reshape(rows, head_count, HD), cosine, sine
    ).reshape(rows, local_width)
    key_grad = unrotate(key_grad.reshape(rows, head_count, HD), cosine, sine).reshape(
        rows, local_width
    )
    grad_qk_gain = jnp.stack(
        [
            jnp.sum(query_grad * query_raw * scale_query, axis=0),
            jnp.sum(key_grad * key_raw * scale_key, axis=0),
        ],
        axis=0,
    )
    weighted_query = qk_gain[0] * query_grad
    weighted_key = qk_gain[1] * key_grad
    inner_sums = lax.psum(
        jnp.stack(
            [jnp.sum(weighted_query * query_raw, axis=1), jnp.sum(weighted_key * key_raw, axis=1)],
            axis=1,
        ),
        "tensor",
    )
    query_raw_grad = (
        scale_query * weighted_query - query_raw * (scale_query**3 / width) * inner_sums[:, 0:1]
    ).astype(jnp.bfloat16)
    key_raw_grad = (
        scale_key * weighted_key - key_raw * (scale_key**3 / width) * inner_sums[:, 1:2]
    ).astype(jnp.bfloat16)
    value_raw_grad = value_grad.astype(jnp.bfloat16)
    grad_w_query = jnp.einsum(
        "td,te->de", normed, query_raw_grad, preferred_element_type=jnp.float32
    )
    grad_w_key = jnp.einsum("td,te->de", normed, key_raw_grad, preferred_element_type=jnp.float32)
    grad_w_value = jnp.einsum(
        "td,te->de", normed, value_raw_grad, preferred_element_type=jnp.float32
    )
    normed_part = jnp.einsum(
        "te,de->td", query_raw_grad, w_query, preferred_element_type=jnp.float32
    )
    normed_part = normed_part + jnp.einsum(
        "te,de->td", key_raw_grad, w_key, preferred_element_type=jnp.float32
    )
    normed_part = normed_part + jnp.einsum(
        "te,de->td", value_raw_grad, w_value, preferred_element_type=jnp.float32
    )
    normed_grad = lax.psum(normed_part.astype(jnp.bfloat16), "tensor").astype(jnp.float32)
    weighted_one = attn_gain * normed_grad
    grad_attn_gain = jnp.sum(normed_grad * source * scale_one, axis=0)
    input_grad = (
        hidden_grad
        + scale_one * weighted_one
        - source * (scale_one**3 / width) * jnp.sum(weighted_one * source, axis=1, keepdims=True)
    )
    summed = (
        lax.psum_scatter(
            grad_w_query.astype(jnp.bfloat16), "expert", scatter_dimension=0, tiled=True
        ).astype(jnp.float32),
        lax.psum_scatter(
            grad_w_key.astype(jnp.bfloat16), "expert", scatter_dimension=0, tiled=True
        ).astype(jnp.float32),
        lax.psum_scatter(
            grad_w_value.astype(jnp.bfloat16), "expert", scatter_dimension=0, tiled=True
        ).astype(jnp.float32),
        lax.psum_scatter(
            grad_w_out.astype(jnp.bfloat16), "expert", scatter_dimension=1, tiled=True
        ).astype(jnp.float32),
        lax.psum_scatter(
            grad_attn_gain.astype(jnp.bfloat16), "expert", scatter_dimension=0, tiled=True
        ).astype(jnp.float32),
        lax.psum_scatter(
            grad_ffn_gain.astype(jnp.bfloat16), "expert", scatter_dimension=0, tiled=True
        ).astype(jnp.float32),
        lax.psum_scatter(
            grad_qk_gain.astype(jnp.bfloat16), "expert", scatter_dimension=1, tiled=True
        ).astype(jnp.float32),
        lax.psum_scatter(
            grad_router.astype(jnp.bfloat16), "expert", scatter_dimension=0, tiled=True
        ).astype(jnp.float32),
    )
    return (
        output,
        input_grad,
        summed[0],
        summed[1],
        summed[2],
        summed[3],
        summed[4],
        summed[5],
        summed[6],
        summed[7],
        grad_w_gate,
        grad_w_up,
        grad_w_down,
    )


def compact(
    tokens, w_query, w_key, w_value, w_out, attn_gain, ffn_gain, qk_gain, router, w_gate, w_up, w_down,
    routes, cont_group, cotangent,
):
    rows, width = tokens.shape
    local_width = w_query.shape[1]
    head_count = local_width // HD
    experts_total = router.shape[1]
    local_experts = w_gate.shape[0]
    ranks = lax.axis_size("expert")
    device = lax.axis_index("expert")
    full = jnp.float32
    group, position, tag = layout(rows, ranks, device, cont_group)
    channel = jnp.arange(HD)
    frequency = 10000.0 ** (-(channel % (HD // 2)).astype(full) * 2.0 / HD)
    angle = position.astype(full)[:, None] * frequency[None, :]
    cosine = jnp.cos(angle)
    sine = jnp.sin(angle) * jnp.where(channel < HD // 2, -1.0, 1.0)
    bias = jnp.where(attention_mask(group, position, tag, ranks), 0.0, masked_value).astype(full)
    all_experts = jnp.pad(router, ((0, 0), (0, LANE - experts_total)))
    expert_bias = jnp.where(jnp.arange(LANE) < experts_total, 0.0, masked_value).astype(full)[None]
    turned_routes = jnp.tile(jnp.pad(routes.T, ((0, -routes.shape[1] % 8), (0, 0)), constant_values=-1), (2, 1))
    hits = routes[:, :, None] == jnp.arange(experts_total, dtype=jnp.int32)
    routed = jnp.pad(jnp.any(hits, axis=1).astype(full), ((0, 0), (0, LANE - experts_total)))
    (
        attention, normed, normed_two, attended, query_rot, keys_values, query_raw, key_raw, stats, routes_all, arrived,
    ) = front(
        tokens, attn_gain[None], ffn_gain[None], w_query, w_key, w_value, w_out, qk_gain, cosine, sine, bias,
        turned_routes,
    )
    arrived_grad = lax.all_gather(cotangent, "expert", axis=0)
    names = routes_all[:, : turned_routes.shape[0] // 2]
    expert_mask = jnp.any(names[:, :, :, None] == jnp.arange(LANE, dtype=jnp.int32), axis=1).astype(full)
    reduced, gated, gate_grad, up_grad, mixed_part = experts_fused(
        arrived, arrived_grad, expert_mask, all_experts, expert_bias, w_gate, w_up, w_down
    )
    (
        query_raw_grad, key_raw_grad, value_raw_grad, grad_qk_gain, hidden_grad, attention_grad, extras,
    ) = backward(
        reduced, tokens, attention, cotangent, normed_two, all_experts, expert_bias, routed, ffn_gain[None],
        w_out, query_rot, keys_values, bias, stats, query_raw, key_raw, cosine, sine, qk_gain, experts_total,
    )
    small_part = local_width // ranks
    share = width // ranks
    gains = grad_qk_gain.reshape(2, ranks, small_part).transpose(1, 2, 0).astype(jnp.bfloat16)
    extras = extras.reshape(ranks, share, LANE) + jnp.pad(
        gains, ((0, 0), (0, share - small_part), (experts_total + 1, LANE - experts_total - 3))
    )
    normed_grad, sums, w_out_grad, gain_total, mixture, grad_w_gate, grad_w_up, grad_w_down = closing(
        normed, query_raw_grad, key_raw_grad, value_raw_grad, attended, attention_grad, extras, w_query, w_key, w_value,
        mixed_part, arrived, arrived_grad, gated, gate_grad, up_grad, local_experts, experts_total + 3,
    )
    source = tokens.astype(full)
    hidden = source + attention.astype(full)
    scale_one = stats[:, 0:1]
    normed_grad = normed_grad.astype(full)
    output = (hidden + mixture.astype(full)).astype(jnp.bfloat16)
    weighted_one = attn_gain * normed_grad
    input_grad = (
        hidden_grad
        + scale_one * weighted_one
        - source * (scale_one**3 / width) * jnp.sum(weighted_one * source, axis=1, keepdims=True)
    )
    edge = 4 * local_width
    return (
        output,
        input_grad,
        sums[:, :local_width],
        sums[:, local_width : 2 * local_width],
        sums[:, 2 * local_width : 3 * local_width],
        w_out_grad,
        gain_total[0] / lax.dynamic_slice_in_dim(attn_gain, device * share, share),
        sums[:, edge + experts_total],
        sums[:small_part, edge + experts_total + 1 : edge + experts_total + 3].T,
        sums[:, edge : edge + experts_total],
        grad_w_gate.astype(full),
        grad_w_up.astype(full),
        grad_w_down.astype(full),
    )


def layout(rows, ranks, device, cont_group):
    span = ranks // 2
    prompt_len = PROMPT_DEV * span
    local = jnp.arange(rows, dtype=jnp.int32)
    is_prompt = local < PROMPT_DEV
    after = jnp.maximum(local - PROMPT_DEV, 0)
    slot_cont = after // CLEN
    cont_pick = jnp.sum(
        jnp.where(
            slot_cont[:, None] == jnp.arange(CONT_DEV, dtype=jnp.int32)[None, :], cont_group[None, :], 0
        ),
        axis=1,
    )
    group = jnp.where(is_prompt, device // span, cont_pick)
    position = jnp.where(is_prompt, device % span * PROMPT_DEV + local, prompt_len + after % CLEN)
    tag = jnp.where(is_prompt, -1, slot_cont)
    return group, position, tag


def attention_mask(group, position, tag, ranks):
    prompt_len = PROMPT_DEV * (ranks // 2)
    key_index = jnp.arange(ranks * PROMPT_DEV, dtype=jnp.int32)
    prompt_mask = (group[:, None] == (key_index // prompt_len)[None, :]) & (
        (key_index % prompt_len)[None, :] <= position[:, None]
    )
    own_mask = (tag[:, None] == tag[None, PROMPT_DEV:]) & (
        position[None, PROMPT_DEV:] <= position[:, None]
    )
    return jnp.concatenate([prompt_mask, own_mask], axis=1)


def solution(mesh):
    small = mesh.shape["expert"] == 8
    return jax.shard_map(
        compact if small else body,
        mesh=mesh,
        in_specs=(
            P("expert", None),
            P(None, "tensor"),
            P(None, "tensor"),
            P(None, "tensor"),
            P("tensor", None),
            P(),
            P(),
            P(None, "tensor"),
            P(),
            P("expert", None, "tensor"),
            P("expert", None, "tensor"),
            P("expert", "tensor", None),
            P("expert", None),
            P("expert"),
            P("expert", None),
        ),
        out_specs=(
            P("expert", None),
            P("expert", None),
            P("expert", "tensor"),
            P("expert", "tensor"),
            P("expert", "tensor"),
            P("tensor", "expert"),
            P("expert"),
            P("expert"),
            P(None, ("tensor", "expert")),
            P("expert", None),
            P("expert", None, "tensor"),
            P("expert", None, "tensor"),
            P("expert", "tensor", None),
        ),
        check_vma=False,
    )
```

```python
import functools

import jax
import jax.numpy as jnp
from jax import lax
from jax.experimental import pallas as pl
from jax.experimental.pallas import tpu as pltpu
from jax.sharding import PartitionSpec as P

HD = 128
PROMPT_DEV = 128
CLEN = 256
CONT_DEV = 1


epsilon = 1e-05
masked_value = -1e30


MESH = pl.DeviceIdType.MESH
STEP = 16
LANE = 128


def remote(source, target, sent, received, **where):
    return pltpu.make_async_remote_copy(
        src_ref=source,
        dst_ref=target,
        send_sem=sent,
        recv_sem=received,
        device_id=where,
        device_id_type=MESH,
    )


def greet(places):
    barrier = pltpu.get_barrier_semaphore()
    for condition, where in places:
        def signal(where=where):
            pl.semaphore_signal(barrier, inc=1, device_id=where, device_id_type=MESH)
        if condition is None:
            signal()
        else:
            pl.when(condition)(signal)
    count = 0
    for condition, _ in places:
        count = count + (1 if condition is None else jnp.where(condition, 1, 0))
    pl.semaphore_wait(barrier, count)


class Line:
    def __init__(self, own, arrived, spare, total, sems, step=STEP):
        self.step = step
        self.own, self.arrived, self.spare, self.total = own, arrived, spare, total
        self.up_sent, self.far_got, self.near_got, self.far_sent, self.near_sent, self.down_got = (
            sems.at[i] for i in range(6)
        )
        self.size = lax.axis_size("tensor")
        self.here = lax.axis_index("tensor")
        self.root = self.size // 2 - 1
        self.rise_steps = self.size - 1 - self.root
        self.trip = 2 * self.rise_steps
        self.half = own.shape[0] // 2
        self.pieces = self.half // step

    @staticmethod
    def semaphores(rows, step=STEP):
        return pltpu.SemaphoreType.DMA((6, 2, rows // 2 // step))

    @staticmethod
    def spare_shape(rows, width):
        return pltpu.VMEM((rows // 2, width), jnp.bfloat16)

    def neighbours(self):
        here, size = self.here, self.size
        return [
            (here > 0, {"tensor": jnp.maximum(here - 1, 0)}),
            (here < size - 1, {"tensor": jnp.minimum(here + 1, size - 1)}),
        ]

    def place(self, lane):
        return self.here if lane == 0 else self.size - 1 - self.here

    def device(self, lane, place):
        return place if lane == 0 else self.size - 1 - place

    def rows(self, lane, piece):
        return pl.ds(pl.multiple_of(lane * self.half + piece * self.step, self.step), self.step)

    def landing(self, piece):
        return pl.ds(pl.multiple_of(piece * self.step, self.step), self.step)

    def far_up(self, lane, piece):
        rows, place = self.rows(lane, piece), self.place(lane)
        inward = jnp.where(place > self.root, place - 1, place + 1)
        return remote(
            self.own.at[rows], self.arrived.at[rows],
            self.up_sent.at[lane, piece], self.far_got.at[lane, piece], tensor=self.device(lane, inward),
        )

    def near_up(self, lane, piece):
        return remote(
            self.own.at[self.rows(lane, piece)], self.spare.at[self.landing(piece)],
            self.up_sent.at[lane, piece], self.near_got.at[lane, piece], tensor=self.device(lane, self.root),
        )

    def down(self, lane, piece, away):
        rows = self.rows(lane, piece)
        sent = self.far_sent if away == 1 else self.near_sent
        return remote(
            self.total.at[rows], self.total.at[rows],
            sent.at[lane, piece], self.down_got.at[lane, piece], tensor=self.device(lane, self.place(lane) + away),
        )

    def rise(self, lane, piece):
        place, root = self.place(lane), self.root
        rows = self.rows(lane, piece)

        def value(field):
            return field.astype(jnp.float32)

        @pl.when((place > root) & (place < self.size - 1) | (place > 0) & (place < root))
        def _():
            self.far_up(lane, piece).wait_recv()
            self.own[rows] = (value(self.own[rows]) + value(self.arrived[rows])).astype(jnp.bfloat16)

        @pl.when(place == root)
        def _():
            self.far_up(lane, piece).wait_recv()
            summed = value(self.own[rows]) + value(self.arrived[rows])
            if root > 0:
                self.near_up(lane, piece).wait_recv()
                summed = summed + value(self.spare[self.landing(piece)])
            self.total[rows] = summed.astype(jnp.bfloat16)
            self.down(lane, piece, 1).start()
            if root > 0:
                self.down(lane, piece, -1).start()

        if root > 0:

            @pl.when(place == root - 1)
            def _():
                self.near_up(lane, piece).start()

        @pl.when((place > root) | (place < root - 1))
        def _():
            self.far_up(lane, piece).start()

    def fall(self, lane, piece):
        place, root = self.place(lane), self.root

        @pl.when(place != root)
        def _():
            self.down(lane, piece, 1).wait_recv()

        @pl.when((place > root) & (place < self.size - 1))
        def _():
            self.down(lane, piece, 1).start()

        @pl.when((place > 0) & (place < root))
        def _():
            self.down(lane, piece, -1).start()

    def advance(self, step):
        for lane in range(2):
            place = self.place(lane)
            steps_in = self.rise_steps - jnp.abs(place - self.root)
            piece = step - steps_in

            @pl.when((piece >= 0) & (piece < self.pieces))
            def _():
                self.rise(lane, piece)

        for lane in range(2):
            place = self.place(lane)
            piece = step - self.rise_steps - jnp.abs(place - self.root)

            @pl.when((piece >= 0) & (piece < self.pieces))
            def _():
                self.fall(lane, piece)

    def step_body(self, step, carry):
        self.advance(step)
        return carry

    def steps(self):
        return self.pieces + self.trip

    def finish(self):
        def one(piece, carry):
            for lane in range(2):
                place, root = self.place(lane), self.root

                @pl.when(place != root)
                def _():
                    self.far_up(lane, piece).wait_send()

                @pl.when((place >= root) & (place < self.size - 1))
                def _():
                    self.down(lane, piece, 1).wait_send()

                @pl.when((place <= root) & (place > 0))
                def _():
                    self.down(lane, piece, -1).wait_send()
            return carry

        lax.fori_loop(0, self.pieces, one, 0)


class Place:
    def __init__(self):
        here = lax.axis_index("expert")
        self.here = here
        self.core, self.x, self.y = here % 2, here // 2 % 2, here // 4
        self.sibling = here + 1 - 2 * self.core
        self.x_chip = here + 2 - 4 * self.x
        self.y_chip = here + 4 - 8 * self.y

    def neighbours(self):
        return [(None, {"expert": i}) for i in (self.sibling, self.x_chip, self.y_chip)]

    def block(self, chip, core):
        x = self.x + (1 - chip // 2) * (1 - 2 * self.x)
        y = self.y + (1 - chip % 2) * (1 - 2 * self.y)
        return 4 * y + 2 * x + core


class Plane(Place):
    def __init__(self, own, spare, paired, from_x, from_y, pair_sems, x_sems, y_sems, by_device=False, step=STEP):
        self.step = step
        self.by_device = by_device
        self.own, self.spare, self.paired, self.from_x, self.from_y = own, spare, paired, from_x, from_y
        self.pair_sems, self.x_sems, self.y_sems = pair_sems, x_sems, y_sems
        super().__init__()
        self.half = own.shape[1] // 2
        self.pieces = self.half // step

    @staticmethod
    def semaphores(rows, step=STEP):
        pieces = rows // 2 // step
        return [
            pltpu.SemaphoreType.DMA((2, 4)),
            pltpu.SemaphoreType.DMA((2, 3, pieces)),
            pltpu.SemaphoreType.DMA((2, 3, pieces)),
        ]

    def pair_copy(self, chip):
        place = self.block(chip, 1 - self.core) if self.by_device else chip
        return remote(
            self.spare.at[place], self.paired.at[chip],
            self.pair_sems.at[0, chip], self.pair_sems.at[1, chip], expert=self.sibling,
        )

    def rows(self, side, piece):
        return pl.ds(pl.multiple_of(side * self.half + piece * self.step, self.step), self.step)

    def landing(self, piece):
        return pl.ds(pl.multiple_of(piece * self.step, self.step), self.step)

    def x_copy(self, kind, piece):
        chip, side = ((0, 0), (1, 0), (1, 1))[kind]
        return remote(
            self.own.at[chip, self.rows(side, piece)], self.from_x.at[kind, self.landing(piece)],
            self.x_sems.at[0, kind, piece], self.x_sems.at[1, kind, piece], expert=self.x_chip,
        )

    def y_copy(self, kind, piece):
        chip, side = ((0, 1), (2, 1), (2, 0))[kind]
        return remote(
            self.own.at[chip, self.rows(side, piece)], self.from_y.at[kind, self.landing(piece)],
            self.y_sems.at[0, kind, piece], self.y_sems.at[1, kind, piece], expert=self.y_chip,
        )

    def add_pair(self, chip, side, piece):
        rows = self.rows(side, piece)
        self.own[chip, rows] = (
            self.own[chip, rows].astype(jnp.float32) + self.paired[chip, rows].astype(jnp.float32)
        ).astype(jnp.bfloat16)

    def each(self, step):
        def one(piece, carry):
            step(piece)
            return carry

        lax.fori_loop(0, self.pieces, one, 0)

    def send_first(self, chip):
        def step(piece):
            if chip in (0, 1):
                self.add_pair(chip, 0, piece)
                self.x_copy(chip, piece).start()
            if chip in (0, 2):
                self.add_pair(chip, 1, piece)
                self.y_copy(chip // 2, piece).start()

        self.each(step)

    def first_piece(self, piece):
        for chip, side in ((0, 0), (0, 1), (1, 0), (2, 1)):
            self.add_pair(chip, side, piece)
        for kind in range(2):
            self.x_copy(kind, piece).start()
            self.y_copy(kind, piece).start()

    def second_piece(self, piece):
        landed = self.landing(piece)
        self.y_copy(0, piece).wait_recv()
        rows = self.rows(1, piece)
        self.own[1, rows] = (
            self.own[1, rows].astype(jnp.float32)
            + self.paired[1, rows].astype(jnp.float32)
            + self.from_y[0, landed].astype(jnp.float32)
        ).astype(jnp.bfloat16)
        self.x_copy(2, piece).start()
        self.x_copy(0, piece).wait_recv()
        rows = self.rows(0, piece)
        self.own[2, rows] = (
            self.own[2, rows].astype(jnp.float32)
            + self.paired[2, rows].astype(jnp.float32)
            + self.from_x[0, landed].astype(jnp.float32)
        ).astype(jnp.bfloat16)
        self.y_copy(2, piece).start()

    def send_second(self):
        self.each(self.second_piece)

    def last_sum(self, piece):
        landed = self.landing(piece)
        sums = []
        for side in range(2):
            first, second = (self.x_copy(1, piece), self.y_copy(2, piece)) if side == 0 else (self.y_copy(1, piece), self.x_copy(2, piece))
            first.wait_recv()
            second.wait_recv()
            a, b = (self.from_x[1, landed], self.from_y[2, landed]) if side == 0 else (self.from_y[1, landed], self.from_x[2, landed])
            rows = self.rows(side, piece)
            sums.append(
                self.own[3, rows].astype(jnp.float32)
                + self.paired[3, rows].astype(jnp.float32)
                + a.astype(jnp.float32)
                + b.astype(jnp.float32)
            )
        return sums

    def finish(self):
        for chip in range(4):
            self.pair_copy(chip).wait_send()

        def step(piece):
            for kind in range(3):
                self.x_copy(kind, piece).wait_send()
                self.y_copy(kind, piece).wait_send()

        self.each(step)


class Gather:
    def __init__(self, source, target, place, x_sems, y_sems, far_sems, pair_sems, own_sem, pieces):
        self.source, self.target = source, target
        self.place = place
        self.x_sems, self.y_sems, self.far_sems, self.pair_sems, self.own_sem = x_sems, y_sems, far_sems, pair_sems, own_sem
        self.pieces = pieces
        self.rows_each = source.shape[0] // pieces

    @staticmethod
    def semaphores(pieces):
        return [
            pltpu.SemaphoreType.DMA((2, pieces)),
            pltpu.SemaphoreType.DMA((2, pieces)),
            pltpu.SemaphoreType.DMA((2, pieces)),
            pltpu.SemaphoreType.DMA((2, 4, pieces)),
            pltpu.SemaphoreType.DMA,
        ]

    def rows(self, piece):
        return pl.ds(piece * self.rows_each, self.rows_each)

    def own_copy(self):
        return pltpu.make_async_copy(self.source, self.target.at[self.place.here], self.own_sem)

    def x_copy(self, piece):
        rows = self.rows(piece)
        return remote(
            self.source.at[rows], self.target.at[self.place.here, rows],
            self.x_sems.at[0, piece], self.x_sems.at[1, piece], expert=self.place.x_chip,
        )

    def y_copy(self, piece):
        rows = self.rows(piece)
        return remote(
            self.source.at[rows], self.target.at[self.place.here, rows],
            self.y_sems.at[0, piece], self.y_sems.at[1, piece], expert=self.place.y_chip,
        )

    def far_copy(self, piece):
        rows = self.rows(piece)
        came, goes = (
            (self.place.x_chip, self.place.y_chip) if piece % 2 == 0 else (self.place.y_chip, self.place.x_chip)
        )
        return remote(
            self.target.at[came, rows], self.target.at[came, rows],
            self.far_sems.at[0, piece], self.far_sems.at[1, piece], expert=goes,
        )

    def pair_copy(self, kind, piece):
        rows = self.rows(piece)
        block = self.place.block(kind, self.place.core)
        source = self.source.at[rows] if kind == 3 else self.target.at[block, rows]
        return remote(
            source, self.target.at[block, rows],
            self.pair_sems.at[0, kind, piece], self.pair_sems.at[1, kind, piece], expert=self.place.sibling,
        )

    def start_piece(self, piece):
        self.x_copy(piece).start()
        self.y_copy(piece).start()
        self.pair_copy(3, piece).start()

    def start(self):
        self.own_copy().start()
        for piece in range(self.pieces):
            self.start_piece(piece)

    def near(self, piece):
        self.x_copy(piece).wait_recv()
        if piece % 2 == 0:
            self.far_copy(piece).start()
        self.pair_copy(1, piece).start()
        self.y_copy(piece).wait_recv()
        if piece % 2 == 1:
            self.far_copy(piece).start()
        self.pair_copy(2, piece).start()

    def far(self, piece):
        self.far_copy(piece).wait_recv()
        self.pair_copy(0, piece).start()

    def paired(self, kind, piece):
        self.pair_copy(kind, piece).wait_recv()

    def finish(self):
        for piece in range(self.pieces):
            self.x_copy(piece).wait_send()
            self.y_copy(piece).wait_send()
            self.far_copy(piece).wait_send()
            for kind in range(4):
                self.pair_copy(kind, piece).wait_send()


def wide_dot(left, right):
    return jnp.dot(left, right, preferred_element_type=jnp.float32)


def turned_dot(left, right):
    return lax.dot_general(left, right, (((1,), (1,)), ((), ())), preferred_element_type=jnp.float32)


BLOCK_STEP = 32


def expert_kernel(
    x_all, g_early, g_late, mask, router, bias, w_gate, w_up, w_down,
    reduced, gated_all, gate_all, up_all, mixed_all,
    x_buf, g_buf, part, paired, from_x, from_y, line_in, line_spare, small, mixed,
    in_sems, out_sems, pair_sems, x_sems, y_sems, line_sems,
):
    experts, width, hidden = w_gate.shape
    rows = x_buf.shape[1]
    tile = min(512, width)
    early = g_early.shape[1]
    plane = Plane(part.at[1], part.at[0], paired, from_x, from_y, pair_sems, x_sems, y_sems, step=BLOCK_STEP)
    line = Line(part.at[1, 3], line_in, line_spare, reduced, line_sems, step=BLOCK_STEP)
    first_expert = lax.axis_index("expert") * experts
    outs = (gated_all, gate_all, up_all)

    def block_of(i):
        return plane.block(i // 2, (plane.core + 1 - i % 2) % 2)

    def fetch(i):
        slot, block = i % 2, block_of(i)
        return (
            pltpu.make_async_copy(x_all.at[block], x_buf.at[slot], in_sems.at[0, slot]),
            pltpu.make_async_copy(g_early.at[block], g_buf.at[slot, 0:early], in_sems.at[1, slot]),
            pltpu.make_async_copy(g_late.at[block], g_buf.at[slot, early:rows], in_sems.at[2, slot]),
        )

    def store(i):
        slot, block = i % 2, block_of(i)
        return [
            pltpu.make_async_copy(small.at[slot, n], outs[n].at[block], out_sems.at[n, slot])
            for n in range(3)
        ] + [pltpu.make_async_copy(mixed.at[slot], mixed_all.at[block], out_sems.at[3, slot])]

    def compute(i):
        slot = i % 2
        block = block_of(i)
        x = x_buf.at[slot]
        g = g_buf.at[slot]
        logits = wide_dot(x[...], router[...]) + bias[...]
        weights = jnp.exp(logits - jnp.max(logits, axis=1, keepdims=True))
        gates = weights / jnp.sum(weights, axis=1, keepdims=True)
        named = mask[block]
        column = lax.broadcasted_iota(jnp.int32, (rows, LANE), 1)
        extra = jnp.zeros((rows, LANE), jnp.float32)
        for j in range(experts):
            gate_pre = wide_dot(x[...], w_gate[j])
            up_pre = wide_dot(x[...], w_up[j])
            raw = turned_dot(g[...], w_down[j])
            gate = jnp.sum(jnp.where(column == first_expert + j, gates, 0.0), axis=1, keepdims=True)
            gate = gate * named[:, j : j + 1]
            sigma = jax.nn.sigmoid(gate_pre)
            activated = gate_pre * sigma
            inner = activated * up_pre
            act = gate * raw
            span = slice(j * hidden, (j + 1) * hidden)
            small[slot, 0, :, span] = (gate * inner).astype(jnp.bfloat16)
            small[slot, 1, :, span] = (
                act * up_pre * sigma * (1.0 + gate_pre * (1.0 - sigma))
            ).astype(jnp.bfloat16)
            small[slot, 2, :, span] = (act * activated).astype(jnp.bfloat16)
            gain = jnp.sum(raw * inner, axis=1, keepdims=True)
            extra = jnp.where(column == first_expert + j, gain, extra)
        for start in range(0, width, tile):
            columns = slice(start, start + tile)
            slot_grad = None
            mix = None
            for j in range(experts):
                span = slice(j * hidden, (j + 1) * hidden)
                term = turned_dot(small[slot, 1, :, span], w_gate[j, columns]) + turned_dot(
                    small[slot, 2, :, span], w_up[j, columns]
                )
                more = wide_dot(small[slot, 0, :, span], w_down[j, :, columns])
                slot_grad = term if slot_grad is None else slot_grad + term
                mix = more if mix is None else mix + more
            part[i % 2, i // 2, :, columns] = slot_grad.astype(jnp.bfloat16)
            mixed[slot, :, columns] = mix.astype(jnp.bfloat16)
        part[i % 2, i // 2, :, width:] = extra.astype(jnp.bfloat16)

    for copy in fetch(0):
        copy.start()
    greet(plane.neighbours() + line.neighbours())

    def step(i, carry):
        @pl.when(i < 7)
        def _():
            for copy in fetch(i + 1):
                copy.start()

        for copy in fetch(i):
            copy.wait()

        @pl.when(i >= 2)
        def _():
            for copy in store(i - 2):
                copy.wait()

        compute(i)
        for copy in store(i):
            copy.start()

        @pl.when(i % 2 == 0)
        def _():
            plane.pair_copy(i // 2).start()

        @pl.when(i % 2 == 1)
        def _():
            plane.pair_copy(i // 2).wait_recv()

        for chip in range(3):

            @pl.when(i == 2 * chip + 1)
            def _():
                plane.send_first(chip)
                if chip == 2:
                    plane.send_second()

        return carry

    lax.fori_loop(0, 8, step, 0)

    def last(step, carry):
        @pl.when(step < plane.pieces)
        def _():
            for side, total in enumerate(plane.last_sum(step)):
                plane.own[3, plane.rows(side, step)] = total.astype(jnp.bfloat16)

        line.advance(step)
        return carry

    lax.fori_loop(0, line.steps(), last, 0)
    for i in (6, 7):
        for copy in store(i):
            copy.wait()
    plane.finish()
    line.finish()


def experts_fused(arrived, grad_early, grad_late, mask, router, bias, w_gate, w_up, w_down):
    ranks, rows, width = arrived.shape
    experts, _, hidden = w_gate.shape
    wide = width + LANE
    inner = experts * hidden
    half = rows // 2
    low = jnp.bfloat16
    any_space = pl.BlockSpec(memory_space=pl.ANY)
    vmem = pl.BlockSpec(memory_space=pltpu.VMEM)
    small_shape = jax.ShapeDtypeStruct((ranks, rows, inner), low)
    return pl.pallas_call(
        expert_kernel,
        out_shape=(
            jax.ShapeDtypeStruct((rows, wide), low), small_shape, small_shape, small_shape,
            jax.ShapeDtypeStruct((ranks, rows, width), low),
        ),
        in_specs=[any_space] * 3 + [vmem] * 6,
        out_specs=(vmem, any_space, any_space, any_space, any_space),
        scratch_shapes=[
            pltpu.VMEM((2, rows, width), low),
            pltpu.VMEM((2, rows, width), low),
            pltpu.VMEM((2, 4, rows, wide), low),
            pltpu.VMEM((4, rows, wide), low),
            pltpu.VMEM((3, half, wide), low),
            pltpu.VMEM((3, half, wide), low),
            pltpu.VMEM((rows, wide), low),
            Line.spare_shape(rows, wide),
            pltpu.VMEM((2, 3, rows, inner), low),
            pltpu.VMEM((2, rows, width), low),
            pltpu.SemaphoreType.DMA((3, 2)),
            pltpu.SemaphoreType.DMA((4, 2)),
            *Plane.semaphores(rows, step=BLOCK_STEP),
            Line.semaphores(rows, step=BLOCK_STEP),
        ],
        compiler_params=pltpu.CompilerParams(
            collective_id=0, has_side_effects=True, vmem_limit_bytes=61 * 2**20
        ),
        cost_estimate=pl.CostEstimate(
            flops=12 * ranks * rows * width * inner, bytes_accessed=8 * ranks * rows * width, transcendentals=0
        ),
    )(arrived, grad_early, grad_late, mask, router, bias, w_gate, w_up, w_down)


def crossed_dot(left, right):
    return lax.dot_general(left, right, (((0,), (0,)), ((), ())), preferred_element_type=jnp.float32)


def closing_kernel(
    normed, query_grad, key_grad, value_grad, attended, attention_grad, extras,
    w_query, w_key, w_value, mixed, x_all, g_early, g_late, gated_all, gate_all, up_all,
    total, sums, turned, gain, mixture, gate_out, up_out, down_out,
    line_own, line_in, line_spare, part, paired, from_x, from_y,
    mix_own, mix_paired, mix_x, mix_y, mix_in, mix_spare, tiles, factors, results, downs,
    line_sems, pair_sems, x_sems, y_sems, mix_line_sems, mix_pair_sems, mix_x_sems, mix_y_sems,
    load_sems, weight_sems, factor_sems, tile_sems, out_sems,
    gains, mine, theirs, peer_sent, peer_got,
    *,
    gain_column,
):
    width = normed.shape[1]
    heads = query_grad.shape[1]
    share = part.shape[2]
    experts, _, hidden = gate_out.shape
    column_tile = min(512, width // 2)
    tile = tiles.shape[3]
    early = g_early.shape[1]
    count = width // tile
    line = Line(line_own, line_in, line_spare, total, line_sems)
    plane = Plane(part.at[1], part.at[0], paired, from_x, from_y, pair_sems, x_sems, y_sems)
    mix = Plane(mix_own, mixed, mix_paired, mix_x, mix_y, mix_pair_sems, mix_x_sems, mix_y_sems, by_device=True)
    mix_line = Line(mix_own.at[3], mix_in, mix_spare, mixture, mix_line_sems)
    peers = Peers(mine, theirs, peer_sent, peer_got)
    half = width // 2

    def load_own(chip):
        return pltpu.make_async_copy(mixed.at[mix.block(chip, mix.core)], mix_own.at[chip], load_sems.at[chip])

    weight_loads = [
        pltpu.make_async_copy(w_query, factors.at[0, 0:width], weight_sems.at[0]),
        pltpu.make_async_copy(w_key, factors.at[1, 0:width], weight_sems.at[1]),
        pltpu.make_async_copy(w_value.at[0:half], factors.at[0, width : width + half], weight_sems.at[2]),
        pltpu.make_async_copy(w_value.at[half:], factors.at[1, width : width + half], weight_sems.at[3]),
    ]

    def factor_load(matrix):
        return pltpu.make_async_copy(
            (gate_all, up_all, gated_all)[matrix], factors.at[matrix % 2], factor_sems.at[matrix]
        )

    def tile_copies(s, of_grad=False):
        columns = pl.ds(pl.multiple_of(s % count * tile, tile), tile)
        if of_grad:
            parts = g_early.at[:, :, columns], g_late.at[:, :, columns]
        else:
            parts = x_all.at[:, 0:early, columns], x_all.at[:, early:, columns]
        return (
            pltpu.make_async_copy(parts[0], tiles.at[s % 2, :, 0:early], tile_sems.at[0, s % 2]),
            pltpu.make_async_copy(parts[1], tiles.at[s % 2, :, early:], tile_sems.at[1, s % 2]),
        )

    def start_tile(s):
        @pl.when(s < 2 * count)
        def _():
            for copy in tile_copies(s):
                copy.start()

        @pl.when(s >= 2 * count)
        def _():
            for copy in tile_copies(s, of_grad=True):
                copy.start()

    def across(target, s):
        rows = pl.ds(pl.multiple_of(s % count * tile, tile), tile)
        return [
            pltpu.make_async_copy(
                results.at[s % 2, :, j * hidden : (j + 1) * hidden], target.at[j, rows], out_sems.at[0, s % 2, j]
            )
            for j in range(experts)
        ]

    def down(s):
        columns = pl.ds(pl.multiple_of(s % count * tile, tile), tile)
        return [
            pltpu.make_async_copy(
                downs.at[s % 2, j * hidden : (j + 1) * hidden], down_out.at[j, :, columns], out_sems.at[1, s % 2, j]
            )
            for j in range(experts)
        ]

    def expert_tile(s):
        @pl.when(s + 1 < 3 * count)
        def _():
            start_tile(s + 1)

        for matrix in range(3):

            @pl.when(s == matrix * count)
            def _():
                factor_load(matrix).wait()

        for copy in tile_copies(s):
            copy.wait()

        def held():
            return tiles[s % 2].reshape(tiles.shape[1] * tiles.shape[2], tile)

        @pl.when(s < 2 * count)
        def _():
            @pl.when(s >= 2)
            def _():
                for copy in across(gate_out, s):
                    copy.wait()

            results[s % 2] = crossed_dot(held(), factors[s // count]).astype(jnp.bfloat16)

            @pl.when(s < count)
            def _():
                for copy in across(gate_out, s):
                    copy.start()

            @pl.when(s >= count)
            def _():
                for copy in across(up_out, s):
                    copy.start()

        @pl.when(s >= 2 * count)
        def _():
            @pl.when(s >= 2 * count + 2)
            def _():
                for copy in down(s):
                    copy.wait()

            downs[s % 2] = crossed_dot(factors[0], held()).astype(jnp.bfloat16)
            for copy in down(s):
                copy.start()

        @pl.when(s == count - 1)
        def _():
            factor_load(2).start()

    def dense_block(i):
        chip, sub = i // 2, i % 2
        block = plane.block(chip, (plane.core + 1 - sub) % 2)
        columns = pl.ds(pl.multiple_of(block * share, share), share)
        source = normed[:, columns]
        part[sub, chip, :, 0:heads] = crossed_dot(source, query_grad[...]).astype(jnp.bfloat16)
        part[sub, chip, :, heads : 2 * heads] = crossed_dot(source, key_grad[...]).astype(jnp.bfloat16)
        part[sub, chip, :, 2 * heads : 3 * heads] = crossed_dot(source, value_grad[...]).astype(jnp.bfloat16)
        part[sub, chip, :, 3 * heads : 4 * heads] = crossed_dot(
            attention_grad[:, columns], attended[...]
        ).astype(jnp.bfloat16)
        part[sub, chip, :, 4 * heads :] = extras[block] + gains[columns]

        @pl.when(sub == 0)
        def _():
            plane.pair_copy(chip).start()

    for copy in weight_loads:
        copy.start()
    for chip in range(4):
        load_own(chip).start()
    greet(plane.neighbours() + peers.neighbours())
    for chip in range(4):
        mix.pair_copy(chip).start()
    for copy in weight_loads:
        copy.wait()
    for start in range(0, width, column_tile):
        columns = slice(start, start + column_tile)
        later = width + start % half
        line_own[:, columns] = (
            turned_dot(query_grad[...], factors[0, columns])
            + turned_dot(key_grad[...], factors[1, columns])
            + turned_dot(value_grad[...], factors[start // half, later : later + column_tile])
        ).astype(jnp.bfloat16)
    place = lax.broadcasted_iota(jnp.int32, (normed.shape[0], LANE), 1)
    chosen = jnp.where(place == gain_column, 1.0, 0.0).astype(jnp.bfloat16)
    for start in range(0, width, column_tile):
        columns = slice(start, start + column_tile)
        pull = line_own[:, columns].astype(jnp.float32) * normed[:, columns].astype(jnp.float32)
        gains[columns] = crossed_dot(pull.astype(jnp.bfloat16), chosen).astype(jnp.bfloat16)
    factor_load(0).start()
    factor_load(1).start()
    start_tile(0)
    mix_second, mix_last, dense_first, dense_second, dense_last = PLAN

    def step(s, carry):
        line.advance(s)

        @pl.when(s == 0)
        def _():
            for chip in range(3):
                load_own(chip).wait()
                mix.pair_copy(chip).wait_recv()
            for piece in range(AHEAD):
                mix.first_piece(piece)

        @pl.when(s == mix_last - 1)
        def _():
            load_own(3).wait()
            mix.pair_copy(3).wait_recv()

        @pl.when((s > 0) & (s + AHEAD - 1 < mix.pieces))
        def _():
            mix.first_piece(s + AHEAD - 1)

        @pl.when((s >= mix_second) & (s - mix_second < mix.pieces))
        def _():
            mix.second_piece(s - mix_second)

        @pl.when((s >= mix_last) & (s - mix_last < mix.pieces))
        def _():
            piece = s - mix_last
            for side, summed in enumerate(mix.last_sum(piece)):
                mix_own[3, mix.rows(side, piece)] = summed.astype(jnp.bfloat16)

        mix_line.advance(s - mix_last)

        @pl.when((s >= 4) & (s < 12))
        def _():
            dense_block(s - 4)

        @pl.when(s == dense_first)
        def _():
            for chip in range(4):
                plane.pair_copy(chip).wait_recv()
            for chip in range(3):
                plane.send_first(chip)

        @pl.when((s >= dense_second) & (s - dense_second < plane.pieces))
        def _():
            plane.second_piece(s - dense_second)

        @pl.when((s >= dense_last) & (s - dense_last < plane.pieces))
        def _():
            piece = s - dense_last
            for side, summed in enumerate(plane.last_sum(piece)):
                sums[plane.rows(side, piece)] = summed

        @pl.when(s < 3 * count)
        def _():
            expert_tile(s)

        return carry

    steps = jnp.maximum(mix_last + mix_line.steps(), jnp.maximum(3 * count, dense_last + plane.pieces))
    lax.fori_loop(0, steps, step, 0)
    column = 4 * heads + gain_column
    mine[...] = to_rows([sums[:, column : column + 1]], share)
    peers.start()
    turned[...] = sums[:, 3 * heads : 4 * heads].T
    for s in (2 * count - 2, 2 * count - 1):
        for copy in across(up_out, s):
            copy.wait()
    for s in (3 * count - 2, 3 * count - 1):
        for copy in down(s):
            copy.wait()
    gain[...] = peers.total()
    for each in (plane, line, mix, mix_line, peers):
        each.finish()


PLAN = (1, 3, 12, 15, 18)
AHEAD = 2
TILE = 256


def closing(
    normed, query_grad, key_grad, value_grad, attended, attention_grad, extras, w_query, w_key, w_value,
    mixed, arrived, grad_early, grad_late, gated, gate_grad, up_grad, experts, gain_column,
):
    rows, width = normed.shape
    heads = query_grad.shape[1]
    ranks, share, more = extras.shape
    wide = 4 * heads + more
    inner = gated.shape[2]
    hidden = inner // experts
    low = jnp.bfloat16
    tile = min(TILE, width // 2)
    vmem = pl.BlockSpec(memory_space=pltpu.VMEM)
    any_space = pl.BlockSpec(memory_space=pl.ANY)
    every = ranks * rows
    size = lax.axis_size("tensor")
    return pl.pallas_call(
        functools.partial(closing_kernel, gain_column=gain_column),
        out_shape=(
            jax.ShapeDtypeStruct((rows, width), low),
            jax.ShapeDtypeStruct((share, wide), jnp.float32),
            jax.ShapeDtypeStruct((heads, share), jnp.float32),
            jax.ShapeDtypeStruct((8, share), jnp.float32),
            jax.ShapeDtypeStruct((rows, width), low),
            jax.ShapeDtypeStruct((experts, width, hidden), low),
            jax.ShapeDtypeStruct((experts, width, hidden), low),
            jax.ShapeDtypeStruct((experts, hidden, width), low),
        ),
        in_specs=[vmem] * 7 + [any_space] * 10,
        out_specs=(vmem,) * 5 + (any_space,) * 3,
        scratch_shapes=[
            pltpu.VMEM((rows, width), low),
            pltpu.VMEM((rows, width), low),
            Line.spare_shape(rows, width),
            pltpu.VMEM((2, 4, share, wide), low),
            pltpu.VMEM((4, share, wide), low),
            pltpu.VMEM((3, share // 2, wide), low),
            pltpu.VMEM((3, share // 2, wide), low),
            pltpu.VMEM((4, rows, width), low),
            pltpu.VMEM((4, rows, width), low),
            pltpu.VMEM((3, rows // 2, width), low),
            pltpu.VMEM((3, rows // 2, width), low),
            pltpu.VMEM((rows, width), low),
            Line.spare_shape(rows, width),
            pltpu.VMEM((2, ranks, rows, tile), low),
            pltpu.VMEM((2, every, inner), low),
            pltpu.VMEM((2, tile, inner), low),
            pltpu.VMEM((2, inner, tile), low),
            Line.semaphores(rows),
            *Plane.semaphores(share),
            Line.semaphores(rows),
            *Plane.semaphores(rows),
            pltpu.SemaphoreType.DMA((4,)),
            pltpu.SemaphoreType.DMA((4,)),
            pltpu.SemaphoreType.DMA((3,)),
            pltpu.SemaphoreType.DMA((2, 2)),
            pltpu.SemaphoreType.DMA((2, 2, experts)),
            pltpu.VMEM((width, LANE), low),
            pltpu.VMEM((8, share), jnp.float32),
            pltpu.VMEM((size - 1, 8, share), jnp.float32),
            pltpu.SemaphoreType.DMA((size - 1,)),
            pltpu.SemaphoreType.DMA((size - 1,)),
        ],
        compiler_params=pltpu.CompilerParams(
            collective_id=2, has_side_effects=True, vmem_limit_bytes=63 * 2**20
        ),
    )(
        normed, query_grad, key_grad, value_grad, attended, attention_grad, extras, w_query, w_key, w_value,
        mixed, arrived, grad_early, grad_late,
        gated.reshape(every, inner), gate_grad.reshape(every, inner), up_grad.reshape(every, inner),
    )


class Peers:
    def __init__(self, mine, theirs, sent, got):
        self.mine, self.theirs, self.sent, self.got = mine, theirs, sent, got
        self.size = lax.axis_size("tensor")
        self.here = lax.axis_index("tensor")

    def neighbours(self):
        return [(None, {"tensor": (self.here + d) % self.size}) for d in range(1, self.size)]

    def copies(self):
        return [
            remote(
                self.mine, self.theirs.at[d - 1], self.sent.at[d - 1], self.got.at[d - 1],
                tensor=(self.here + d) % self.size,
            )
            for d in range(1, self.size)
        ]

    def start(self):
        for copy in self.copies():
            copy.start()

    def total(self):
        result = self.mine[...]
        for d, copy in enumerate(self.copies()):
            copy.wait_recv()
            result = result + self.theirs[d]
        return result

    def finish(self):
        for copy in self.copies():
            copy.wait_send()


def to_rows(columns, rows):
    lane = lax.broadcasted_iota(jnp.int32, (rows, LANE), 1)
    field = jnp.zeros((rows, LANE), jnp.float32)
    for i, column in enumerate(columns):
        field = jnp.where(lane == i, column, field)
    return field.T[:8]


def to_columns(sums):
    padded = jnp.concatenate([sums, jnp.zeros((LANE - 8, sums.shape[1]), jnp.float32)], axis=0)
    return padded.T


def swapped(field):
    half = HD // 2
    return jnp.concatenate([field[:, half:], field[:, :half]], axis=1)


def loads(pairs, sems):
    copies = [pltpu.make_async_copy(source, target, sems.at[i]) for i, (source, target) in enumerate(pairs)]
    for copy in copies:
        copy.start()
    return copies


SPREAD = 32
SPREAD_LAG = 2


def front_kernel(
    tokens, attn_gain, ffn_gain, w_query, key_far, value_far, out_far, qk_gain, cosine, sine, bias_far, routes, cotangent,
    total, normed, normed_two, attended, query_rot, keys_values, query_raw, key_raw, stats, routes_all, arrived, grad_early,
    line_own, line_in, line_spare, prompt, mine, theirs, two, w_key, w_value, w_out, bias,
    load_sems, line_sems, peer_sent, peer_got, *gather_sems,
):
    rows, width = tokens.shape
    local = w_query.shape[1]
    heads = local // HD
    factor = HD ** (-0.5)
    own_blocks = rows // PROMPT_DEV - 1
    devices = keys_values.shape[0] - own_blocks
    place = Place()
    line = Line(line_own, line_in, line_spare, total, line_sems)
    peers = Peers(mine, theirs, peer_sent, peer_got)
    names = Gather(routes, routes_all, place, *gather_sems[0:5], pieces=2)
    prompts = Gather(prompt, keys_values, place, *gather_sems[5:10], pieces=2)
    spread = Gather(normed_two, arrived, place, *gather_sems[10:15], pieces=rows // SPREAD)
    load_key, load_value, load_out, load_bias = loads(
        ((key_far, w_key), (value_far, w_value), (out_far, w_out), (bias_far, bias)), load_sems
    )
    above = Gather(cotangent.at[0 : grad_early.shape[1]], grad_early, place, *gather_sems[15:20], pieces=2)
    greet(place.neighbours() + peers.neighbours())
    names.start()
    above.start()
    source = tokens[...].astype(jnp.float32)
    scale_one = lax.rsqrt(jnp.sum(source * source, axis=1, keepdims=True) / width + epsilon)
    normed[...] = (source * scale_one * attn_gain[...]).astype(jnp.bfloat16)
    query_raw[...] = wide_dot(normed[...], w_query[...])
    load_key.wait()
    key_raw[...] = wide_dot(normed[...], w_key[...])
    mine[...] = to_rows(
        [
            jnp.sum(query_raw[...] * query_raw[...], axis=1, keepdims=True),
            jnp.sum(key_raw[...] * key_raw[...], axis=1, keepdims=True),
        ],
        rows,
    )
    peers.start()
    load_value.wait()
    value = wide_dot(normed[...], w_value[...]).astype(jnp.bfloat16)
    prompt[:, local:] = value[:PROMPT_DEV]
    for i in range(own_blocks):
        keys_values[devices + i, :, local:] = value[(i + 1) * PROMPT_DEV : (i + 2) * PROMPT_DEV]
    squares = to_columns(peers.total())
    scale_query = lax.rsqrt(squares[:, 0:1] / width + epsilon)
    scale_key = lax.rsqrt(squares[:, 1:2] / width + epsilon)
    for head in range(heads):
        columns = slice(head * HD, (head + 1) * HD)
        turned = key_raw[:, columns] * scale_key * qk_gain[1:2, columns]
        turned = (turned * cosine[...] + swapped(turned) * sine[...]).astype(jnp.bfloat16)
        prompt[:, columns] = turned[:PROMPT_DEV]
        for i in range(own_blocks):
            keys_values[devices + i, :, columns] = turned[(i + 1) * PROMPT_DEV : (i + 2) * PROMPT_DEV]
    prompts.own_copy().start()
    for piece in range(2):
        prompts.start_piece(piece)
    for head in range(heads):
        columns = slice(head * HD, (head + 1) * HD)
        turned = query_raw[:, columns] * scale_query * qk_gain[0:1, columns]
        turned = turned * cosine[...] + swapped(turned) * sine[...]
        query_rot[:, columns] = turned.astype(jnp.bfloat16)
    for piece in range(2):
        prompts.near(piece)
    for piece in range(2):
        names.near(piece)
    for piece in range(2):
        prompts.far(piece)
        names.far(piece)
    prompts.own_copy().wait()
    for kind in range(4):
        for piece in range(2):
            prompts.paired(kind, piece)
            names.paired(kind, piece)
    load_bias.wait()
    load_out.wait()
    for piece in range(2):
        above.near(piece)
    lane = lax.broadcasted_iota(jnp.int32, (rows, LANE), 1)
    kept = jnp.where(lane == 0, scale_one, 0.0)
    kept = jnp.where(lane == 1, scale_query, kept)
    kept = jnp.where(lane == 2, scale_key, kept)
    count = keys_values.shape[0] * PROMPT_DEV
    for head in range(heads):
        columns = slice(head * HD, (head + 1) * HD)
        keys = keys_values[:, :, columns].reshape(count, HD)
        values = keys_values[:, :, local + head * HD : local + (head + 1) * HD].reshape(count, HD)
        scores = turned_dot(query_rot[:, columns], keys) * factor + bias[...]
        top = jnp.max(scores, axis=1, keepdims=True)
        weights = jnp.exp(scores - top)
        whole = jnp.sum(weights, axis=1, keepdims=True)
        shares = (weights / whole).astype(jnp.bfloat16)
        attended[:, columns] = wide_dot(shares, values).astype(jnp.bfloat16)
        kept = jnp.where(lane == 8 + head, top + jnp.log(whole), kept)
    tile = min(512, width)
    for start in range(0, width, tile):
        columns = slice(start, start + tile)
        line_own[:, columns] = wide_dot(attended[...], w_out[:, columns]).astype(jnp.bfloat16)
    ratio = SPREAD // STEP
    groups = line.pieces // ratio

    def norm_rows(piece):
        span = slice(piece * SPREAD, (piece + 1) * SPREAD)
        hidden = tokens[span].astype(jnp.float32) + total[span].astype(jnp.float32)
        scale = lax.rsqrt(jnp.sum(hidden * hidden, axis=1, keepdims=True) / width + epsilon)
        normed_two[span] = (hidden * scale * ffn_gain[...]).astype(jnp.bfloat16)
        two[span] = jnp.broadcast_to(scale, (SPREAD, LANE))

    done = 0
    passed = 0
    for group in range(groups):
        ready = line.trip + (group + 1) * ratio
        lax.fori_loop(done, ready, line.step_body, 0)
        done = ready
        for piece in (group, groups + group):
            norm_rows(piece)
            spread.start_piece(piece)
        if group >= SPREAD_LAG:
            for piece in (passed, groups + passed):
                spread.near(piece)
            passed += 1
    spread.own_copy().start()
    for piece in range(2):
        above.far(piece)
    for group in range(passed, groups):
        for piece in (group, groups + group):
            spread.near(piece)
    for group in range(groups):
        for piece in (group, groups + group):
            spread.far(piece)
    stats[...] = jnp.where(lane == 3, two[...], kept)
    for kind in range(4):
        for piece in range(spread.pieces):
            spread.paired(kind, piece)
    spread.own_copy().wait()
    for kind in range(4):
        for piece in range(2):
            above.paired(kind, piece)
    above.own_copy().wait()
    names.own_copy().wait()
    for each in (names, prompts, spread, above, line, peers):
        each.finish()


def front(tokens, attn_gain, ffn_gain, w_query, w_key, w_value, w_out, qk_gain, cosine, sine, bias, routes, cotangent):
    rows, width = tokens.shape
    local = w_query.shape[1]
    ranks = lax.axis_size("expert")
    size = lax.axis_size("tensor")
    low, full = jnp.bfloat16, jnp.float32
    vmem = pl.BlockSpec(memory_space=pltpu.VMEM)
    any_space = pl.BlockSpec(memory_space=pl.ANY)
    blocks = ranks + rows // PROMPT_DEV - 1
    return pl.pallas_call(
        front_kernel,
        out_shape=(
            jax.ShapeDtypeStruct((rows, width), low),
            jax.ShapeDtypeStruct((rows, width), low),
            jax.ShapeDtypeStruct((rows, width), low),
            jax.ShapeDtypeStruct((rows, local), low),
            jax.ShapeDtypeStruct((rows, local), low),
            jax.ShapeDtypeStruct((blocks, PROMPT_DEV, 2 * local), low),
            jax.ShapeDtypeStruct((rows, local), full),
            jax.ShapeDtypeStruct((rows, local), full),
            jax.ShapeDtypeStruct((rows, LANE), full),
            jax.ShapeDtypeStruct((ranks,) + routes.shape, jnp.int32),
            jax.ShapeDtypeStruct((ranks, rows, width), low),
            jax.ShapeDtypeStruct((ranks, rows // 2, width), low),
        ),
        in_specs=[vmem] * 4 + [any_space] * 3 + [vmem] * 3 + [any_space, vmem, any_space],
        out_specs=(vmem,) * 10 + (any_space,) * 2,
        scratch_shapes=[
            pltpu.VMEM((rows, width), low),
            pltpu.VMEM((rows, width), low),
            Line.spare_shape(rows, width),
            pltpu.VMEM((PROMPT_DEV, 2 * local), low),
            pltpu.VMEM((8, rows), full),
            pltpu.VMEM((size - 1, 8, rows), full),
            pltpu.VMEM((rows, LANE), full),
            *(pltpu.VMEM(array.shape, array.dtype) for array in (w_key, w_value, w_out, bias)),
            pltpu.SemaphoreType.DMA((4,)),
            Line.semaphores(rows),
            pltpu.SemaphoreType.DMA((size - 1,)),
            pltpu.SemaphoreType.DMA((size - 1,)),
            *Gather.semaphores(2),
            *Gather.semaphores(2),
            *Gather.semaphores(rows // SPREAD),
            *Gather.semaphores(2),
        ],
        compiler_params=pltpu.CompilerParams(
            collective_id=1, has_side_effects=True, vmem_limit_bytes=60 * 2**20
        ),
        cost_estimate=pl.CostEstimate(flops=100 * 10**9, bytes_accessed=200 * 10**6, transcendentals=0),
    )(tokens, attn_gain, ffn_gain, w_query, w_key, w_value, w_out, qk_gain, cosine, sine, bias, routes, cotangent)


def backward_kernel(
    reduced, tokens, attention, cotangent, normed_two, router, expert_bias, routed, ffn_gain,
    out_far, turned_far, keys_far, bias_far, stats, query_far, raw_far, cosine, sine, qk_gain,
    query_out, key_out, value_out, gain_out, hidden_grad, attention_grad, extras,
    out_grad, query_grad, prompt_grads, own_grads, own, paired, from_x, from_y, mine, theirs,
    w_out, query_rot, keys_values, bias, query_raw, key_raw, load_sems,
    pair_sems, x_sems, y_sems, peer_sent, peer_got,
    *,
    gain_column,
):
    rows, local = query_rot.shape
    width = attention_grad.shape[1]
    heads = local // HD
    factor = HD ** (-0.5)
    own_blocks = rows // PROMPT_DEV - 1
    devices = keys_values.shape[0] - own_blocks
    count = keys_values.shape[0] * PROMPT_DEV
    reach = devices * PROMPT_DEV
    plane = Plane(own, prompt_grads, paired, from_x, from_y, pair_sems, x_sems, y_sems, by_device=True)
    peers = Peers(mine, theirs, peer_sent, peer_got)
    load_out, *load_heads, load_query, load_raw = loads(
        (
            (out_far, w_out), (turned_far, query_rot), (keys_far, keys_values), (bias_far, bias),
            (query_far, query_raw), (raw_far, key_raw),
        ),
        load_sems,
    )
    greet(plane.neighbours() + peers.neighbours())
    tile = min(512, width)
    starts = range(0, width, tile)
    scale_two = stats[:, 3:4]
    logits = wide_dot(normed_two[...], router[...]) + expert_bias[...]
    weights = jnp.exp(logits - jnp.max(logits, axis=1, keepdims=True))
    chances = weights / jnp.sum(weights, axis=1, keepdims=True)
    chance_grad = routed[...] * reduced[:, width:].astype(jnp.float32)
    logit_grad = (
        chances * (chance_grad - jnp.sum(chances * chance_grad, axis=1, keepdims=True))
    ).astype(jnp.bfloat16)

    def hidden_of(columns):
        return tokens[:, columns].astype(jnp.float32) + attention[:, columns].astype(jnp.float32)

    def input_part(columns):
        return reduced[:, columns].astype(jnp.float32) + turned_dot(logit_grad, router[columns])

    pull = jnp.zeros((rows, 1), jnp.float32)
    for start in starts:
        columns = slice(start, start + tile)
        weighted = ffn_gain[:, columns] * input_part(columns)
        hidden_grad[:, columns] = weighted
        pull = pull + jnp.sum(weighted * hidden_of(columns), axis=1, keepdims=True)
    pull = scale_two * scale_two * scale_two / width * pull
    for start in starts:
        columns = slice(start, start + tile)
        grad = (
            cotangent[:, columns].astype(jnp.float32)
            + scale_two * hidden_grad[:, columns]
            - hidden_of(columns) * pull
        )
        hidden_grad[:, columns] = grad
        attention_grad[:, columns] = grad.astype(jnp.bfloat16)
    load_out.wait()
    out_grad[...] = turned_dot(attention_grad[...], w_out[...]).astype(jnp.bfloat16)
    for load in load_heads:
        load.wait()
    for head in range(heads):
        columns = slice(head * HD, (head + 1) * HD)
        other = slice(local + head * HD, local + (head + 1) * HD)
        keys = keys_values[:, :, columns].reshape(count, HD)
        values = keys_values[:, :, other].reshape(count, HD)
        query, above = query_rot[:, columns], out_grad[:, columns]
        scores = turned_dot(query, keys) * factor + bias[...]
        shares = jnp.exp(scores - stats[:, 8 + head : 9 + head])
        share_grad = turned_dot(above, values)
        delta = jnp.sum(shares * share_grad, axis=1, keepdims=True)
        score_grad = (shares * (share_grad - delta)).astype(jnp.bfloat16)
        query_grad[:, columns] = wide_dot(score_grad, keys) * factor
        key_grad = crossed_dot(score_grad, query) * factor
        value_grad = crossed_dot(shares.astype(jnp.bfloat16), above)
        prompt_grads[:, :, columns] = key_grad[:reach].astype(jnp.bfloat16).reshape(devices, PROMPT_DEV, HD)
        prompt_grads[:, :, other] = value_grad[:reach].astype(jnp.bfloat16).reshape(devices, PROMPT_DEV, HD)
        own_grads[PROMPT_DEV:, columns] = key_grad[reach:]
        own_grads[PROMPT_DEV:, other] = value_grad[reach:]
    for chip in range(4):
        plane.pair_copy(chip).start()
    for chip in range(4):
        own[chip] = prompt_grads[plane.block(chip, plane.core)]
    for chip in range(4):
        plane.pair_copy(chip).wait_recv()
        if chip < 3:
            plane.send_first(chip)

    def normed_part(source, raw, row, scale):
        inner = jnp.zeros((rows, 1), jnp.float32)
        for head in range(heads):
            columns = slice(head * HD, (head + 1) * HD)
            grad = source[:, columns]
            grad = grad * cosine[...] - swapped(grad) * sine[...]
            gain_out[row : row + 1, columns] = jnp.sum(grad * raw[:, columns] * scale, axis=0, keepdims=True)
            grad = qk_gain[row : row + 1, columns] * grad
            source[:, columns] = grad
            inner = inner + jnp.sum(grad * raw[:, columns], axis=1, keepdims=True)
        return inner

    load_query.wait()
    load_raw.wait()
    scale_query, scale_key = stats[:, 1:2], stats[:, 2:3]
    query_inner = normed_part(query_grad, query_raw, 0, scale_query)
    plane.send_second()
    chosen = lax.broadcasted_iota(jnp.int32, (rows, LANE), 1) == gain_column
    chosen = jnp.where(chosen, 1.0, 0.0).astype(jnp.bfloat16)
    for start in starts:
        columns = slice(start, start + tile)
        sway = input_part(columns) * hidden_of(columns) * scale_two
        extras[columns] = (
            crossed_dot(normed_two[:, columns], logit_grad) + crossed_dot(sway.astype(jnp.bfloat16), chosen)
        ).astype(jnp.bfloat16)

    def last(piece, carry):
        for side, summed in enumerate(plane.last_sum(piece)):
            own_grads[plane.rows(side, piece)] = summed
        return carry

    lax.fori_loop(0, plane.pieces, last, 0)
    key_inner = normed_part(own_grads, key_raw, 1, scale_key)
    mine[...] = to_rows([query_inner, key_inner], rows)
    peers.start()
    value_out[...] = own_grads[:, local:].astype(jnp.bfloat16)
    inner = to_columns(peers.total())
    for out, source, raw, scale, i in (
        (query_out, query_grad, query_raw, scale_query, 0),
        (key_out, own_grads, key_raw, scale_key, 1),
    ):
        pull = scale * scale * scale / width * inner[:, i : i + 1]
        out[...] = (scale * source[:, :local] - raw[...] * pull).astype(jnp.bfloat16)
    plane.finish()
    peers.finish()


def backward(
    reduced, tokens, attention, cotangent, normed_two, router, expert_bias, routed, ffn_gain,
    w_out, query_rot, keys_values, bias, stats, query_raw, key_raw, cosine, sine, qk_gain, gain_column,
):
    rows, local = query_rot.shape
    size = lax.axis_size("tensor")
    ranks = lax.axis_size("expert")
    low, full = jnp.bfloat16, jnp.float32
    vmem = pl.BlockSpec(memory_space=pltpu.VMEM)
    any_space = pl.BlockSpec(memory_space=pl.ANY)
    small = jax.ShapeDtypeStruct((rows, local), low)
    return pl.pallas_call(
        functools.partial(backward_kernel, gain_column=gain_column),
        out_shape=(
            small, small, small, jax.ShapeDtypeStruct((2, local), full),
            jax.ShapeDtypeStruct(tokens.shape, full), jax.ShapeDtypeStruct(tokens.shape, low),
            jax.ShapeDtypeStruct((tokens.shape[1], LANE), low),
        ),
        in_specs=[vmem] * 9 + [any_space] * 4 + [vmem] + [any_space] * 2 + [vmem] * 3,
        out_specs=(vmem,) * 7,
        scratch_shapes=[
            pltpu.VMEM((rows, local), low),
            pltpu.VMEM((rows, local), full),
            pltpu.VMEM((ranks, PROMPT_DEV, 2 * local), low),
            pltpu.VMEM((rows, 2 * local), full),
            pltpu.VMEM((4, PROMPT_DEV, 2 * local), low),
            pltpu.VMEM((4, PROMPT_DEV, 2 * local), low),
            pltpu.VMEM((3, PROMPT_DEV // 2, 2 * local), low),
            pltpu.VMEM((3, PROMPT_DEV // 2, 2 * local), low),
            pltpu.VMEM((8, rows), full),
            pltpu.VMEM((size - 1, 8, rows), full),
            *(
                pltpu.VMEM(array.shape, array.dtype)
                for array in (w_out, query_rot, keys_values, bias, query_raw, key_raw)
            ),
            pltpu.SemaphoreType.DMA((6,)),
            *Plane.semaphores(PROMPT_DEV),
            pltpu.SemaphoreType.DMA((size - 1,)),
            pltpu.SemaphoreType.DMA((size - 1,)),
        ],
        compiler_params=pltpu.CompilerParams(
            collective_id=3, has_side_effects=True, vmem_limit_bytes=60 * 2**20
        ),
    )(
        reduced, tokens, attention, cotangent, normed_two, router, expert_bias, routed, ffn_gain,
        w_out, query_rot, keys_values, bias, stats, query_raw, key_raw, cosine, sine, qk_gain,
    )


def rotate(field, cosine, sine):
    half = field.shape[-1] // 2
    first = field[..., :half]
    second = field[..., half:]
    return jnp.concatenate(
        [first * cosine - second * sine, second * cosine + first * sine], axis=-1
    )


def unrotate(grad, cosine, sine):
    half = grad.shape[-1] // 2
    first = grad[..., :half]
    second = grad[..., half:]
    return jnp.concatenate(
        [first * cosine + second * sine, second * cosine - first * sine], axis=-1
    )


def experts(normed_two, cotangent, gates, w_gate, w_up, w_down, experts_total):
    local_experts = w_gate.shape[0]
    device = lax.axis_index("expert")
    arrived = lax.all_gather(normed_two, "expert", axis=0, tiled=True)
    arrived_grad = lax.all_gather(cotangent, "expert", axis=0, tiled=True)
    gate_pre = jnp.einsum("rd,jdf->jrf", arrived, w_gate, preferred_element_type=jnp.float32)
    up_pre = jnp.einsum("rd,jdf->jrf", arrived, w_up, preferred_element_type=jnp.float32)
    raw_grad = jnp.einsum("rd,jfd->jrf", arrived_grad, w_down, preferred_element_type=jnp.float32)
    sigma = jax.nn.sigmoid(gate_pre)
    activated = gate_pre * sigma
    inner = activated * up_pre
    gated = (gates[:, :, None] * inner).astype(jnp.bfloat16)
    mixed_part = jnp.einsum("jrf,jfd->rd", gated, w_down, preferred_element_type=jnp.float32)
    mixture = lax.psum(
        lax.psum_scatter(
            mixed_part.astype(jnp.bfloat16), "expert", scatter_dimension=0, tiled=True
        ),
        "tensor",
    ).astype(jnp.float32)
    gate_grad_part = jnp.sum(raw_grad * inner, axis=2)
    act_grad = gates[:, :, None] * raw_grad
    up_grad = (act_grad * activated).astype(jnp.bfloat16)
    gate_grad = (act_grad * up_pre * sigma * (1.0 + gate_pre * (1.0 - sigma))).astype(jnp.bfloat16)
    grad_w_down = jnp.einsum("jrf,rd->jfd", gated, arrived_grad, preferred_element_type=jnp.float32)
    grad_w_gate = jnp.einsum("rd,jrf->jdf", arrived, gate_grad, preferred_element_type=jnp.float32)
    grad_w_up = jnp.einsum("rd,jrf->jdf", arrived, up_grad, preferred_element_type=jnp.float32)
    slot_grad = jnp.einsum("jrf,jdf->rd", gate_grad, w_gate, preferred_element_type=jnp.float32)
    slot_grad = slot_grad + jnp.einsum(
        "jrf,jdf->rd", up_grad, w_up, preferred_element_type=jnp.float32
    )
    moe_input_grad = lax.psum(
        lax.psum_scatter(
            slot_grad.astype(jnp.bfloat16), "expert", scatter_dimension=0, tiled=True
        ),
        "tensor",
    ).astype(jnp.float32)
    placed = jnp.zeros((arrived.shape[0], experts_total), jnp.float32)
    placed = lax.dynamic_update_slice_in_dim(placed, gate_grad_part.T, device * local_experts, 1)
    chance_grad = lax.psum(
        lax.psum_scatter(placed, "expert", scatter_dimension=0, tiled=True), "tensor"
    )
    return mixture, moe_input_grad, chance_grad, [grad_w_gate, grad_w_up, grad_w_down]


def body(
    tokens,
    w_query,
    w_key,
    w_value,
    w_out,
    attn_gain,
    ffn_gain,
    qk_gain,
    router,
    w_gate,
    w_up,
    w_down,
    routes,
    cont_group,
    cotangent,
):
    rows, width = tokens.shape
    local_width = w_query.shape[1]
    head_count = local_width // HD
    experts_total = router.shape[1]
    local_experts = w_gate.shape[0]
    ranks = lax.axis_size("expert")
    device = lax.axis_index("expert")
    span = ranks // 2
    prompt_len = PROMPT_DEV * span
    factor = HD ** (-0.5)
    local = jnp.arange(rows, dtype=jnp.int32)
    is_prompt = local < PROMPT_DEV
    after = jnp.maximum(local - PROMPT_DEV, 0)
    slot_cont = after // CLEN
    cont_pick = jnp.sum(
        jnp.where(
            slot_cont[:, None] == jnp.arange(CONT_DEV, dtype=jnp.int32)[None, :],
            cont_group[None, :],
            0,
        ),
        axis=1,
    )
    group = jnp.where(is_prompt, device // span, cont_pick)
    position = jnp.where(is_prompt, device % span * PROMPT_DEV + local, prompt_len + after % CLEN)
    tag = jnp.where(is_prompt, -1, slot_cont)
    frequency = 10000.0 ** (-jnp.arange(HD // 2, dtype=jnp.float32) * 2.0 / HD)
    angle = position.astype(jnp.float32)[:, None] * frequency[None, :]
    cosine = jnp.cos(angle)[:, None, :]
    sine = jnp.sin(angle)[:, None, :]
    source = tokens.astype(jnp.float32)
    scale_one = lax.rsqrt(jnp.mean(source * source, axis=1, keepdims=True) + epsilon)
    normed = (source * scale_one * attn_gain).astype(jnp.bfloat16)
    query_raw = jnp.dot(normed, w_query, preferred_element_type=jnp.float32)
    key_raw = jnp.dot(normed, w_key, preferred_element_type=jnp.float32)
    value_raw = jnp.dot(normed, w_value, preferred_element_type=jnp.float32)
    squares = lax.psum(
        jnp.stack(
            [jnp.sum(query_raw * query_raw, axis=1), jnp.sum(key_raw * key_raw, axis=1)], axis=1
        ),
        "tensor",
    )
    scale_query = lax.rsqrt(squares[:, 0:1] / width + epsilon)
    scale_key = lax.rsqrt(squares[:, 1:2] / width + epsilon)
    query_rot = (
        rotate((query_raw * scale_query * qk_gain[0]).reshape(rows, head_count, HD), cosine, sine)
        .reshape(rows, local_width)
        .astype(jnp.bfloat16)
    )
    key_rot = (
        rotate((key_raw * scale_key * qk_gain[1]).reshape(rows, head_count, HD), cosine, sine)
        .reshape(rows, local_width)
        .astype(jnp.bfloat16)
    )
    value_low = value_raw.astype(jnp.bfloat16)
    prompt_keys, prompt_values = (
        lax.all_gather(key_rot[:PROMPT_DEV], "expert", axis=0, tiled=True),
        lax.all_gather(value_low[:PROMPT_DEV], "expert", axis=0, tiled=True),
    )
    prompt_count = prompt_keys.shape[0]
    all_keys = jnp.concatenate([prompt_keys, key_rot[PROMPT_DEV:]], axis=0)
    all_values = jnp.concatenate([prompt_values, value_low[PROMPT_DEV:]], axis=0)
    key_index = jnp.arange(prompt_count, dtype=jnp.int32)
    prompt_mask = (group[:, None] == (key_index // prompt_len)[None, :]) & (
        (key_index % prompt_len)[None, :] <= position[:, None]
    )
    own_mask = (tag[:, None] == tag[None, PROMPT_DEV:]) & (
        position[None, PROMPT_DEV:] <= position[:, None]
    )
    mask = jnp.concatenate([prompt_mask, own_mask], axis=1)

    def head_scores(query_head, key_head):
        scores = (
            jnp.einsum("qd,kd->qk", query_head, key_head, preferred_element_type=jnp.float32)
            * factor
        )
        return jnp.where(mask, scores, masked_value)

    outputs = []
    log_totals = []
    for head in range(head_count):
        start = head * HD
        scores = head_scores(query_rot[:, start : start + HD], all_keys[:, start : start + HD])
        top = jnp.max(scores, axis=1, keepdims=True)
        weights = jnp.exp(scores - top)
        total = jnp.sum(weights, axis=1, keepdims=True)
        shares = (weights / total).astype(jnp.bfloat16)
        outputs.append(
            jnp.dot(shares, all_values[:, start : start + HD], preferred_element_type=jnp.float32)
        )
        log_totals.append(top + jnp.log(total))
    attended = jnp.concatenate(outputs, axis=1).astype(jnp.bfloat16)
    attention = lax.psum(jnp.dot(attended, w_out, preferred_element_type=jnp.float32), "tensor")
    hidden = source + attention
    scale_two = lax.rsqrt(jnp.mean(hidden * hidden, axis=1, keepdims=True) + epsilon)
    normed_two = (hidden * scale_two * ffn_gain).astype(jnp.bfloat16)
    logits = jnp.dot(normed_two, router, preferred_element_type=jnp.float32)
    top = jnp.max(logits, axis=1, keepdims=True)
    weights = jnp.exp(logits - top)
    chances = weights / jnp.sum(weights, axis=1, keepdims=True)
    hits = (routes[:, :, None] == jnp.arange(experts_total, dtype=jnp.int32)[None, None, :]).astype(
        jnp.float32
    )
    rows_mask = jnp.sum(hits, axis=1)
    routed = lax.all_gather(
        (rows_mask * chances).astype(jnp.float32), "expert", axis=0, tiled=True
    )
    gates = lax.dynamic_slice_in_dim(routed, device * local_experts, local_experts, 1).T
    grad_out = cotangent.astype(jnp.float32)
    pieces = max(1, ranks * rows // 4096)
    piece = rows // pieces
    split_gates = gates.reshape(local_experts, ranks, rows)
    results = []
    weight_grads = None
    for number in range(pieces):
        part = slice(number * piece, (number + 1) * piece)
        sources = (normed_two[part], cotangent[part])
        if results:
            sources, results, weight_grads = lax.optimization_barrier(
                (sources, results, weight_grads)
            )
        *result, grads = experts(
            *sources,
            split_gates[:, :, part].reshape(local_experts, ranks * piece),
            w_gate,
            w_up,
            w_down,
            experts_total,
        )
        results.append(result)
        weight_grads = grads if weight_grads is None else [a + b for a, b in zip(weight_grads, grads)]
    mixture, moe_input_grad, chance_grad = (
        jnp.concatenate(list(group_of), axis=0) for group_of in zip(*results)
    )
    grad_w_gate, grad_w_up, grad_w_down = weight_grads
    chance_grad = rows_mask * chance_grad
    output = (hidden + mixture).astype(jnp.bfloat16)
    logit_grad = (
        chances * (chance_grad - jnp.sum(chances * chance_grad, axis=1, keepdims=True))
    ).astype(jnp.bfloat16)
    grad_router = jnp.einsum(
        "td,te->de", normed_two, logit_grad, preferred_element_type=jnp.float32
    )
    normed_two_grad = moe_input_grad + jnp.einsum(
        "te,de->td", logit_grad, router, preferred_element_type=jnp.float32
    )
    weighted_two = ffn_gain * normed_two_grad
    grad_ffn_gain = jnp.sum(normed_two_grad * hidden * scale_two, axis=0)
    hidden_grad = (
        grad_out
        + scale_two * weighted_two
        - hidden * (scale_two**3 / width) * jnp.sum(weighted_two * hidden, axis=1, keepdims=True)
    )
    attention_grad = hidden_grad.astype(jnp.bfloat16)
    grad_w_out = jnp.einsum(
        "td,te->de", attended, attention_grad, preferred_element_type=jnp.float32
    )
    attended_grad = jnp.einsum(
        "te,de->td", attention_grad, w_out, preferred_element_type=jnp.float32
    ).astype(jnp.bfloat16)
    query_grads = []
    key_grads = []
    value_grads = []
    for head in range(head_count):
        start = head * HD
        query_head = query_rot[:, start : start + HD]
        key_head = all_keys[:, start : start + HD]
        value_head = all_values[:, start : start + HD]
        out_grad_head = attended_grad[:, start : start + HD]
        recomputed = jnp.exp(head_scores(query_head, key_head) - log_totals[head])
        share_grad = jnp.einsum(
            "qd,kd->qk", out_grad_head, value_head, preferred_element_type=jnp.float32
        )
        delta = jnp.sum(recomputed * share_grad, axis=1, keepdims=True)
        score_grad = (recomputed * (share_grad - delta)).astype(jnp.bfloat16)
        query_grads.append(
            jnp.dot(score_grad, key_head, preferred_element_type=jnp.float32) * factor
        )
        key_grads.append(
            jnp.einsum("qk,qd->kd", score_grad, query_head, preferred_element_type=jnp.float32)
            * factor
        )
        value_grads.append(
            jnp.einsum(
                "qk,qd->kd",
                recomputed.astype(jnp.bfloat16),
                out_grad_head,
                preferred_element_type=jnp.float32,
            )
        )
    key_grad_all = jnp.concatenate(key_grads, axis=1)
    value_grad_all = jnp.concatenate(value_grads, axis=1)
    prompt_key_grad, prompt_value_grad = (
        lax.psum_scatter(
            key_grad_all[:prompt_count].astype(jnp.bfloat16),
            "expert",
            scatter_dimension=0,
            tiled=True,
        ).astype(jnp.float32),
        lax.psum_scatter(
            value_grad_all[:prompt_count].astype(jnp.bfloat16),
            "expert",
            scatter_dimension=0,
            tiled=True,
        ).astype(jnp.float32),
    )
    key_grad = jnp.concatenate([prompt_key_grad, key_grad_all[prompt_count:]], axis=0)
    value_grad = jnp.concatenate([prompt_value_grad, value_grad_all[prompt_count:]], axis=0)
    query_grad = unrotate(
        jnp.concatenate(query_grads, axis=1).reshape(rows, head_count, HD), cosine, sine
    ).reshape(rows, local_width)
    key_grad = unrotate(key_grad.reshape(rows, head_count, HD), cosine, sine).reshape(
        rows, local_width
    )
    grad_qk_gain = jnp.stack(
        [
            jnp.sum(query_grad * query_raw * scale_query, axis=0),
            jnp.sum(key_grad * key_raw * scale_key, axis=0),
        ],
        axis=0,
    )
    weighted_query = qk_gain[0] * query_grad
    weighted_key = qk_gain[1] * key_grad
    inner_sums = lax.psum(
        jnp.stack(
            [jnp.sum(weighted_query * query_raw, axis=1), jnp.sum(weighted_key * key_raw, axis=1)],
            axis=1,
        ),
        "tensor",
    )
    query_raw_grad = (
        scale_query * weighted_query - query_raw * (scale_query**3 / width) * inner_sums[:, 0:1]
    ).astype(jnp.bfloat16)
    key_raw_grad = (
        scale_key * weighted_key - key_raw * (scale_key**3 / width) * inner_sums[:, 1:2]
    ).astype(jnp.bfloat16)
    value_raw_grad = value_grad.astype(jnp.bfloat16)
    grad_w_query = jnp.einsum(
        "td,te->de", normed, query_raw_grad, preferred_element_type=jnp.float32
    )
    grad_w_key = jnp.einsum("td,te->de", normed, key_raw_grad, preferred_element_type=jnp.float32)
    grad_w_value = jnp.einsum(
        "td,te->de", normed, value_raw_grad, preferred_element_type=jnp.float32
    )
    normed_part = jnp.einsum(
        "te,de->td", query_raw_grad, w_query, preferred_element_type=jnp.float32
    )
    normed_part = normed_part + jnp.einsum(
        "te,de->td", key_raw_grad, w_key, preferred_element_type=jnp.float32
    )
    normed_part = normed_part + jnp.einsum(
        "te,de->td", value_raw_grad, w_value, preferred_element_type=jnp.float32
    )
    normed_grad = lax.psum(normed_part.astype(jnp.bfloat16), "tensor").astype(jnp.float32)
    weighted_one = attn_gain * normed_grad
    grad_attn_gain = jnp.sum(normed_grad * source * scale_one, axis=0)
    input_grad = (
        hidden_grad
        + scale_one * weighted_one
        - source * (scale_one**3 / width) * jnp.sum(weighted_one * source, axis=1, keepdims=True)
    )
    summed = (
        lax.psum_scatter(
            grad_w_query.astype(jnp.bfloat16), "expert", scatter_dimension=0, tiled=True
        ).astype(jnp.float32),
        lax.psum_scatter(
            grad_w_key.astype(jnp.bfloat16), "expert", scatter_dimension=0, tiled=True
        ).astype(jnp.float32),
        lax.psum_scatter(
            grad_w_value.astype(jnp.bfloat16), "expert", scatter_dimension=0, tiled=True
        ).astype(jnp.float32),
        lax.psum_scatter(
            grad_w_out.astype(jnp.bfloat16), "expert", scatter_dimension=1, tiled=True
        ).astype(jnp.float32),
        lax.psum_scatter(
            grad_attn_gain.astype(jnp.bfloat16), "expert", scatter_dimension=0, tiled=True
        ).astype(jnp.float32),
        lax.psum_scatter(
            grad_ffn_gain.astype(jnp.bfloat16), "expert", scatter_dimension=0, tiled=True
        ).astype(jnp.float32),
        lax.psum_scatter(
            grad_qk_gain.astype(jnp.bfloat16), "expert", scatter_dimension=1, tiled=True
        ).astype(jnp.float32),
        lax.psum_scatter(
            grad_router.astype(jnp.bfloat16), "expert", scatter_dimension=0, tiled=True
        ).astype(jnp.float32),
    )
    return (
        output,
        input_grad,
        summed[0],
        summed[1],
        summed[2],
        summed[3],
        summed[4],
        summed[5],
        summed[6],
        summed[7],
        grad_w_gate,
        grad_w_up,
        grad_w_down,
    )


def compact(
    tokens, w_query, w_key, w_value, w_out, attn_gain, ffn_gain, qk_gain, router, w_gate, w_up, w_down,
    routes, cont_group, cotangent,
):
    rows, width = tokens.shape
    local_width = w_query.shape[1]
    head_count = local_width // HD
    experts_total = router.shape[1]
    local_experts = w_gate.shape[0]
    ranks = lax.axis_size("expert")
    device = lax.axis_index("expert")
    full = jnp.float32
    group, position, tag = layout(rows, ranks, device, cont_group)
    channel = jnp.arange(HD)
    frequency = 10000.0 ** (-(channel % (HD // 2)).astype(full) * 2.0 / HD)
    angle = position.astype(full)[:, None] * frequency[None, :]
    cosine = jnp.cos(angle)
    sine = jnp.sin(angle) * jnp.where(channel < HD // 2, -1.0, 1.0)
    bias = jnp.where(attention_mask(group, position, tag, ranks), 0.0, masked_value).astype(full)
    all_experts = jnp.pad(router, ((0, 0), (0, LANE - experts_total)))
    expert_bias = jnp.where(jnp.arange(LANE) < experts_total, 0.0, masked_value).astype(full)[None]
    turned_routes = jnp.tile(jnp.pad(routes.T, ((0, -routes.shape[1] % 8), (0, 0)), constant_values=-1), (2, 1))
    hits = routes[:, :, None] == jnp.arange(experts_total, dtype=jnp.int32)
    routed = jnp.pad(jnp.any(hits, axis=1).astype(full), ((0, 0), (0, LANE - experts_total)))
    (
        attention, normed, normed_two, attended, query_rot, keys_values, query_raw, key_raw, stats, routes_all, arrived, grad_early,
    ) = front(
        tokens, attn_gain[None], ffn_gain[None], w_query, w_key, w_value, w_out, qk_gain, cosine, sine, bias,
        turned_routes, cotangent,
    )
    grad_late = lax.all_gather(cotangent[rows // 2 :], "expert", axis=0)
    names = routes_all[:, : turned_routes.shape[0] // 2]
    own_expert = device * local_experts + jnp.arange(local_experts, dtype=jnp.int32)
    expert_mask = jnp.any(names[:, :, :, None] == own_expert, axis=1).astype(full)
    expert_mask = jnp.pad(expert_mask, ((0, 0), (0, 0), (0, LANE - local_experts)))
    reduced, gated, gate_grad, up_grad, mixed_part = experts_fused(
        arrived, grad_early, grad_late, expert_mask, all_experts, expert_bias, w_gate, w_up, w_down
    )
    (
        query_raw_grad, key_raw_grad, value_raw_grad, grad_qk_gain, hidden_grad, attention_grad, extras,
    ) = backward(
        reduced, tokens, attention, cotangent, normed_two, all_experts, expert_bias, routed, ffn_gain[None],
        w_out, query_rot, keys_values, bias, stats, query_raw, key_raw, cosine, sine, qk_gain, experts_total,
    )
    small_part = local_width // ranks
    share = width // ranks
    gains = grad_qk_gain.reshape(2, ranks, small_part).transpose(1, 2, 0).astype(jnp.bfloat16)
    extras = extras.reshape(ranks, share, LANE) + jnp.pad(
        gains, ((0, 0), (0, share - small_part), (experts_total + 1, LANE - experts_total - 3))
    )
    normed_grad, sums, w_out_grad, gain_total, mixture, grad_w_gate, grad_w_up, grad_w_down = closing(
        normed, query_raw_grad, key_raw_grad, value_raw_grad, attended, attention_grad, extras, w_query, w_key, w_value,
        mixed_part, arrived, grad_early, grad_late, gated, gate_grad, up_grad, local_experts, experts_total + 3,
    )
    source = tokens.astype(full)
    hidden = source + attention.astype(full)
    scale_one = stats[:, 0:1]
    normed_grad = normed_grad.astype(full)
    output = (hidden + mixture.astype(full)).astype(jnp.bfloat16)
    weighted_one = attn_gain * normed_grad
    input_grad = (
        hidden_grad
        + scale_one * weighted_one
        - source * (scale_one**3 / width) * jnp.sum(weighted_one * source, axis=1, keepdims=True)
    )
    edge = 4 * local_width
    return (
        output,
        input_grad,
        sums[:, :local_width],
        sums[:, local_width : 2 * local_width],
        sums[:, 2 * local_width : 3 * local_width],
        w_out_grad,
        gain_total[0] / lax.dynamic_slice_in_dim(attn_gain, device * share, share),
        sums[:, edge + experts_total],
        sums[:small_part, edge + experts_total + 1 : edge + experts_total + 3].T,
        sums[:, edge : edge + experts_total],
        grad_w_gate.astype(full),
        grad_w_up.astype(full),
        grad_w_down.astype(full),
    )


def layout(rows, ranks, device, cont_group):
    span = ranks // 2
    prompt_len = PROMPT_DEV * span
    local = jnp.arange(rows, dtype=jnp.int32)
    is_prompt = local < PROMPT_DEV
    after = jnp.maximum(local - PROMPT_DEV, 0)
    slot_cont = after // CLEN
    cont_pick = jnp.sum(
        jnp.where(
            slot_cont[:, None] == jnp.arange(CONT_DEV, dtype=jnp.int32)[None, :], cont_group[None, :], 0
        ),
        axis=1,
    )
    group = jnp.where(is_prompt, device // span, cont_pick)
    position = jnp.where(is_prompt, device % span * PROMPT_DEV + local, prompt_len + after % CLEN)
    tag = jnp.where(is_prompt, -1, slot_cont)
    return group, position, tag


def attention_mask(group, position, tag, ranks):
    prompt_len = PROMPT_DEV * (ranks // 2)
    key_index = jnp.arange(ranks * PROMPT_DEV, dtype=jnp.int32)
    prompt_mask = (group[:, None] == (key_index // prompt_len)[None, :]) & (
        (key_index % prompt_len)[None, :] <= position[:, None]
    )
    own_mask = (tag[:, None] == tag[None, PROMPT_DEV:]) & (
        position[None, PROMPT_DEV:] <= position[:, None]
    )
    return jnp.concatenate([prompt_mask, own_mask], axis=1)


def solution(mesh):
    small = mesh.shape["expert"] == 8
    return jax.shard_map(
        compact if small else body,
        mesh=mesh,
        in_specs=(
            P("expert", None),
            P(None, "tensor"),
            P(None, "tensor"),
            P(None, "tensor"),
            P("tensor", None),
            P(),
            P(),
            P(None, "tensor"),
            P(),
            P("expert", None, "tensor"),
            P("expert", None, "tensor"),
            P("expert", "tensor", None),
            P("expert", None),
            P("expert"),
            P("expert", None),
        ),
        out_specs=(
            P("expert", None),
            P("expert", None),
            P("expert", "tensor"),
            P("expert", "tensor"),
            P("expert", "tensor"),
            P("tensor", "expert"),
            P("expert"),
            P("expert"),
            P(None, ("tensor", "expert")),
            P("expert", None),
            P("expert", None, "tensor"),
            P("expert", None, "tensor"),
            P("expert", "tensor", None),
        ),
        check_vma=False,
    )
```

```python
import functools

import jax
import jax.numpy as jnp
from jax import lax
from jax.experimental import pallas as pl
from jax.experimental.pallas import tpu as pltpu
from jax.sharding import PartitionSpec as P

HD = 128
PROMPT_DEV = 128
CLEN = 256
CONT_DEV = 1


epsilon = 1e-05
masked_value = -1e30


MESH = pl.DeviceIdType.MESH
STEP = 16
LANE = 128


def remote(source, target, sent, received, **where):
    return pltpu.make_async_remote_copy(
        src_ref=source,
        dst_ref=target,
        send_sem=sent,
        recv_sem=received,
        device_id=where,
        device_id_type=MESH,
    )


def greet(places):
    barrier = pltpu.get_barrier_semaphore()
    for condition, where in places:
        def signal(where=where):
            pl.semaphore_signal(barrier, inc=1, device_id=where, device_id_type=MESH)
        if condition is None:
            signal()
        else:
            pl.when(condition)(signal)
    count = 0
    for condition, _ in places:
        count = count + (1 if condition is None else jnp.where(condition, 1, 0))
    pl.semaphore_wait(barrier, count)


class Line:
    def __init__(self, own, arrived, spare, total, sems, step=STEP):
        self.step = step
        self.own, self.arrived, self.spare, self.total = own, arrived, spare, total
        self.up_sent, self.far_got, self.near_got, self.far_sent, self.near_sent, self.down_got = (
            sems.at[i] for i in range(6)
        )
        self.size = lax.axis_size("tensor")
        self.here = lax.axis_index("tensor")
        self.root = self.size // 2 - 1
        self.rise_steps = self.size - 1 - self.root
        self.trip = 2 * self.rise_steps
        self.half = own.shape[0] // 2
        self.pieces = self.half // step

    @staticmethod
    def semaphores(rows, step=STEP):
        return pltpu.SemaphoreType.DMA((6, 2, rows // 2 // step))

    @staticmethod
    def spare_shape(rows, width):
        return pltpu.VMEM((rows // 2, width), jnp.bfloat16)

    def neighbours(self):
        here, size = self.here, self.size
        return [
            (here > 0, {"tensor": jnp.maximum(here - 1, 0)}),
            (here < size - 1, {"tensor": jnp.minimum(here + 1, size - 1)}),
        ]

    def place(self, lane):
        return self.here if lane == 0 else self.size - 1 - self.here

    def device(self, lane, place):
        return place if lane == 0 else self.size - 1 - place

    def rows(self, lane, piece):
        return pl.ds(pl.multiple_of(lane * self.half + piece * self.step, self.step), self.step)

    def landing(self, piece):
        return pl.ds(pl.multiple_of(piece * self.step, self.step), self.step)

    def far_up(self, lane, piece):
        rows, place = self.rows(lane, piece), self.place(lane)
        inward = jnp.where(place > self.root, place - 1, place + 1)
        return remote(
            self.own.at[rows], self.arrived.at[rows],
            self.up_sent.at[lane, piece], self.far_got.at[lane, piece], tensor=self.device(lane, inward),
        )

    def near_up(self, lane, piece):
        return remote(
            self.own.at[self.rows(lane, piece)], self.spare.at[self.landing(piece)],
            self.up_sent.at[lane, piece], self.near_got.at[lane, piece], tensor=self.device(lane, self.root),
        )

    def down(self, lane, piece, away):
        rows = self.rows(lane, piece)
        sent = self.far_sent if away == 1 else self.near_sent
        return remote(
            self.total.at[rows], self.total.at[rows],
            sent.at[lane, piece], self.down_got.at[lane, piece], tensor=self.device(lane, self.place(lane) + away),
        )

    def rise(self, lane, piece):
        place, root = self.place(lane), self.root
        rows = self.rows(lane, piece)

        def value(field):
            return field.astype(jnp.float32)

        @pl.when((place > root) & (place < self.size - 1) | (place > 0) & (place < root))
        def _():
            self.far_up(lane, piece).wait_recv()
            self.own[rows] = (value(self.own[rows]) + value(self.arrived[rows])).astype(jnp.bfloat16)

        @pl.when(place == root)
        def _():
            self.far_up(lane, piece).wait_recv()
            summed = value(self.own[rows]) + value(self.arrived[rows])
            if root > 0:
                self.near_up(lane, piece).wait_recv()
                summed = summed + value(self.spare[self.landing(piece)])
            self.total[rows] = summed.astype(jnp.bfloat16)
            self.down(lane, piece, 1).start()
            if root > 0:
                self.down(lane, piece, -1).start()

        if root > 0:

            @pl.when(place == root - 1)
            def _():
                self.near_up(lane, piece).start()

        @pl.when((place > root) | (place < root - 1))
        def _():
            self.far_up(lane, piece).start()

    def fall(self, lane, piece):
        place, root = self.place(lane), self.root

        @pl.when(place != root)
        def _():
            self.down(lane, piece, 1).wait_recv()

        @pl.when((place > root) & (place < self.size - 1))
        def _():
            self.down(lane, piece, 1).start()

        @pl.when((place > 0) & (place < root))
        def _():
            self.down(lane, piece, -1).start()

    def advance(self, step):
        for lane in range(2):
            place = self.place(lane)
            steps_in = self.rise_steps - jnp.abs(place - self.root)
            piece = step - steps_in

            @pl.when((piece >= 0) & (piece < self.pieces))
            def _():
                self.rise(lane, piece)

        for lane in range(2):
            place = self.place(lane)
            piece = step - self.rise_steps - jnp.abs(place - self.root)

            @pl.when((piece >= 0) & (piece < self.pieces))
            def _():
                self.fall(lane, piece)

    def step_body(self, step, carry):
        self.advance(step)
        return carry

    def steps(self):
        return self.pieces + self.trip

    def finish(self):
        def one(piece, carry):
            for lane in range(2):
                place, root = self.place(lane), self.root

                @pl.when(place != root)
                def _():
                    self.far_up(lane, piece).wait_send()

                @pl.when((place >= root) & (place < self.size - 1))
                def _():
                    self.down(lane, piece, 1).wait_send()

                @pl.when((place <= root) & (place > 0))
                def _():
                    self.down(lane, piece, -1).wait_send()
            return carry

        lax.fori_loop(0, self.pieces, one, 0)


class Place:
    def __init__(self):
        here = lax.axis_index("expert")
        self.here = here
        self.core, self.x, self.y = here % 2, here // 2 % 2, here // 4
        self.sibling = here + 1 - 2 * self.core
        self.x_chip = here + 2 - 4 * self.x
        self.y_chip = here + 4 - 8 * self.y

    def neighbours(self):
        return [(None, {"expert": i}) for i in (self.sibling, self.x_chip, self.y_chip)]

    def block(self, chip, core):
        x = self.x + (1 - chip // 2) * (1 - 2 * self.x)
        y = self.y + (1 - chip % 2) * (1 - 2 * self.y)
        return 4 * y + 2 * x + core


class Plane(Place):
    def __init__(self, own, spare, paired, from_x, from_y, pair_sems, x_sems, y_sems, by_device=False, step=STEP):
        self.step = step
        self.by_device = by_device
        self.own, self.spare, self.paired, self.from_x, self.from_y = own, spare, paired, from_x, from_y
        self.pair_sems, self.x_sems, self.y_sems = pair_sems, x_sems, y_sems
        super().__init__()
        self.half = own.shape[1] // 2
        self.pieces = self.half // step

    @staticmethod
    def semaphores(rows, step=STEP):
        pieces = rows // 2 // step
        return [
            pltpu.SemaphoreType.DMA((2, 4)),
            pltpu.SemaphoreType.DMA((2, 3, pieces)),
            pltpu.SemaphoreType.DMA((2, 3, pieces)),
        ]

    def pair_copy(self, chip):
        place = self.block(chip, 1 - self.core) if self.by_device else chip
        return remote(
            self.spare.at[place], self.paired.at[chip],
            self.pair_sems.at[0, chip], self.pair_sems.at[1, chip], expert=self.sibling,
        )

    def rows(self, side, piece):
        return pl.ds(pl.multiple_of(side * self.half + piece * self.step, self.step), self.step)

    def landing(self, piece):
        return pl.ds(pl.multiple_of(piece * self.step, self.step), self.step)

    def x_copy(self, kind, piece):
        chip, side = ((0, 0), (1, 0), (1, 1))[kind]
        return remote(
            self.own.at[chip, self.rows(side, piece)], self.from_x.at[kind, self.landing(piece)],
            self.x_sems.at[0, kind, piece], self.x_sems.at[1, kind, piece], expert=self.x_chip,
        )

    def y_copy(self, kind, piece):
        chip, side = ((0, 1), (2, 1), (2, 0))[kind]
        return remote(
            self.own.at[chip, self.rows(side, piece)], self.from_y.at[kind, self.landing(piece)],
            self.y_sems.at[0, kind, piece], self.y_sems.at[1, kind, piece], expert=self.y_chip,
        )

    def add_pair(self, chip, side, piece):
        rows = self.rows(side, piece)
        self.own[chip, rows] = (
            self.own[chip, rows].astype(jnp.float32) + self.paired[chip, rows].astype(jnp.float32)
        ).astype(jnp.bfloat16)

    def each(self, step):
        def one(piece, carry):
            step(piece)
            return carry

        lax.fori_loop(0, self.pieces, one, 0)

    def send_first(self, chip):
        def step(piece):
            if chip in (0, 1):
                self.add_pair(chip, 0, piece)
                self.x_copy(chip, piece).start()
            if chip in (0, 2):
                self.add_pair(chip, 1, piece)
                self.y_copy(chip // 2, piece).start()

        self.each(step)

    def first_piece(self, piece):
        for chip, side in ((0, 0), (0, 1), (1, 0), (2, 1)):
            self.add_pair(chip, side, piece)
        for kind in range(2):
            self.x_copy(kind, piece).start()
            self.y_copy(kind, piece).start()

    def second_piece(self, piece):
        landed = self.landing(piece)
        self.y_copy(0, piece).wait_recv()
        rows = self.rows(1, piece)
        self.own[1, rows] = (
            self.own[1, rows].astype(jnp.float32)
            + self.paired[1, rows].astype(jnp.float32)
            + self.from_y[0, landed].astype(jnp.float32)
        ).astype(jnp.bfloat16)
        self.x_copy(2, piece).start()
        self.x_copy(0, piece).wait_recv()
        rows = self.rows(0, piece)
        self.own[2, rows] = (
            self.own[2, rows].astype(jnp.float32)
            + self.paired[2, rows].astype(jnp.float32)
            + self.from_x[0, landed].astype(jnp.float32)
        ).astype(jnp.bfloat16)
        self.y_copy(2, piece).start()

    def send_second(self):
        self.each(self.second_piece)

    def last_sum(self, piece):
        landed = self.landing(piece)
        sums = []
        for side in range(2):
            first, second = (self.x_copy(1, piece), self.y_copy(2, piece)) if side == 0 else (self.y_copy(1, piece), self.x_copy(2, piece))
            first.wait_recv()
            second.wait_recv()
            a, b = (self.from_x[1, landed], self.from_y[2, landed]) if side == 0 else (self.from_y[1, landed], self.from_x[2, landed])
            rows = self.rows(side, piece)
            sums.append(
                self.own[3, rows].astype(jnp.float32)
                + self.paired[3, rows].astype(jnp.float32)
                + a.astype(jnp.float32)
                + b.astype(jnp.float32)
            )
        return sums

    def finish(self):
        for chip in range(4):
            self.pair_copy(chip).wait_send()

        def step(piece):
            for kind in range(3):
                self.x_copy(kind, piece).wait_send()
                self.y_copy(kind, piece).wait_send()

        self.each(step)


class Gather:
    def __init__(self, source, target, place, x_sems, y_sems, far_sems, pair_sems, own_sem, pieces):
        self.source, self.target = source, target
        self.place = place
        self.x_sems, self.y_sems, self.far_sems, self.pair_sems, self.own_sem = x_sems, y_sems, far_sems, pair_sems, own_sem
        self.pieces = pieces
        self.rows_each = source.shape[0] // pieces

    @staticmethod
    def semaphores(pieces):
        return [
            pltpu.SemaphoreType.DMA((2, pieces)),
            pltpu.SemaphoreType.DMA((2, pieces)),
            pltpu.SemaphoreType.DMA((2, pieces)),
            pltpu.SemaphoreType.DMA((2, 4, pieces)),
            pltpu.SemaphoreType.DMA,
        ]

    def rows(self, piece):
        return pl.ds(piece * self.rows_each, self.rows_each)

    def own_copy(self):
        return pltpu.make_async_copy(self.source, self.target.at[self.place.here], self.own_sem)

    def x_copy(self, piece):
        rows = self.rows(piece)
        return remote(
            self.source.at[rows], self.target.at[self.place.here, rows],
            self.x_sems.at[0, piece], self.x_sems.at[1, piece], expert=self.place.x_chip,
        )

    def y_copy(self, piece):
        rows = self.rows(piece)
        return remote(
            self.source.at[rows], self.target.at[self.place.here, rows],
            self.y_sems.at[0, piece], self.y_sems.at[1, piece], expert=self.place.y_chip,
        )

    def far_copy(self, piece):
        rows = self.rows(piece)
        came, goes = (
            (self.place.x_chip, self.place.y_chip) if piece % 2 == 0 else (self.place.y_chip, self.place.x_chip)
        )
        return remote(
            self.target.at[came, rows], self.target.at[came, rows],
            self.far_sems.at[0, piece], self.far_sems.at[1, piece], expert=goes,
        )

    def pair_copy(self, kind, piece):
        rows = self.rows(piece)
        block = self.place.block(kind, self.place.core)
        source = self.source.at[rows] if kind == 3 else self.target.at[block, rows]
        return remote(
            source, self.target.at[block, rows],
            self.pair_sems.at[0, kind, piece], self.pair_sems.at[1, kind, piece], expert=self.place.sibling,
        )

    def start_piece(self, piece):
        self.x_copy(piece).start()
        self.y_copy(piece).start()
        self.pair_copy(3, piece).start()

    def start(self):
        self.own_copy().start()
        for piece in range(self.pieces):
            self.start_piece(piece)

    def near(self, piece):
        self.x_copy(piece).wait_recv()
        if piece % 2 == 0:
            self.far_copy(piece).start()
        self.pair_copy(1, piece).start()
        self.y_copy(piece).wait_recv()
        if piece % 2 == 1:
            self.far_copy(piece).start()
        self.pair_copy(2, piece).start()

    def far(self, piece):
        self.far_copy(piece).wait_recv()
        self.pair_copy(0, piece).start()

    def paired(self, kind, piece):
        self.pair_copy(kind, piece).wait_recv()

    def finish(self):
        for piece in range(self.pieces):
            self.x_copy(piece).wait_send()
            self.y_copy(piece).wait_send()
            self.far_copy(piece).wait_send()
            for kind in range(4):
                self.pair_copy(kind, piece).wait_send()


def wide_dot(left, right):
    return jnp.dot(left, right, preferred_element_type=jnp.float32)


def turned_dot(left, right):
    return lax.dot_general(left, right, (((1,), (1,)), ((), ())), preferred_element_type=jnp.float32)


BLOCK_STEP = 32


def expert_kernel(
    x_all, g_all, mask, router, bias, w_gate, w_up, w_down,
    reduced, gated_all, gate_all, up_all, mixed_all,
    x_buf, g_buf, part, paired, from_x, from_y, line_in, line_spare, small, mixed,
    in_sems, out_sems, pair_sems, x_sems, y_sems, line_sems,
):
    experts, width, hidden = w_gate.shape
    rows = x_buf.shape[1]
    tile = min(512, width)
    plane = Plane(part.at[1], part.at[0], paired, from_x, from_y, pair_sems, x_sems, y_sems, step=BLOCK_STEP)
    line = Line(part.at[1, 3], line_in, line_spare, reduced, line_sems, step=BLOCK_STEP)
    first_expert = lax.axis_index("expert") * experts
    outs = (gated_all, gate_all, up_all)

    def block_of(i):
        return plane.block(i // 2, (plane.core + 1 - i % 2) % 2)

    def fetch(i):
        slot, block = i % 2, block_of(i)
        return (
            pltpu.make_async_copy(x_all.at[block], x_buf.at[slot], in_sems.at[0, slot]),
            pltpu.make_async_copy(g_all.at[block], g_buf.at[slot], in_sems.at[1, slot]),
        )

    def store(i):
        slot, block = i % 2, block_of(i)
        return [
            pltpu.make_async_copy(small.at[slot, n], outs[n].at[block], out_sems.at[n, slot])
            for n in range(3)
        ] + [pltpu.make_async_copy(mixed.at[slot], mixed_all.at[block], out_sems.at[3, slot])]

    def compute(i):
        slot = i % 2
        block = block_of(i)
        x = x_buf.at[slot]
        g = g_buf.at[slot]
        logits = wide_dot(x[...], router[...]) + bias[...]
        weights = jnp.exp(logits - jnp.max(logits, axis=1, keepdims=True))
        gates = weights / jnp.sum(weights, axis=1, keepdims=True)
        named = mask[block]
        column = lax.broadcasted_iota(jnp.int32, (rows, LANE), 1)
        extra = jnp.zeros((rows, LANE), jnp.float32)
        for j in range(experts):
            gate_pre = wide_dot(x[...], w_gate[j])
            up_pre = wide_dot(x[...], w_up[j])
            raw = turned_dot(g[...], w_down[j])
            gate = jnp.sum(jnp.where(column == first_expert + j, gates, 0.0), axis=1, keepdims=True)
            gate = gate * named[:, j : j + 1]
            sigma = jax.nn.sigmoid(gate_pre)
            activated = gate_pre * sigma
            inner = activated * up_pre
            act = gate * raw
            span = slice(j * hidden, (j + 1) * hidden)
            small[slot, 0, :, span] = (gate * inner).astype(jnp.bfloat16)
            small[slot, 1, :, span] = (
                act * up_pre * sigma * (1.0 + gate_pre * (1.0 - sigma))
            ).astype(jnp.bfloat16)
            small[slot, 2, :, span] = (act * activated).astype(jnp.bfloat16)
            gain = jnp.sum(raw * inner, axis=1, keepdims=True)
            extra = jnp.where(column == first_expert + j, gain, extra)
        for start in range(0, width, tile):
            columns = slice(start, start + tile)
            slot_grad = None
            mix = None
            for j in range(experts):
                span = slice(j * hidden, (j + 1) * hidden)
                term = turned_dot(small[slot, 1, :, span], w_gate[j, columns]) + turned_dot(
                    small[slot, 2, :, span], w_up[j, columns]
                )
                more = wide_dot(small[slot, 0, :, span], w_down[j, :, columns])
                slot_grad = term if slot_grad is None else slot_grad + term
                mix = more if mix is None else mix + more
            part[i % 2, i // 2, :, columns] = slot_grad.astype(jnp.bfloat16)
            mixed[slot, :, columns] = mix.astype(jnp.bfloat16)
        part[i % 2, i // 2, :, width:] = extra.astype(jnp.bfloat16)

    for copy in fetch(0):
        copy.start()
    greet(plane.neighbours() + line.neighbours())

    def step(i, carry):
        @pl.when(i < 7)
        def _():
            for copy in fetch(i + 1):
                copy.start()

        for copy in fetch(i):
            copy.wait()

        @pl.when(i >= 2)
        def _():
            for copy in store(i - 2):
                copy.wait()

        compute(i)
        for copy in store(i):
            copy.start()

        @pl.when(i % 2 == 0)
        def _():
            plane.pair_copy(i // 2).start()

        @pl.when(i % 2 == 1)
        def _():
            plane.pair_copy(i // 2).wait_recv()

        for chip in range(3):

            @pl.when(i == 2 * chip + 1)
            def _():
                plane.send_first(chip)
                if chip == 2:
                    plane.send_second()

        return carry

    lax.fori_loop(0, 8, step, 0)

    def last(step, carry):
        @pl.when(step < plane.pieces)
        def _():
            for side, total in enumerate(plane.last_sum(step)):
                plane.own[3, plane.rows(side, step)] = total.astype(jnp.bfloat16)

        line.advance(step)
        return carry

    lax.fori_loop(0, line.steps(), last, 0)
    for i in (6, 7):
        for copy in store(i):
            copy.wait()
    plane.finish()
    line.finish()


def experts_fused(arrived, arrived_grad, mask, router, bias, w_gate, w_up, w_down):
    ranks, rows, width = arrived.shape
    experts, _, hidden = w_gate.shape
    wide = width + LANE
    inner = experts * hidden
    half = rows // 2
    low = jnp.bfloat16
    any_space = pl.BlockSpec(memory_space=pl.ANY)
    vmem = pl.BlockSpec(memory_space=pltpu.VMEM)
    small_shape = jax.ShapeDtypeStruct((ranks, rows, inner), low)
    return pl.pallas_call(
        expert_kernel,
        out_shape=(
            jax.ShapeDtypeStruct((rows, wide), low), small_shape, small_shape, small_shape,
            jax.ShapeDtypeStruct((ranks, rows, width), low),
        ),
        in_specs=[any_space, any_space] + [vmem] * 6,
        out_specs=(vmem, any_space, any_space, any_space, any_space),
        scratch_shapes=[
            pltpu.VMEM((2, rows, width), low),
            pltpu.VMEM((2, rows, width), low),
            pltpu.VMEM((2, 4, rows, wide), low),
            pltpu.VMEM((4, rows, wide), low),
            pltpu.VMEM((3, half, wide), low),
            pltpu.VMEM((3, half, wide), low),
            pltpu.VMEM((rows, wide), low),
            Line.spare_shape(rows, wide),
            pltpu.VMEM((2, 3, rows, inner), low),
            pltpu.VMEM((2, rows, width), low),
            pltpu.SemaphoreType.DMA((2, 2)),
            pltpu.SemaphoreType.DMA((4, 2)),
            *Plane.semaphores(rows, step=BLOCK_STEP),
            Line.semaphores(rows, step=BLOCK_STEP),
        ],
        compiler_params=pltpu.CompilerParams(
            collective_id=0, has_side_effects=True, vmem_limit_bytes=61 * 2**20
        ),
        cost_estimate=pl.CostEstimate(
            flops=12 * ranks * rows * width * inner, bytes_accessed=8 * ranks * rows * width, transcendentals=0
        ),
    )(arrived, arrived_grad, mask, router, bias, w_gate, w_up, w_down)


def crossed_dot(left, right):
    return lax.dot_general(left, right, (((0,), (0,)), ((), ())), preferred_element_type=jnp.float32)


def closing_kernel(
    normed, query_grad, key_grad, value_grad, attended, attention_grad, extras,
    w_query, w_key, w_value, mixed, x_all, g_all, gated_all, gate_all, up_all,
    total, sums, turned, gain, mixture, gate_out, up_out, down_out,
    line_own, line_in, line_spare, part, paired, from_x, from_y,
    mix_own, mix_paired, mix_x, mix_y, mix_in, mix_spare, tiles, factors, results, downs,
    line_sems, pair_sems, x_sems, y_sems, mix_line_sems, mix_pair_sems, mix_x_sems, mix_y_sems,
    load_sems, weight_sems, factor_sems, tile_sems, out_sems,
    gains, mine, theirs, peer_sent, peer_got,
    *,
    gain_column,
):
    width = normed.shape[1]
    heads = query_grad.shape[1]
    share = part.shape[2]
    experts, _, hidden = gate_out.shape
    column_tile = min(512, width // 2)
    tile = tiles.shape[2]
    count = width // tile
    line = Line(line_own, line_in, line_spare, total, line_sems)
    plane = Plane(part.at[1], part.at[0], paired, from_x, from_y, pair_sems, x_sems, y_sems)
    mix = Plane(mix_own, mixed, mix_paired, mix_x, mix_y, mix_pair_sems, mix_x_sems, mix_y_sems, by_device=True)
    mix_line = Line(mix_own.at[3], mix_in, mix_spare, mixture, mix_line_sems)
    peers = Peers(mine, theirs, peer_sent, peer_got)
    half = width // 2

    def load_own(chip):
        return pltpu.make_async_copy(mixed.at[mix.block(chip, mix.core)], mix_own.at[chip], load_sems.at[chip])

    weight_loads = [
        pltpu.make_async_copy(w_query, factors.at[0, 0:width], weight_sems.at[0]),
        pltpu.make_async_copy(w_key, factors.at[1, 0:width], weight_sems.at[1]),
        pltpu.make_async_copy(w_value.at[0:half], factors.at[0, width : width + half], weight_sems.at[2]),
        pltpu.make_async_copy(w_value.at[half:], factors.at[1, width : width + half], weight_sems.at[3]),
    ]

    def factor_load(matrix):
        return pltpu.make_async_copy(
            (gate_all, up_all, gated_all)[matrix], factors.at[matrix % 2], factor_sems.at[matrix]
        )

    def tile_copy(source, s):
        columns = pl.ds(pl.multiple_of(s % count * tile, tile), tile)
        return pltpu.make_async_copy(source.at[:, columns], tiles.at[s % 2], tile_sems.at[s % 2])

    def start_tile(s):
        @pl.when(s < 2 * count)
        def _():
            tile_copy(x_all, s).start()

        @pl.when(s >= 2 * count)
        def _():
            tile_copy(g_all, s).start()

    def across(target, s):
        rows = pl.ds(pl.multiple_of(s % count * tile, tile), tile)
        return [
            pltpu.make_async_copy(
                results.at[s % 2, :, j * hidden : (j + 1) * hidden], target.at[j, rows], out_sems.at[0, s % 2, j]
            )
            for j in range(experts)
        ]

    def down(s):
        columns = pl.ds(pl.multiple_of(s % count * tile, tile), tile)
        return [
            pltpu.make_async_copy(
                downs.at[s % 2, j * hidden : (j + 1) * hidden], down_out.at[j, :, columns], out_sems.at[1, s % 2, j]
            )
            for j in range(experts)
        ]

    def expert_tile(s):
        @pl.when(s + 1 < 3 * count)
        def _():
            start_tile(s + 1)

        for matrix in range(3):

            @pl.when(s == matrix * count)
            def _():
                factor_load(matrix).wait()

        tile_copy(x_all, s).wait()

        @pl.when(s < 2 * count)
        def _():
            @pl.when(s >= 2)
            def _():
                for copy in across(gate_out, s):
                    copy.wait()

            results[s % 2] = crossed_dot(tiles[s % 2], factors[s // count]).astype(jnp.bfloat16)

            @pl.when(s < count)
            def _():
                for copy in across(gate_out, s):
                    copy.start()

            @pl.when(s >= count)
            def _():
                for copy in across(up_out, s):
                    copy.start()

        @pl.when(s >= 2 * count)
        def _():
            @pl.when(s >= 2 * count + 2)
            def _():
                for copy in down(s):
                    copy.wait()

            downs[s % 2] = crossed_dot(factors[0], tiles[s % 2]).astype(jnp.bfloat16)
            for copy in down(s):
                copy.start()

        @pl.when(s == count - 1)
        def _():
            factor_load(2).start()

    def dense_block(i):
        chip, sub = i // 2, i % 2
        block = plane.block(chip, (plane.core + 1 - sub) % 2)
        columns = pl.ds(pl.multiple_of(block * share, share), share)
        source = normed[:, columns]
        part[sub, chip, :, 0:heads] = crossed_dot(source, query_grad[...]).astype(jnp.bfloat16)
        part[sub, chip, :, heads : 2 * heads] = crossed_dot(source, key_grad[...]).astype(jnp.bfloat16)
        part[sub, chip, :, 2 * heads : 3 * heads] = crossed_dot(source, value_grad[...]).astype(jnp.bfloat16)
        part[sub, chip, :, 3 * heads : 4 * heads] = crossed_dot(
            attention_grad[:, columns], attended[...]
        ).astype(jnp.bfloat16)
        part[sub, chip, :, 4 * heads :] = extras[block] + gains[columns]

        @pl.when(sub == 0)
        def _():
            plane.pair_copy(chip).start()

    for copy in weight_loads:
        copy.start()
    for chip in range(4):
        load_own(chip).start()
    greet(plane.neighbours() + peers.neighbours())
    for chip in range(4):
        mix.pair_copy(chip).start()
    for copy in weight_loads:
        copy.wait()
    for start in range(0, width, column_tile):
        columns = slice(start, start + column_tile)
        later = width + start % half
        line_own[:, columns] = (
            turned_dot(query_grad[...], factors[0, columns])
            + turned_dot(key_grad[...], factors[1, columns])
            + turned_dot(value_grad[...], factors[start // half, later : later + column_tile])
        ).astype(jnp.bfloat16)
    place = lax.broadcasted_iota(jnp.int32, (normed.shape[0], LANE), 1)
    chosen = jnp.where(place == gain_column, 1.0, 0.0).astype(jnp.bfloat16)
    for start in range(0, width, column_tile):
        columns = slice(start, start + column_tile)
        pull = line_own[:, columns].astype(jnp.float32) * normed[:, columns].astype(jnp.float32)
        gains[columns] = crossed_dot(pull.astype(jnp.bfloat16), chosen).astype(jnp.bfloat16)
    factor_load(0).start()
    factor_load(1).start()
    start_tile(0)
    mix_second, mix_last, dense_first, dense_second, dense_last = PLAN

    def step(s, carry):
        line.advance(s)

        @pl.when(s == 0)
        def _():
            for chip in range(3):
                load_own(chip).wait()
                mix.pair_copy(chip).wait_recv()
            for piece in range(AHEAD):
                mix.first_piece(piece)

        @pl.when(s == mix_last - 1)
        def _():
            load_own(3).wait()
            mix.pair_copy(3).wait_recv()

        @pl.when((s > 0) & (s + AHEAD - 1 < mix.pieces))
        def _():
            mix.first_piece(s + AHEAD - 1)

        @pl.when((s >= mix_second) & (s - mix_second < mix.pieces))
        def _():
            mix.second_piece(s - mix_second)

        @pl.when((s >= mix_last) & (s - mix_last < mix.pieces))
        def _():
            piece = s - mix_last
            for side, summed in enumerate(mix.last_sum(piece)):
                mix_own[3, mix.rows(side, piece)] = summed.astype(jnp.bfloat16)

        mix_line.advance(s - mix_last)

        @pl.when((s >= 4) & (s < 12))
        def _():
            dense_block(s - 4)

        @pl.when(s == dense_first)
        def _():
            for chip in range(4):
                plane.pair_copy(chip).wait_recv()
            for chip in range(3):
                plane.send_first(chip)

        @pl.when((s >= dense_second) & (s - dense_second < plane.pieces))
        def _():
            plane.second_piece(s - dense_second)

        @pl.when((s >= dense_last) & (s - dense_last < plane.pieces))
        def _():
            piece = s - dense_last
            for side, summed in enumerate(plane.last_sum(piece)):
                sums[plane.rows(side, piece)] = summed

        @pl.when(s < 3 * count)
        def _():
            expert_tile(s)

        return carry

    steps = jnp.maximum(mix_last + mix_line.steps(), jnp.maximum(3 * count, dense_last + plane.pieces))
    lax.fori_loop(0, steps, step, 0)
    column = 4 * heads + gain_column
    mine[...] = to_rows([sums[:, column : column + 1]], share)
    peers.start()
    turned[...] = sums[:, 3 * heads : 4 * heads].T
    for s in (2 * count - 2, 2 * count - 1):
        for copy in across(up_out, s):
            copy.wait()
    for s in (3 * count - 2, 3 * count - 1):
        for copy in down(s):
            copy.wait()
    gain[...] = peers.total()
    for each in (plane, line, mix, mix_line, peers):
        each.finish()


PLAN = (1, 3, 12, 15, 18)
AHEAD = 2
TILE = 256


def closing(
    normed, query_grad, key_grad, value_grad, attended, attention_grad, extras, w_query, w_key, w_value,
    mixed, arrived, arrived_grad, gated, gate_grad, up_grad, experts, gain_column,
):
    rows, width = normed.shape
    heads = query_grad.shape[1]
    ranks, share, more = extras.shape
    wide = 4 * heads + more
    inner = gated.shape[2]
    hidden = inner // experts
    low = jnp.bfloat16
    tile = min(TILE, width // 2)
    vmem = pl.BlockSpec(memory_space=pltpu.VMEM)
    any_space = pl.BlockSpec(memory_space=pl.ANY)
    every = ranks * rows
    size = lax.axis_size("tensor")
    return pl.pallas_call(
        functools.partial(closing_kernel, gain_column=gain_column),
        out_shape=(
            jax.ShapeDtypeStruct((rows, width), low),
            jax.ShapeDtypeStruct((share, wide), jnp.float32),
            jax.ShapeDtypeStruct((heads, share), jnp.float32),
            jax.ShapeDtypeStruct((8, share), jnp.float32),
            jax.ShapeDtypeStruct((rows, width), low),
            jax.ShapeDtypeStruct((experts, width, hidden), low),
            jax.ShapeDtypeStruct((experts, width, hidden), low),
            jax.ShapeDtypeStruct((experts, hidden, width), low),
        ),
        in_specs=[vmem] * 7 + [any_space] * 9,
        out_specs=(vmem,) * 5 + (any_space,) * 3,
        scratch_shapes=[
            pltpu.VMEM((rows, width), low),
            pltpu.VMEM((rows, width), low),
            Line.spare_shape(rows, width),
            pltpu.VMEM((2, 4, share, wide), low),
            pltpu.VMEM((4, share, wide), low),
            pltpu.VMEM((3, share // 2, wide), low),
            pltpu.VMEM((3, share // 2, wide), low),
            pltpu.VMEM((4, rows, width), low),
            pltpu.VMEM((4, rows, width), low),
            pltpu.VMEM((3, rows // 2, width), low),
            pltpu.VMEM((3, rows // 2, width), low),
            pltpu.VMEM((rows, width), low),
            Line.spare_shape(rows, width),
            pltpu.VMEM((2, every, tile), low),
            pltpu.VMEM((2, every, inner), low),
            pltpu.VMEM((2, tile, inner), low),
            pltpu.VMEM((2, inner, tile), low),
            Line.semaphores(rows),
            *Plane.semaphores(share),
            Line.semaphores(rows),
            *Plane.semaphores(rows),
            pltpu.SemaphoreType.DMA((4,)),
            pltpu.SemaphoreType.DMA((4,)),
            pltpu.SemaphoreType.DMA((3,)),
            pltpu.SemaphoreType.DMA((2,)),
            pltpu.SemaphoreType.DMA((2, 2, experts)),
            pltpu.VMEM((width, LANE), low),
            pltpu.VMEM((8, share), jnp.float32),
            pltpu.VMEM((size - 1, 8, share), jnp.float32),
            pltpu.SemaphoreType.DMA((size - 1,)),
            pltpu.SemaphoreType.DMA((size - 1,)),
        ],
        compiler_params=pltpu.CompilerParams(
            collective_id=2, has_side_effects=True, vmem_limit_bytes=63 * 2**20
        ),
    )(
        normed, query_grad, key_grad, value_grad, attended, attention_grad, extras, w_query, w_key, w_value,
        mixed, arrived.reshape(every, width), arrived_grad.reshape(every, width),
        gated.reshape(every, inner), gate_grad.reshape(every, inner), up_grad.reshape(every, inner),
    )


class Peers:
    def __init__(self, mine, theirs, sent, got):
        self.mine, self.theirs, self.sent, self.got = mine, theirs, sent, got
        self.size = lax.axis_size("tensor")
        self.here = lax.axis_index("tensor")

    def neighbours(self):
        return [(None, {"tensor": (self.here + d) % self.size}) for d in range(1, self.size)]

    def copies(self):
        return [
            remote(
                self.mine, self.theirs.at[d - 1], self.sent.at[d - 1], self.got.at[d - 1],
                tensor=(self.here + d) % self.size,
            )
            for d in range(1, self.size)
        ]

    def start(self):
        for copy in self.copies():
            copy.start()

    def total(self):
        result = self.mine[...]
        for d, copy in enumerate(self.copies()):
            copy.wait_recv()
            result = result + self.theirs[d]
        return result

    def finish(self):
        for copy in self.copies():
            copy.wait_send()


def to_rows(columns, rows):
    lane = lax.broadcasted_iota(jnp.int32, (rows, LANE), 1)
    field = jnp.zeros((rows, LANE), jnp.float32)
    for i, column in enumerate(columns):
        field = jnp.where(lane == i, column, field)
    return field.T[:8]


def to_columns(sums):
    padded = jnp.concatenate([sums, jnp.zeros((LANE - 8, sums.shape[1]), jnp.float32)], axis=0)
    return padded.T


def swapped(field):
    half = HD // 2
    return jnp.concatenate([field[:, half:], field[:, :half]], axis=1)


def loads(pairs, sems):
    copies = [pltpu.make_async_copy(source, target, sems.at[i]) for i, (source, target) in enumerate(pairs)]
    for copy in copies:
        copy.start()
    return copies


SPREAD = 32
SPREAD_LAG = 2


def front_kernel(
    tokens, attn_gain, ffn_gain, w_query, key_far, value_far, out_far, qk_gain, cosine, sine, bias_far, routes,
    total, normed, normed_two, attended, query_rot, keys_values, query_raw, key_raw, stats, routes_all, arrived,
    line_own, line_in, line_spare, prompt, mine, theirs, two, w_key, w_value, w_out, bias,
    load_sems, line_sems, peer_sent, peer_got, *gather_sems,
):
    rows, width = tokens.shape
    local = w_query.shape[1]
    heads = local // HD
    factor = HD ** (-0.5)
    own_blocks = rows // PROMPT_DEV - 1
    devices = keys_values.shape[0] - own_blocks
    place = Place()
    line = Line(line_own, line_in, line_spare, total, line_sems)
    peers = Peers(mine, theirs, peer_sent, peer_got)
    names = Gather(routes, routes_all, place, *gather_sems[0:5], pieces=2)
    prompts = Gather(prompt, keys_values, place, *gather_sems[5:10], pieces=2)
    spread = Gather(normed_two, arrived, place, *gather_sems[10:15], pieces=rows // SPREAD)
    load_key, load_value, load_out, load_bias = loads(
        ((key_far, w_key), (value_far, w_value), (out_far, w_out), (bias_far, bias)), load_sems
    )
    greet(place.neighbours() + peers.neighbours())
    names.start()
    source = tokens[...].astype(jnp.float32)
    scale_one = lax.rsqrt(jnp.sum(source * source, axis=1, keepdims=True) / width + epsilon)
    normed[...] = (source * scale_one * attn_gain[...]).astype(jnp.bfloat16)
    query_raw[...] = wide_dot(normed[...], w_query[...])
    load_key.wait()
    key_raw[...] = wide_dot(normed[...], w_key[...])
    mine[...] = to_rows(
        [
            jnp.sum(query_raw[...] * query_raw[...], axis=1, keepdims=True),
            jnp.sum(key_raw[...] * key_raw[...], axis=1, keepdims=True),
        ],
        rows,
    )
    peers.start()
    load_value.wait()
    value = wide_dot(normed[...], w_value[...]).astype(jnp.bfloat16)
    prompt[:, local:] = value[:PROMPT_DEV]
    for i in range(own_blocks):
        keys_values[devices + i, :, local:] = value[(i + 1) * PROMPT_DEV : (i + 2) * PROMPT_DEV]
    squares = to_columns(peers.total())
    scale_query = lax.rsqrt(squares[:, 0:1] / width + epsilon)
    scale_key = lax.rsqrt(squares[:, 1:2] / width + epsilon)
    for head in range(heads):
        columns = slice(head * HD, (head + 1) * HD)
        turned = key_raw[:, columns] * scale_key * qk_gain[1:2, columns]
        turned = (turned * cosine[...] + swapped(turned) * sine[...]).astype(jnp.bfloat16)
        prompt[:, columns] = turned[:PROMPT_DEV]
        for i in range(own_blocks):
            keys_values[devices + i, :, columns] = turned[(i + 1) * PROMPT_DEV : (i + 2) * PROMPT_DEV]
    prompts.own_copy().start()
    for piece in range(2):
        prompts.start_piece(piece)
    for head in range(heads):
        columns = slice(head * HD, (head + 1) * HD)
        turned = query_raw[:, columns] * scale_query * qk_gain[0:1, columns]
        turned = turned * cosine[...] + swapped(turned) * sine[...]
        query_rot[:, columns] = turned.astype(jnp.bfloat16)
    for piece in range(2):
        prompts.near(piece)
    for piece in range(2):
        names.near(piece)
    for piece in range(2):
        prompts.far(piece)
        names.far(piece)
    prompts.own_copy().wait()
    for kind in range(4):
        for piece in range(2):
            prompts.paired(kind, piece)
            names.paired(kind, piece)
    load_bias.wait()
    load_out.wait()
    lane = lax.broadcasted_iota(jnp.int32, (rows, LANE), 1)
    kept = jnp.where(lane == 0, scale_one, 0.0)
    kept = jnp.where(lane == 1, scale_query, kept)
    kept = jnp.where(lane == 2, scale_key, kept)
    count = keys_values.shape[0] * PROMPT_DEV
    for head in range(heads):
        columns = slice(head * HD, (head + 1) * HD)
        keys = keys_values[:, :, columns].reshape(count, HD)
        values = keys_values[:, :, local + head * HD : local + (head + 1) * HD].reshape(count, HD)
        scores = turned_dot(query_rot[:, columns], keys) * factor + bias[...]
        top = jnp.max(scores, axis=1, keepdims=True)
        weights = jnp.exp(scores - top)
        whole = jnp.sum(weights, axis=1, keepdims=True)
        shares = (weights / whole).astype(jnp.bfloat16)
        attended[:, columns] = wide_dot(shares, values).astype(jnp.bfloat16)
        kept = jnp.where(lane == 8 + head, top + jnp.log(whole), kept)
    tile = min(512, width)
    for start in range(0, width, tile):
        columns = slice(start, start + tile)
        line_own[:, columns] = wide_dot(attended[...], w_out[:, columns]).astype(jnp.bfloat16)
    ratio = SPREAD // STEP
    groups = line.pieces // ratio

    def norm_rows(piece):
        span = slice(piece * SPREAD, (piece + 1) * SPREAD)
        hidden = tokens[span].astype(jnp.float32) + total[span].astype(jnp.float32)
        scale = lax.rsqrt(jnp.sum(hidden * hidden, axis=1, keepdims=True) / width + epsilon)
        normed_two[span] = (hidden * scale * ffn_gain[...]).astype(jnp.bfloat16)
        two[span] = jnp.broadcast_to(scale, (SPREAD, LANE))

    done = 0
    passed = 0
    for group in range(groups):
        ready = line.trip + (group + 1) * ratio
        lax.fori_loop(done, ready, line.step_body, 0)
        done = ready
        for piece in (group, groups + group):
            norm_rows(piece)
            spread.start_piece(piece)
        if group >= SPREAD_LAG:
            for piece in (passed, groups + passed):
                spread.near(piece)
            passed += 1
    spread.own_copy().start()
    for group in range(passed, groups):
        for piece in (group, groups + group):
            spread.near(piece)
    for group in range(groups):
        for piece in (group, groups + group):
            spread.far(piece)
    stats[...] = jnp.where(lane == 3, two[...], kept)
    for kind in range(4):
        for piece in range(spread.pieces):
            spread.paired(kind, piece)
    spread.own_copy().wait()
    names.own_copy().wait()
    for each in (names, prompts, spread, line, peers):
        each.finish()


def front(tokens, attn_gain, ffn_gain, w_query, w_key, w_value, w_out, qk_gain, cosine, sine, bias, routes):
    rows, width = tokens.shape
    local = w_query.shape[1]
    ranks = lax.axis_size("expert")
    size = lax.axis_size("tensor")
    low, full = jnp.bfloat16, jnp.float32
    vmem = pl.BlockSpec(memory_space=pltpu.VMEM)
    any_space = pl.BlockSpec(memory_space=pl.ANY)
    blocks = ranks + rows // PROMPT_DEV - 1
    return pl.pallas_call(
        front_kernel,
        out_shape=(
            jax.ShapeDtypeStruct((rows, width), low),
            jax.ShapeDtypeStruct((rows, width), low),
            jax.ShapeDtypeStruct((rows, width), low),
            jax.ShapeDtypeStruct((rows, local), low),
            jax.ShapeDtypeStruct((rows, local), low),
            jax.ShapeDtypeStruct((blocks, PROMPT_DEV, 2 * local), low),
            jax.ShapeDtypeStruct((rows, local), full),
            jax.ShapeDtypeStruct((rows, local), full),
            jax.ShapeDtypeStruct((rows, LANE), full),
            jax.ShapeDtypeStruct((ranks,) + routes.shape, jnp.int32),
            jax.ShapeDtypeStruct((ranks, rows, width), low),
        ),
        in_specs=[vmem] * 4 + [any_space] * 3 + [vmem] * 3 + [any_space, vmem],
        out_specs=(vmem,) * 10 + (any_space,),
        scratch_shapes=[
            pltpu.VMEM((rows, width), low),
            pltpu.VMEM((rows, width), low),
            Line.spare_shape(rows, width),
            pltpu.VMEM((PROMPT_DEV, 2 * local), low),
            pltpu.VMEM((8, rows), full),
            pltpu.VMEM((size - 1, 8, rows), full),
            pltpu.VMEM((rows, LANE), full),
            *(pltpu.VMEM(array.shape, array.dtype) for array in (w_key, w_value, w_out, bias)),
            pltpu.SemaphoreType.DMA((4,)),
            Line.semaphores(rows),
            pltpu.SemaphoreType.DMA((size - 1,)),
            pltpu.SemaphoreType.DMA((size - 1,)),
            *Gather.semaphores(2),
            *Gather.semaphores(2),
            *Gather.semaphores(rows // SPREAD),
        ],
        compiler_params=pltpu.CompilerParams(
            collective_id=1, has_side_effects=True, vmem_limit_bytes=60 * 2**20
        ),
        cost_estimate=pl.CostEstimate(flops=100 * 10**9, bytes_accessed=200 * 10**6, transcendentals=0),
    )(tokens, attn_gain, ffn_gain, w_query, w_key, w_value, w_out, qk_gain, cosine, sine, bias, routes)


def backward_kernel(
    reduced, tokens, attention, cotangent, normed_two, router, expert_bias, routed, ffn_gain,
    out_far, turned_far, keys_far, bias_far, stats, query_far, raw_far, cosine, sine, qk_gain,
    query_out, key_out, value_out, gain_out, hidden_grad, attention_grad, extras,
    out_grad, query_grad, prompt_grads, own_grads, own, paired, from_x, from_y, mine, theirs,
    w_out, query_rot, keys_values, bias, query_raw, key_raw, load_sems,
    pair_sems, x_sems, y_sems, peer_sent, peer_got,
    *,
    gain_column,
):
    rows, local = query_rot.shape
    width = attention_grad.shape[1]
    heads = local // HD
    factor = HD ** (-0.5)
    own_blocks = rows // PROMPT_DEV - 1
    devices = keys_values.shape[0] - own_blocks
    count = keys_values.shape[0] * PROMPT_DEV
    reach = devices * PROMPT_DEV
    plane = Plane(own, prompt_grads, paired, from_x, from_y, pair_sems, x_sems, y_sems, by_device=True)
    peers = Peers(mine, theirs, peer_sent, peer_got)
    load_out, *load_heads, load_query, load_raw = loads(
        (
            (out_far, w_out), (turned_far, query_rot), (keys_far, keys_values), (bias_far, bias),
            (query_far, query_raw), (raw_far, key_raw),
        ),
        load_sems,
    )
    greet(plane.neighbours() + peers.neighbours())
    tile = min(512, width)
    starts = range(0, width, tile)
    scale_two = stats[:, 3:4]
    logits = wide_dot(normed_two[...], router[...]) + expert_bias[...]
    weights = jnp.exp(logits - jnp.max(logits, axis=1, keepdims=True))
    chances = weights / jnp.sum(weights, axis=1, keepdims=True)
    chance_grad = routed[...] * reduced[:, width:].astype(jnp.float32)
    logit_grad = (
        chances * (chance_grad - jnp.sum(chances * chance_grad, axis=1, keepdims=True))
    ).astype(jnp.bfloat16)

    def hidden_of(columns):
        return tokens[:, columns].astype(jnp.float32) + attention[:, columns].astype(jnp.float32)

    def input_part(columns):
        return reduced[:, columns].astype(jnp.float32) + turned_dot(logit_grad, router[columns])

    pull = jnp.zeros((rows, 1), jnp.float32)
    for start in starts:
        columns = slice(start, start + tile)
        weighted = ffn_gain[:, columns] * input_part(columns)
        hidden_grad[:, columns] = weighted
        pull = pull + jnp.sum(weighted * hidden_of(columns), axis=1, keepdims=True)
    pull = scale_two * scale_two * scale_two / width * pull
    for start in starts:
        columns = slice(start, start + tile)
        grad = (
            cotangent[:, columns].astype(jnp.float32)
            + scale_two * hidden_grad[:, columns]
            - hidden_of(columns) * pull
        )
        hidden_grad[:, columns] = grad
        attention_grad[:, columns] = grad.astype(jnp.bfloat16)
    load_out.wait()
    out_grad[...] = turned_dot(attention_grad[...], w_out[...]).astype(jnp.bfloat16)
    for load in load_heads:
        load.wait()
    for head in range(heads):
        columns = slice(head * HD, (head + 1) * HD)
        other = slice(local + head * HD, local + (head + 1) * HD)
        keys = keys_values[:, :, columns].reshape(count, HD)
        values = keys_values[:, :, other].reshape(count, HD)
        query, above = query_rot[:, columns], out_grad[:, columns]
        scores = turned_dot(query, keys) * factor + bias[...]
        shares = jnp.exp(scores - stats[:, 8 + head : 9 + head])
        share_grad = turned_dot(above, values)
        delta = jnp.sum(shares * share_grad, axis=1, keepdims=True)
        score_grad = (shares * (share_grad - delta)).astype(jnp.bfloat16)
        query_grad[:, columns] = wide_dot(score_grad, keys) * factor
        key_grad = crossed_dot(score_grad, query) * factor
        value_grad = crossed_dot(shares.astype(jnp.bfloat16), above)
        prompt_grads[:, :, columns] = key_grad[:reach].astype(jnp.bfloat16).reshape(devices, PROMPT_DEV, HD)
        prompt_grads[:, :, other] = value_grad[:reach].astype(jnp.bfloat16).reshape(devices, PROMPT_DEV, HD)
        own_grads[PROMPT_DEV:, columns] = key_grad[reach:]
        own_grads[PROMPT_DEV:, other] = value_grad[reach:]
    for chip in range(4):
        plane.pair_copy(chip).start()
    for chip in range(4):
        own[chip] = prompt_grads[plane.block(chip, plane.core)]
    for chip in range(4):
        plane.pair_copy(chip).wait_recv()
        if chip < 3:
            plane.send_first(chip)

    def normed_part(source, raw, row, scale):
        inner = jnp.zeros((rows, 1), jnp.float32)
        for head in range(heads):
            columns = slice(head * HD, (head + 1) * HD)
            grad = source[:, columns]
            grad = grad * cosine[...] - swapped(grad) * sine[...]
            gain_out[row : row + 1, columns] = jnp.sum(grad * raw[:, columns] * scale, axis=0, keepdims=True)
            grad = qk_gain[row : row + 1, columns] * grad
            source[:, columns] = grad
            inner = inner + jnp.sum(grad * raw[:, columns], axis=1, keepdims=True)
        return inner

    load_query.wait()
    load_raw.wait()
    scale_query, scale_key = stats[:, 1:2], stats[:, 2:3]
    query_inner = normed_part(query_grad, query_raw, 0, scale_query)
    plane.send_second()
    chosen = lax.broadcasted_iota(jnp.int32, (rows, LANE), 1) == gain_column
    chosen = jnp.where(chosen, 1.0, 0.0).astype(jnp.bfloat16)
    for start in starts:
        columns = slice(start, start + tile)
        sway = input_part(columns) * hidden_of(columns) * scale_two
        extras[columns] = (
            crossed_dot(normed_two[:, columns], logit_grad) + crossed_dot(sway.astype(jnp.bfloat16), chosen)
        ).astype(jnp.bfloat16)

    def last(piece, carry):
        for side, summed in enumerate(plane.last_sum(piece)):
            own_grads[plane.rows(side, piece)] = summed
        return carry

    lax.fori_loop(0, plane.pieces, last, 0)
    key_inner = normed_part(own_grads, key_raw, 1, scale_key)
    mine[...] = to_rows([query_inner, key_inner], rows)
    peers.start()
    value_out[...] = own_grads[:, local:].astype(jnp.bfloat16)
    inner = to_columns(peers.total())
    for out, source, raw, scale, i in (
        (query_out, query_grad, query_raw, scale_query, 0),
        (key_out, own_grads, key_raw, scale_key, 1),
    ):
        pull = scale * scale * scale / width * inner[:, i : i + 1]
        out[...] = (scale * source[:, :local] - raw[...] * pull).astype(jnp.bfloat16)
    plane.finish()
    peers.finish()


def backward(
    reduced, tokens, attention, cotangent, normed_two, router, expert_bias, routed, ffn_gain,
    w_out, query_rot, keys_values, bias, stats, query_raw, key_raw, cosine, sine, qk_gain, gain_column,
):
    rows, local = query_rot.shape
    size = lax.axis_size("tensor")
    ranks = lax.axis_size("expert")
    low, full = jnp.bfloat16, jnp.float32
    vmem = pl.BlockSpec(memory_space=pltpu.VMEM)
    any_space = pl.BlockSpec(memory_space=pl.ANY)
    small = jax.ShapeDtypeStruct((rows, local), low)
    return pl.pallas_call(
        functools.partial(backward_kernel, gain_column=gain_column),
        out_shape=(
            small, small, small, jax.ShapeDtypeStruct((2, local), full),
            jax.ShapeDtypeStruct(tokens.shape, full), jax.ShapeDtypeStruct(tokens.shape, low),
            jax.ShapeDtypeStruct((tokens.shape[1], LANE), low),
        ),
        in_specs=[vmem] * 9 + [any_space] * 4 + [vmem] + [any_space] * 2 + [vmem] * 3,
        out_specs=(vmem,) * 7,
        scratch_shapes=[
            pltpu.VMEM((rows, local), low),
            pltpu.VMEM((rows, local), full),
            pltpu.VMEM((ranks, PROMPT_DEV, 2 * local), low),
            pltpu.VMEM((rows, 2 * local), full),
            pltpu.VMEM((4, PROMPT_DEV, 2 * local), low),
            pltpu.VMEM((4, PROMPT_DEV, 2 * local), low),
            pltpu.VMEM((3, PROMPT_DEV // 2, 2 * local), low),
            pltpu.VMEM((3, PROMPT_DEV // 2, 2 * local), low),
            pltpu.VMEM((8, rows), full),
            pltpu.VMEM((size - 1, 8, rows), full),
            *(
                pltpu.VMEM(array.shape, array.dtype)
                for array in (w_out, query_rot, keys_values, bias, query_raw, key_raw)
            ),
            pltpu.SemaphoreType.DMA((6,)),
            *Plane.semaphores(PROMPT_DEV),
            pltpu.SemaphoreType.DMA((size - 1,)),
            pltpu.SemaphoreType.DMA((size - 1,)),
        ],
        compiler_params=pltpu.CompilerParams(
            collective_id=3, has_side_effects=True, vmem_limit_bytes=60 * 2**20
        ),
    )(
        reduced, tokens, attention, cotangent, normed_two, router, expert_bias, routed, ffn_gain,
        w_out, query_rot, keys_values, bias, stats, query_raw, key_raw, cosine, sine, qk_gain,
    )


def rotate(field, cosine, sine):
    half = field.shape[-1] // 2
    first = field[..., :half]
    second = field[..., half:]
    return jnp.concatenate(
        [first * cosine - second * sine, second * cosine + first * sine], axis=-1
    )


def unrotate(grad, cosine, sine):
    half = grad.shape[-1] // 2
    first = grad[..., :half]
    second = grad[..., half:]
    return jnp.concatenate(
        [first * cosine + second * sine, second * cosine - first * sine], axis=-1
    )


def experts(normed_two, cotangent, gates, w_gate, w_up, w_down, experts_total):
    local_experts = w_gate.shape[0]
    device = lax.axis_index("expert")
    arrived = lax.all_gather(normed_two, "expert", axis=0, tiled=True)
    arrived_grad = lax.all_gather(cotangent, "expert", axis=0, tiled=True)
    gate_pre = jnp.einsum("rd,jdf->jrf", arrived, w_gate, preferred_element_type=jnp.float32)
    up_pre = jnp.einsum("rd,jdf->jrf", arrived, w_up, preferred_element_type=jnp.float32)
    raw_grad = jnp.einsum("rd,jfd->jrf", arrived_grad, w_down, preferred_element_type=jnp.float32)
    sigma = jax.nn.sigmoid(gate_pre)
    activated = gate_pre * sigma
    inner = activated * up_pre
    gated = (gates[:, :, None] * inner).astype(jnp.bfloat16)
    mixed_part = jnp.einsum("jrf,jfd->rd", gated, w_down, preferred_element_type=jnp.float32)
    mixture = lax.psum(
        lax.psum_scatter(
            mixed_part.astype(jnp.bfloat16), "expert", scatter_dimension=0, tiled=True
        ),
        "tensor",
    ).astype(jnp.float32)
    gate_grad_part = jnp.sum(raw_grad * inner, axis=2)
    act_grad = gates[:, :, None] * raw_grad
    up_grad = (act_grad * activated).astype(jnp.bfloat16)
    gate_grad = (act_grad * up_pre * sigma * (1.0 + gate_pre * (1.0 - sigma))).astype(jnp.bfloat16)
    grad_w_down = jnp.einsum("jrf,rd->jfd", gated, arrived_grad, preferred_element_type=jnp.float32)
    grad_w_gate = jnp.einsum("rd,jrf->jdf", arrived, gate_grad, preferred_element_type=jnp.float32)
    grad_w_up = jnp.einsum("rd,jrf->jdf", arrived, up_grad, preferred_element_type=jnp.float32)
    slot_grad = jnp.einsum("jrf,jdf->rd", gate_grad, w_gate, preferred_element_type=jnp.float32)
    slot_grad = slot_grad + jnp.einsum(
        "jrf,jdf->rd", up_grad, w_up, preferred_element_type=jnp.float32
    )
    moe_input_grad = lax.psum(
        lax.psum_scatter(
            slot_grad.astype(jnp.bfloat16), "expert", scatter_dimension=0, tiled=True
        ),
        "tensor",
    ).astype(jnp.float32)
    placed = jnp.zeros((arrived.shape[0], experts_total), jnp.float32)
    placed = lax.dynamic_update_slice_in_dim(placed, gate_grad_part.T, device * local_experts, 1)
    chance_grad = lax.psum(
        lax.psum_scatter(placed, "expert", scatter_dimension=0, tiled=True), "tensor"
    )
    return mixture, moe_input_grad, chance_grad, [grad_w_gate, grad_w_up, grad_w_down]


def body(
    tokens,
    w_query,
    w_key,
    w_value,
    w_out,
    attn_gain,
    ffn_gain,
    qk_gain,
    router,
    w_gate,
    w_up,
    w_down,
    routes,
    cont_group,
    cotangent,
):
    rows, width = tokens.shape
    local_width = w_query.shape[1]
    head_count = local_width // HD
    experts_total = router.shape[1]
    local_experts = w_gate.shape[0]
    ranks = lax.axis_size("expert")
    device = lax.axis_index("expert")
    span = ranks // 2
    prompt_len = PROMPT_DEV * span
    factor = HD ** (-0.5)
    local = jnp.arange(rows, dtype=jnp.int32)
    is_prompt = local < PROMPT_DEV
    after = jnp.maximum(local - PROMPT_DEV, 0)
    slot_cont = after // CLEN
    cont_pick = jnp.sum(
        jnp.where(
            slot_cont[:, None] == jnp.arange(CONT_DEV, dtype=jnp.int32)[None, :],
            cont_group[None, :],
            0,
        ),
        axis=1,
    )
    group = jnp.where(is_prompt, device // span, cont_pick)
    position = jnp.where(is_prompt, device % span * PROMPT_DEV + local, prompt_len + after % CLEN)
    tag = jnp.where(is_prompt, -1, slot_cont)
    frequency = 10000.0 ** (-jnp.arange(HD // 2, dtype=jnp.float32) * 2.0 / HD)
    angle = position.astype(jnp.float32)[:, None] * frequency[None, :]
    cosine = jnp.cos(angle)[:, None, :]
    sine = jnp.sin(angle)[:, None, :]
    source = tokens.astype(jnp.float32)
    scale_one = lax.rsqrt(jnp.mean(source * source, axis=1, keepdims=True) + epsilon)
    normed = (source * scale_one * attn_gain).astype(jnp.bfloat16)
    query_raw = jnp.dot(normed, w_query, preferred_element_type=jnp.float32)
    key_raw = jnp.dot(normed, w_key, preferred_element_type=jnp.float32)
    value_raw = jnp.dot(normed, w_value, preferred_element_type=jnp.float32)
    squares = lax.psum(
        jnp.stack(
            [jnp.sum(query_raw * query_raw, axis=1), jnp.sum(key_raw * key_raw, axis=1)], axis=1
        ),
        "tensor",
    )
    scale_query = lax.rsqrt(squares[:, 0:1] / width + epsilon)
    scale_key = lax.rsqrt(squares[:, 1:2] / width + epsilon)
    query_rot = (
        rotate((query_raw * scale_query * qk_gain[0]).reshape(rows, head_count, HD), cosine, sine)
        .reshape(rows, local_width)
        .astype(jnp.bfloat16)
    )
    key_rot = (
        rotate((key_raw * scale_key * qk_gain[1]).reshape(rows, head_count, HD), cosine, sine)
        .reshape(rows, local_width)
        .astype(jnp.bfloat16)
    )
    value_low = value_raw.astype(jnp.bfloat16)
    prompt_keys, prompt_values = (
        lax.all_gather(key_rot[:PROMPT_DEV], "expert", axis=0, tiled=True),
        lax.all_gather(value_low[:PROMPT_DEV], "expert", axis=0, tiled=True),
    )
    prompt_count = prompt_keys.shape[0]
    all_keys = jnp.concatenate([prompt_keys, key_rot[PROMPT_DEV:]], axis=0)
    all_values = jnp.concatenate([prompt_values, value_low[PROMPT_DEV:]], axis=0)
    key_index = jnp.arange(prompt_count, dtype=jnp.int32)
    prompt_mask = (group[:, None] == (key_index // prompt_len)[None, :]) & (
        (key_index % prompt_len)[None, :] <= position[:, None]
    )
    own_mask = (tag[:, None] == tag[None, PROMPT_DEV:]) & (
        position[None, PROMPT_DEV:] <= position[:, None]
    )
    mask = jnp.concatenate([prompt_mask, own_mask], axis=1)

    def head_scores(query_head, key_head):
        scores = (
            jnp.einsum("qd,kd->qk", query_head, key_head, preferred_element_type=jnp.float32)
            * factor
        )
        return jnp.where(mask, scores, masked_value)

    outputs = []
    log_totals = []
    for head in range(head_count):
        start = head * HD
        scores = head_scores(query_rot[:, start : start + HD], all_keys[:, start : start + HD])
        top = jnp.max(scores, axis=1, keepdims=True)
        weights = jnp.exp(scores - top)
        total = jnp.sum(weights, axis=1, keepdims=True)
        shares = (weights / total).astype(jnp.bfloat16)
        outputs.append(
            jnp.dot(shares, all_values[:, start : start + HD], preferred_element_type=jnp.float32)
        )
        log_totals.append(top + jnp.log(total))
    attended = jnp.concatenate(outputs, axis=1).astype(jnp.bfloat16)
    attention = lax.psum(jnp.dot(attended, w_out, preferred_element_type=jnp.float32), "tensor")
    hidden = source + attention
    scale_two = lax.rsqrt(jnp.mean(hidden * hidden, axis=1, keepdims=True) + epsilon)
    normed_two = (hidden * scale_two * ffn_gain).astype(jnp.bfloat16)
    logits = jnp.dot(normed_two, router, preferred_element_type=jnp.float32)
    top = jnp.max(logits, axis=1, keepdims=True)
    weights = jnp.exp(logits - top)
    chances = weights / jnp.sum(weights, axis=1, keepdims=True)
    hits = (routes[:, :, None] == jnp.arange(experts_total, dtype=jnp.int32)[None, None, :]).astype(
        jnp.float32
    )
    rows_mask = jnp.sum(hits, axis=1)
    routed = lax.all_gather(
        (rows_mask * chances).astype(jnp.float32), "expert", axis=0, tiled=True
    )
    gates = lax.dynamic_slice_in_dim(routed, device * local_experts, local_experts, 1).T
    grad_out = cotangent.astype(jnp.float32)
    pieces = max(1, ranks * rows // 4096)
    piece = rows // pieces
    split_gates = gates.reshape(local_experts, ranks, rows)
    results = []
    weight_grads = None
    for number in range(pieces):
        part = slice(number * piece, (number + 1) * piece)
        sources = (normed_two[part], cotangent[part])
        if results:
            sources, results, weight_grads = lax.optimization_barrier(
                (sources, results, weight_grads)
            )
        *result, grads = experts(
            *sources,
            split_gates[:, :, part].reshape(local_experts, ranks * piece),
            w_gate,
            w_up,
            w_down,
            experts_total,
        )
        results.append(result)
        weight_grads = grads if weight_grads is None else [a + b for a, b in zip(weight_grads, grads)]
    mixture, moe_input_grad, chance_grad = (
        jnp.concatenate(list(group_of), axis=0) for group_of in zip(*results)
    )
    grad_w_gate, grad_w_up, grad_w_down = weight_grads
    chance_grad = rows_mask * chance_grad
    output = (hidden + mixture).astype(jnp.bfloat16)
    logit_grad = (
        chances * (chance_grad - jnp.sum(chances * chance_grad, axis=1, keepdims=True))
    ).astype(jnp.bfloat16)
    grad_router = jnp.einsum(
        "td,te->de", normed_two, logit_grad, preferred_element_type=jnp.float32
    )
    normed_two_grad = moe_input_grad + jnp.einsum(
        "te,de->td", logit_grad, router, preferred_element_type=jnp.float32
    )
    weighted_two = ffn_gain * normed_two_grad
    grad_ffn_gain = jnp.sum(normed_two_grad * hidden * scale_two, axis=0)
    hidden_grad = (
        grad_out
        + scale_two * weighted_two
        - hidden * (scale_two**3 / width) * jnp.sum(weighted_two * hidden, axis=1, keepdims=True)
    )
    attention_grad = hidden_grad.astype(jnp.bfloat16)
    grad_w_out = jnp.einsum(
        "td,te->de", attended, attention_grad, preferred_element_type=jnp.float32
    )
    attended_grad = jnp.einsum(
        "te,de->td", attention_grad, w_out, preferred_element_type=jnp.float32
    ).astype(jnp.bfloat16)
    query_grads = []
    key_grads = []
    value_grads = []
    for head in range(head_count):
        start = head * HD
        query_head = query_rot[:, start : start + HD]
        key_head = all_keys[:, start : start + HD]
        value_head = all_values[:, start : start + HD]
        out_grad_head = attended_grad[:, start : start + HD]
        recomputed = jnp.exp(head_scores(query_head, key_head) - log_totals[head])
        share_grad = jnp.einsum(
            "qd,kd->qk", out_grad_head, value_head, preferred_element_type=jnp.float32
        )
        delta = jnp.sum(recomputed * share_grad, axis=1, keepdims=True)
        score_grad = (recomputed * (share_grad - delta)).astype(jnp.bfloat16)
        query_grads.append(
            jnp.dot(score_grad, key_head, preferred_element_type=jnp.float32) * factor
        )
        key_grads.append(
            jnp.einsum("qk,qd->kd", score_grad, query_head, preferred_element_type=jnp.float32)
            * factor
        )
        value_grads.append(
            jnp.einsum(
                "qk,qd->kd",
                recomputed.astype(jnp.bfloat16),
                out_grad_head,
                preferred_element_type=jnp.float32,
            )
        )
    key_grad_all = jnp.concatenate(key_grads, axis=1)
    value_grad_all = jnp.concatenate(value_grads, axis=1)
    prompt_key_grad, prompt_value_grad = (
        lax.psum_scatter(
            key_grad_all[:prompt_count].astype(jnp.bfloat16),
            "expert",
            scatter_dimension=0,
            tiled=True,
        ).astype(jnp.float32),
        lax.psum_scatter(
            value_grad_all[:prompt_count].astype(jnp.bfloat16),
            "expert",
            scatter_dimension=0,
            tiled=True,
        ).astype(jnp.float32),
    )
    key_grad = jnp.concatenate([prompt_key_grad, key_grad_all[prompt_count:]], axis=0)
    value_grad = jnp.concatenate([prompt_value_grad, value_grad_all[prompt_count:]], axis=0)
    query_grad = unrotate(
        jnp.concatenate(query_grads, axis=1).reshape(rows, head_count, HD), cosine, sine
    ).reshape(rows, local_width)
    key_grad = unrotate(key_grad.reshape(rows, head_count, HD), cosine, sine).reshape(
        rows, local_width
    )
    grad_qk_gain = jnp.stack(
        [
            jnp.sum(query_grad * query_raw * scale_query, axis=0),
            jnp.sum(key_grad * key_raw * scale_key, axis=0),
        ],
        axis=0,
    )
    weighted_query = qk_gain[0] * query_grad
    weighted_key = qk_gain[1] * key_grad
    inner_sums = lax.psum(
        jnp.stack(
            [jnp.sum(weighted_query * query_raw, axis=1), jnp.sum(weighted_key * key_raw, axis=1)],
            axis=1,
        ),
        "tensor",
    )
    query_raw_grad = (
        scale_query * weighted_query - query_raw * (scale_query**3 / width) * inner_sums[:, 0:1]
    ).astype(jnp.bfloat16)
    key_raw_grad = (
        scale_key * weighted_key - key_raw * (scale_key**3 / width) * inner_sums[:, 1:2]
    ).astype(jnp.bfloat16)
    value_raw_grad = value_grad.astype(jnp.bfloat16)
    grad_w_query = jnp.einsum(
        "td,te->de", normed, query_raw_grad, preferred_element_type=jnp.float32
    )
    grad_w_key = jnp.einsum("td,te->de", normed, key_raw_grad, preferred_element_type=jnp.float32)
    grad_w_value = jnp.einsum(
        "td,te->de", normed, value_raw_grad, preferred_element_type=jnp.float32
    )
    normed_part = jnp.einsum(
        "te,de->td", query_raw_grad, w_query, preferred_element_type=jnp.float32
    )
    normed_part = normed_part + jnp.einsum(
        "te,de->td", key_raw_grad, w_key, preferred_element_type=jnp.float32
    )
    normed_part = normed_part + jnp.einsum(
        "te,de->td", value_raw_grad, w_value, preferred_element_type=jnp.float32
    )
    normed_grad = lax.psum(normed_part.astype(jnp.bfloat16), "tensor").astype(jnp.float32)
    weighted_one = attn_gain * normed_grad
    grad_attn_gain = jnp.sum(normed_grad * source * scale_one, axis=0)
    input_grad = (
        hidden_grad
        + scale_one * weighted_one
        - source * (scale_one**3 / width) * jnp.sum(weighted_one * source, axis=1, keepdims=True)
    )
    summed = (
        lax.psum_scatter(
            grad_w_query.astype(jnp.bfloat16), "expert", scatter_dimension=0, tiled=True
        ).astype(jnp.float32),
        lax.psum_scatter(
            grad_w_key.astype(jnp.bfloat16), "expert", scatter_dimension=0, tiled=True
        ).astype(jnp.float32),
        lax.psum_scatter(
            grad_w_value.astype(jnp.bfloat16), "expert", scatter_dimension=0, tiled=True
        ).astype(jnp.float32),
        lax.psum_scatter(
            grad_w_out.astype(jnp.bfloat16), "expert", scatter_dimension=1, tiled=True
        ).astype(jnp.float32),
        lax.psum_scatter(
            grad_attn_gain.astype(jnp.bfloat16), "expert", scatter_dimension=0, tiled=True
        ).astype(jnp.float32),
        lax.psum_scatter(
            grad_ffn_gain.astype(jnp.bfloat16), "expert", scatter_dimension=0, tiled=True
        ).astype(jnp.float32),
        lax.psum_scatter(
            grad_qk_gain.astype(jnp.bfloat16), "expert", scatter_dimension=1, tiled=True
        ).astype(jnp.float32),
        lax.psum_scatter(
            grad_router.astype(jnp.bfloat16), "expert", scatter_dimension=0, tiled=True
        ).astype(jnp.float32),
    )
    return (
        output,
        input_grad,
        summed[0],
        summed[1],
        summed[2],
        summed[3],
        summed[4],
        summed[5],
        summed[6],
        summed[7],
        grad_w_gate,
        grad_w_up,
        grad_w_down,
    )


def compact(
    tokens, w_query, w_key, w_value, w_out, attn_gain, ffn_gain, qk_gain, router, w_gate, w_up, w_down,
    routes, cont_group, cotangent,
):
    rows, width = tokens.shape
    local_width = w_query.shape[1]
    head_count = local_width // HD
    experts_total = router.shape[1]
    local_experts = w_gate.shape[0]
    ranks = lax.axis_size("expert")
    device = lax.axis_index("expert")
    full = jnp.float32
    group, position, tag = layout(rows, ranks, device, cont_group)
    channel = jnp.arange(HD)
    frequency = 10000.0 ** (-(channel % (HD // 2)).astype(full) * 2.0 / HD)
    angle = position.astype(full)[:, None] * frequency[None, :]
    cosine = jnp.cos(angle)
    sine = jnp.sin(angle) * jnp.where(channel < HD // 2, -1.0, 1.0)
    bias = jnp.where(attention_mask(group, position, tag, ranks), 0.0, masked_value).astype(full)
    all_experts = jnp.pad(router, ((0, 0), (0, LANE - experts_total)))
    expert_bias = jnp.where(jnp.arange(LANE) < experts_total, 0.0, masked_value).astype(full)[None]
    turned_routes = jnp.tile(jnp.pad(routes.T, ((0, -routes.shape[1] % 8), (0, 0)), constant_values=-1), (2, 1))
    hits = routes[:, :, None] == jnp.arange(experts_total, dtype=jnp.int32)
    routed = jnp.pad(jnp.any(hits, axis=1).astype(full), ((0, 0), (0, LANE - experts_total)))
    (
        attention, normed, normed_two, attended, query_rot, keys_values, query_raw, key_raw, stats, routes_all, arrived,
    ) = front(
        tokens, attn_gain[None], ffn_gain[None], w_query, w_key, w_value, w_out, qk_gain, cosine, sine, bias,
        turned_routes,
    )
    arrived_grad = lax.all_gather(cotangent, "expert", axis=0)
    names = routes_all[:, : turned_routes.shape[0] // 2]
    own_expert = device * local_experts + jnp.arange(local_experts, dtype=jnp.int32)
    expert_mask = jnp.any(names[:, :, :, None] == own_expert, axis=1).astype(full)
    expert_mask = jnp.pad(expert_mask, ((0, 0), (0, 0), (0, LANE - local_experts)))
    reduced, gated, gate_grad, up_grad, mixed_part = experts_fused(
        arrived, arrived_grad, expert_mask, all_experts, expert_bias, w_gate, w_up, w_down
    )
    (
        query_raw_grad, key_raw_grad, value_raw_grad, grad_qk_gain, hidden_grad, attention_grad, extras,
    ) = backward(
        reduced, tokens, attention, cotangent, normed_two, all_experts, expert_bias, routed, ffn_gain[None],
        w_out, query_rot, keys_values, bias, stats, query_raw, key_raw, cosine, sine, qk_gain, experts_total,
    )
    small_part = local_width // ranks
    share = width // ranks
    gains = grad_qk_gain.reshape(2, ranks, small_part).transpose(1, 2, 0).astype(jnp.bfloat16)
    extras = extras.reshape(ranks, share, LANE) + jnp.pad(
        gains, ((0, 0), (0, share - small_part), (experts_total + 1, LANE - experts_total - 3))
    )
    normed_grad, sums, w_out_grad, gain_total, mixture, grad_w_gate, grad_w_up, grad_w_down = closing(
        normed, query_raw_grad, key_raw_grad, value_raw_grad, attended, attention_grad, extras, w_query, w_key, w_value,
        mixed_part, arrived, arrived_grad, gated, gate_grad, up_grad, local_experts, experts_total + 3,
    )
    source = tokens.astype(full)
    hidden = source + attention.astype(full)
    scale_one = stats[:, 0:1]
    normed_grad = normed_grad.astype(full)
    output = (hidden + mixture.astype(full)).astype(jnp.bfloat16)
    weighted_one = attn_gain * normed_grad
    input_grad = (
        hidden_grad
        + scale_one * weighted_one
        - source * (scale_one**3 / width) * jnp.sum(weighted_one * source, axis=1, keepdims=True)
    )
    edge = 4 * local_width
    return (
        output,
        input_grad,
        sums[:, :local_width],
        sums[:, local_width : 2 * local_width],
        sums[:, 2 * local_width : 3 * local_width],
        w_out_grad,
        gain_total[0] / lax.dynamic_slice_in_dim(attn_gain, device * share, share),
        sums[:, edge + experts_total],
        sums[:small_part, edge + experts_total + 1 : edge + experts_total + 3].T,
        sums[:, edge : edge + experts_total],
        grad_w_gate.astype(full),
        grad_w_up.astype(full),
        grad_w_down.astype(full),
    )


def layout(rows, ranks, device, cont_group):
    span = ranks // 2
    prompt_len = PROMPT_DEV * span
    local = jnp.arange(rows, dtype=jnp.int32)
    is_prompt = local < PROMPT_DEV
    after = jnp.maximum(local - PROMPT_DEV, 0)
    slot_cont = after // CLEN
    cont_pick = jnp.sum(
        jnp.where(
            slot_cont[:, None] == jnp.arange(CONT_DEV, dtype=jnp.int32)[None, :], cont_group[None, :], 0
        ),
        axis=1,
    )
    group = jnp.where(is_prompt, device // span, cont_pick)
    position = jnp.where(is_prompt, device % span * PROMPT_DEV + local, prompt_len + after % CLEN)
    tag = jnp.where(is_prompt, -1, slot_cont)
    return group, position, tag


def attention_mask(group, position, tag, ranks):
    prompt_len = PROMPT_DEV * (ranks // 2)
    key_index = jnp.arange(ranks * PROMPT_DEV, dtype=jnp.int32)
    prompt_mask = (group[:, None] == (key_index // prompt_len)[None, :]) & (
        (key_index % prompt_len)[None, :] <= position[:, None]
    )
    own_mask = (tag[:, None] == tag[None, PROMPT_DEV:]) & (
        position[None, PROMPT_DEV:] <= position[:, None]
    )
    return jnp.concatenate([prompt_mask, own_mask], axis=1)


def solution(mesh):
    small = mesh.shape["expert"] == 8
    return jax.shard_map(
        compact if small else body,
        mesh=mesh,
        in_specs=(
            P("expert", None),
            P(None, "tensor"),
            P(None, "tensor"),
            P(None, "tensor"),
            P("tensor", None),
            P(),
            P(),
            P(None, "tensor"),
            P(),
            P("expert", None, "tensor"),
            P("expert", None, "tensor"),
            P("expert", "tensor", None),
            P("expert", None),
            P("expert"),
            P("expert", None),
        ),
        out_specs=(
            P("expert", None),
            P("expert", None),
            P("expert", "tensor"),
            P("expert", "tensor"),
            P("expert", "tensor"),
            P("tensor", "expert"),
            P("expert"),
            P("expert"),
            P(None, ("tensor", "expert")),
            P("expert", None),
            P("expert", None, "tensor"),
            P("expert", None, "tensor"),
            P("expert", "tensor", None),
        ),
        check_vma=False,
    )
```
